32 devices in a mesh: grp: 2 (over x), ens: 4 (over y, core), dp: 4 (over z).
Axes of the slice: x: 2, y: 2, z: 4, core: 2. Of those that a mesh axis runs over, the one named last changes fastest.
Arguments:
- states: float32 [16384, 34], P('dp'), may hold values from -6 to 6
- actions: float32 [16384, 6], P('dp'), may hold values from -0.95 to 0.95
- rewards: float32 [16384], P('dp'), may hold values from -6 to 6
- done: int32 [16384], P('dp'), may hold values 0 or 1
- noise: float32 [16384, 12], P('dp'), may hold values from -5 to 5
- counts: int32 [4], P('dp'), may hold values from 1 to 4096, as said below
- crit_edge: float32 [2, 8, 24, 256], P('grp', 'ens'), may hold values from -0.75 to 0.75
- crit_hidden: float32 [2, 8, 2, 256, 256], P('grp', 'ens'), may hold values from -0.375 to 0.375
- crit_bias: float32 [2, 8, 4, 256], P('grp', 'ens'), may hold values from -1 to 1
- edge_m: float32 [8, 24, 256], P('ens'), may hold values from -0.03125 to 0.03125
- edge_v: float32 [8, 24, 256], P('ens'), may hold values from 6.1035156e-05 to 0.00024414062
- hidden_m: float32 [8, 2, 256, 256], P('ens'), may hold values from -0.0046875 to 0.0046875
- hidden_v: float32 [8, 2, 256, 256], P('ens'), may hold values from 1.3732911e-06 to 5.4931643e-06
- bias_m: float32 [8, 4, 256], P('ens'), may hold values from -0.0125 to 0.0125
- bias_v: float32 [8, 4, 256], P('ens'), may hold values from 9.765625e-06 to 3.90625e-05
- act_edge: float32 [29, 256], replicated, may hold values from -0.75 to 0.75
- act_hidden: float32 [2, 256, 256], replicated, may hold values from -0.375 to 0.375
- act_bias: float32 [4, 256], replicated, may hold values from -1 to 1
- act_edge_m: float32 [29, 256], replicated, may hold values from -0.003125 to 0.003125
- act_edge_v: float32 [29, 256], replicated, may hold values from 6.1035155e-07 to 2.4414062e-06
- act_hidden_m: float32 [2, 256, 256], replicated, may hold values from -0.003125 to 0.003125
- act_hidden_v: float32 [2, 256, 256], replicated, may hold values from 6.1035155e-07 to 2.4414062e-06
- act_bias_m: float32 [4, 256], replicated, may hold values from -0.003125 to 0.003125
- act_bias_v: float32 [4, 256], replicated, may hold values from 6.1035155e-07 to 2.4414062e-06
Outputs:
- new_crit_edge: float32 [2, 8, 24, 256], P('grp', 'ens')
- new_crit_hidden: float32 [2, 8, 2, 256, 256], P('grp', 'ens')
- new_crit_bias: float32 [2, 8, 4, 256], P('grp', 'ens')
- new_edge_m: float32 [8, 24, 256], P('ens')
- new_edge_v: float32 [8, 24, 256], P('ens')
- new_hidden_m: float32 [8, 2, 256, 256], P('ens')
- new_hidden_v: float32 [8, 2, 256, 256], P('ens')
- new_bias_m: float32 [8, 4, 256], P('ens')
- new_bias_v: float32 [8, 4, 256], P('ens')
- new_act_edge: float32 [29, 256], replicated
- new_act_hidden: float32 [2, 256, 256], replicated
- new_act_bias: float32 [4, 256], replicated
- new_act_edge_m: float32 [29, 256], replicated
- new_act_edge_v: float32 [29, 256], replicated
- new_act_hidden_m: float32 [2, 256, 256], replicated
- new_act_hidden_v: float32 [2, 256, 256], replicated
- new_act_bias_m: float32 [4, 256], replicated
- new_act_bias_v: float32 [4, 256], replicated
- member_sums: float32 [8, 2], P('ens')
- actor_sums: float32 [2], replicated
The draws below stay inside these ranges and needn't reach their ends.
Inputs may be any that keep to these rules, and one draw needn't show every extreme that they name: The counts rise along the shards, and the last shard's count is 4096.
All inputs are finite; a program needn't handle non-finite values. No bound on the sum of `done` on one device may be relied on, other than what follows from the above.
Results may differ from the reference program's by a relative error of at most 0.0003.
Values may be sent and summed in bfloat16 or wider, within the bound.
A program may use at most 704 MiB of HBM per device.

```python
import math
import jax
import jax.numpy as jnp
from jax import lax

OBS = 17
ACT = 6
HID = 256
ROWS_DEV = 4096
STEP = 5
CRITICS = 8
TOTAL = 16384
N_GRP = 2
N_DP = 4


def draw_counts(key, part):
    key = jax.random.fold_in(key, 7)
    shard = jnp.arange(N_DP, dtype=jnp.int32)
    floor_count = ROWS_DEV // 3
    base = floor_count + (ROWS_DEV - floor_count) * shard // max(N_DP - 1, 1)
    jitter = jax.random.randint(key, (N_DP,), 0, ROWS_DEV // 8 + 1, dtype=jnp.int32)
    drawn = jnp.clip(base - jitter, 1, ROWS_DEV)
    return jnp.where(shard == N_DP - 1, ROWS_DEV, drawn).astype(jnp.int32)


def set_ends(result, key, smallest, high):
    place = [jax.random.randint(jax.random.fold_in(key, axis), (), 0, length) for axis, length in enumerate(result.shape)]
    main_axis = result.shape.index(max(result.shape))
    neighbour = place[:main_axis] + [(place[main_axis] + 1) % result.shape[main_axis]] + place[main_axis + 1:]
    return result.at[tuple(place)].set(smallest).at[tuple(neighbour)].set(high)


def block_scale(rng, dims, split, smallest, largest):
    factor_of = 1.0
    for dim, shards_of in split:
        draws = jax.random.uniform(jax.random.fold_in(jax.random.fold_in(rng, 6), dim), (shards_of,), jnp.float32, smallest / len(split), largest / len(split))
        factor_of = factor_of * jnp.repeat(jnp.exp(draws), dims[dim] // shards_of).reshape((-1,) + (1,) * (len(dims) - 1 - dim))
    return factor_of


def scatter_about(own_key, shape, width, reach, cuts=(), kind=jnp.bfloat16):
    values = width * jax.random.normal(own_key, shape, jnp.float32)
    if cuts:
        values = values * block_scale(own_key, shape, cuts, -0.22, 0.18)
    return jnp.clip(values, -reach, reach).astype(kind)


def setup_inputs(seed: int = 0) -> dict:
    seeds = jax.random.split(jax.random.key(seed), 25)
    return {
        "states": scatter_about(seeds[0], (TOTAL, 2 * OBS), 1.0, 6.0, ((0, 4),), jnp.float32),
        "actions": jnp.clip(jax.random.uniform(seeds[1], (TOTAL, ACT), jnp.float32, -0.95, 0.95) * block_scale(seeds[1], (TOTAL, ACT), ((0, 4),), -0.4, 0.0), -0.95, 0.95),
        "rewards": scatter_about(seeds[2], (TOTAL,), 1.0, 6.0, ((0, 4),), jnp.float32),
        "done": set_ends((jax.random.randint(seeds[3], (TOTAL,), 0, 8) < 1).astype(jnp.int32), jax.random.fold_in(seeds[3], 1), 0, 1),
        "noise": scatter_about(seeds[4], (TOTAL, 2 * ACT), 1.0, 5.0, ((0, 4),), jnp.float32),
        "counts": draw_counts(jax.random.fold_in(seeds[24], 71), 0),
        "crit_edge": scatter_about(seeds[6], (N_GRP, CRITICS, OBS + ACT + 1, HID), 64 ** -0.5, 0.75, ((0, 2), (1, 4)), jnp.float32),
        "crit_hidden": scatter_about(seeds[7], (N_GRP, CRITICS, 2, HID, HID), HID ** -0.5, 0.375, ((0, 2), (1, 4)), jnp.float32),
        "crit_bias": scatter_about(seeds[8], (N_GRP, CRITICS, 4, HID), 0.2, 1.0, ((0, 2), (1, 4)), jnp.float32),
        "edge_m": scatter_about(seeds[9], (CRITICS, OBS + ACT + 1, HID), (1.0 / (N_DP * ROWS_DEV) ** 0.5), 0.03125, ((0, 4),), jnp.float32),
        "edge_v": jnp.clip(jnp.exp(math.log(0.00024414062) - 1.3862944 * jax.random.uniform(seeds[10], (CRITICS, OBS + ACT + 1, HID), jnp.float32) ** block_scale(seeds[10], (CRITICS, OBS + ACT + 1, HID), ((0, 4),), -0.2, 0.2)), 6.103515625e-05, 0.00024414062),
        "hidden_m": scatter_about(seeds[11], (CRITICS, 2, HID, HID), (0.15 / (N_DP * ROWS_DEV) ** 0.5), 0.0046875, ((0, 4),), jnp.float32),
        "hidden_v": jnp.clip(jnp.exp(math.log(5.4931642807787284e-06) - 1.3862944 * jax.random.uniform(seeds[12], (CRITICS, 2, HID, HID), jnp.float32) ** block_scale(seeds[12], (CRITICS, 2, HID, HID), ((0, 4),), -0.2, 0.2)), 1.3732910701946821e-06, 5.4931642807787284e-06),
        "bias_m": scatter_about(seeds[13], (CRITICS, 4, HID), (0.4 / (N_DP * ROWS_DEV) ** 0.5), 0.0125, ((0, 4),), jnp.float32),
        "bias_v": jnp.clip(jnp.exp(math.log(3.9062499126885086e-05) - 1.3862944 * jax.random.uniform(seeds[14], (CRITICS, 4, HID), jnp.float32) ** block_scale(seeds[14], (CRITICS, 4, HID), ((0, 4),), -0.2, 0.2)), 9.765624781721272e-06, 3.9062499126885086e-05),
        "act_edge": scatter_about(seeds[15], (OBS + 2 * ACT, HID), 64 ** -0.5, 0.75, (), jnp.float32),
        "act_hidden": scatter_about(seeds[16], (2, HID, HID), HID ** -0.5, 0.375, (), jnp.float32),
        "act_bias": scatter_about(seeds[17], (4, HID), 0.2, 1.0, (), jnp.float32),
        "act_edge_m": scatter_about(seeds[18], (OBS + 2 * ACT, HID), (0.1 / (N_DP * ROWS_DEV) ** 0.5), 0.003125, (), jnp.float32),
        "act_edge_v": jnp.clip(jnp.exp(jax.random.uniform(seeds[19], (OBS + 2 * ACT, HID), jnp.float32, math.log(6.103515488575795e-07), math.log(2.441406195430318e-06))), 6.103515488575795e-07, 2.441406195430318e-06),
        "act_hidden_m": scatter_about(seeds[20], (2, HID, HID), (0.1 / (N_DP * ROWS_DEV) ** 0.5), 0.003125, (), jnp.float32),
        "act_hidden_v": jnp.clip(jnp.exp(jax.random.uniform(seeds[21], (2, HID, HID), jnp.float32, math.log(6.103515488575795e-07), math.log(2.441406195430318e-06))), 6.103515488575795e-07, 2.441406195430318e-06),
        "act_bias_m": scatter_about(seeds[22], (4, HID), (0.1 / (N_DP * ROWS_DEV) ** 0.5), 0.003125, (), jnp.float32),
        "act_bias_v": jnp.clip(jnp.exp(jax.random.uniform(seeds[23], (4, HID), jnp.float32, math.log(6.103515488575795e-07), math.log(2.441406195430318e-06))), 6.103515488575795e-07, 2.441406195430318e-06),
    }


GAMMA = 0.99
ALPHA = 0.2
ETA = 1.0
LEARN = 0.03
BETA_ONE = 0.5
BETA_TWO = 0.5
DECAY = 0.01
EPS = 1e-08
TAU = 0.05
LOG_LO = -5.0
LOG_HI = 2.0
HALF_LOG_TWO_PI = 0.9189385332046727
LOG_TWO = 0.6931471805599453

@jax.custom_vjp
def low(v):
    return lax.optimization_barrier(v.astype(jnp.bfloat16)).astype(jnp.float32)

@jax.custom_vjp
def low_back(v):
    return v

def low_keep(v):
    return (low(v), None)

def low_pass(kept, grad):
    return (grad,)

def back_keep(v):
    return (v, None)

def back_low(kept, grad):
    return (low(grad),)
low.defvjp(low_keep, low_pass)
low_back.defvjp(back_keep, back_low)

def matmul(left, right):
    return jnp.dot(left, right, precision=lax.Precision.HIGHEST)

def critic_q(edge, hidden, bias, inputs):
    layer = jax.nn.silu(matmul(inputs, edge[:-1]) + bias[0])
    layer = jax.nn.silu(matmul(layer, hidden[0]) + bias[1])
    layer = jax.nn.silu(matmul(layer, hidden[1]) + bias[2])
    return matmul(layer, edge[-1]) + bias[3, 0]

def actor_sample(edge, hidden, bias, observ, normal):
    layer = jax.nn.silu(matmul(observ, edge[:OBS]) + bias[0])
    layer = jax.nn.silu(matmul(layer, hidden[0]) + bias[1])
    layer = jax.nn.silu(matmul(layer, hidden[1]) + bias[2])
    output = matmul(layer, edge[OBS:].T) + bias[3, :2 * ACT]
    center = output[:, :ACT]
    log_std = LOG_LO + 0.5 * (LOG_HI - LOG_LO) * (jnp.tanh(output[:, ACT:]) + 1.0)
    latent = center + jnp.exp(log_std) * normal
    logp = lax.optimization_barrier(jnp.sum(-0.5 * normal * normal - log_std - HALF_LOG_TWO_PI - 2.0 * (LOG_TWO - latent - jax.nn.softplus(-2.0 * latent)), axis=1))
    return (jnp.tanh(latent), logp)

def member_terms(edge, hidden, bias, observ, action):

    def value_of(act_in):
        return critic_q(edge, hidden, bias, jnp.concatenate([observ, act_in], 1))
    value, back = jax.vjp(value_of, action)
    slope = back(jnp.ones_like(value))[0]
    unit = slope * lax.rsqrt(lax.optimization_barrier(jnp.sum(slope * slope, 1, keepdims=True)) + 0.01)
    return (value, unit)

def adamw(param, grad, first, second):
    first_new = BETA_ONE * first + (1.0 - BETA_ONE) * grad
    second_new = BETA_TWO * second + (1.0 - BETA_TWO) * grad * grad
    ratio = first_new / (1.0 - BETA_ONE ** STEP) / (jnp.sqrt(second_new / (1.0 - BETA_TWO ** STEP)) + EPS)
    return (param - LEARN * (ratio + DECAY * param), first_new, second_new)

def reference(states, actions, rewards, done, noise, counts, crit_edge, crit_hidden, crit_bias, edge_m, edge_v, hidden_m, hidden_v, bias_m, bias_v, act_edge, act_hidden, act_bias, act_edge_m, act_edge_v, act_hidden_m, act_hidden_v, act_bias_m, act_bias_v):
    observ = states[:, :OBS]
    nexts = states[:, OBS:]
    row_ids = jnp.arange(states.shape[0], dtype=jnp.int32)
    valid = (row_ids % ROWS_DEV < counts[row_ids // ROWS_DEV]).astype(jnp.float32)
    total = jnp.sum(counts).astype(jnp.float32)
    next_act, next_logp = actor_sample(act_edge, act_hidden, act_bias, nexts, noise[:, ACT:])
    next_in = jnp.concatenate([nexts, next_act], 1)
    target_q = lax.map(lambda p: critic_q(p[0], p[1], p[2], next_in), (crit_edge[0], crit_hidden[0], crit_bias[0]))
    target = rewards + GAMMA * (1.0 - done.astype(jnp.float32)) * (lax.optimization_barrier(jnp.min(target_q, 0)) - ALPHA * next_logp)
    online = (crit_edge[1], crit_hidden[1], crit_bias[1])

    def critic_loss(params):
        value, unit = lax.map(lambda p: member_terms(p[0], p[1], p[2], observ, actions), params)
        spread = lax.optimization_barrier(jnp.sum(unit, 0))
        errors = lax.optimization_barrier(jnp.sum(valid * (value - target) ** 2, 1))
        diverse = lax.optimization_barrier(jnp.sum(valid * lax.optimization_barrier(jnp.sum(unit * (spread - unit), 2)), 1))
        loss = (jnp.sum(errors) + ETA / (CRITICS - 1) * jnp.sum(diverse)) / total
        return (loss, jnp.stack([errors, diverse], 1))
    loss_c, back_c, member_sums = jax.vjp(critic_loss, online, has_aux=True)
    crit_grads = back_c(jnp.ones_like(loss_c))[0]

    def actor_loss(aparams):
        pi_act, pi_logp = actor_sample(aparams[0], aparams[1], aparams[2], observ, noise[:, :ACT])
        pi_in = jnp.concatenate([observ, pi_act], 1)
        pi_q = lax.map(lambda p: critic_q(p[0], p[1], p[2], pi_in), online)
        summed = jnp.sum(valid * (ALPHA * pi_logp - lax.optimization_barrier(jnp.mean(pi_q, 0))))
        return (summed / total, summed)
    loss_a, back_a, actor_sum = jax.vjp(actor_loss, (act_edge, act_hidden, act_bias), has_aux=True)
    act_grads = back_a(jnp.ones_like(loss_a))[0]
    crit_out = []
    crit_moments = []
    for full, grad, first, second in zip((crit_edge, crit_hidden, crit_bias), crit_grads, (edge_m, hidden_m, bias_m), (edge_v, hidden_v, bias_v)):
        master, first_new, second_new = adamw(full[1], grad, first, second)
        polyak = TAU * low(master) + (1.0 - TAU) * full[0]
        crit_out.append(jnp.stack([polyak, master], 0))
        crit_moments += [first_new, second_new]
    act_out = []
    act_moments = []
    for param, grad, first, second in zip((act_edge, act_hidden, act_bias), act_grads, (act_edge_m, act_hidden_m, act_bias_m), (act_edge_v, act_hidden_v, act_bias_v)):
        master, first_new, second_new = adamw(param, grad, first, second)
        act_out.append(master)
        act_moments += [first_new, second_new]
    actor_sums = jnp.stack([actor_sum, total])
    return (crit_out[0], crit_out[1], crit_out[2], crit_moments[0], crit_moments[1], crit_moments[2], crit_moments[3], crit_moments[4], crit_moments[5], act_out[0], act_out[1], act_out[2], act_moments[0], act_moments[1], act_moments[2], act_moments[3], act_moments[4], act_moments[5], member_sums, actor_sums)
```

```python
import functools

import jax
import jax.numpy as jnp
from jax import lax
from jax.experimental import pallas as pl
from jax.experimental.pallas import tpu as pltpu
from jax.sharding import PartitionSpec as P

OBS = 17
ACT = 6
HID = 256
STEP = 5
BLOCK = 1024

GAMMA = 0.99
ALPHA = 0.2
ETA = 1.0
LEARN = 0.03
BETA_ONE = 0.5
BETA_TWO = 0.5
DECAY = 0.01
EPS = 1e-08
TAU = 0.05
HALF_LOG_TWO_PI = 0.9189385332046727
LOG_TWO = 0.6931471805599453

F32 = jnp.float32
BF16 = jnp.bfloat16

ROW_OBS, ROW_NEXT, ROW_ACT, ROW_NOISE, ROW_NOISE2, ROW_SCAL, ROWS = 0, 24, 48, 56, 64, 72, 80


def dot(a, b):
    return lax.dot_general(a, b, (((1,), (0,)), ((), ())), preferred_element_type=F32)


def dot_t(a, b):
    return lax.dot_general(a, b, (((1,), (1,)), ((), ())), preferred_element_type=F32)


def split(w):
    high = w.astype(BF16).astype(F32)
    return high, w - high


def halves(p):
    n = p.shape[0] // 2
    return p[:n] + p[n:]


def prep_input(stage, w1, edge, bias, n_in):
    stage[...] = jnp.zeros_like(stage)
    stage[0:OBS, :] = edge[0:OBS, :]
    stage[OBS : OBS + 1, :] = bias[0:1, :]
    if n_in > OBS:
        stage[24 : 24 + ACT, :] = edge[OBS : OBS + ACT, :]
    high, low = split(0.5 * stage[0:32, :])
    w1[...] = jnp.concatenate([high, low], 0).T.astype(BF16)


def prep_hidden(fwd, bwd, hidden):
    w = 0.5 * hidden
    if fwd is not None:
        high, low = split(w.T)
        fwd[...] = jnp.concatenate([high, low], 0).astype(BF16)
    if bwd is not None:
        high, low = split(w)
        bwd[...] = jnp.concatenate([high, low], 0).astype(BF16)


def silu_half(u):
    t = jnp.tanh(u)
    return u + u * t, t


def kernel(
    n_dp,
    rows,
    x_in, c_edge, c_hidden, c_bias, a_edge, a_hidden, a_bias,
    out_c, out_a,
    x_b, pi_b, pi_act, stage, vec, tvec, avec,
    p_edge, p_hidden, p_bias,
    w1, f0, f1, b0, b1, ga, t1w, eq,
    tw1, tf0, tf1, teq,
    aw1, af0, af1, ab0, ab1, ao, aot,
    h1x, h2x, h3s, s1, s2, s3, k1, k2, k3, d1s, d2s, d3s,
    ah1x, ah2x, ah3, as1, as2, as3, heads,
    value, unit_f, unit_out, unit_in, dg_b, dv_b,
    slope_out, slope_in, q_own, least, least_in, target,
    acc_h1, acc_h1t, acc_h0, acc_h0t, acc_x, acc_t, acc_last, acc_o,
    sem_param_s, sem_param_r, sem_pi_s, sem_pi_r, sem_least_s, sem_least_r, sem_unit_s, sem_unit_r, sem_slope_s, sem_slope_r,
):
    g = lax.axis_index("grp")
    e = lax.axis_index("ens")
    me = g * 4 + e
    blocks = rows // BLOCK
    half = rows // 2
    online = g == 1
    targetd = g == 0

    def dev(gg, ee):
        return {"grp": gg, "ens": ee}

    def remote(src, dst, send, recv, where):
        return pltpu.make_async_remote_copy(
            src_ref=src, dst_ref=dst, send_sem=send, recv_sem=recv, device_id=where, device_id_type=pl.DeviceIdType.MESH
        )

    barrier = pltpu.get_barrier_semaphore()
    for k in range(1, 8):
        p = lax.rem(me + k, 8)
        pl.semaphore_signal(barrier, inc=1, device_id=dev(p // 4, lax.rem(p, 4)), device_id_type=pl.DeviceIdType.MESH)
    pl.semaphore_wait(barrier, 7)

    def param_copies():
        where = dev(0, e)
        return [
            remote(c_edge.at[1], p_edge, sem_param_s.at[0], sem_param_r.at[0], where),
            remote(c_bias.at[1], p_bias, sem_param_s.at[1], sem_param_r.at[1], where),
            remote(c_hidden.at[1, 0], p_hidden.at[0], sem_param_s.at[2], sem_param_r.at[2], where),
            remote(c_hidden.at[1, 1], p_hidden.at[1], sem_param_s.at[3], sem_param_r.at[3], where),
        ]

    @pl.when(online)
    def _():
        for c in param_copies():
            c.start()

    obs = x_in[ROW_OBS : ROW_OBS + 24, :]
    xin = jnp.concatenate([obs, x_in[ROW_ACT : ROW_ACT + 8, :]], 0).astype(BF16)
    x_b[0:32, :] = xin
    x_b[32:64, :] = xin

    def prep_critic(edge, hid0, hid1, bias, w1_, f0_, f1_, b0_, b1_, vec_, eq_, ga_, t1_):
        prep_input(stage, w1_, edge, bias, OBS + ACT)
        prep_hidden(f0_, b0_, hid0[...])
        prep_hidden(f1_, b1_, hid1[...])
        stage[...] = jnp.zeros_like(stage)
        stage[0:1, :] = 0.5 * bias[1:2, :]
        stage[1:2, :] = 0.5 * bias[2:3, :]
        stage[2:3, :] = edge[23:24, :]
        vec_[...] = stage[...].T
        stage[...] = jnp.zeros_like(stage)
        high, low = split(edge[23:24, :])
        stage[0:1, :] = high
        stage[1:2, :] = low
        eq_[...] = stage[0:16, :].astype(BF16)
        if ga_ is not None:
            stage[...] = jnp.zeros_like(stage)
            stage[0:ACT, :] = 0.5 * edge[OBS : OBS + ACT, :]
            high, low = split(stage[0:8, :])
            both = jnp.concatenate([high, low], 0)
            ga_[...] = both.astype(BF16)
            stage[0:16, :] = both
            t1_[...] = stage[...].T[:, 0:16].astype(BF16)

    def prep_actor():
        prep_input(stage, aw1, a_edge, a_bias, OBS)
        prep_hidden(af0, ab0, a_hidden[0])
        prep_hidden(af1, ab1, a_hidden[1])
        stage[...] = jnp.zeros_like(stage)
        stage[0:1, :] = 0.5 * a_bias[1:2, :]
        stage[1:2, :] = 0.5 * a_bias[2:3, :]
        stage[2:3, :] = a_bias[3:4, :]
        avec[...] = stage[...].T
        stage[...] = jnp.zeros_like(stage)
        stage[0:ACT, :] = a_edge[OBS : OBS + ACT, :]
        stage[8 : 8 + ACT, :] = a_edge[OBS + ACT : OBS + 2 * ACT, :]
        high, low = split(stage[0:16, :])
        both = jnp.concatenate([high, low], 0)
        ao[...] = both.astype(BF16)
        stage[0:32, :] = both
        aot[...] = stage[...].T[:, 0:32].astype(BF16)

    prep_actor()

    def actor_block(src, sl, noise_row, keep):
        u = dot(aw1[...], src[:, sl])
        h, t = silu_half(u)
        hb = h.astype(BF16)
        if keep:
            ah1x[0:HID, sl] = hb
            as1[:, sl] = ((1.0 + t) + h * (1.0 - t)).astype(BF16)
        u = halves(dot(af0[...], hb)) + avec[:, 0:1]
        h, t = silu_half(u)
        hb = h.astype(BF16)
        if keep:
            ah2x[0:HID, sl] = hb
            as2[:, sl] = ((1.0 + t) + h * (1.0 - t)).astype(BF16)
        u = halves(dot(af1[...], hb)) + avec[:, 1:2]
        h, t = silu_half(u)
        hb = h.astype(BF16)
        if keep:
            ah3[:, sl] = hb
            as3[:, sl] = ((1.0 + t) + h * (1.0 - t)).astype(BF16)
        out = halves(dot(ao[...], hb))
        eps = x_in[noise_row : noise_row + 8, sl]
        ok = (lax.broadcasted_iota(jnp.int32, (8, 1), 0) < ACT).astype(F32)
        center = out[0:8] + avec[0:8, 2:3] * ok
        th = jnp.tanh(out[8:16] + avec[6:14, 2:3] * ok)
        log_std = 3.5 * th - 1.5
        spread_e = jnp.exp(log_std) * eps
        latent = center + spread_e
        soft = jnp.maximum(-2.0 * latent, 0.0) + jnp.log(1.0 + jnp.exp(-2.0 * jnp.abs(latent)))
        terms = -0.5 * eps * eps - log_std - HALF_LOG_TWO_PI - 2.0 * (LOG_TWO - latent - soft)
        logp = jnp.sum(terms * ok, axis=0, keepdims=True)
        sample = jnp.tanh(latent) * ok
        return sample, logp, th, spread_e

    @pl.when(online)
    def _():
        ones = (lax.broadcasted_iota(jnp.int32, (16, rows), 0) == 0).astype(BF16)
        ah1x[HID : HID + 16, :] = ones
        ah2x[HID : HID + 16, :] = ones

        def body(i, _):
            sl = pl.ds(pl.multiple_of(i * BLOCK, BLOCK), BLOCK)
            sample, logp, th, spread_e = actor_block(x_b, sl, ROW_NOISE, True)
            pi_act[:, sl] = sample
            heads[0:8, sl] = th
            heads[8:16, sl] = spread_e
            heads[16:17, sl] = logp
            return 0

        lax.fori_loop(0, blocks, body, 0)
        remote(pi_act, pi_act, sem_pi_s, sem_pi_r, dev(0, e)).start()
        prep_critic(c_edge.at[0], c_hidden.at[0, 0], c_hidden.at[0, 1], c_bias.at[0], w1, f0, f1, b0, b1, vec, eq, ga, t1w)
        vec[0:1, 8:9] = c_bias[0, 3:4, 0:1]

    def least_copies():
        out = []
        for k in range(1, 4):
            out.append(remote(least, least_in.at[k], sem_least_s.at[k], sem_least_r.at[k], dev(0, lax.rem(e + k, 4))))
        for k in range(4):
            out.append(remote(least, least_in.at[k], sem_least_s.at[4 + k], sem_least_r.at[k], dev(1, lax.rem(e + k, 4))))
        return out

    @pl.when(targetd)
    def _():
        for m in range(2):
            prep_critic(
                c_edge.at[m], c_hidden.at[m, 0], c_hidden.at[m, 1], c_bias.at[m],
                tw1.at[m], tf0.at[m], tf1.at[m], None, None, tvec.at[m], teq.at[m], None, None,
            )
            tvec[m, 0:1, 8:9] = c_bias[m, 3:4, 0:1]
        pi_b[0:32, :] = jnp.concatenate([x_in[ROW_NEXT : ROW_NEXT + 24, :], jnp.zeros((8, rows), F32)], 0).astype(BF16)
        pi_b[32:64, :] = pi_b[0:32, :]

        def body(i, _):
            sl = pl.ds(pl.multiple_of(i * BLOCK, BLOCK), BLOCK)
            sample, logp, th, spread_e = actor_block(pi_b, sl, ROW_NOISE2, False)
            nx = jnp.concatenate([x_in[ROW_NEXT : ROW_NEXT + 24, sl], sample], 0).astype(BF16)
            nx = jnp.concatenate([nx, nx], 0)
            low = None
            for m in range(2):
                h, t = silu_half(dot(tw1[m], nx))
                h, t = silu_half(halves(dot(tf0[m], h.astype(BF16))) + tvec[m, :, 0:1])
                h, t = silu_half(halves(dot(tf1[m], h.astype(BF16))) + tvec[m, :, 1:2])
                r = dot(teq[m], h.astype(BF16))
                q = r[0:1] + r[1:2] + tvec[m, 0:1, 8:9]
                low = q if low is None else jnp.minimum(low, q)
            least[:, sl] = low - ALPHA * logp
            return 0

        lax.fori_loop(0, blocks, body, 0)
        for c in least_copies():
            c.start()
        for c in param_copies():
            c.wait_recv()
        prep_critic(p_edge, p_hidden.at[0], p_hidden.at[1], p_bias, w1, f0, f1, b0, b1, vec, eq, ga, t1w)
        vec[0:1, 8:9] = p_bias[3:4, 0:1]

    ones = (lax.broadcasted_iota(jnp.int32, (16, rows), 0) == 0).astype(BF16)
    h1x[HID : HID + 16, :] = ones
    h2x[HID : HID + 16, :] = ones

    def curves(u):
        h, t = silu_half(u)
        c = 1.0 + t
        d = 1.0 - t
        return h, c + h * d, (c * d) * (1.0 - u * t)

    def body_a(i, _):
        sl = pl.ds(pl.multiple_of(i * BLOCK, BLOCK), BLOCK)
        h, a1, q1 = curves(dot(w1[...], x_b[:, sl]))
        hb = h.astype(BF16)
        h1x[0:HID, sl] = hb
        s1[:, sl] = a1.astype(BF16)
        h, a2, q2 = curves(halves(dot(f0[...], hb)) + vec[:, 0:1])
        hb = h.astype(BF16)
        h2x[0:HID, sl] = hb
        s2[:, sl] = a2.astype(BF16)
        h, a3, q3 = curves(halves(dot(f1[...], hb)) + vec[:, 1:2])
        hb = h.astype(BF16)
        h3s[:, sl] = hb
        s3[:, sl] = a3.astype(BF16)
        r = dot(eq[...], hb)
        value[:, sl] = r[0:1] + r[1:2] + vec[0:1, 8:9]
        last = vec[:, 2:3]
        db = (last * a3).astype(BF16)
        d3s[:, sl] = db
        k3[:, sl] = (last * q3).astype(BF16)
        m = halves(dot(b1[...], db))
        db = (m * a2).astype(BF16)
        d2s[:, sl] = db
        k2[:, sl] = (m * q2).astype(BF16)
        m = halves(dot(b0[...], db))
        db = (m * a1).astype(BF16)
        d1s[:, sl] = db
        k1[:, sl] = (m * q1).astype(BF16)
        slope = halves(dot(ga[...], db))
        inv = lax.rsqrt(jnp.sum(slope * slope, axis=0, keepdims=True) + 0.01)
        unit_f[0:8, sl] = slope * inv
        unit_f[8:9, sl] = inv
        return 0

    lax.fori_loop(0, blocks, body_a, 0)
    unit_out[...] = jnp.concatenate([unit_f[0:8, 0:half], unit_f[0:8, half:rows]], 0).astype(BF16)

    def unit_copies():
        out = []
        for k in range(1, 8):
            p = lax.rem(me + k, 8)
            out.append(
                remote(unit_out, unit_in.at[k - 1], sem_unit_s.at[k - 1], sem_unit_r.at[k - 1], dev(p // 4, lax.rem(p, 4)))
            )
        return out

    for c in unit_copies():
        c.start()

    @pl.when(targetd)
    def _():
        remote(pi_act, pi_act, sem_pi_s, sem_pi_r, dev(0, e)).wait_recv()

    pin = jnp.concatenate([obs, pi_act[...]], 0).astype(BF16)
    pi_b[0:32, :] = pin
    pi_b[32:64, :] = pin

    def body_p(i, _):
        sl = pl.ds(pl.multiple_of(i * BLOCK, BLOCK), BLOCK)

        def act(u):
            h, t = silu_half(u)
            hb, tb = h.astype(BF16), t.astype(BF16)
            one = jnp.ones((), BF16)
            return hb, (one + tb) + hb * (one - tb)

        h, a1 = act(dot(w1[...], pi_b[:, sl]))
        h, a2 = act(dot(f0[0:HID, :], h) + vec[:, 0:1])
        h, a3 = act(dot(f1[0:HID, :], h) + vec[:, 1:2])
        r = dot(eq[...], h)
        q_own[:, sl] = r[0:1] + r[1:2] + vec[0:1, 8:9]
        d = vec[:, 2:3].astype(BF16) * a3
        d = dot(b1[0:HID, :], d).astype(BF16) * a2
        d = dot(b0[0:HID, :], d).astype(BF16) * a1
        slope = halves(dot(ga[...], d))
        unit_f[16:24, sl] = slope
        return 0

    lax.fori_loop(0, blocks, body_p, 0)
    rid = lax.broadcasted_iota(jnp.int32, (8, 1), 0)
    packed = unit_f[16:24, :] + jnp.where(rid == 6, q_own[...], 0.0)
    slope_out[...] = jnp.concatenate([packed[:, 0:half], packed[:, half:rows]], 0).astype(BF16)

    def slope_copy(k):
        return remote(slope_out, slope_in.at[me_slot(k)], sem_slope_s.at[k], sem_slope_r.at[me_slot(k)], dev(1, lax.rem(e + k, 4)))

    def me_slot(k):
        return g * 4 + k

    @pl.when(targetd)
    def _():
        slope_copy(0).start()

    for k in range(1, 4):
        slope_copy(k).start()

    @pl.when(targetd)
    def _():
        least_in[0] = least[...]
        for c in least_copies()[:3]:
            c.wait_recv()

    @pl.when(online)
    def _():
        for c in least_copies()[3:]:
            c.wait_recv()

    low = jnp.minimum(jnp.minimum(least_in[0], least_in[1]), jnp.minimum(least_in[2], least_in[3]))
    scal = x_in[ROW_SCAL : ROW_SCAL + 8, :]
    target[...] = scal[0:1] + scal[1:2] * low

    for c in unit_copies():
        c.wait_recv()
    spread = unit_out[...].astype(F32)
    for k in range(7):
        spread = spread + unit_in[k].astype(F32)
    spread = jnp.concatenate([spread[0:8], spread[8:16]], 1)
    unit = unit_f[0:8, :]
    inv = unit_f[8:9, :]
    valid = scal[2:3]
    critics = 8
    d_unit = (2.0 * ETA / (critics - 1)) * valid * (spread - unit)
    along = jnp.sum(d_unit * unit, axis=0, keepdims=True)
    dg = (d_unit - unit * along) * inv
    gap = value[...] - target[...]
    dv = 2.0 * valid * gap
    diverse = jnp.sum(valid * jnp.sum(unit * (spread - unit), axis=0, keepdims=True), axis=1, keepdims=True)
    errors = jnp.sum(valid * gap * gap, axis=1, keepdims=True)
    dv_sum = jnp.sum(dv, axis=1, keepdims=True)
    dgb = dg.astype(BF16)
    dg_b[...] = jnp.concatenate([dgb, dgb], 0)
    rid16 = lax.broadcasted_iota(jnp.int32, (16, 1), 0)
    dv_b[...] = jnp.where(rid16 == 0, dv, jnp.where(rid16 == 1, 1.0, 0.0)).astype(BF16)

    for acc in (acc_h1, acc_h1t, acc_h0, acc_h0t, acc_x, acc_t, acc_last):
        acc[...] = jnp.zeros_like(acc)

    def body_b(i, _):
        sl = pl.ds(pl.multiple_of(i * BLOCK, BLOCK), BLOCK)
        a1, a2, a3 = s1[:, sl], s2[:, sl], s3[:, sl]
        rows_dv = dv_b[:, sl]
        dvh = (rows_dv[0:1].astype(F32) * 0.5).astype(BF16)
        tp1 = dot(t1w[...], dg_b[:, sl]).astype(BF16)
        th1 = a1 * tp1
        tp2 = halves(dot(f0[...], th1)).astype(BF16)
        th2 = a2 * tp2
        tp3 = halves(dot(f1[...], th2)).astype(BF16)
        th3 = a3 * tp3
        d3 = d3s[:, sl]
        ap3 = dvh * d3 + k3[:, sl] * tp3
        last = dot_t(rows_dv, h3s[:, sl])
        lone = dot_t(rows_dv, th3)
        acc_last[...] += last[0:8] + jnp.where(rid == 0, lone[1:2], 0.0)
        acc_h1[...] += dot_t(h2x[:, sl], ap3)
        acc_h1t[...] += dot_t(th2, d3)
        ah = halves(dot(b1[...], ap3)).astype(BF16)
        ap2 = a2 * ah + k2[:, sl] * tp2
        acc_h0[...] += dot_t(h1x[:, sl], ap2)
        acc_h0t[...] += dot_t(th1, d2s[:, sl])
        ah = halves(dot(b0[...], ap2)).astype(BF16)
        ap1 = a1 * ah + k1[:, sl] * tp1
        acc_x[...] += dot_t(x_b[0:32, sl], ap1)
        acc_t[...] += dot_t(dg_b[:, sl], d1s[:, sl])
        return 0

    lax.fori_loop(0, blocks, body_b, 0)
    out_c[0:HID, :] = acc_h0[0:HID, :] + 0.5 * acc_h0t[...]
    out_c[HID : 2 * HID, :] = acc_h1[0:HID, :] + 0.5 * acc_h1t[...]
    rid32 = lax.broadcasted_iota(jnp.int32, (32, 1), 0)
    lane = lax.broadcasted_iota(jnp.int32, (1, HID), 1)
    stats = jnp.where(lane == 0, dv_sum, jnp.where(lane == 1, errors, jnp.where(lane == 2, diverse, 0.0)))
    small = acc_x[...]
    small = small + jnp.where(rid32 == 18, acc_h0[HID : HID + 1, :], 0.0)
    small = small + jnp.where(rid32 == 19, acc_h1[HID : HID + 1, :], 0.0)
    small = small + jnp.where(rid32 == 20, stats, 0.0)
    small = small + jnp.where(rid32 == 23, acc_last[0:1, :], 0.0)
    out_c[2 * HID : 2 * HID + 24, :] = small[0:24]
    out_c[2 * HID + 24 : 2 * HID + 32, :] = small[24:32] + 0.5 * acc_t[0:8, :]

    @pl.when(targetd)
    def _():
        out_a[...] = jnp.zeros_like(out_a)

    @pl.when(online)
    def _():
        total = slope_out[...].astype(F32)
        for k in range(4):
            remote(slope_out, slope_in.at[k], sem_slope_s.at[0], sem_slope_r.at[k], dev(1, e)).wait_recv()
            total = total + slope_in[k].astype(F32)
        for k in range(5, 8):
            remote(slope_out, slope_in.at[k], sem_slope_s.at[0], sem_slope_r.at[k], dev(1, e)).wait_recv()
            total = total + slope_in[k].astype(F32)
        total = jnp.concatenate([total[0:8], total[8:16]], 1) * (1.0 / critics)
        valid = x_in[ROW_SCAL + 2 : ROW_SCAL + 3, :]
        d_sample = -valid * total
        d_logp = ALPHA * valid
        sample = pi_act[...]
        th = heads[0:8, :]
        spread_e = heads[8:16, :]
        eps = x_in[ROW_NOISE : ROW_NOISE + 8, :]
        ok = (rid < ACT).astype(F32)
        dz = (d_sample * (1.0 - sample * sample) + d_logp * 2.0 * sample) * ok
        dls = (dz * spread_e - d_logp) * (3.5 * (1.0 - th * th)) * ok
        dout = jnp.concatenate([dz, dls], 0).astype(BF16)
        heads[24:40, :] = dout.astype(F32)
        logp = heads[16:17, :]
        actor_sum = jnp.sum(valid * (ALPHA * logp - total[6:7]), axis=1, keepdims=True)
        count = jnp.sum(valid, axis=1, keepdims=True)
        for acc in (acc_h1, acc_h0, acc_x, acc_o):
            acc[...] = jnp.zeros_like(acc)

        def body_c(i, _):
            sl = pl.ds(pl.multiple_of(i * BLOCK, BLOCK), BLOCK)
            do = heads[24:40, sl].astype(BF16)
            h3 = ah3[:, sl]
            acc_o[0:16, :] += dot_t(do, h3)
            d3 = (dot(aot[...], jnp.concatenate([do, do], 0)) * (0.5 * as3[:, sl].astype(F32))).astype(BF16)
            acc_h1[...] += dot_t(ah2x[:, sl], d3)
            d2 = (halves(dot(ab1[...], d3)) * as2[:, sl].astype(F32)).astype(BF16)
            acc_h0[...] += dot_t(ah1x[:, sl], d2)
            d1 = (halves(dot(ab0[...], d2)) * as1[:, sl].astype(F32)).astype(BF16)
            acc_x[...] += dot_t(x_b[0:32, sl], d1)
            one = (lax.broadcasted_iota(jnp.int32, (16, BLOCK), 0) == 0).astype(BF16)
            acc_o[16:32, 0:128] += dot_t(one, jnp.concatenate([do, jnp.zeros((112, BLOCK), BF16)], 0))
            return 0

        lax.fori_loop(0, blocks, body_c, 0)
        out_a[0:HID, :] = acc_h0[0:HID, :]
        out_a[HID : 2 * HID, :] = acc_h1[0:HID, :]
        stats = jnp.where(lane == 0, actor_sum, jnp.where(lane == 1, count, 0.0))
        small = acc_x[...]
        small = small + jnp.where(rid32 == 18, acc_h0[HID : HID + 1, :], 0.0)
        small = small + jnp.where(rid32 == 19, acc_h1[HID : HID + 1, :], 0.0)
        small = small + jnp.where(rid32 == 20, acc_o[16:17, :], 0.0)
        small = small + jnp.where(rid32 == 21, stats, 0.0)
        out_a[2 * HID : 2 * HID + 32, :] = small
        out_a[2 * HID + 32 : 2 * HID + 48, :] = acc_o[0:16, :]

    @pl.when(online)
    def _():
        for c in param_copies():
            c.wait_send()
        remote(pi_act, pi_act, sem_pi_s, sem_pi_r, dev(0, e)).wait_send()

    @pl.when(targetd)
    def _():
        for c in least_copies():
            c.wait_send()
        slope_copy(0).wait_send()

    for k in range(1, 4):
        slope_copy(k).wait_send()
    for c in unit_copies():
        c.wait_send()


def fused(n_dp, rows, packed, own, aparams):
    v = pltpu.VMEM
    big = lambda n=HID: v((n, rows), BF16)
    dma = pltpu.SemaphoreType.DMA
    scratch = [
        v((64, rows), BF16), v((64, rows), BF16), v((8, rows), F32),
        v((128, HID), F32), v((HID, 128), F32), v((2, HID, 128), F32), v((HID, 128), F32),
        v((24, HID), F32), v((2, HID, HID), F32), v((4, HID), F32),
        v((HID, 64), BF16), v((512, HID), BF16), v((512, HID), BF16), v((512, HID), BF16), v((512, HID), BF16),
        v((16, HID), BF16), v((HID, 16), BF16), v((16, HID), BF16),
        v((2, HID, 64), BF16), v((2, 512, HID), BF16), v((2, 512, HID), BF16), v((2, 16, HID), BF16),
        v((HID, 64), BF16), v((512, HID), BF16), v((512, HID), BF16), v((512, HID), BF16), v((512, HID), BF16),
        v((32, HID), BF16), v((HID, 32), BF16),
        big(272), big(272), big(), big(), big(), big(), big(), big(), big(), big(), big(), big(),
        big(272), big(272), big(), v((HID, rows), BF16), v((HID, rows), BF16), v((HID, rows), BF16), v((40, rows), F32),
        v((1, rows), F32), v((24, rows), F32), v((16, rows // 2), BF16), v((7, 16, rows // 2), BF16),
        v((16, rows), BF16), v((16, rows), BF16),
        v((16, rows // 2), BF16), v((8, 16, rows // 2), BF16), v((1, rows), F32),
        v((1, rows), F32), v((4, 1, rows), F32), v((1, rows), F32),
        v((272, HID), F32), v((HID, HID), F32), v((272, HID), F32), v((HID, HID), F32),
        v((32, HID), F32), v((16, HID), F32), v((8, HID), F32), v((32, HID), F32),
        dma((4,)), dma((4,)), dma, dma, dma((8,)), dma((4,)), dma((7,)), dma((7,)), dma((4,)), dma((8,)),
    ]
    spec = pl.BlockSpec(memory_space=pltpu.VMEM)
    return pl.pallas_call(
        functools.partial(kernel, n_dp, rows),
        out_shape=(jax.ShapeDtypeStruct((544, HID), F32), jax.ShapeDtypeStruct((560, HID), F32)),
        in_specs=[spec] * 7,
        out_specs=(spec, spec),
        scratch_shapes=scratch,
        compiler_params=pltpu.CompilerParams(collective_id=0, has_side_effects=True, vmem_limit_bytes=62 * 2**20),
        name="edac_gradients",
    )(packed, *own, *aparams)


def adamw(param, grad, first, second):
    first_new = BETA_ONE * first + (1.0 - BETA_ONE) * grad
    second_new = BETA_TWO * second + (1.0 - BETA_TWO) * grad * grad
    ratio = first_new / (1.0 - BETA_ONE**STEP) / (jnp.sqrt(second_new / (1.0 - BETA_TWO**STEP)) + EPS)
    return (param - LEARN * (ratio + DECAY * param), first_new, second_new)


def body(
    n_dp,
    states, actions, rewards, done, noise, counts,
    crit_edge, crit_hidden, crit_bias, edge_m, edge_v, hidden_m, hidden_v, bias_m, bias_v,
    act_edge, act_hidden, act_bias, act_edge_m, act_edge_v, act_hidden_m, act_hidden_v, act_bias_m, act_bias_v,
):
    rows = states.shape[0]
    online = lax.axis_index("grp") == 1
    own = (crit_edge[0], crit_hidden[0], crit_bias[0])
    aparams = (act_edge, act_hidden, act_bias)
    valid = (jnp.arange(rows, dtype=jnp.int32) < counts[0]).astype(F32)
    states_t, actions_t, noise_t = states.T, actions.T, noise.T
    zero = lambda n: jnp.zeros((n, rows), F32)
    one = jnp.ones((1, rows), F32)
    packed = jnp.concatenate(
        [
            states_t[:OBS], one, zero(6), states_t[OBS:], one, zero(6),
            actions_t, zero(2), noise_t[:ACT], zero(2), noise_t[ACT:], zero(2),
            rewards[None], GAMMA * (1.0 - done.astype(F32))[None], valid[None], zero(5),
        ],
        0,
    )
    grad_c, grad_a = fused(n_dp, rows, packed, own, aparams)
    grad_c, grad_a = lax.psum((grad_c, grad_a), "dp")
    both = lax.all_gather(grad_c, "grp")[::-1]
    grad_a = lax.psum(grad_a, "grp")
    total = grad_a[2 * HID + 21, 1]
    scale = 1.0 / total
    small = both[:, 2 * HID :]
    g_edge = jnp.concatenate([small[:, 0:OBS], small[:, 24 : 24 + ACT], small[:, 23:24]], 1) * scale
    g_hidden = both[:, : 2 * HID].reshape(2, 2, HID, HID) * scale
    lane = jnp.arange(HID) == 0
    g_bias = jnp.concatenate([small[:, 17:20], jnp.where(lane, small[:, 20:21], 0.0)], 1) * scale
    member_sums = small[:, 20, 1:3]
    smalla = grad_a[2 * HID :]
    ga_edge = jnp.concatenate([smalla[0:OBS], smalla[32 : 32 + ACT], smalla[40 : 40 + ACT]], 0) * scale
    ga_hidden = grad_a[: 2 * HID].reshape(2, HID, HID) * scale
    out_bias = jnp.concatenate([smalla[20, 0:ACT], smalla[20, 8 : 8 + ACT], jnp.zeros((HID - 2 * ACT,), F32)])[None]
    ga_bias = jnp.concatenate([smalla[17:20], out_bias], 0) * scale
    actor_sums = smalla[21, 0:2]
    onl = [lax.ppermute(p, "grp", [(1, 0)]) for p in own]
    onl = [jnp.where(online, a, b) for a, b in zip(own, onl)]
    outs, moments = [], []
    for p, mine, grad, m, v in zip(onl, own, (g_edge, g_hidden, g_bias), (edge_m, hidden_m, bias_m), (edge_v, hidden_v, bias_v)):
        master, m_new, v_new = adamw(p, grad, m, v)
        polyak = TAU * master.astype(BF16).astype(F32) + (1.0 - TAU) * mine
        outs.append(jnp.where(online, master, polyak)[None])
        moments += [m_new, v_new]
    aouts, amoments = [], []
    for p, grad, m, v in zip(
        aparams, (ga_edge, ga_hidden, ga_bias), (act_edge_m, act_hidden_m, act_bias_m), (act_edge_v, act_hidden_v, act_bias_v)
    ):
        master, m_new, v_new = adamw(p, grad, m, v)
        aouts.append(master)
        amoments += [m_new, v_new]
    return (*outs, *moments, *aouts, *amoments, member_sums, actor_sums)


def solution(mesh):
    member = P("grp", "ens", None, None)
    hidden = P("grp", "ens", None, None, None)
    mom = P("ens", None, None)
    mom_h = P("ens", None, None, None)
    return jax.shard_map(
        functools.partial(body, mesh.shape["dp"]),
        mesh=mesh,
        in_specs=(
            P("dp", None), P("dp", None), P("dp"), P("dp"), P("dp", None), P("dp"),
            member, hidden, member, mom, mom, mom_h, mom_h, mom, mom,
        ) + (P(),) * 9,
        out_specs=(member, hidden, member, mom, mom, mom_h, mom_h, mom, mom) + (P(),) * 9 + (P("ens", None), P()),
        check_vma=False,
    )
```

```python
import functools

import jax
import jax.numpy as jnp
from jax import lax
from jax.experimental import pallas as pl
from jax.experimental.pallas import tpu as pltpu
from jax.sharding import PartitionSpec as P

OBS = 17
ACT = 6
HID = 256
STEP = 5
BLOCK = 1024

GAMMA = 0.99
ALPHA = 0.2
ETA = 1.0
LEARN = 0.03
BETA_ONE = 0.5
BETA_TWO = 0.5
DECAY = 0.01
EPS = 1e-08
TAU = 0.05
HALF_LOG_TWO_PI = 0.9189385332046727
LOG_TWO = 0.6931471805599453

F32 = jnp.float32
BF16 = jnp.bfloat16

CRITIC_SMALL, ACTOR_SMALL = 32, 64


def dot(a, b):
    return lax.dot_general(a, b, (((1,), (0,)), ((), ())), preferred_element_type=F32)


def dot_t(a, b):
    return lax.dot_general(a, b, (((1,), (1,)), ((), ())), preferred_element_type=F32)


def split(w):
    high = w.astype(BF16).astype(F32)
    return high, w - high


def halves(p):
    n = p.shape[0] // 2
    return p[:n] + p[n:]


def prep_input(stage, w1, edge, bias, n_in):
    stage[...] = jnp.zeros_like(stage)
    stage[0:OBS, :] = edge[0:OBS, :]
    stage[OBS : OBS + 1, :] = bias[0:1, :]
    if n_in > OBS:
        stage[24 : 24 + ACT, :] = edge[OBS : OBS + ACT, :]
    high, low = split(0.5 * stage[0:32, :])
    w1[...] = jnp.concatenate([high, low], 0).T.astype(BF16)


def prep_hidden(fwd, bwd, hidden):
    w = 0.5 * hidden
    if fwd is not None:
        high, low = split(w.T)
        fwd[...] = jnp.concatenate([high, low], 0).astype(BF16)
    if bwd is not None:
        high, low = split(w)
        bwd[...] = jnp.concatenate([high, low], 0).astype(BF16)


def silu_half(u):
    t = jnp.tanh(u)
    return u + u * t, t


def up(n, by):
    return -(-n // by) * by


def kernel(
    n_dp,
    rows,
    keep,
    states, actions, noise, rewards, done, counts, c_edge, c_hidden, c_bias, a_edge, a_hidden, a_bias,
    out_c, out_a, out_pe, out_ph, out_pb,
    xs, ns, eps_s, x_b, pi_b, pi_act, stage, vec, tvec, avec,
    p_edge, p_hidden, p_bias,
    w1, f0, f1, b0, b1, ga, t1w, eq,
    tw1, tf0, tf1, teq,
    aw1, af0, af1, ab0, ab1, ao, aot,
    h1x, h2x, h3s, s1, s2, s3, k1, k2, k3, d1s, d2s, d3s,
    heads,
    value, unit_f, unit_out, unit_in, dg_b, dv_b,
    slope_out, slope_in, q_own, least, least_in, target,
    acc_h1, acc_h1t, acc_h0, acc_h0t, acc_x, acc_t, acc_last, acc_o,
    part_c, part_a, sum_c, sum_a, in_h1, in_h0, in_sm, in_ac,
    sem_param_s, sem_param_r, sem_pi_s, sem_pi_r, sem_least_s, sem_least_r, sem_unit_s, sem_unit_r, sem_slope_s, sem_slope_r,
    rs_s, rs_r, ag_s, ag_r, xf_s, xf_r, ef_s, ef_r, sem_out,
):
    g = lax.axis_index("grp")
    e = lax.axis_index("ens")
    z = lax.axis_index("dp")
    me = g * 4 + e
    blocks = rows // BLOCK
    half = rows // 2
    online = g == 1
    targetd = g == 0
    critics = 8

    def dev(gg, ee):
        return {"grp": gg, "ens": ee}

    def remote(src, dst, send, recv, where):
        return pltpu.make_async_remote_copy(
            src_ref=src, dst_ref=dst, send_sem=send, recv_sem=recv, device_id=where, device_id_type=pl.DeviceIdType.MESH
        )

    barrier = pltpu.get_barrier_semaphore()
    for k in range(1, 8):
        p = lax.rem(me + k, 8)
        pl.semaphore_signal(barrier, inc=1, device_id=dev(p // 4, lax.rem(p, 4)), device_id_type=pl.DeviceIdType.MESH)
    for k in range(1, n_dp):
        pl.semaphore_signal(barrier, inc=1, device_id={"dp": lax.rem(z + k, n_dp)}, device_id_type=pl.DeviceIdType.MESH)
    pl.semaphore_wait(barrier, 7 + n_dp - 1)

    def param_copy(m, what):
        where = dev(0, e)
        src, dst = (
            (c_edge.at[m], p_edge.at[m]),
            (c_bias.at[m], p_bias.at[m]),
            (c_hidden.at[m, 0], p_hidden.at[m, 0]),
            (c_hidden.at[m, 1], p_hidden.at[m, 1]),
        )[what]
        return remote(src, dst, sem_param_s.at[m, what], sem_param_r.at[m, what], where)

    @pl.when(online)
    def _():
        for m in (1, 0):
            for what in range(4):
                param_copy(m, what).start()

    ones_row = jnp.ones((1, rows), F32)
    xs[...] = jnp.zeros_like(xs)
    xs[0:OBS, :] = states[0:OBS, :]
    xs[OBS : OBS + 1, :] = ones_row
    xs[24 : 24 + ACT, :] = actions[...]
    eps_s[...] = jnp.zeros_like(eps_s)
    xin = xs[...].astype(BF16)
    x_b[0:32, :] = xin
    x_b[32:64, :] = xin

    @pl.when(online)
    def _():
        eps_s[0:ACT, :] = noise[0:ACT, :]

    @pl.when(targetd)
    def _():
        eps_s[0:ACT, :] = noise[ACT : 2 * ACT, :]
        ns[...] = jnp.zeros_like(ns)
        ns[0:OBS, :] = states[OBS : 2 * OBS, :]
        ns[OBS : OBS + 1, :] = ones_row

    row_id = lax.broadcasted_iota(jnp.int32, (1, rows), 1)
    valid = jnp.where(row_id < counts[0], 1.0, 0.0)

    def prep_critic(edge, hid0, hid1, bias, w1_, f0_, f1_, b0_, b1_, vec_, eq_, ga_, t1_):
        prep_input(stage, w1_, edge, bias, OBS + ACT)
        prep_hidden(f0_, b0_, hid0[...])
        prep_hidden(f1_, b1_, hid1[...])
        stage[...] = jnp.zeros_like(stage)
        stage[0:1, :] = 0.5 * bias[1:2, :]
        stage[1:2, :] = 0.5 * bias[2:3, :]
        stage[2:3, :] = edge[23:24, :]
        vec_[...] = stage[...].T
        vec_[0:1, 8:9] = bias[3:4, 0:1]
        stage[...] = jnp.zeros_like(stage)
        high, low = split(edge[23:24, :])
        stage[0:1, :] = high
        stage[1:2, :] = low
        eq_[...] = stage[0:16, :].astype(BF16)
        if ga_ is not None:
            stage[...] = jnp.zeros_like(stage)
            stage[0:ACT, :] = 0.5 * edge[OBS : OBS + ACT, :]
            high, low = split(stage[0:8, :])
            both = jnp.concatenate([high, low], 0)
            ga_[...] = both.astype(BF16)
            stage[0:16, :] = both
            t1_[...] = stage[...].T[:, 0:16].astype(BF16)

    def prep_actor():
        prep_input(stage, aw1, a_edge, a_bias, OBS)
        prep_hidden(af0, ab0, a_hidden[0])
        prep_hidden(af1, ab1, a_hidden[1])
        stage[...] = jnp.zeros_like(stage)
        stage[0:1, :] = 0.5 * a_bias[1:2, :]
        stage[1:2, :] = 0.5 * a_bias[2:3, :]
        stage[2:3, :] = a_bias[3:4, :]
        avec[...] = stage[...].T
        stage[...] = jnp.zeros_like(stage)
        stage[0:ACT, :] = a_edge[OBS : OBS + ACT, :]
        stage[8 : 8 + ACT, :] = a_edge[OBS + ACT : OBS + 2 * ACT, :]
        high, low = split(stage[0:16, :])
        ao[...] = jnp.concatenate([high, low], 0).astype(BF16)
        stage[...] = jnp.zeros_like(stage)
        stage[0 : 2 * ACT, :] = a_edge[OBS : OBS + 2 * ACT, :]
        high, low = split(stage[0:16, :])
        stage[0:32, :] = jnp.concatenate([high, low], 0)
        aot[...] = stage[...].T[:, 0:32].astype(BF16)

    prep_actor()

    def actor_layers(src):
        kept = []
        hb = None
        for w, b in ((aw1, None), (af0, 0), (af1, 1)):
            u = dot(w[...], src) if b is None else halves(dot(w[...], hb)) + avec[:, b : b + 1]
            h, t = silu_half(u)
            hb = h.astype(BF16)
            kept.append((hb, h, t))
        return kept

    ok8 = (lax.broadcasted_iota(jnp.int32, (8, 1), 0) < ACT).astype(F32)

    def actor_heads(hb, sl):
        out = halves(dot(ao[...], hb))
        eps = eps_s[:, sl]
        center = out[0:8] + avec[0:8, 2:3] * ok8
        th = jnp.tanh(out[8:16] + avec[6:14, 2:3] * ok8)
        log_std = 3.5 * th - 1.5
        spread_e = jnp.exp(log_std) * eps
        latent = center + spread_e
        soft = jnp.maximum(-2.0 * latent, 0.0) + jnp.log(1.0 + jnp.exp(-2.0 * jnp.abs(latent)))
        terms = -0.5 * eps * eps - log_std - HALF_LOG_TWO_PI - 2.0 * (LOG_TWO - latent - soft)
        logp = jnp.sum(terms * ok8, axis=0, keepdims=True)
        sample = jnp.tanh(latent) * ok8
        return sample, logp, th, spread_e

    @pl.when(online)
    def _():
        def body(i, _):
            sl = pl.ds(pl.multiple_of(i * BLOCK, BLOCK), BLOCK)
            kept = actor_layers(x_b[:, sl])
            sample, logp, th, spread_e = actor_heads(kept[2][0], sl)
            pi_act[:, sl] = sample
            heads[0:8, sl] = th
            heads[8:16, sl] = spread_e
            heads[16:17, sl] = logp
            return 0

        lax.fori_loop(0, blocks, body, 0)
        remote(pi_act, pi_act, sem_pi_s, sem_pi_r, dev(0, e)).start()
        prep_critic(c_edge.at[0], c_hidden.at[0, 0], c_hidden.at[0, 1], c_bias.at[0], w1, f0, f1, b0, b1, vec, eq, ga, t1w)

    def least_online(k):
        return remote(least, least_in.at[k], sem_least_s.at[4 + k], sem_least_r.at[k], dev(1, lax.rem(e + k, 4)))

    def least_target(k):
        return remote(least, least_in.at[k], sem_least_s.at[k], sem_least_r.at[k], dev(0, lax.rem(e + k, 4)))

    @pl.when(targetd)
    def _():
        for m in range(2):
            prep_critic(
                c_edge.at[m], c_hidden.at[m, 0], c_hidden.at[m, 1], c_bias.at[m],
                tw1.at[m], tf0.at[m], tf1.at[m], None, None, tvec.at[m], teq.at[m], None, None,
            )

        def body(i, _):
            sl = pl.ds(pl.multiple_of(i * BLOCK, BLOCK), BLOCK)
            nx = ns[:, sl].astype(BF16)
            kept = actor_layers(jnp.concatenate([nx, nx], 0))
            sample, logp, th, spread_e = actor_heads(kept[2][0], sl)
            nx = jnp.concatenate([ns[0:24, sl], sample], 0).astype(BF16)
            nx = jnp.concatenate([nx, nx], 0)
            low = None
            for m in range(2):
                h, t = silu_half(dot(tw1[m], nx))
                h, t = silu_half(halves(dot(tf0[m], h.astype(BF16))) + tvec[m, :, 0:1])
                h, t = silu_half(halves(dot(tf1[m], h.astype(BF16))) + tvec[m, :, 1:2])
                r = dot(teq[m], h.astype(BF16))
                q = r[0:1] + r[1:2] + tvec[m, 0:1, 8:9]
                low = q if low is None else jnp.minimum(low, q)
            least[:, sl] = low - ALPHA * logp
            return 0

        lax.fori_loop(0, blocks, body, 0)
        for k in range(1, 4):
            least_target(k).start()
        for k in range(4):
            least_online(k).start()
        for what in range(4):
            param_copy(1, what).wait_recv()
        prep_critic(p_edge.at[1], p_hidden.at[1, 0], p_hidden.at[1, 1], p_bias.at[1], w1, f0, f1, b0, b1, vec, eq, ga, t1w)
        remote(pi_act, pi_act, sem_pi_s, sem_pi_r, dev(0, e)).wait_recv()

    pin = jnp.concatenate([xs[0:24, :], pi_act[...]], 0).astype(BF16)
    pi_b[0:32, :] = pin
    pi_b[32:64, :] = pin

    def body_p(i, _):
        sl = pl.ds(pl.multiple_of(i * BLOCK, BLOCK), BLOCK)

        def act(u):
            h, t = silu_half(u)
            hb, tb = h.astype(BF16), t.astype(BF16)
            one = jnp.ones((), BF16)
            return hb, (one + tb) + hb * (one - tb)

        h, a1 = act(dot(w1[...], pi_b[:, sl]))
        h, a2 = act(dot(f0[0:HID, :], h) + vec[:, 0:1])
        h, a3 = act(dot(f1[0:HID, :], h) + vec[:, 1:2])
        r = dot(eq[...], h)
        q_own[:, sl] = r[0:1] + r[1:2] + vec[0:1, 8:9]
        d = vec[:, 2:3].astype(BF16) * a3
        d = dot(b1[0:HID, :], d).astype(BF16) * a2
        d = dot(b0[0:HID, :], d).astype(BF16) * a1
        unit_f[16:24, sl] = halves(dot(ga[...], d))
        return 0

    lax.fori_loop(0, blocks, body_p, 0)
    rid = lax.broadcasted_iota(jnp.int32, (8, 1), 0)
    packed = unit_f[16:24, :] + jnp.where(rid == 6, q_own[...], 0.0)
    slope_out[...] = jnp.concatenate([packed[:, 0:half], packed[:, half:rows]], 0).astype(BF16)

    def slope_copy(k):
        slot = g * 4 + k
        return remote(slope_out, slope_in.at[slot], sem_slope_s.at[k], sem_slope_r.at[slot], dev(1, lax.rem(e + k, 4)))

    @pl.when(targetd)
    def _():
        slope_copy(0).start()

    for k in range(1, 4):
        slope_copy(k).start()

    ones = (lax.broadcasted_iota(jnp.int32, (16, rows), 0) == 0).astype(BF16)
    h1x[HID : HID + 16, :] = ones
    h2x[HID : HID + 16, :] = ones

    def curves(u):
        h, t = silu_half(u)
        c = 1.0 + t
        d = 1.0 - t
        return h, c + h * d, (c * d) * (1.0 - u * t)

    def body_a(i, _):
        sl = pl.ds(pl.multiple_of(i * BLOCK, BLOCK), BLOCK)
        h, a1, q1 = curves(dot(w1[...], x_b[:, sl]))
        hb = h.astype(BF16)
        h1x[0:HID, sl] = hb
        s1[:, sl] = a1.astype(BF16)
        h, a2, q2 = curves(halves(dot(f0[...], hb)) + vec[:, 0:1])
        hb = h.astype(BF16)
        h2x[0:HID, sl] = hb
        s2[:, sl] = a2.astype(BF16)
        h, a3, q3 = curves(halves(dot(f1[...], hb)) + vec[:, 1:2])
        hb = h.astype(BF16)
        h3s[:, sl] = hb
        s3[:, sl] = a3.astype(BF16)
        r = dot(eq[...], hb)
        value[:, sl] = r[0:1] + r[1:2] + vec[0:1, 8:9]
        last = vec[:, 2:3]
        db = (last * a3).astype(BF16)
        d3s[:, sl] = db
        k3[:, sl] = (last * q3).astype(BF16)
        m = halves(dot(b1[...], db))
        db = (m * a2).astype(BF16)
        d2s[:, sl] = db
        k2[:, sl] = (m * q2).astype(BF16)
        m = halves(dot(b0[...], db))
        db = (m * a1).astype(BF16)
        d1s[:, sl] = db
        k1[:, sl] = (m * q1).astype(BF16)
        slope = halves(dot(ga[...], db))
        inv = lax.rsqrt(jnp.sum(slope * slope, axis=0, keepdims=True) + 0.01)
        unit_f[0:8, sl] = slope * inv
        unit_f[8:9, sl] = inv
        return 0

    lax.fori_loop(0, blocks, body_a, 0)
    unit_out[...] = jnp.concatenate([unit_f[0:8, 0:half], unit_f[0:8, half:rows]], 0).astype(BF16)

    def unit_copy(k):
        p = lax.rem(me + k, 8)
        return remote(unit_out, unit_in.at[k - 1], sem_unit_s.at[k - 1], sem_unit_r.at[k - 1], dev(p // 4, lax.rem(p, 4)))

    for k in range(1, 8):
        unit_copy(k).start()

    class Exchange:
        def __init__(self, index, part, into, inbox, base, count, wide):
            self.index, self.part, self.into, self.inbox, self.base, self.count, self.wide = index, part, into, inbox, base, count, wide
            self.each = count // (n_dp * (4 if wide else 1))

        def rows_of(self, shard):
            first = self.base + (e * n_dp + shard if self.wide else shard) * self.each
            return pl.ds(pl.multiple_of(first, 8), self.each)

        def scatter(self, k):
            to = lax.rem(z + k, n_dp)
            return remote(
                self.part.at[self.rows_of(to)], self.inbox.at[k - 1], rs_s.at[self.index, k - 1], rs_r.at[self.index, k - 1], {"dp": to}
            )

        def gather(self, k):
            mine = self.into.at[self.rows_of(z)]
            return remote(mine, mine, ag_s.at[self.index, k - 1], ag_r.at[self.index, k - 1], {"dp": lax.rem(z + k, n_dp)})

        def across(self, k):
            there = self.into.at[self.rows_of(lax.rem(z + n_dp - k, n_dp))]
            return remote(there, there, xf_s.at[self.index, k], xf_r.at[self.index, k], dev(1 - g, e))

        def start(self):
            for k in range(1, n_dp):
                self.scatter(k).start()

        def reduce(self):
            total = self.part[self.rows_of(z), :]
            for k in range(1, n_dp):
                self.scatter(k).wait_recv()
                total = total + self.inbox[k - 1]
            self.into[self.rows_of(z), :] = total
            for k in range(1, n_dp):
                self.gather(k).start()
            self.across(0).start()

        def forward(self):
            for k in range(1, n_dp):
                self.gather(k).wait_recv()
                self.across(k).start()

        def sent(self):
            for k in range(1, n_dp):
                self.scatter(k).wait_send()
                self.gather(k).wait_send()
            for k in range(n_dp):
                self.across(k).wait_send()

        def arrived(self):
            for k in range(n_dp):
                self.across(k).wait_recv()

    small_c = part_c.shape[0] - 2 * HID
    ex_h1 = Exchange(0, part_c, sum_c.at[g], in_h1, HID, HID, False)
    ex_h0 = Exchange(1, part_c, sum_c.at[g], in_h0, 0, HID, False)
    ex_sm = Exchange(2, part_c, sum_c.at[g], in_sm, 2 * HID, small_c, False)
    ex_ac = Exchange(3, part_a, sum_a, in_ac, 0, part_a.shape[0], True)
    quarter = part_a.shape[0] // 4

    def spread_actor(k):
        mine = sum_a.at[pl.ds(pl.multiple_of(e * quarter, 8), quarter)]
        return remote(mine, mine, ef_s.at[k - 1], ef_r.at[k - 1], dev(g, lax.rem(e + k, 4)))

    lane = lax.broadcasted_iota(jnp.int32, (1, HID), 1)
    rid32 = lax.broadcasted_iota(jnp.int32, (32, 1), 0)

    @pl.when(online)
    def _():
        total = slope_out[...].astype(F32)
        for k in (0, 1, 2, 3, 5, 6, 7):
            remote(slope_out, slope_in.at[k], sem_slope_s.at[0], sem_slope_r.at[k], dev(1, e)).wait_recv()
            total = total + slope_in[k].astype(F32)
        total = jnp.concatenate([total[0:8], total[8:16]], 1) * (1.0 / critics)
        d_sample = -valid * total
        d_logp = ALPHA * valid
        sample = pi_act[...]
        th = heads[0:8, :]
        spread_e = heads[8:16, :]
        dz = (d_sample * (1.0 - sample * sample) + d_logp * 2.0 * sample) * ok8
        dls = (dz * spread_e - d_logp) * (3.5 * (1.0 - th * th)) * ok8
        heads[24:40, :] = jnp.zeros((16, rows), F32)
        heads[24:30, :] = dz[0:ACT]
        heads[30:36, :] = dls[0:ACT]
        actor_sum = jnp.sum(valid * (ALPHA * heads[16:17, :] - total[6:7]), axis=1, keepdims=True)
        count = jnp.sum(valid, axis=1, keepdims=True)
        for acc in (acc_h1, acc_h0, acc_x, acc_o):
            acc[...] = jnp.zeros_like(acc)
        one16 = (lax.broadcasted_iota(jnp.int32, (16, BLOCK), 0) == 0).astype(BF16)

        def body_c(i, _):
            sl = pl.ds(pl.multiple_of(i * BLOCK, BLOCK), BLOCK)
            kept = actor_layers(x_b[:, sl])
            slopes = [(1.0 + t) + h * (1.0 - t) for _, h, t in kept]
            do = heads[24:40, sl].astype(BF16)
            acc_o[0:16, :] += dot_t(do, kept[2][0])
            d3 = (dot(aot[...], jnp.concatenate([do, do], 0)) * (0.5 * slopes[2])).astype(BF16)
            acc_h1[...] += dot_t(jnp.concatenate([kept[1][0], one16], 0), d3)
            d2 = (halves(dot(ab1[...], d3)) * slopes[1]).astype(BF16)
            acc_h0[...] += dot_t(jnp.concatenate([kept[0][0], one16], 0), d2)
            d1 = (halves(dot(ab0[...], d2)) * slopes[0]).astype(BF16)
            acc_x[...] += dot_t(x_b[0:32, sl], d1)
            acc_o[16:32, 0:128] += dot_t(one16, jnp.concatenate([do, jnp.zeros((112, BLOCK), BF16)], 0))
            return 0

        lax.fori_loop(0, blocks, body_c, 0)
        part_a[0:HID, :] = acc_h0[0:HID, :]
        part_a[HID : 2 * HID, :] = acc_h1[0:HID, :]
        stats = jnp.where(lane == 0, actor_sum, jnp.where(lane == 1, count, 0.0))
        small = acc_x[...]
        small = small + jnp.where(rid32 == 18, acc_h0[HID : HID + 1, :], 0.0)
        small = small + jnp.where(rid32 == 19, acc_h1[HID : HID + 1, :], 0.0)
        small = small + jnp.where(rid32 == 20, acc_o[16:17, :], 0.0)
        small = small + jnp.where(rid32 == 21, stats, 0.0)
        part_a[2 * HID : 2 * HID + 32, :] = small
        part_a[2 * HID + 32 : 2 * HID + 48, :] = acc_o[0:16, :]
        rest = part_a.shape[0] - 2 * HID - 48
        part_a[2 * HID + 48 :, :] = jnp.zeros((rest, HID), F32)
        ex_ac.start()

    @pl.when(targetd)
    def _():
        least_in[0] = least[...]
        for k in range(1, 4):
            least_target(k).wait_recv()

    @pl.when(online)
    def _():
        for k in range(4):
            least_online(k).wait_recv()

    low = jnp.minimum(jnp.minimum(least_in[0], least_in[1]), jnp.minimum(least_in[2], least_in[3]))
    target[...] = rewards[...] + GAMMA * (1.0 - done[...].astype(F32)) * low

    spread = unit_out[...].astype(F32)
    for k in range(1, 8):
        unit_copy(k).wait_recv()
        spread = spread + unit_in[k - 1].astype(F32)
    spread = jnp.concatenate([spread[0:8], spread[8:16]], 1)
    unit = unit_f[0:8, :]
    inv = unit_f[8:9, :]
    d_unit = (2.0 * ETA / (critics - 1)) * valid * (spread - unit)
    along = jnp.sum(d_unit * unit, axis=0, keepdims=True)
    dg = (d_unit - unit * along) * inv
    gap = value[...] - target[...]
    dv = 2.0 * valid * gap
    diverse = jnp.sum(valid * jnp.sum(unit * (spread - unit), axis=0, keepdims=True), axis=1, keepdims=True)
    errors = jnp.sum(valid * gap * gap, axis=1, keepdims=True)
    dv_sum = jnp.sum(dv, axis=1, keepdims=True)
    dgb = dg.astype(BF16)
    dg_b[...] = jnp.concatenate([dgb, dgb], 0)
    rid16 = lax.broadcasted_iota(jnp.int32, (16, 1), 0)
    dv_b[...] = jnp.where(rid16 == 0, dv, jnp.where(rid16 == 1, 1.0, 0.0)).astype(BF16)

    for acc in (acc_h1, acc_h1t, acc_h0, acc_h0t, acc_x, acc_t, acc_last):
        acc[...] = jnp.zeros_like(acc)

    def body_b1(i, _):
        sl = pl.ds(pl.multiple_of(i * BLOCK, BLOCK), BLOCK)
        rows_dv = dv_b[:, sl]
        dvh = (rows_dv[0:1].astype(F32) * 0.5).astype(BF16)
        tp = dot(t1w[...], dg_b[:, sl]).astype(BF16)
        k1[:, sl] = k1[:, sl] * tp
        th1 = s1[:, sl] * tp
        tp = halves(dot(f0[...], th1)).astype(BF16)
        k2[:, sl] = k2[:, sl] * tp
        th2 = s2[:, sl] * tp
        tp = halves(dot(f1[...], th2)).astype(BF16)
        th3 = s3[:, sl] * tp
        d3 = d3s[:, sl]
        ap3 = dvh * d3 + k3[:, sl] * tp
        k3[:, sl] = ap3
        last = dot_t(rows_dv, h3s[:, sl])
        lone = dot_t(rows_dv, th3)
        acc_last[...] += last[0:8] + jnp.where(rid == 0, lone[1:2], 0.0)
        h3s[:, sl] = th1
        acc_h1[...] += dot_t(h2x[:, sl], ap3)
        acc_h1t[...] += dot_t(th2, d3)
        return 0

    def body_b2(i, _):
        sl = pl.ds(pl.multiple_of(i * BLOCK, BLOCK), BLOCK)
        ah = halves(dot(b1[...], k3[:, sl])).astype(BF16)
        ap2 = s2[:, sl] * ah + k2[:, sl]
        k2[:, sl] = ap2
        acc_h0[...] += dot_t(h1x[:, sl], ap2)
        acc_h0t[...] += dot_t(h3s[:, sl], d2s[:, sl])
        return 0

    def body_b3(i, _):
        sl = pl.ds(pl.multiple_of(i * BLOCK, BLOCK), BLOCK)
        ah = halves(dot(b0[...], k2[:, sl])).astype(BF16)
        ap1 = s1[:, sl] * ah + k1[:, sl]
        acc_x[...] += dot_t(x_b[0:32, sl], ap1)
        acc_t[...] += dot_t(dg_b[:, sl], d1s[:, sl])
        return 0

    lax.fori_loop(0, blocks, body_b1, 0)
    part_c[HID : 2 * HID, :] = acc_h1[0:HID, :] + 0.5 * acc_h1t[...]
    ex_h1.start()

    @pl.when(online)
    def _():
        ex_ac.reduce()

    lax.fori_loop(0, blocks, body_b2, 0)
    part_c[0:HID, :] = acc_h0[0:HID, :] + 0.5 * acc_h0t[...]
    ex_h0.start()
    ex_h1.reduce()

    @pl.when(online)
    def _():
        ex_ac.forward()
        for k in range(1, 4):
            spread_actor(k).start()

    lax.fori_loop(0, blocks, body_b3, 0)
    stats = jnp.where(lane == 0, errors, jnp.where(lane == 1, diverse, 0.0))
    small = acc_x[...]
    small = small + jnp.where(rid32 == 18, acc_h0[HID : HID + 1, :], 0.0)
    small = small + jnp.where(rid32 == 19, acc_h1[HID : HID + 1, :], 0.0)
    small = small + jnp.where(rid32 == 20, stats, 0.0)
    small = small + jnp.where(rid32 == 22, jnp.where(lane == 0, dv_sum, 0.0), 0.0)
    small = small + jnp.where(rid32 == 23, acc_last[0:1, :], 0.0)
    part_c[2 * HID : 2 * HID + 24, :] = small[0:24]
    part_c[2 * HID + 24 : 2 * HID + 32, :] = small[24:32] + 0.5 * acc_t[0:8, :]
    if small_c > 32:
        part_c[2 * HID + 32 :, :] = jnp.zeros((small_c - 32, HID), F32)
    ex_sm.start()
    ex_h1.forward()
    ex_h0.reduce()
    ex_sm.reduce()

    @pl.when(targetd)
    def _():
        ex_ac.arrived()
        for k in range(1, 4):
            spread_actor(k).start()

    ex_h0.forward()
    ex_sm.forward()

    def local(src, dst, k):
        return pltpu.make_async_copy(src, dst, sem_out.at[k])

    @pl.when(online)
    def _():
        for copy in (local(c_edge, out_pe, 0), local(c_hidden, out_ph, 1), local(c_bias, out_pb, 2)):
            copy.start()
            copy.wait()

    @pl.when(targetd)
    def _():
        for what in range(4):
            param_copy(0, what).wait_recv()
        for copy in (local(p_edge, out_pe, 0), local(p_hidden, out_ph, 1), local(p_bias, out_pb, 2)):
            copy.start()
            copy.wait()

    for k in range(1, 4):
        spread_actor(k).wait_recv()
    copy_a = local(sum_a, out_a, 3)
    copy_a.start()
    for ex in (ex_h1, ex_h0, ex_sm):
        ex.arrived()
    copy_c = local(sum_c, out_c, 4)
    copy_c.start()

    @pl.when(online)
    def _():
        for m in range(2):
            for what in range(4):
                param_copy(m, what).wait_send()
        remote(pi_act, pi_act, sem_pi_s, sem_pi_r, dev(0, e)).wait_send()
        ex_ac.sent()

    @pl.when(targetd)
    def _():
        for k in range(1, 4):
            least_target(k).wait_send()
        for k in range(4):
            least_online(k).wait_send()
        slope_copy(0).wait_send()

    for k in range(1, 4):
        slope_copy(k).wait_send()
        spread_actor(k).wait_send()
    for k in range(1, 8):
        unit_copy(k).wait_send()
    for ex in (ex_h1, ex_h0, ex_sm):
        ex.sent()
    copy_a.wait()
    copy_c.wait()


def sizes(n_dp):
    return 2 * HID + up(CRITIC_SMALL, 8 * n_dp), up(2 * HID + ACTOR_SMALL, 32 * n_dp)


def fused(n_dp, rows, data, own, aparams):
    v = pltpu.VMEM
    big = lambda n=HID: v((n, rows), BF16)
    dma = pltpu.SemaphoreType.DMA
    size_c, size_a = sizes(n_dp)
    scratch = [
        v((32, rows), F32), v((32, rows), F32), v((8, rows), F32),
        v((64, rows), BF16), v((64, rows), BF16), v((8, rows), F32),
        v((128, HID), F32), v((HID, 128), F32), v((2, HID, 128), F32), v((HID, 128), F32),
        v((2, 24, HID), F32), v((2, 2, HID, HID), F32), v((2, 4, HID), F32),
        v((HID, 64), BF16), v((512, HID), BF16), v((512, HID), BF16), v((512, HID), BF16), v((512, HID), BF16),
        v((16, HID), BF16), v((HID, 16), BF16), v((16, HID), BF16),
        v((2, HID, 64), BF16), v((2, 512, HID), BF16), v((2, 512, HID), BF16), v((2, 16, HID), BF16),
        v((HID, 64), BF16), v((512, HID), BF16), v((512, HID), BF16), v((512, HID), BF16), v((512, HID), BF16),
        v((32, HID), BF16), v((HID, 32), BF16),
        big(272), big(272), big(), big(), big(), big(), big(), big(), big(), big(), big(), big(),
        v((40, rows), F32),
        v((1, rows), F32), v((24, rows), F32), v((16, rows // 2), BF16), v((7, 16, rows // 2), BF16),
        v((16, rows), BF16), v((16, rows), BF16),
        v((16, rows // 2), BF16), v((8, 16, rows // 2), BF16), v((1, rows), F32),
        v((1, rows), F32), v((4, 1, rows), F32), v((1, rows), F32),
        v((272, HID), F32), v((HID, HID), F32), v((272, HID), F32), v((HID, HID), F32),
        v((32, HID), F32), v((16, HID), F32), v((8, HID), F32), v((32, HID), F32),
        v((size_c, HID), F32), v((size_a, HID), F32), v((2, size_c, HID), F32), v((size_a, HID), F32),
        v((n_dp - 1, HID // n_dp, HID), F32), v((n_dp - 1, HID // n_dp, HID), F32),
        v((n_dp - 1, (size_c - 2 * HID) // n_dp, HID), F32), v((n_dp - 1, size_a // (4 * n_dp), HID), F32),
        dma((2, 4)), dma((2, 4)), dma, dma, dma((8,)), dma((4,)), dma((7,)), dma((7,)), dma((4,)), dma((8,)),
        dma((4, n_dp - 1)), dma((4, n_dp - 1)), dma((4, n_dp - 1)), dma((4, n_dp - 1)), dma((4, n_dp)), dma((4, n_dp)),
        dma((3,)), dma((3,)), dma((5,)),
    ]
    spec = pl.BlockSpec(memory_space=pltpu.VMEM)
    anyspace = pl.BlockSpec(memory_space=pl.ANY)
    shape = lambda *s: jax.ShapeDtypeStruct(s, F32)
    return pl.pallas_call(
        functools.partial(kernel, n_dp, rows, False),
        out_shape=(
            shape(2, size_c, HID), shape(size_a, HID), shape(2, 24, HID), shape(2, 2, HID, HID), shape(2, 4, HID),
        ),
        in_specs=[spec] * 5 + [pl.BlockSpec(memory_space=pltpu.SMEM)] + [spec] * 6,
        out_specs=(anyspace,) * 5,
        scratch_shapes=scratch,
        compiler_params=pltpu.CompilerParams(collective_id=0, has_side_effects=True, vmem_limit_bytes=63 * 2**20),
        name="edac_gradients",
    )(*data, *own, *aparams)


def adamw(param, grad, first, second):
    first_new = BETA_ONE * first + (1.0 - BETA_ONE) * grad
    second_new = BETA_TWO * second + (1.0 - BETA_TWO) * grad * grad
    ratio = first_new / (1.0 - BETA_ONE**STEP) / (jnp.sqrt(second_new / (1.0 - BETA_TWO**STEP)) + EPS)
    return (param - LEARN * (ratio + DECAY * param), first_new, second_new)


def update_kernel(
    gh, gs, gah, gas,
    own_e, own_h, own_b, on_e, on_h, on_b, em, ev, hm, hv, bm, bv,
    ae, ah, ab, aem, aev, ahm, ahv, abm, abv,
    o_e, o_h, o_b, o_em, o_ev, o_hm, o_hv, o_bm, o_bv,
    o_ae, o_ah, o_ab, o_aem, o_aev, o_ahm, o_ahv, o_abm, o_abv, o_ms, o_as,
    ge, gb, gae, gab,
):
    online = lax.axis_index("grp") == 1
    scale = 1.0 / gas[21:22, 1:2]

    def critic(own, param, grad, first, second):
        master, m_new, v_new = adamw(param, grad, first, second)
        polyak = TAU * master.astype(BF16).astype(F32) + (1.0 - TAU) * own
        return jnp.where(online, master, polyak), m_new, v_new

    o_h[0, 0], o_hm[0, 0], o_hv[0, 0] = critic(own_h[0, 0], on_h[0, 0], gh[0] * scale, hm[0, 0], hv[0, 0])
    o_ah[0], o_ahm[0], o_ahv[0] = adamw(ah[0], gah[...] * scale, ahm[0], ahv[0])

    @pl.when(pl.program_id(0) == 0)
    def _():
        for m in range(2):
            small = gs.at[1 - m]
            ge[0:OBS, :] = small[0:OBS, :]
            ge[OBS : OBS + ACT, :] = small[24 : 24 + ACT, :]
            ge[23:24, :] = small[23:24, :]
            gb[0:3, :] = small[17:20, :]
            gb[3:4, :] = small[22:23, :]
            o_e[m], o_em[m], o_ev[m] = critic(own_e[m], on_e[m], ge[...] * scale, em[m], ev[m])
            o_b[m], o_bm[m], o_bv[m] = critic(own_b[m], on_b[m], gb[...] * scale, bm[m], bv[m])
            o_ms[m : m + 1, :] = small[20:21, 0:2]
        gae[0:OBS, :] = gas[0:OBS, :]
        gae[OBS : OBS + 2 * ACT, :] = gas[32 : 32 + 2 * ACT, :]
        gab[0:3, :] = gas[17:20, :]
        gab[3:4, :] = gas[20:21, :]
        o_ae[...], o_aem[...], o_aev[...] = adamw(ae[...], gae[...] * scale, aem[...], aev[...])
        o_ab[...], o_abm[...], o_abv[...] = adamw(ab[...], gab[...] * scale, abm[...], abv[...])
        o_as[...] = gas[21:22, 0:2]


def update(grads, own, online, moments, aparams, amoments):
    size_c = grads[0].shape[1]
    shape = lambda *s: jax.ShapeDtypeStruct(s, F32)
    whole = lambda *s: pl.BlockSpec(s, lambda i: (0,) * len(s))
    mat = pl.BlockSpec((1, 1, HID, HID), lambda i: (i // 2, i % 2, 0, 0))
    amat = pl.BlockSpec((1, HID // 2, HID), lambda i: (i // 2, i % 2, 0))
    edge, bias, aedge, abias = whole(2, 24, HID), whole(2, 4, HID), whole(29, HID), whole(4, HID)
    in_specs = [
        pl.BlockSpec((1, HID, HID), lambda i: (1 - i // 2, i % 2, 0)),
        pl.BlockSpec((2, 32, HID), lambda i: (0, 16, 0)),
        pl.BlockSpec((HID // 2, HID), lambda i: (i, 0)),
        pl.BlockSpec((ACTOR_SMALL, HID), lambda i: (8, 0)),
        edge, mat, bias, edge, mat, bias, edge, edge, mat, mat, bias, bias,
        aedge, amat, abias, aedge, aedge, amat, amat, abias, abias,
    ]
    out_specs = (edge, mat, bias, edge, edge, mat, mat, bias, bias, aedge, amat, abias, aedge, aedge, amat, amat, abias, abias,
                 whole(2, 2), whole(1, 2))
    e_, h_, b_ = shape(2, 24, HID), shape(2, 2, HID, HID), shape(2, 4, HID)
    ae_, ah_, ab_ = shape(29, HID), shape(2, HID, HID), shape(4, HID)
    return pl.pallas_call(
        update_kernel,
        grid=(4,),
        out_shape=(e_, h_, b_, e_, e_, h_, h_, b_, b_, ae_, ah_, ab_, ae_, ae_, ah_, ah_, ab_, ab_, shape(2, 2), shape(1, 2)),
        in_specs=in_specs,
        out_specs=out_specs,
        scratch_shapes=[pltpu.VMEM((24, HID), F32), pltpu.VMEM((4, HID), F32), pltpu.VMEM((29, HID), F32), pltpu.VMEM((4, HID), F32)],
        name="adamw",
    )(grads[0], grads[0], grads[1], grads[1], *own, *online, *moments, *aparams, *amoments)


def body(
    n_dp,
    states, actions, rewards, done, noise, counts,
    crit_edge, crit_hidden, crit_bias, edge_m, edge_v, hidden_m, hidden_v, bias_m, bias_v,
    act_edge, act_hidden, act_bias, act_edge_m, act_edge_v, act_hidden_m, act_hidden_v, act_bias_m, act_bias_v,
):
    rows = states.shape[0]
    own = (crit_edge[0], crit_hidden[0], crit_bias[0])
    aparams = (act_edge, act_hidden, act_bias)
    data = (states.T, actions.T, noise.T, rewards[None], done[None], counts)
    grad_c, grad_a, on_e, on_h, on_b = fused(n_dp, rows, data, own, aparams)
    out = update(
        (grad_c, grad_a), own, (on_e, on_h, on_b),
        (edge_m, edge_v, hidden_m, hidden_v, bias_m, bias_v), aparams,
        (act_edge_m, act_edge_v, act_hidden_m, act_hidden_v, act_bias_m, act_bias_v),
    )
    return (*(o[None] for o in out[:3]), *out[3:19], out[19][0])


def solution(mesh):
    member = P("grp", "ens", None, None)
    hidden = P("grp", "ens", None, None, None)
    mom = P("ens", None, None)
    mom_h = P("ens", None, None, None)
    return jax.shard_map(
        functools.partial(body, mesh.shape["dp"]),
        mesh=mesh,
        in_specs=(
            P("dp", None), P("dp", None), P("dp"), P("dp"), P("dp", None), P("dp"),
            member, hidden, member, mom, mom, mom_h, mom_h, mom, mom,
        ) + (P(),) * 9,
        out_specs=(member, hidden, member, mom, mom, mom_h, mom_h, mom, mom) + (P(),) * 9 + (P("ens", None), P()),
        check_vma=False,
    )
```

```python
import functools

import jax
import jax.numpy as jnp
from jax import lax
from jax.experimental import pallas as pl
from jax.experimental.pallas import tpu as pltpu
from jax.sharding import PartitionSpec as P

OBS = 17
ACT = 6
HID = 256
STEP = 5
FOLD_ROWS = 2816
LANES = 128

GAMMA = 0.99
ALPHA = 0.2
ETA = 1.0
LEARN = 0.03
BETA_ONE = 0.5
BETA_TWO = 0.5
DECAY = 0.01
EPS = 1e-08
TAU = 0.05
HALF_LOG_TWO_PI = 0.9189385332046727
LOG_TWO = 0.6931471805599453

F32 = jnp.float32
BF16 = jnp.bfloat16

CRITIC_SMALL, ACTOR_SMALL = 32, 64


def dot(a, b):
    return lax.dot_general(a, b, (((1,), (0,)), ((), ())), preferred_element_type=F32)


def dot_t(a, b):
    return lax.dot_general(a, b, (((1,), (1,)), ((), ())), preferred_element_type=F32)


def split(w):
    high = w.astype(BF16).astype(F32)
    return high, w - high


def halves(p):
    n = p.shape[0] // 2
    return p[:n] + p[n:]


def prep_input(stage, w1, edge, bias, n_in):
    stage[...] = jnp.zeros_like(stage)
    stage[0:OBS, :] = edge[0:OBS, :]
    stage[OBS : OBS + 1, :] = bias[0:1, :]
    if n_in > OBS:
        stage[24 : 24 + ACT, :] = edge[OBS : OBS + ACT, :]
    high, low = split(0.5 * stage[0:32, :])
    w1[...] = jnp.concatenate([high, low, high], 0).T.astype(BF16)


def prep_hidden(fwd, bwd, hidden):
    w = 0.5 * hidden
    if fwd is not None:
        high, low = split(w.T)
        fwd[...] = jnp.concatenate([high, low], 0).astype(BF16)
    if bwd is not None:
        high, low = split(w)
        bwd[...] = jnp.concatenate([high, low], 0).astype(BF16)


def silu_half(u):
    t = jnp.tanh(u)
    return u + u * t, t


def up(n, by):
    return -(-n // by) * by


def kernel(
    n_dp,
    rows,
    block,
    fold,
    states, actions, noise, rewards, done, counts, mask, c_edge, c_hidden, c_bias, a_edge, a_hidden, a_bias,
    out_c, out_a, out_pe, out_ph, out_pb, out_low,
    xs, ns, eps_s, far_x, far_n, far_e, here_x, here_n, here_e, x_b, pi_b, pi_act, stage, vec, tvec, avec,
    p_edge, p_hidden, p_bias, low_out, low_in,
    w1, f0, f1, b0, b1, ga, t1w, eq,
    tw1, tf0, tf1, teq,
    aw1, af0, af1, ab0, ab1, ao, aot,
    h1x, h2x, h3s, s1, s2, s3, k1, k2, k3, d1s, d2s, d3s,
    heads, ah1x, ah2x, ah3, as1, as2, as3,
    value, unit_f, u_mine, u_peer, u_pair, u_far, u_total, dg_b, dv_b, dvh,
    q_mine, q_peer, q_pair, q_far, q_total, q_own, least, least_in,
    acc_h1, acc_h1t, acc_h0, acc_h0t, acc_x, acc_t, acc_last, acc_o,
    part_c, part_a, sum_c, sum_a, in_h1, in_h0, in_sm, in_ac,
    fold_s, fold_r, sem_param_s, sem_param_r, sem_piece_s, sem_piece_r, sem_low_s, sem_low_r, sem_pi_s, sem_pi_r, sem_least_s, sem_least_r, es_s, es_r,
    rs_s, rs_r, ag_s, ag_r, xf_s, xf_r, ef_s, ef_r, sem_out, *boxes,
):
    g = lax.axis_index("grp")
    e = lax.axis_index("ens")
    z = lax.axis_index("dp")
    me = g * 4 + e
    blocks = rows // block
    extra = states.shape[1] - rows
    lower = z < n_dp // 2
    upper = z >= n_dp - n_dp // 2
    half = rows // 2
    online = g == 1
    targetd = g == 0
    critics = 8
    coded = bool(boxes)

    def dev(gg, ee):
        return {"grp": gg, "ens": ee}

    def remote(src, dst, send, recv, where):
        return pltpu.make_async_remote_copy(
            src_ref=src, dst_ref=dst, send_sem=send, recv_sem=recv, device_id=where, device_id_type=pl.DeviceIdType.MESH
        )

    barrier = pltpu.get_barrier_semaphore()
    for k in range(1, 8):
        p = lax.rem(me + k, 8)
        pl.semaphore_signal(barrier, inc=1, device_id=dev(p // 4, lax.rem(p, 4)), device_id_type=pl.DeviceIdType.MESH)
    for k in range(1, n_dp):
        pl.semaphore_signal(barrier, inc=1, device_id={"dp": lax.rem(z + k, n_dp)}, device_id_type=pl.DeviceIdType.MESH)
    pl.semaphore_wait(barrier, 7 + n_dp - 1)

    piece = HID // n_dp

    def piece_of(shard):
        return pl.ds(pl.multiple_of(shard * piece, 8), piece)

    def param_copy(what):
        src, dst = (
            (c_hidden.at[1, 1, piece_of(z)], p_hidden.at[1, piece_of(z)]),
            (c_edge.at[1], p_edge),
            (c_bias.at[1], p_bias),
            (c_hidden.at[1, 0], p_hidden.at[0]),
        )[what]
        return remote(src, dst, sem_param_s.at[what], sem_param_r.at[what], dev(0, e))

    def param_spread(k):
        mine = p_hidden.at[1, piece_of(z)]
        return remote(mine, mine, sem_piece_s.at[k - 1], sem_piece_r.at[k - 1], {"dp": lax.rem(z + k, n_dp)})

    def low_copy():
        return remote(low_out, low_in, sem_low_s, sem_low_r, dev(0, e))

    @pl.when(online)
    def _():
        for what in range(4):
            param_copy(what).start()

    lane_id = lax.broadcasted_iota(jnp.int32, (1, states.shape[1]), 1)
    if fold:
        code = jnp.where(lane_id < counts[0], 2.0, 0.0) + done[...].astype(F32)
    else:
        code = 2.0 * mask[...] + done[...].astype(F32)

    def lay_out(x, n, e8, sl):
        ones_row = jnp.ones((1, x.shape[1]), F32)
        x[...] = jnp.zeros_like(x)
        x[0:OBS, :] = states[0:OBS, sl]
        x[OBS : OBS + 1, :] = ones_row
        x[24 : 24 + ACT, :] = actions[:, sl]
        e8[6:7, :] = rewards[:, sl]
        e8[7:8, :] = code[:, sl]

        @pl.when(online)
        def _():
            e8[0:ACT, :] = noise[0:ACT, sl]

        @pl.when(targetd)
        def _():
            e8[0:ACT, :] = noise[ACT : 2 * ACT, sl]
            n[...] = jnp.zeros_like(n)
            n[0:OBS, :] = states[OBS : 2 * OBS, sl]
            n[OBS : OBS + 1, :] = ones_row

    core = lax.rem(e, 2)
    other_core = e + 1 - 2 * core
    far_chip = lax.rem(e + 2, 4)

    def fold_copy(what, hop):
        here, there = ((here_n, far_n), (here_e, far_e), (here_x, far_x))[what]
        if hop == 0:
            return remote(here.at[core], there.at[core], fold_s.at[what, 0], fold_r.at[what, 0], {"dp": n_dp - 1 - z})
        return remote(there.at[core], there.at[core], fold_s.at[what, 1], fold_r.at[what, 1], dev(g, other_core))

    def merge(into, pieces, bound):
        first, count = rows - extra, extra // LANES
        per = count // 2
        order = [count - 1 - k for k in range(count)]
        there = jnp.concatenate(
            [pieces[b // per, :, (b % per) * LANES : (b % per + 1) * LANES] for b in order], 1
        ).astype(F32)
        lanes = lax.broadcasted_iota(jnp.int32, (1, extra), 1) + first
        into[:, first:rows] = jnp.where(lanes < bound, into[:, first:rows], there)

    if fold:
        bound = (jnp.minimum(counts[0], rows) + LANES - 1) // LANES * LANES

        @pl.when(upper)
        def _():
            lay_out(xs.at[:, 0:extra], ns.at[:, 0:extra], eps_s.at[:, 0:extra], slice(rows, rows + extra))
            for h in range(2):
                part = slice(h * extra // 2, (h + 1) * extra // 2)
                here_e[h] = eps_s[:, part]
                here_x[h] = xs[:, part]

            @pl.when(targetd)
            def _():
                for h in range(2):
                    here_n[h] = ns[:, h * extra // 2 : (h + 1) * extra // 2]
                fold_copy(0, 0).start()

            fold_copy(1, 0).start()
            fold_copy(2, 0).start()

    lay_out(xs, ns, eps_s, slice(0, rows))

    def fold_in(whats):
        if fold:
            @pl.when(lower)
            def _():
                for what in whats:
                    fold_copy(what, 0).wait_recv()
                    fold_copy(what, 1).start()
                for what in whats:
                    fold_copy(what, 1).wait_recv()
                    merge((ns, eps_s, xs)[what], (far_n, far_e, far_x)[what], bound)

    def put_x():
        high, low = split(xs[...])
        xin = high.astype(BF16)
        x_b[0:32, :] = xin
        x_b[32:64, :] = xin
        x_b[64:96, :] = low.astype(BF16)

    def prep_critic(edge, hid0, hid1, bias, w1_, f0_, f1_, b0_, b1_, vec_, eq_, ga_, t1_):
        prep_input(stage, w1_, edge, bias, OBS + ACT)
        prep_hidden(f0_, b0_, hid0[...])
        prep_hidden(f1_, b1_, hid1[...])
        stage[...] = jnp.zeros_like(stage)
        stage[0:1, :] = 0.5 * bias[1:2, :]
        stage[1:2, :] = 0.5 * bias[2:3, :]
        stage[2:3, :] = edge[23:24, :]
        vec_[...] = stage[...].T
        vec_[0:1, 8:9] = bias[3:4, 0:1]
        stage[...] = jnp.zeros_like(stage)
        high, low = split(edge[23:24, :])
        stage[0:1, :] = high
        stage[1:2, :] = low
        eq_[...] = stage[0:16, :].astype(BF16)
        if ga_ is not None:
            stage[...] = jnp.zeros_like(stage)
            stage[0:ACT, :] = 0.5 * edge[OBS : OBS + ACT, :]
            high, low = split(stage[0:8, :])
            both = jnp.concatenate([high, low], 0)
            ga_[...] = both.astype(BF16)
            stage[0:16, :] = both
            t1_[...] = stage[...].T[:, 0:16].astype(BF16)

    def prep_actor():
        prep_input(stage, aw1, a_edge, a_bias, OBS)
        prep_hidden(af0, ab0, a_hidden[0])
        prep_hidden(af1, ab1, a_hidden[1])
        stage[...] = jnp.zeros_like(stage)
        stage[0:1, :] = 0.5 * a_bias[1:2, :]
        stage[1:2, :] = 0.5 * a_bias[2:3, :]
        stage[2:3, :] = a_bias[3:4, :]
        avec[...] = stage[...].T
        stage[...] = jnp.zeros_like(stage)
        stage[0:ACT, :] = a_edge[OBS : OBS + ACT, :]
        stage[8 : 8 + ACT, :] = a_edge[OBS + ACT : OBS + 2 * ACT, :]
        high, low = split(stage[0:16, :])
        ao[...] = jnp.concatenate([high, low], 0).astype(BF16)
        stage[...] = jnp.zeros_like(stage)
        stage[0 : 2 * ACT, :] = a_edge[OBS : OBS + 2 * ACT, :]
        high, low = split(stage[0:16, :])
        stage[0:32, :] = jnp.concatenate([high, low], 0)
        aot[...] = stage[...].T[:, 0:32].astype(BF16)

    prep_actor()

    def actor_layers(src):
        kept = []
        hb = None
        for w, b in ((aw1, None), (af0, 0), (af1, 1)):
            u = dot(w[...], src) if b is None else halves(dot(w[...], hb)) + avec[:, b : b + 1]
            h, t = silu_half(u)
            hb = h.astype(BF16)
            kept.append((hb, h, t))
        return kept

    ok8 = (lax.broadcasted_iota(jnp.int32, (8, 1), 0) < ACT).astype(F32)

    def actor_heads(hb, sl):
        out = halves(dot(ao[...], hb))
        eps = eps_s[:, sl]
        center = out[0:8] + avec[0:8, 2:3] * ok8
        th = jnp.tanh(out[8:16] + avec[6:14, 2:3] * ok8)
        log_std = 3.5 * th - 1.5
        spread_e = jnp.exp(log_std) * eps
        latent = center + spread_e
        soft = jnp.maximum(-2.0 * latent, 0.0) + jnp.log(1.0 + jnp.exp(-2.0 * jnp.abs(latent)))
        terms = -0.5 * eps * eps - log_std - HALF_LOG_TWO_PI - 2.0 * (LOG_TWO - latent - soft)
        logp = jnp.sum(terms * ok8, axis=0, keepdims=True)
        sample = jnp.tanh(latent) * ok8
        return sample, logp, th, spread_e

    @pl.when(targetd)
    def _():
        param_copy(0).wait_recv()
        for k in range(1, n_dp):
            param_spread(k).start()

    @pl.when(online)
    def _():
        put_x()

        def body(i, _):
            @pl.when(i == 1)
            def _():
                fold_in((1, 2))
                if fold:
                    put_x()

            sl = pl.ds(pl.multiple_of(i * block, block), block)
            kept = actor_layers(x_b[:, sl])
            if fold:
                for store, curve, (hb, h, t) in zip((ah1x, ah2x, ah3), (as1, as2, as3), kept):
                    store[0:HID, sl] = hb
                    curve[:, sl] = (1.0 + t) + h * (1.0 - t)
            sample, logp, th, spread_e = actor_heads(kept[2][0], sl)
            pi_act[:, sl] = sample
            heads[0:8, sl] = th
            heads[8:16, sl] = spread_e
            heads[16:17, sl] = logp
            return 0

        lax.fori_loop(0, blocks, body, 0)
        remote(pi_act, pi_act, sem_pi_s, sem_pi_r, dev(0, e)).start()
        prep_critic(c_edge.at[0], c_hidden.at[0, 0], c_hidden.at[0, 1], c_bias.at[0], w1, f0, f1, b0, b1, vec, eq, ga, t1w)

    def least_online(k):
        return remote(least, least_in.at[k], sem_least_s.at[4 + k], sem_least_r.at[k], dev(1, lax.rem(e + k, 4)))

    def least_target(k):
        return remote(least, least_in.at[k], sem_least_s.at[k], sem_least_r.at[k], dev(0, lax.rem(e + k, 4)))

    @pl.when(targetd)
    def _():
        for m in range(2):
            prep_critic(
                c_edge.at[m], c_hidden.at[m, 0], c_hidden.at[m, 1], c_bias.at[m],
                tw1.at[m], tf0.at[m], tf1.at[m], None, None, tvec.at[m], teq.at[m], None, None,
            )

        def body(i, _):
            @pl.when(i == 1)
            def _():
                fold_in((0, 1))

            sl = pl.ds(pl.multiple_of(i * block, block), block)
            high, rest = split(ns[:, sl])
            nx, rest = high.astype(BF16), rest.astype(BF16)
            kept = actor_layers(jnp.concatenate([nx, nx, rest], 0))
            sample, logp, th, spread_e = actor_heads(kept[2][0], sl)
            high, rest = split(jnp.concatenate([ns[0:24, sl], sample], 0))
            nx = high.astype(BF16)
            nx = jnp.concatenate([nx, nx, rest.astype(BF16)], 0)
            low = None
            for m in range(2):
                h, t = silu_half(dot(tw1[m], nx))
                h, t = silu_half(halves(dot(tf0[m], h.astype(BF16))) + tvec[m, :, 0:1])
                h, t = silu_half(halves(dot(tf1[m], h.astype(BF16))) + tvec[m, :, 1:2])
                r = dot(teq[m], h.astype(BF16))
                q = r[0:1] + r[1:2] + tvec[m, 0:1, 8:9]
                low = q if low is None else jnp.minimum(low, q)
            least[:, sl] = low - ALPHA * logp
            return 0

        lax.fori_loop(0, blocks, body, 0)
        for k in range(1, 4):
            least_target(k).start()
        for k in range(4):
            least_online(k).start()
        for what in range(1, 4):
            param_copy(what).wait_recv()
        for k in range(1, n_dp):
            param_spread(k).wait_recv()
        prep_critic(p_edge, p_hidden.at[0], p_hidden.at[1], p_bias, w1, f0, f1, b0, b1, vec, eq, ga, t1w)
        fold_in((2,))
        put_x()
        remote(pi_act, pi_act, sem_pi_s, sem_pi_r, dev(0, e)).wait_recv()

    valid = jnp.where(eps_s[7:8, :] > 1.5, 1.0, 0.0)

    class EnsembleSum:
        def __init__(self, index, mine, peer, pair, far, total, only_online):
            self.index, self.mine, self.peer, self.pair, self.far, self.total, self.only_online = (
                index, mine, peer, pair, far, total, only_online,
            )

        def to_core(self):
            return remote(self.mine.at[1 - core], self.peer, es_s.at[self.index, 0], es_r.at[self.index, 0], dev(g, other_core))

        def to_chip(self, k):
            across = (1 - g, g, 1 - g)[k]
            where = dev(across, (e, far_chip, far_chip)[k])
            return remote(self.pair, self.far.at[k], es_s.at[self.index, 1 + k], es_r.at[self.index, 1 + k], where)

        def back(self):
            return remote(self.total.at[core], self.total.at[core], es_s.at[self.index, 4], es_r.at[self.index, 4], dev(g, other_core))

        def begin(self, first, second):
            self.mine[0] = first
            self.mine[1] = second
            self.to_core().start()

        def middle(self):
            self.to_core().wait_recv()
            self.pair[...] = self.mine[core] + self.peer[...]
            if not self.only_online:
                for k in range(3):
                    self.to_chip(k).start()
            else:
                @pl.when(targetd)
                def _():
                    self.to_chip(0).start()
                    self.to_chip(2).start()

                @pl.when(online)
                def _():
                    self.to_chip(1).start()

        def last(self):
            for k in range(3):
                self.to_chip(k).wait_recv()
            self.total[core] = self.pair[...] + self.far[0] + self.far[1] + self.far[2]
            self.back().start()

        def whole(self):
            self.back().wait_recv()
            return jnp.concatenate([self.total[0], self.total[1]], 1)

        def sent(self):
            self.to_core().wait_send()
            if not self.only_online:
                for k in range(3):
                    self.to_chip(k).wait_send()
                self.back().wait_send()
            else:
                @pl.when(targetd)
                def _():
                    self.to_chip(0).wait_send()
                    self.to_chip(2).wait_send()

                @pl.when(online)
                def _():
                    self.to_chip(1).wait_send()
                    self.back().wait_send()

    unit_sum = EnsembleSum(0, u_mine, u_peer, u_pair, u_far, u_total, False)
    slope_sum = EnsembleSum(1, q_mine, q_peer, q_pair, q_far, q_total, True)

    pin = jnp.concatenate([xs[0:24, :], pi_act[...]], 0).astype(BF16)
    pi_b[0:32, :] = pin
    pi_b[32:64, :] = pin

    def body_p(i, _):
        sl = pl.ds(pl.multiple_of(i * block, block), block)

        def act(u):
            h, t = silu_half(u)
            hb, tb = h.astype(BF16), t.astype(BF16)
            one = jnp.ones((), BF16)
            return hb, (one + tb) + hb * (one - tb)

        h, a1 = act(dot(w1[:, 0:64], pi_b[:, sl]))
        h, a2 = act(dot(f0[0:HID, :], h) + vec[:, 0:1])
        h, a3 = act(dot(f1[0:HID, :], h) + vec[:, 1:2])
        r = dot(eq[...], h)
        q_own[:, sl] = r[0:1] + r[1:2] + vec[0:1, 8:9]
        d = vec[:, 2:3].astype(BF16) * a3
        d = dot(b1[0:HID, :], d).astype(BF16) * a2
        d = dot(b0[0:HID, :], d).astype(BF16) * a1
        unit_f[16:24, sl] = halves(dot(ga[...], d))
        return 0

    lax.fori_loop(0, blocks, body_p, 0)
    rid = lax.broadcasted_iota(jnp.int32, (8, 1), 0)
    packed = unit_f[16:24, :] + jnp.where(rid == 6, q_own[...], 0.0)
    slope_sum.begin(packed[:, 0:half], packed[:, half:rows])

    ones = (lax.broadcasted_iota(jnp.int32, (16, rows), 0) == 0).astype(BF16)
    h1x[HID : HID + 16, :] = ones
    h2x[HID : HID + 16, :] = ones

    def curves(u):
        h, t = silu_half(u)
        c = 1.0 + t
        d = 1.0 - t
        return h, c + h * d, (c * d) * (1.0 - u * t)

    def body_a(i, _):
        @pl.when(i == 1)
        def _():
            slope_sum.middle()

        sl = pl.ds(pl.multiple_of(i * block, block), block)
        h, a1, q1 = curves(dot(w1[...], x_b[:, sl]))
        hb = h.astype(BF16)
        h1x[0:HID, sl] = hb
        s1[:, sl] = a1.astype(BF16)
        h, a2, q2 = curves(halves(dot(f0[...], hb)) + vec[:, 0:1])
        hb = h.astype(BF16)
        h2x[0:HID, sl] = hb
        s2[:, sl] = a2.astype(BF16)
        h, a3, q3 = curves(halves(dot(f1[...], hb)) + vec[:, 1:2])
        hb = h.astype(BF16)
        h3s[:, sl] = hb
        s3[:, sl] = a3.astype(BF16)
        r = dot(eq[...], hb)
        value[:, sl] = r[0:1] + r[1:2] + vec[0:1, 8:9]
        last = vec[:, 2:3]
        db = (last * a3).astype(BF16)
        d3s[:, sl] = db
        k3[:, sl] = (last * q3).astype(BF16)
        m = halves(dot(b1[...], db))
        db = (m * a2).astype(BF16)
        d2s[:, sl] = db
        k2[:, sl] = (m * q2).astype(BF16)
        m = halves(dot(b0[...], db))
        db = (m * a1).astype(BF16)
        d1s[:, sl] = db
        k1[:, sl] = (m * q1).astype(BF16)
        slope = halves(dot(ga[...], db))
        inv = lax.rsqrt(jnp.sum(slope * slope, axis=0, keepdims=True) + 0.01)
        unit_f[0:8, sl] = slope * inv
        unit_f[8:9, sl] = inv
        return 0

    lax.fori_loop(0, blocks, body_a, 0)
    unit_sum.begin(unit_f[0:8, 0:half], unit_f[0:8, half:rows])
    unit_sum.middle()

    class Exchange:
        def __init__(self, index, part, into, inbox, base, count, wide):
            self.index, self.part, self.into, self.inbox, self.base, self.count, self.wide = index, part, into, inbox, base, count, wide
            self.each = count // (n_dp * (4 if wide else 1))

        def rows_of(self, shard):
            first = self.base + (e * n_dp + shard if self.wide else shard) * self.each
            return pl.ds(pl.multiple_of(first, 8), self.each)

        def scatter(self, k):
            to = lax.rem(z + k, n_dp)
            return remote(
                self.part.at[self.rows_of(to)], self.inbox.at[k - 1], rs_s.at[self.index, k - 1, 0], rs_r.at[self.index, k - 1, 0], {"dp": to}
            )

        def gather(self, k):
            mine = self.into.at[self.rows_of(z)]
            return remote(mine, mine, ag_s.at[self.index, k - 1, 0], ag_r.at[self.index, k - 1, 0], {"dp": lax.rem(z + k, n_dp)})

        def across(self, k):
            there = self.into.at[self.rows_of(lax.rem(z + n_dp - k, n_dp))]
            return remote(there, there, xf_s.at[self.index, k, 0], xf_r.at[self.index, k, 0], dev(1 - g, e))

        def start(self):
            for k in range(1, n_dp):
                self.scatter(k).start()

        def reduce(self):
            total = self.part[self.rows_of(z), :]
            for k in range(1, n_dp):
                self.scatter(k).wait_recv()
                total = total + self.inbox[k - 1]
            self.into[self.rows_of(z), :] = total
            for k in range(1, n_dp):
                self.gather(k).start()
            self.across(0).start()

        def forward(self):
            for k in range(1, n_dp):
                self.gather(k).wait_recv()
                self.across(k).start()

        def sent(self):
            for k in range(1, n_dp):
                self.scatter(k).wait_send()
                self.gather(k).wait_send()
            for k in range(n_dp):
                self.across(k).wait_send()

        def arrived(self):
            for k in range(n_dp):
                self.across(k).wait_recv()

    class Coded(Exchange):
        def __init__(self, index, part, out, base, count, lead, wide, boxes):
            self.index, self.part, self.out, self.base, self.count, self.lead, self.wide = index, part, out, base, count, lead, wide
            self.out_w, self.out_s, self.in_w, self.in_s, self.all_w, self.all_s = boxes
            self.each = count // (n_dp * (4 if wide else 1))

        def pack(self, x):
            top = jnp.maximum(jnp.max(jnp.abs(x), axis=0, keepdims=True), 1e-30)
            q = jnp.round(x * (32767.0 / top)).astype(jnp.int32)
            h = self.each // 2
            return jnp.bitwise_or(jnp.bitwise_and(q[:h], 65535), jnp.left_shift(q[h:], 16)), top * (1.0 / 32767.0)

        def unpack(self, w, scale):
            low = jnp.right_shift(jnp.left_shift(w, 16), 16)
            high = jnp.right_shift(w, 16)
            return jnp.concatenate([low, high], 0).astype(F32) * scale

        def scatter(self, k):
            to = lax.rem(z + k, n_dp)
            return Both([
                remote(o.at[to], i.at[k - 1], rs_s.at[self.index, k - 1, q], rs_r.at[self.index, k - 1, q], {"dp": to})
                for q, (o, i) in enumerate(((self.out_w, self.in_w), (self.out_s, self.in_s)))
            ])

        def gather(self, k):
            return Both([
                remote(
                    a.at[self.lead, z], a.at[self.lead, z], ag_s.at[self.index, k - 1, q], ag_r.at[self.index, k - 1, q],
                    {"dp": lax.rem(z + k, n_dp)},
                )
                for q, a in enumerate((self.all_w, self.all_s))
            ])

        def across(self, k):
            there = lax.rem(z + n_dp - k, n_dp)
            return Both([
                remote(
                    a.at[self.lead, there], a.at[self.lead, there], xf_s.at[self.index, k, q], xf_r.at[self.index, k, q], dev(1 - g, e)
                )
                for q, a in enumerate((self.all_w, self.all_s))
            ])

        def start(self):
            for shard in range(n_dp):
                w, scale = self.pack(self.part[self.rows_of(shard), :])
                self.out_w[shard] = w
                self.out_s[shard] = scale
            for k in range(1, n_dp):
                self.scatter(k).start()

        def reduce(self):
            total = self.part[self.rows_of(z), :]
            for k in range(1, n_dp):
                self.scatter(k).wait_recv()
                total = total + self.unpack(self.in_w[k - 1], self.in_s[k - 1])
            w, scale = self.pack(total)
            self.all_w[self.lead, z] = w
            self.all_s[self.lead, z] = scale
            for k in range(1, n_dp):
                self.gather(k).start()
            self.across(0).start()

        def decode(self):
            for lead in range(self.all_w.shape[0]):
                for shard in range(n_dp):
                    x = self.unpack(self.all_w[lead, shard], self.all_s[lead, shard])
                    if self.wide:
                        first = (lead * n_dp + shard) * self.each
                        self.out[first : first + self.each, :] = x
                    else:
                        first = self.base + shard * self.each
                        self.out[lead, first : first + self.each, :] = x

    class Both:
        def __init__(self, copies):
            self.copies = copies

        def start(self):
            for c in self.copies:
                c.start()

        def wait_recv(self):
            for c in self.copies:
                c.wait_recv()

        def wait_send(self):
            for c in self.copies:
                c.wait_send()

    small_c = part_c.shape[0] - 2 * HID
    if coded:
        box_h1, box_h0, box_ac = boxes[0:6], boxes[6:12], boxes[12:18]
    if coded:
        ex_h1 = Coded(0, part_c, sum_c, HID, HID, g, False, box_h1)
        ex_h0 = Coded(1, part_c, sum_c, 0, HID, g, False, box_h0)
        ex_ac = Coded(3, part_a, sum_a, 0, 2 * HID, e, True, box_ac)
        ex_as = Exchange(4, part_a, sum_a, in_ac, 2 * HID, ACTOR_SMALL, False)
        actor = (ex_ac, ex_as)
    else:
        ex_h1 = Exchange(0, part_c, sum_c.at[g], in_h1, HID, HID, False)
        ex_h0 = Exchange(1, part_c, sum_c.at[g], in_h0, 0, HID, False)
        ex_ac = Exchange(3, part_a, sum_a, in_ac, 0, part_a.shape[0], True)
        actor = (ex_ac,)
    ex_sm = Exchange(2, part_c, sum_c.at[g], in_sm, 2 * HID, small_c, False)

    def spread_actor(k):
        if coded:
            mine = ex_ac.all_w.at[e]
        else:
            quarter = part_a.shape[0] // 4
            mine = sum_a.at[pl.ds(pl.multiple_of(e * quarter, 8), quarter)]
        return remote(mine, mine, ef_s.at[k - 1], ef_r.at[k - 1], dev(g, lax.rem(e + k, 4)))

    def spread_scale(k):
        mine = ex_ac.all_s.at[e]
        return remote(mine, mine, ef_s.at[2 + k], ef_r.at[2 + k], dev(g, lax.rem(e + k, 4)))

    def spread_start():
        for k in range(1, 4):
            spread_actor(k).start()
            if coded:
                spread_scale(k).start()

    lane = lax.broadcasted_iota(jnp.int32, (1, HID), 1)
    rid32 = lax.broadcasted_iota(jnp.int32, (32, 1), 0)

    def local(src, dst, k):
        return pltpu.make_async_copy(src, dst, sem_out.at[k])

    def own_outputs():
        return (
            local(c_edge.at[1], out_pe, 0), local(c_hidden.at[1], out_ph, 1), local(c_bias.at[1], out_pb, 2), local(low_out, out_low, 5),
        )

    def far_outputs():
        return local(p_edge, out_pe, 0), local(p_hidden, out_ph, 1), local(p_bias, out_pb, 2), local(low_in, out_low, 5)

    @pl.when(online)
    def _():
        slope_sum.last()
        total = slope_sum.whole() * (1.0 / critics)
        d_sample = -valid * total
        d_logp = ALPHA * valid
        sample = pi_act[...]
        th = heads[0:8, :]
        spread_e = heads[8:16, :]
        dz = (d_sample * (1.0 - sample * sample) + d_logp * 2.0 * sample) * ok8
        dls = (dz * spread_e - d_logp) * (3.5 * (1.0 - th * th)) * ok8
        heads[24:40, :] = jnp.zeros((16, rows), F32)
        heads[24:30, :] = dz[0:ACT]
        heads[30:36, :] = dls[0:ACT]
        actor_sum = jnp.sum(valid * (ALPHA * heads[16:17, :] - total[6:7]), axis=1, keepdims=True)
        done_rows = jnp.sum(valid, axis=1, keepdims=True)
        count = counts[0].astype(F32) if fold else 0.0
        for acc in (acc_h1, acc_h0, acc_x, acc_o):
            acc[...] = jnp.zeros_like(acc)
        one16 = (lax.broadcasted_iota(jnp.int32, (16, block), 0) == 0).astype(BF16)
        if fold:
            ah1x[HID : HID + 16, :] = h1x[HID : HID + 16, :]
            ah2x[HID : HID + 16, :] = h1x[HID : HID + 16, :]

        def body_c(i, _):
            sl = pl.ds(pl.multiple_of(i * block, block), block)
            if fold:
                tall1, tall2, top = ah1x[:, sl], ah2x[:, sl], ah3[:, sl]
                slopes = [as1[:, sl], as2[:, sl], as3[:, sl]]
            else:
                kept = actor_layers(x_b[:, sl])
                tall1, tall2 = (jnp.concatenate([kept[k][0], one16], 0) for k in range(2))
                top = kept[2][0]
                slopes = [(1.0 + t) + h * (1.0 - t) for _, h, t in kept]
            do = heads[24:40, sl].astype(BF16)
            acc_o[0:16, :] += dot_t(do, top)
            d3 = (dot(aot[...], jnp.concatenate([do, do], 0)) * (0.5 * slopes[2])).astype(BF16)
            acc_h1[...] += dot_t(tall2, d3)
            d2 = (halves(dot(ab1[...], d3)) * slopes[1]).astype(BF16)
            acc_h0[...] += dot_t(tall1, d2)
            d1 = (halves(dot(ab0[...], d2)) * slopes[0]).astype(BF16)
            acc_x[...] += dot_t(x_b[0:32, sl], d1)
            acc_o[16:32, 0:128] += dot_t(one16, jnp.concatenate([do, jnp.zeros((112, block), BF16)], 0))
            return 0

        lax.fori_loop(0, blocks, body_c, 0)
        part_a[0:HID, :] = acc_h0[0:HID, :]
        part_a[HID : 2 * HID, :] = acc_h1[0:HID, :]
        stats = jnp.where(lane == 0, actor_sum, jnp.where(lane == 1, count, jnp.where(lane == 2, done_rows, 0.0)))
        small = acc_x[...]
        small = small + jnp.where(rid32 == 18, acc_h0[HID : HID + 1, :], 0.0)
        small = small + jnp.where(rid32 == 19, acc_h1[HID : HID + 1, :], 0.0)
        small = small + jnp.where(rid32 == 20, acc_o[16:17, :], 0.0)
        small = small + jnp.where(rid32 == 21, stats, 0.0)
        part_a[2 * HID : 2 * HID + 32, :] = small
        part_a[2 * HID + 32 : 2 * HID + 48, :] = acc_o[0:16, :]
        rest = part_a.shape[0] - 2 * HID - 48
        part_a[2 * HID + 48 :, :] = jnp.zeros((rest, HID), F32)
        for ex in actor:
            ex.start()

    @pl.when(targetd)
    def _():
        least_in[0] = least[...]
        for k in range(1, 4):
            least_target(k).wait_recv()

    @pl.when(online)
    def _():
        for k in range(4):
            least_online(k).wait_recv()

    low = jnp.minimum(jnp.minimum(least_in[0], least_in[1]), jnp.minimum(least_in[2], least_in[3]))
    target = eps_s[6:7, :] + GAMMA * (1.0 + 2.0 * valid - eps_s[7:8, :]) * low

    unit_sum.last()
    spread = unit_sum.whole()
    unit = unit_f[0:8, :]
    inv = unit_f[8:9, :]
    d_unit = (2.0 * ETA / (critics - 1)) * valid * (spread - unit)
    along = jnp.sum(d_unit * unit, axis=0, keepdims=True)
    dg = (d_unit - unit * along) * inv
    gap = value[...] - target
    dv = 2.0 * valid * gap
    diverse = jnp.sum(valid * jnp.sum(unit * (spread - unit), axis=0, keepdims=True), axis=1, keepdims=True)
    errors = jnp.sum(valid * gap * gap, axis=1, keepdims=True)
    dv_sum = jnp.sum(dv, axis=1, keepdims=True)
    dvh[...] = 0.5 * dv
    dgb = dg.astype(BF16)
    dg_b[...] = jnp.concatenate([dgb, dgb], 0)
    rid16 = lax.broadcasted_iota(jnp.int32, (16, 1), 0)
    dv_b[...] = jnp.where(rid16 == 0, dv, jnp.where(rid16 == 1, 1.0, 0.0)).astype(BF16)

    for acc in (acc_h1, acc_h1t, acc_h0, acc_h0t, acc_x, acc_t, acc_last):
        acc[...] = jnp.zeros_like(acc)

    def body_b1(i, _):
        sl = pl.ds(pl.multiple_of(i * block, block), block)
        tp = dot(t1w[...], dg_b[:, sl])
        k1[:, sl] = (k1[:, sl].astype(F32) * tp).astype(BF16)
        th1 = (s1[:, sl].astype(F32) * tp).astype(BF16)
        tp = halves(dot(f0[...], th1))
        k2[:, sl] = (k2[:, sl].astype(F32) * tp).astype(BF16)
        th2 = (s2[:, sl].astype(F32) * tp).astype(BF16)
        tp = halves(dot(f1[...], th2))
        th3 = (s3[:, sl].astype(F32) * tp).astype(BF16)
        d3 = d3s[:, sl]
        ap3 = (dvh[:, sl] * d3.astype(F32) + k3[:, sl].astype(F32) * tp).astype(BF16)
        k3[:, sl] = ap3
        rows_dv = dv_b[:, sl]
        last = dot_t(rows_dv, h3s[:, sl])
        lone = dot_t(rows_dv, th3)
        acc_last[...] += last[0:8] + jnp.where(rid == 0, lone[1:2], 0.0)
        h3s[:, sl] = th1
        acc_h1[...] += dot_t(h2x[:, sl], ap3)
        acc_h1t[...] += dot_t(th2, d3)
        return 0

    def body_b2(i, _):
        sl = pl.ds(pl.multiple_of(i * block, block), block)
        ah = halves(dot(b1[...], k3[:, sl]))
        ap2 = (s2[:, sl].astype(F32) * ah + k2[:, sl].astype(F32)).astype(BF16)
        k2[:, sl] = ap2
        acc_h0[...] += dot_t(h1x[:, sl], ap2)
        acc_h0t[...] += dot_t(h3s[:, sl], d2s[:, sl])
        return 0

    def body_b3(i, _):
        sl = pl.ds(pl.multiple_of(i * block, block), block)
        ah = halves(dot(b0[...], k2[:, sl]))
        ap1 = (s1[:, sl].astype(F32) * ah + k1[:, sl].astype(F32)).astype(BF16)
        acc_x[...] += dot_t(x_b[0:32, sl], ap1)
        acc_t[...] += dot_t(dg_b[:, sl], d1s[:, sl])
        return 0

    @pl.when(online)
    def _():
        low_out[0:HID, :] = c_hidden[0, 0].astype(BF16)
        low_out[HID : 2 * HID, :] = c_hidden[0, 1].astype(BF16)
        stage[...] = jnp.zeros_like(stage)
        stage[0:24, :] = c_edge[0]
        stage[24:28, :] = c_bias[0]
        low_out[2 * HID :, :] = stage[0:32, :].astype(BF16)
        low_copy().start()

    lax.fori_loop(0, blocks, body_b1, 0)
    part_c[HID : 2 * HID, :] = acc_h1[0:HID, :] + 0.5 * acc_h1t[...]
    ex_h1.start()

    @pl.when(online)
    def _():
        for ex in actor:
            ex.reduce()

    lax.fori_loop(0, blocks, body_b2, 0)
    part_c[0:HID, :] = acc_h0[0:HID, :] + 0.5 * acc_h0t[...]
    ex_h0.start()
    ex_h1.reduce()

    @pl.when(online)
    def _():
        for ex in actor:
            ex.forward()
        spread_start()

    lax.fori_loop(0, blocks, body_b3, 0)
    stats = jnp.where(lane == 0, errors, jnp.where(lane == 1, diverse, 0.0))
    small = acc_x[...]
    small = small + jnp.where(rid32 == 18, acc_h0[HID : HID + 1, :], 0.0)
    small = small + jnp.where(rid32 == 19, acc_h1[HID : HID + 1, :], 0.0)
    small = small + jnp.where(rid32 == 20, stats, 0.0)
    small = small + jnp.where(rid32 == 22, jnp.where(lane == 0, dv_sum, 0.0), 0.0)
    small = small + jnp.where(rid32 == 23, acc_last[0:1, :], 0.0)
    part_c[2 * HID : 2 * HID + 24, :] = small[0:24]
    part_c[2 * HID + 24 : 2 * HID + 32, :] = small[24:32] + 0.5 * acc_t[0:8, :]
    if small_c > 32:
        part_c[2 * HID + 32 :, :] = jnp.zeros((small_c - 32, HID), F32)
    ex_sm.start()
    ex_h1.forward()
    ex_h0.reduce()
    ex_sm.reduce()

    @pl.when(targetd)
    def _():
        for ex in actor:
            ex.arrived()
        spread_start()

    ex_h0.forward()
    ex_sm.forward()

    @pl.when(online)
    def _():
        for copy in own_outputs():
            copy.start()

    @pl.when(targetd)
    def _():
        low_copy().wait_recv()
        for copy in far_outputs():
            copy.start()

    for k in range(1, 4):
        spread_actor(k).wait_recv()
        if coded:
            spread_scale(k).wait_recv()
    if coded:
        ex_ac.decode()
    copy_a = local(sum_a, out_a, 3)
    copy_a.start()
    for ex in (ex_h1, ex_h0, ex_sm):
        ex.arrived()
    if coded:
        ex_h1.decode()
        ex_h0.decode()
    copy_c = local(sum_c, out_c, 4)
    copy_c.start()

    @pl.when(online)
    def _():
        for what in range(4):
            param_copy(what).wait_send()
        low_copy().wait_send()
        remote(pi_act, pi_act, sem_pi_s, sem_pi_r, dev(0, e)).wait_send()
        for ex in actor:
            ex.sent()

    @pl.when(targetd)
    def _():
        for k in range(1, 4):
            least_target(k).wait_send()
        for k in range(4):
            least_online(k).wait_send()
        for k in range(1, n_dp):
            param_spread(k).wait_send()

    if fold:
        @pl.when(upper)
        def _():
            for what in (1, 2):
                fold_copy(what, 0).wait_send()

        @pl.when(lower)
        def _():
            for what in (1, 2):
                fold_copy(what, 1).wait_send()

        @pl.when(jnp.logical_and(upper, targetd))
        def _():
            fold_copy(0, 0).wait_send()

        @pl.when(jnp.logical_and(lower, targetd))
        def _():
            fold_copy(0, 1).wait_send()

    unit_sum.sent()
    slope_sum.sent()
    for k in range(1, 4):
        spread_actor(k).wait_send()
        if coded:
            spread_scale(k).wait_send()
    for ex in (ex_h1, ex_h0, ex_sm):
        ex.sent()
    copy_a.wait()
    copy_c.wait()

    @pl.when(online)
    def _():
        for copy in own_outputs():
            copy.wait()

    @pl.when(targetd)
    def _():
        for copy in far_outputs():
            copy.wait()


def sizes(n_dp):
    return 2 * HID + up(CRITIC_SMALL, 8 * n_dp), up(2 * HID + ACTOR_SMALL, 32 * n_dp)


def fused(n_dp, rows, block, fold, data, own, aparams):
    v = pltpu.VMEM
    big = lambda n=HID: v((n, rows), BF16)
    dma = pltpu.SemaphoreType.DMA
    size_c, size_a = sizes(n_dp)
    coded = 2 * HID % (64 * n_dp) == 0
    h8 = lambda *n: v((*n, 8, rows // 2), F32)
    sums = [h8(2), h8(), h8(), h8(3), h8(2)]
    extra = (data[0].shape[1] - rows) // 2 if fold else LANES
    moved = [v((2, 32, extra), F32), v((2, 32, extra), F32), v((2, 8, extra), F32)]
    kept = (lambda n, t: v((n, rows), t)) if fold else (lambda n, t: v((16, LANES), t))
    scratch = [
        v((32, rows), F32), v((32, rows), F32), v((8, rows), F32), *moved, *moved,
        v((96, rows), BF16), v((64, rows), BF16), v((8, rows), F32),
        v((128, HID), F32), v((HID, 128), F32), v((2, HID, 128), F32), v((HID, 128), F32),
        v((24, HID), F32), v((2, HID, HID), F32), v((4, HID), F32), v((544, HID), BF16), v((544, HID), BF16),
        v((HID, 96), BF16), v((512, HID), BF16), v((512, HID), BF16), v((512, HID), BF16), v((512, HID), BF16),
        v((16, HID), BF16), v((HID, 16), BF16), v((16, HID), BF16),
        v((2, HID, 96), BF16), v((2, 512, HID), BF16), v((2, 512, HID), BF16), v((2, 16, HID), BF16),
        v((HID, 96), BF16), v((512, HID), BF16), v((512, HID), BF16), v((512, HID), BF16), v((512, HID), BF16),
        v((32, HID), BF16), v((HID, 32), BF16),
        big(272), big(272), big(), big(), big(), big(), big(), big(), big(), big(), big(), big(),
        v((40, rows), F32), kept(272, BF16), kept(272, BF16), kept(HID, BF16), kept(HID, F32), kept(HID, F32), kept(HID, F32),
        v((1, rows), F32), v((24, rows), F32), *sums,
        v((16, rows), BF16), v((16, rows), BF16), v((1, rows), F32),
        *sums, v((1, rows), F32),
        v((1, rows), F32), v((4, 1, rows), F32),
        v((272, HID), F32), v((HID, HID), F32), v((272, HID), F32), v((HID, HID), F32),
        v((32, HID), F32), v((16, HID), F32), v((8, HID), F32), v((32, HID), F32),
        v((size_c, HID), F32), v((size_a, HID), F32), v((2, size_c, HID), F32), v((size_a, HID), F32),
        *[v((1, 8, HID) if coded else (n_dp - 1, HID // n_dp, HID), F32) for _ in range(2)],
        v((n_dp - 1, (size_c - 2 * HID) // n_dp, HID), F32),
        v((n_dp - 1, (ACTOR_SMALL if coded else size_a // 4) // n_dp, HID), F32),
        dma((3, 2)), dma((3, 2)), dma((4,)), dma((4,)), dma((n_dp - 1,)), dma((n_dp - 1,)), dma, dma, dma, dma, dma((8,)), dma((4,)), dma((2, 5)), dma((2, 5)),
        dma((5, n_dp - 1, 2)), dma((5, n_dp - 1, 2)), dma((5, n_dp - 1, 2)), dma((5, n_dp - 1, 2)), dma((5, n_dp, 2)), dma((5, n_dp, 2)),
        dma((6,)), dma((6,)), dma((6,)),
    ]
    if coded:
        for each, lead in ((HID // n_dp, 2), (HID // n_dp, 2), (2 * HID // (4 * n_dp), 4)):
            word, scale = (each // 2, HID), (1, HID)
            for outer in ((n_dp,), (n_dp - 1,), (lead, n_dp)):
                scratch += [v((*outer, *word), jnp.int32), v((*outer, *scale), F32)]
    spec = pl.BlockSpec(memory_space=pltpu.VMEM)
    anyspace = pl.BlockSpec(memory_space=pl.ANY)
    shape = lambda *s: jax.ShapeDtypeStruct(s, F32)
    return pl.pallas_call(
        functools.partial(kernel, n_dp, rows, block, fold),
        out_shape=(
            shape(2, size_c, HID), shape(size_a, HID), shape(24, HID), shape(2, HID, HID), shape(4, HID),
            jax.ShapeDtypeStruct((544, HID), BF16),
        ),
        in_specs=[spec] * 5 + [pl.BlockSpec(memory_space=pltpu.SMEM)] + [spec] * 7,
        out_specs=(anyspace,) * 6,
        scratch_shapes=scratch,
        compiler_params=pltpu.CompilerParams(collective_id=0 if fold else 1, has_side_effects=True, vmem_limit_bytes=63 * 2**20),
        name="edac_gradients" if fold else "edac_rest",
    )(*data, *own, *aparams)


def adamw(param, grad, first, second):
    first_new = BETA_ONE * first + (1.0 - BETA_ONE) * grad
    second_new = BETA_TWO * second + (1.0 - BETA_TWO) * grad * grad
    ratio = first_new / (1.0 - BETA_ONE**STEP) / (jnp.sqrt(second_new / (1.0 - BETA_TWO**STEP)) + EPS)
    return (param - LEARN * (ratio + DECAY * param), first_new, second_new)


def update_kernel(
    gh, gs, gah, gas,
    own_e, own_h, own_b, on_e, on_h, on_b, low_h, low_s, em, ev, hm, hv, bm, bv,
    ae, ah, ab, aem, aev, ahm, ahv, abm, abv,
    o_e, o_h, o_b, o_em, o_ev, o_hm, o_hv, o_bm, o_bv,
    o_ae, o_ah, o_ab, o_aem, o_aev, o_ahm, o_ahv, o_abm, o_abv, o_ms, o_as,
    ge, gb, gae, gab,
):
    online = lax.axis_index("grp") == 1
    scale = 1.0 / gas[21:22, 1:2]

    def critic(own, param, grad, first, second):
        master, m_new, v_new = adamw(jnp.where(online, own, param), grad, first, second)
        polyak = TAU * master.astype(BF16).astype(F32) + (1.0 - TAU) * own
        return jnp.where(online, master, polyak), m_new, v_new

    o_h[0, 0], o_hm[0, 0], o_hv[0, 0] = critic(
        own_h[0, 0], jnp.where(pl.program_id(0) < 2, low_h[...].astype(F32), on_h[0]), gh[0] * scale, hm[0, 0], hv[0, 0]
    )
    o_ah[0], o_ahm[0], o_ahv[0] = adamw(ah[0], gah[...] * scale, ahm[0], ahv[0])

    @pl.when(pl.program_id(0) == 0)
    def _():
        for m in range(2):
            small = gs.at[1 - m]
            ge[0:OBS, :] = small[0:OBS, :]
            ge[OBS : OBS + ACT, :] = small[24 : 24 + ACT, :]
            ge[23:24, :] = small[23:24, :]
            gb[0:3, :] = small[17:20, :]
            gb[3:4, :] = small[22:23, :]
            low = low_s[...].astype(F32)
            p_e, p_b = (on_e[...], on_b[...]) if m else (low[0:24], low[24:28])
            o_e[m], o_em[m], o_ev[m] = critic(own_e[m], p_e, ge[...] * scale, em[m], ev[m])
            o_b[m], o_bm[m], o_bv[m] = critic(own_b[m], p_b, gb[...] * scale, bm[m], bv[m])
            o_ms[m : m + 1, :] = small[20:21, 0:2]
        gae[0:OBS, :] = gas[0:OBS, :]
        gae[OBS : OBS + 2 * ACT, :] = gas[32 : 32 + 2 * ACT, :]
        gab[0:3, :] = gas[17:20, :]
        gab[3:4, :] = gas[20:21, :]
        o_ae[...], o_aem[...], o_aev[...] = adamw(ae[...], gae[...] * scale, aem[...], aev[...])
        o_ab[...], o_abm[...], o_abv[...] = adamw(ab[...], gab[...] * scale, abm[...], abv[...])
        o_as[...] = gas[21:22, 0:2]


def update(grads, own, online, moments, aparams, amoments):
    size_c = grads[0].shape[1]
    shape = lambda *s: jax.ShapeDtypeStruct(s, F32)
    whole = lambda *s: pl.BlockSpec(s, lambda i: (0,) * len(s))
    mat = pl.BlockSpec((1, 1, HID, HID), lambda i: (i // 2, i % 2, 0, 0))
    amat = pl.BlockSpec((1, HID // 2, HID), lambda i: (i // 2, i % 2, 0))
    edge, bias, aedge, abias = whole(2, 24, HID), whole(2, 4, HID), whole(29, HID), whole(4, HID)
    in_specs = [
        pl.BlockSpec((1, HID, HID), lambda i: (1 - i // 2, i % 2, 0)),
        pl.BlockSpec((2, 32, HID), lambda i: (0, 16, 0)),
        pl.BlockSpec((HID // 2, HID), lambda i: (i, 0)),
        pl.BlockSpec((ACTOR_SMALL, HID), lambda i: (8, 0)),
        edge, mat, bias, whole(24, HID), pl.BlockSpec((1, HID, HID), lambda i: (i % 2, 0, 0)), whole(4, HID),
        pl.BlockSpec((HID, HID), lambda i: (i % 2, 0)), pl.BlockSpec((32, HID), lambda i: (16, 0)), edge, edge, mat, mat, bias, bias,
        aedge, amat, abias, aedge, aedge, amat, amat, abias, abias,
    ]
    out_specs = (edge, mat, bias, edge, edge, mat, mat, bias, bias, aedge, amat, abias, aedge, aedge, amat, amat, abias, abias,
                 whole(2, 2), whole(1, 2))
    e_, h_, b_ = shape(2, 24, HID), shape(2, 2, HID, HID), shape(2, 4, HID)
    ae_, ah_, ab_ = shape(29, HID), shape(2, HID, HID), shape(4, HID)
    return pl.pallas_call(
        update_kernel,
        grid=(4,),
        out_shape=(e_, h_, b_, e_, e_, h_, h_, b_, b_, ae_, ah_, ab_, ae_, ae_, ah_, ah_, ab_, ab_, shape(2, 2), shape(1, 2)),
        in_specs=in_specs,
        out_specs=out_specs,
        scratch_shapes=[pltpu.VMEM((24, HID), F32), pltpu.VMEM((4, HID), F32), pltpu.VMEM((29, HID), F32), pltpu.VMEM((4, HID), F32)],
        name="adamw",
    )(grads[0], grads[0], grads[1], grads[1], *own, *online[:3], online[3], online[3], *moments, *aparams, *amoments)


def body(
    n_dp,
    states, actions, rewards, done, noise, counts,
    crit_edge, crit_hidden, crit_bias, edge_m, edge_v, hidden_m, hidden_v, bias_m, bias_v,
    act_edge, act_hidden, act_bias, act_edge_m, act_edge_v, act_hidden_m, act_hidden_v, act_bias_m, act_bias_v,
):
    size = states.shape[0]
    own = (crit_edge[0], crit_hidden[0], crit_bias[0])
    aparams = (act_edge, act_hidden, act_bias)
    data = (states.T, actions.T, noise.T, rewards[None], done[None], counts)
    moments = (edge_m, edge_v, hidden_m, hidden_v, bias_m, bias_v)
    amoments = (act_edge_m, act_edge_v, act_hidden_m, act_hidden_v, act_bias_m, act_bias_v)
    rows = FOLD_ROWS if size > FOLD_ROWS else size
    grad_c, grad_a, *online = fused(n_dp, rows, rows // 2, True, (*data, jnp.zeros((1, LANES), F32)), own, aparams)

    def finish(grad_c, grad_a):
        return update((grad_c, grad_a), own, online, moments, aparams, amoments)

    def with_rest():
        z = lax.axis_index("dp")
        partner = lax.ppermute(counts, "dp", [(k, n_dp - 1 - k) for k in range(n_dp)])
        at = jnp.arange(size, dtype=jnp.int32)
        taken = (rows // LANES - 1 - (at - rows) // LANES) * LANES >= (jnp.minimum(partner, rows) + LANES - 1) // LANES * LANES
        taken = jnp.where(z >= n_dp - n_dp // 2, taken, False)
        left = jnp.logical_and(jnp.logical_and(at >= rows, at < counts), jnp.logical_not(taken))
        more_c, more_a, *_ = fused(n_dp, size, size // 4, False, (*data, left.astype(F32)[None]), own, aparams)
        return finish(grad_c + more_c, grad_a + more_a)

    sums = grad_a[2 * HID + 21]
    out = lax.cond(sums[1] != sums[2], with_rest, lambda: finish(grad_c, grad_a))
    return (*(o[None] for o in out[:3]), *out[3:19], out[19][0])


def solution(mesh):
    member = P("grp", "ens", None, None)
    hidden = P("grp", "ens", None, None, None)
    mom = P("ens", None, None)
    mom_h = P("ens", None, None, None)
    return jax.shard_map(
        functools.partial(body, mesh.shape["dp"]),
        mesh=mesh,
        in_specs=(
            P("dp", None), P("dp", None), P("dp"), P("dp"), P("dp", None), P("dp"),
            member, hidden, member, mom, mom, mom_h, mom_h, mom, mom,
        ) + (P(),) * 9,
        out_specs=(member, hidden, member, mom, mom, mom_h, mom_h, mom, mom) + (P(),) * 9 + (P("ens", None), P()),
        check_vma=False,
    )
```

```python
import functools

import jax
import jax.numpy as jnp
from jax import lax
from jax.experimental import pallas as pl
from jax.experimental.pallas import tpu as pltpu
from jax.sharding import PartitionSpec as P

OBS = 17
ACT = 6
HID = 256
STEP = 5
FOLD_ROWS = 2816
LANES = 128

GAMMA = 0.99
ALPHA = 0.2
ETA = 1.0
LEARN = 0.03
BETA_ONE = 0.5
BETA_TWO = 0.5
DECAY = 0.01
EPS = 1e-08
TAU = 0.05
HALF_LOG_TWO_PI = 0.9189385332046727
LOG_TWO = 0.6931471805599453

F32 = jnp.float32
BF16 = jnp.bfloat16

CRITIC_SMALL, ACTOR_SMALL = 32, 64


def dot(a, b):
    return lax.dot_general(a, b, (((1,), (0,)), ((), ())), preferred_element_type=F32)


def dot_t(a, b):
    return lax.dot_general(a, b, (((1,), (1,)), ((), ())), preferred_element_type=F32)


def split(w):
    high = w.astype(BF16).astype(F32)
    return high, w - high


def halves(p):
    n = p.shape[0] // 2
    return p[:n] + p[n:]


def prep_input(stage, w1, edge, bias, n_in):
    stage[...] = jnp.zeros_like(stage)
    stage[0:OBS, :] = edge[0:OBS, :]
    stage[OBS : OBS + 1, :] = bias[0:1, :]
    if n_in > OBS:
        stage[24 : 24 + ACT, :] = edge[OBS : OBS + ACT, :]
    high, low = split(0.5 * stage[0:32, :])
    w1[...] = jnp.concatenate([high, low, high], 0).T.astype(BF16)


def prep_hidden(fwd, bwd, hidden):
    w = 0.5 * hidden
    if fwd is not None:
        high, low = split(w.T)
        fwd[...] = jnp.concatenate([high, low], 0).astype(BF16)
    if bwd is not None:
        high, low = split(w)
        bwd[...] = jnp.concatenate([high, low], 0).astype(BF16)


def silu_half(u):
    t = jnp.tanh(u)
    return u + u * t, t


def up(n, by):
    return -(-n // by) * by


def kernel(
    n_dp,
    rows,
    block,
    fold,
    states, actions, noise, rewards, done, counts, mask, c_edge, c_hidden, c_bias, a_edge, a_hidden, a_bias,
    out_c, out_a, out_small, out_high, out_rest, out_low,
    xs, ns, eps_s, far_x, far_e, here_x, here_e, x_b, pi_act, stage, vec, tvec, avec,
    small_out, small_in, high_out, high_in, rest_out, rest_in, low_out, low_in,
    w1, f0, f1, b0, b1, ga, t1w, eq,
    tw1, tf0, tf1, teq,
    aw1, af0, af1, ab0, ab1, ao, aot,
    h1x, h2x, h3s, s1, s2, s3, k1, k2, k3, d1s, d2s, d3s,
    heads, ah1x, ah2x, ah3, as1, as2, as3,
    value, unit_f, u_mine, u_peer, u_pair, u_far, u_total, dg_b, dv_b, dvh, row_sums,
    q_mine, q_peer, q_pair, q_far, q_total, q_own, least, far_least, least_in,
    acc_h1, acc_h1t, acc_h0, acc_h0t, acc_x, acc_t, acc_last, acc_o, acc_c1, acc_c0, acc_cx,
    part_c, part_a, sum_c, sum_a, in_h1, in_h0, in_sm, in_ac,
    fold_s, fold_r, sem_far_s, sem_far_r, sem_param_s, sem_param_r, sem_pi_s, sem_pi_r, sem_least_s, sem_least_r, es_s, es_r,
    rs_s, rs_r, ag_s, ag_r, xf_s, xf_r, ef_s, ef_r, sem_out, *boxes,
):
    g = lax.axis_index("grp")
    e = lax.axis_index("ens")
    z = lax.axis_index("dp")
    me = g * 4 + e
    blocks = rows // block
    extra = states.shape[1] - rows
    lower = z < n_dp // 2
    upper = z >= n_dp - n_dp // 2
    half = rows // 2
    online = g == 1
    targetd = g == 0
    critics = 8
    coded = bool(boxes)

    def dev(gg, ee):
        return {"grp": gg, "ens": ee}

    def remote(src, dst, send, recv, where):
        return pltpu.make_async_remote_copy(
            src_ref=src, dst_ref=dst, send_sem=send, recv_sem=recv, device_id=where, device_id_type=pl.DeviceIdType.MESH
        )

    barrier = pltpu.get_barrier_semaphore()
    for k in range(1, 8):
        p = lax.rem(me + k, 8)
        pl.semaphore_signal(barrier, inc=1, device_id=dev(p // 4, lax.rem(p, 4)), device_id_type=pl.DeviceIdType.MESH)
    for k in range(1, n_dp):
        pl.semaphore_signal(barrier, inc=1, device_id={"dp": lax.rem(z + k, n_dp)}, device_id_type=pl.DeviceIdType.MESH)

    def all_here():
        pl.semaphore_wait(barrier, 7 + n_dp - 1)

    def param_copy(what):
        src, dst = ((small_out, small_in), (high_out, high_in), (rest_out, rest_in), (low_out, low_in))[what]
        return remote(src, dst, sem_param_s.at[what], sem_param_r.at[what], dev(0, e))

    @pl.when(online)
    def _():
        small_out[...] = jnp.zeros_like(small_out)
        for k in range(2):
            small_out[32 * k : 32 * k + 24, :] = c_edge[1 - k]
            small_out[32 * k + 24 : 32 * k + 28, :] = c_bias[1 - k]
            high, low = split(c_hidden[1, k])
            high_out[k * HID : (k + 1) * HID, :] = high.astype(BF16)
            rest_out[k * HID : (k + 1) * HID, :] = low.astype(BF16)
            low_out[k * HID : (k + 1) * HID, :] = c_hidden[0, k].astype(BF16)
        all_here()
        for what in range(2):
            param_copy(what).start()

    lane_id = lax.broadcasted_iota(jnp.int32, (1, states.shape[1]), 1)
    if fold:
        code = jnp.where(lane_id < counts[0], 2.0, 0.0) + done[...].astype(F32)
    else:
        code = 2.0 * mask[...] + done[...].astype(F32)

    ones_row = jnp.ones((1, states.shape[1]), F32)
    xs[...] = jnp.zeros_like(xs)
    xs[0:OBS, :] = states[0:OBS, :]
    xs[OBS : OBS + 1, :] = ones_row
    xs[24 : 24 + ACT, :] = actions[...]
    eps_s[6:7, :] = rewards[...]
    eps_s[7:8, :] = code

    @pl.when(online)
    def _():
        eps_s[0:ACT, :] = noise[0:ACT, :]

    @pl.when(targetd)
    def _():
        eps_s[0:ACT, :] = noise[ACT : 2 * ACT, :]
        ns[...] = jnp.zeros_like(ns)
        ns[0:OBS, :] = states[OBS : 2 * OBS, :]
        ns[OBS : OBS + 1, :] = ones_row

    core = lax.rem(e, 2)
    other_core = e + 1 - 2 * core
    far_chip = lax.rem(e + 2, 4)

    def fold_copy(what, hop):
        here, there = ((here_e, far_e), (here_x, far_x))[what]
        if hop == 0:
            return remote(here.at[core], there.at[core], fold_s.at[what, 0], fold_r.at[what, 0], {"dp": n_dp - 1 - z})
        return remote(there.at[core], there.at[core], fold_s.at[what, 1], fold_r.at[what, 1], dev(g, other_core))

    def least_copy():
        return remote(least.at[:, rows:], far_least, sem_far_s, sem_far_r, {"dp": n_dp - 1 - z})

    def merge(into, blocks_of):
        first = rows - extra
        there = jnp.concatenate([blocks_of(b) for b in range(extra // LANES - 1, -1, -1)], 1).astype(F32)
        lanes = lax.broadcasted_iota(jnp.int32, (1, extra), 1) + first
        bound = (jnp.minimum(counts[0], rows) + LANES - 1) // LANES * LANES
        into[:, first:rows] = jnp.where(lanes < bound, into[:, first:rows], there)

    def in_halves(pieces):
        per = extra // LANES // 2
        return lambda b: pieces[b // per, :, (b % per) * LANES : (b % per + 1) * LANES]

    def fold_out():
        if fold:
            @pl.when(upper)
            def _():
                for h in range(2):
                    part = slice(rows + h * extra // 2, rows + (h + 1) * extra // 2)
                    here_e[h] = eps_s[:, part]
                    here_x[h] = xs[:, part].astype(BF16)
                for what in range(2):
                    fold_copy(what, 0).start()

    def fold_in():
        if fold:
            @pl.when(lower)
            def _():
                for what in range(2):
                    fold_copy(what, 0).wait_recv()
                    fold_copy(what, 1).start()
                for what in range(2):
                    fold_copy(what, 1).wait_recv()
                merge(eps_s, in_halves(far_e))
                merge(xs, in_halves(far_x))

    def put_x():
        high, low = split(xs[:, 0:rows])
        xin = high.astype(BF16)
        x_b[0:32, :] = xin
        x_b[32:64, :] = xin
        x_b[64:96, :] = low.astype(BF16)

    def prep_small(edge, bias, w1_, vec_, eq_, ga_, t1_):
        prep_input(stage, w1_, edge, bias, OBS + ACT)
        stage[...] = jnp.zeros_like(stage)
        stage[0:1, :] = 0.5 * bias[1:2, :]
        stage[1:2, :] = 0.5 * bias[2:3, :]
        stage[2:3, :] = edge[23:24, :]
        vec_[...] = stage[...].T
        vec_[0:1, 8:9] = bias[3:4, 0:1]
        stage[...] = jnp.zeros_like(stage)
        high, low = split(edge[23:24, :])
        stage[0:1, :] = high
        stage[1:2, :] = low
        eq_[...] = stage[0:16, :].astype(BF16)
        if ga_ is not None:
            stage[...] = jnp.zeros_like(stage)
            stage[0:ACT, :] = 0.5 * edge[OBS : OBS + ACT, :]
            high, low = split(stage[0:8, :])
            both = jnp.concatenate([high, low], 0)
            ga_[...] = both.astype(BF16)
            stage[0:16, :] = both
            t1_[...] = stage[...].T[:, 0:16].astype(BF16)

    def prep_actor():
        prep_input(stage, aw1, a_edge, a_bias, OBS)
        prep_hidden(af0, ab0, a_hidden[0])
        prep_hidden(af1, ab1, a_hidden[1])
        stage[...] = jnp.zeros_like(stage)
        stage[0:1, :] = 0.5 * a_bias[1:2, :]
        stage[1:2, :] = 0.5 * a_bias[2:3, :]
        stage[2:3, :] = a_bias[3:4, :]
        avec[...] = stage[...].T
        stage[...] = jnp.zeros_like(stage)
        stage[0:ACT, :] = a_edge[OBS : OBS + ACT, :]
        stage[8 : 8 + ACT, :] = a_edge[OBS + ACT : OBS + 2 * ACT, :]
        high, low = split(stage[0:16, :])
        ao[...] = jnp.concatenate([high, low], 0).astype(BF16)
        stage[...] = jnp.zeros_like(stage)
        stage[0 : 2 * ACT, :] = a_edge[OBS : OBS + 2 * ACT, :]
        high, low = split(stage[0:16, :])
        stage[0:32, :] = jnp.concatenate([high, low], 0)
        aot[...] = stage[...].T[:, 0:32].astype(BF16)

    prep_actor()

    def actor_layers(src):
        kept = []
        hb = None
        for w, b in ((aw1, None), (af0, 0), (af1, 1)):
            u = dot(w[...], src) if b is None else halves(dot(w[...], hb)) + avec[:, b : b + 1]
            h, t = silu_half(u)
            hb = h.astype(BF16)
            kept.append((hb, h, t))
        return kept

    ok8 = (lax.broadcasted_iota(jnp.int32, (8, 1), 0) < ACT).astype(F32)

    def actor_heads(hb, sl):
        out = halves(dot(ao[...], hb))
        eps = eps_s[:, sl]
        center = out[0:8] + avec[0:8, 2:3] * ok8
        th = jnp.tanh(out[8:16] + avec[6:14, 2:3] * ok8)
        log_std = 3.5 * th - 1.5
        spread_e = jnp.exp(log_std) * eps
        latent = center + spread_e
        soft = jnp.maximum(-2.0 * latent, 0.0) + jnp.log(1.0 + jnp.exp(-2.0 * jnp.abs(latent)))
        terms = -0.5 * eps * eps - log_std - HALF_LOG_TWO_PI - 2.0 * (LOG_TWO - latent - soft)
        logp = jnp.sum(terms * ok8, axis=0, keepdims=True)
        sample = jnp.tanh(latent) * ok8
        return sample, logp, th, spread_e

    put_x()

    @pl.when(online)
    def _():
        fold_out()
        prep_small(c_edge.at[0], c_bias.at[0], w1, vec, eq, ga, t1w)
        prep_hidden(f0, b0, c_hidden[0, 0])
        prep_hidden(f1, b1, c_hidden[0, 1])

    def least_online(k):
        return remote(least.at[:, 0:rows], least_in.at[k], sem_least_s.at[4 + k], sem_least_r.at[k], dev(1, lax.rem(e + k, 4)))

    def least_target(k):
        return remote(least.at[:, 0:rows], least_in.at[k], sem_least_s.at[k], sem_least_r.at[k], dev(0, lax.rem(e + k, 4)))

    def half_hidden(part, values):
        to = slice(part * HID, (part + 1) * HID)
        for k, (fwd, bwd) in enumerate(((f0, b0), (f1, b1))):
            w = 0.5 * values[k * HID : (k + 1) * HID, :].astype(F32)
            fwd[to, :] = w.T.astype(BF16)
            bwd[to, :] = w.astype(BF16)

    @pl.when(targetd)
    def _():
        for m in range(2):
            prep_small(c_edge.at[m], c_bias.at[m], tw1.at[m], tvec.at[m], teq.at[m], None, None)
            prep_hidden(tf0.at[m], None, c_hidden[m, 0])
            prep_hidden(tf1.at[m], None, c_hidden[m, 1])

        def body(i, _):
            @pl.when(i == 1)
            def _():
                all_here()
                fold_out()

            first = jnp.minimum(i * block, states.shape[1] - block)
            sl = pl.ds(pl.multiple_of(first, LANES), block)
            high, rest = split(ns[:, sl])
            nx, rest = high.astype(BF16), rest.astype(BF16)
            kept = actor_layers(jnp.concatenate([nx, nx, rest], 0))
            sample, logp, th, spread_e = actor_heads(kept[2][0], sl)
            high, rest = split(jnp.concatenate([ns[0:24, sl], sample], 0))
            nx = high.astype(BF16)
            nx = jnp.concatenate([nx, nx, rest.astype(BF16)], 0)
            low = None
            for m in range(2):
                h, t = silu_half(dot(tw1[m], nx))
                h, t = silu_half(halves(dot(tf0[m], h.astype(BF16))) + tvec[m, :, 0:1])
                h, t = silu_half(halves(dot(tf1[m], h.astype(BF16))) + tvec[m, :, 1:2])
                r = dot(teq[m], h.astype(BF16))
                q = r[0:1] + r[1:2] + tvec[m, 0:1, 8:9]
                low = q if low is None else jnp.minimum(low, q)
            least[:, sl] = low - ALPHA * logp
            return 0

        lax.fori_loop(0, blocks + (jnp.where(upper, 1, 0) if fold else 0), body, 0)
        if fold:
            @pl.when(upper)
            def _():
                least_copy().start()

        for what in range(2):
            param_copy(what).wait_recv()
        prep_small(small_in.at[0:24], small_in.at[24:32], w1, vec, eq, ga, t1w)
        half_hidden(0, high_in)

    def least_out():
        @pl.when(targetd)
        def _():
            if fold:
                @pl.when(lower)
                def _():
                    least_copy().wait_recv()
                    merge(least, lambda b: far_least[:, b * LANES : (b + 1) * LANES])

            for k in range(1, 4):
                least_target(k).start()
            for k in range(4):
                least_online(k).start()

    class EnsembleSum:
        def __init__(self, index, mine, peer, pair, far, total, only_online):
            self.index, self.mine, self.peer, self.pair, self.far, self.total, self.only_online = (
                index, mine, peer, pair, far, total, only_online,
            )

        def to_core(self):
            return remote(self.mine.at[1 - core], self.peer, es_s.at[self.index, 0], es_r.at[self.index, 0], dev(g, other_core))

        def to_chip(self, k):
            across = (1 - g, g, 1 - g)[k]
            where = dev(across, (e, far_chip, far_chip)[k])
            return remote(self.pair, self.far.at[k], es_s.at[self.index, 1 + k], es_r.at[self.index, 1 + k], where)

        def back(self):
            return remote(self.total.at[core], self.total.at[core], es_s.at[self.index, 4], es_r.at[self.index, 4], dev(g, other_core))

        def begin(self, first, second):
            self.mine[0] = first
            self.mine[1] = second
            self.to_core().start()

        def middle(self):
            self.to_core().wait_recv()
            self.pair[...] = self.mine[core] + self.peer[...]
            if not self.only_online:
                for k in range(3):
                    self.to_chip(k).start()
            else:
                @pl.when(targetd)
                def _():
                    self.to_chip(0).start()
                    self.to_chip(2).start()

                @pl.when(online)
                def _():
                    self.to_chip(1).start()

        def first_to_core(self, h, values):
            self.mine[h] = values

            @pl.when(core != h)
            def _():
                self.to_core().start()

            @pl.when(core == h)
            def _():
                self.middle()

        def last_of(self, h):
            @pl.when(core == h)
            def _():
                self.last()

        def back_of(self, h):
            @pl.when(core != h)
            def _():
                self.back().wait_recv()

        def last(self):
            for k in range(3):
                self.to_chip(k).wait_recv()
            self.total[core] = self.pair[...] + self.far[0] + self.far[1] + self.far[2]
            self.back().start()

        def whole(self):
            self.back().wait_recv()
            return jnp.concatenate([self.total[0], self.total[1]], 1)

        def sent(self):
            self.to_core().wait_send()
            if not self.only_online:
                for k in range(3):
                    self.to_chip(k).wait_send()
                self.back().wait_send()
            else:
                @pl.when(targetd)
                def _():
                    self.to_chip(0).wait_send()
                    self.to_chip(2).wait_send()

                @pl.when(online)
                def _():
                    self.to_chip(1).wait_send()
                    self.back().wait_send()

    unit_sum = EnsembleSum(0, u_mine, u_peer, u_pair, u_far, u_total, False)
    slope_sum = EnsembleSum(1, q_mine, q_peer, q_pair, q_far, q_total, True)

    def pi_copy(i):
        part = pi_act.at[:, pl.ds(pl.multiple_of(i * block, block), block)]
        return remote(part, part, sem_pi_s.at[i], sem_pi_r.at[i], dev(0, e))

    def body_p(i, _):
        sl = pl.ds(pl.multiple_of(i * block, block), block)

        @pl.when(i == 1)
        def _():
            fold_in()
            if fold:
                put_x()

        @pl.when(online)
        def _():
            kept = actor_layers(x_b[:, sl])
            if fold:
                for store, curve, (hb, h, t) in zip((ah1x, ah2x, ah3), (as1, as2, as3), kept):
                    store[0:HID, sl] = hb
                    curve[:, sl] = (1.0 + t) + h * (1.0 - t)
            sample, logp, th, spread_e = actor_heads(kept[2][0], sl)
            pi_act[:, sl] = sample
            heads[0:8, sl] = th
            heads[8:16, sl] = spread_e
            heads[16:17, sl] = logp
            pi_copy(i).start()

        @pl.when(jnp.logical_and(online, i == 0))
        def _():
            param_copy(2).start()

        @pl.when(targetd)
        def _():
            pi_copy(i).wait_recv()

        def act(u):
            h, t = silu_half(u)
            hb, tb = h.astype(BF16), t.astype(BF16)
            one = jnp.ones((), BF16)
            return hb, (one + tb) + hb * (one - tb)

        pin = jnp.concatenate([xs[0:24, sl], pi_act[:, sl]], 0).astype(BF16)
        h, a1 = act(dot(w1[:, 0:64], jnp.concatenate([pin, pin], 0)))
        h, a2 = act(dot(f0[0:HID, :], h) + vec[:, 0:1])
        h, a3 = act(dot(f1[0:HID, :], h) + vec[:, 1:2])
        r = dot(eq[...], h)
        q_own[:, sl] = r[0:1] + r[1:2] + vec[0:1, 8:9]
        d = vec[:, 2:3].astype(BF16) * a3
        d = dot(b1[0:HID, :], d).astype(BF16) * a2
        d = dot(b0[0:HID, :], d).astype(BF16) * a1
        unit_f[16:24, sl] = halves(dot(ga[...], d))
        return 0

    lax.fori_loop(0, blocks, body_p, 0)
    rid = lax.broadcasted_iota(jnp.int32, (8, 1), 0)
    packed = unit_f[16:24, :] + jnp.where(rid == 6, q_own[...], 0.0)
    slope_sum.begin(packed[:, 0:half], packed[:, half:rows])

    ones = (lax.broadcasted_iota(jnp.int32, (16, rows), 0) == 0).astype(BF16)
    h1x[HID : HID + 16, :] = ones
    h2x[HID : HID + 16, :] = ones

    def curves(u):
        h, t = silu_half(u)
        c = 1.0 + t
        d = 1.0 - t
        return h, c + h * d, (c * d) * (1.0 - u * t)

    @pl.when(targetd)
    def _():
        param_copy(2).wait_recv()
        half_hidden(1, rest_in)

    valid = jnp.where(eps_s[7:8, 0:rows] > 1.5, 1.0, 0.0)

    def body_a(i, _):
        @pl.when(i == 1)
        def _():
            slope_sum.middle()
            if fold:
                unit_sum.first_to_core(0, unit_f[0:8, 0:half])
            least_out()

            @pl.when(online)
            def _():
                param_copy(3).start()


        sl = pl.ds(pl.multiple_of(i * block, block), block)
        h, a1, q1 = curves(dot(w1[...], x_b[:, sl]))
        hb = h.astype(BF16)
        h1x[0:HID, sl] = hb
        s1[:, sl] = a1.astype(BF16)
        h, a2, q2 = curves(halves(dot(f0[...], hb)) + vec[:, 0:1])
        hb = h.astype(BF16)
        h2x[0:HID, sl] = hb
        s2[:, sl] = a2.astype(BF16)
        h, a3, q3 = curves(halves(dot(f1[...], hb)) + vec[:, 1:2])
        hb = h.astype(BF16)
        h3s[:, sl] = hb
        s3[:, sl] = a3.astype(BF16)
        r = dot(eq[...], hb)
        value[:, sl] = r[0:1] + r[1:2] + vec[0:1, 8:9]
        last = vec[:, 2:3]
        db = (last * a3).astype(BF16)
        d3s[:, sl] = db
        k3[:, sl] = (last * q3).astype(BF16)
        m = halves(dot(b1[...], db))
        db = (m * a2).astype(BF16)
        d2s[:, sl] = db
        k2[:, sl] = (m * q2).astype(BF16)
        m = halves(dot(b0[...], db))
        db = (m * a1).astype(BF16)
        d1s[:, sl] = db
        k1[:, sl] = (m * q1).astype(BF16)
        slope = halves(dot(ga[...], db))
        inv = lax.rsqrt(jnp.sum(slope * slope, axis=0, keepdims=True) + 0.01)
        unit_f[0:8, sl] = slope * inv
        unit_f[8:9, sl] = inv
        return 0

    lax.fori_loop(0, blocks, body_a, 0)
    if fold:
        unit_sum.first_to_core(1, unit_f[0:8, half:rows])
        unit_sum.last_of(0)
    else:
        unit_sum.begin(unit_f[0:8, 0:half], unit_f[0:8, half:rows])
        unit_sum.middle()

    class Exchange:
        def __init__(self, index, part, into, inbox, base, count, wide):
            self.index, self.part, self.into, self.inbox, self.base, self.count, self.wide = index, part, into, inbox, base, count, wide
            self.each = count // (n_dp * (4 if wide else 1))

        def rows_of(self, shard):
            first = self.base + (e * n_dp + shard if self.wide else shard) * self.each
            return pl.ds(pl.multiple_of(first, 8), self.each)

        def scatter(self, k):
            to = lax.rem(z + k, n_dp)
            return remote(
                self.part.at[self.rows_of(to)], self.inbox.at[k - 1], rs_s.at[self.index, k - 1, 0], rs_r.at[self.index, k - 1, 0], {"dp": to}
            )

        def gather(self, k):
            mine = self.into.at[self.rows_of(z)]
            return remote(mine, mine, ag_s.at[self.index, k - 1, 0], ag_r.at[self.index, k - 1, 0], {"dp": lax.rem(z + k, n_dp)})

        def across(self, k):
            there = self.into.at[self.rows_of(lax.rem(z + n_dp - k, n_dp))]
            return remote(there, there, xf_s.at[self.index, k, 0], xf_r.at[self.index, k, 0], dev(1 - g, e))

        def start(self):
            for k in range(1, n_dp):
                self.scatter(k).start()

        def reduce(self, along=True):
            total = self.part[self.rows_of(z), :]
            for k in range(1, n_dp):
                self.scatter(k).wait_recv()
                total = total + self.inbox[k - 1]
            self.into[self.rows_of(z), :] = total
            if along:
                for k in range(1, n_dp):
                    self.gather(k).start()
            self.across(0).start()

        def forward(self):
            for k in range(1, n_dp):
                self.gather(k).wait_recv()
                self.across(k).start()

        def sent(self):
            for k in range(1, n_dp):
                self.scatter(k).wait_send()
                self.gather(k).wait_send()
            for k in range(n_dp):
                self.across(k).wait_send()

        def arrived(self):
            for k in range(n_dp):
                self.across(k).wait_recv()

        def detour(self):
            self.across(0).wait_recv()
            for k in range(1, n_dp):
                self.gather(k).start()

        def back(self):
            for k in range(1, n_dp):
                self.across(k).wait_recv()

        def sent_detour(self):
            @pl.when(online)
            def _():
                for k in range(1, n_dp):
                    self.scatter(k).wait_send()
                self.across(0).wait_send()

            @pl.when(targetd)
            def _():
                for k in range(1, n_dp):
                    self.gather(k).wait_send()
                    self.across(k).wait_send()

    class Coded(Exchange):
        def __init__(self, index, part, out, base, count, lead, wide, boxes):
            self.index, self.part, self.out, self.base, self.count, self.lead, self.wide = index, part, out, base, count, lead, wide
            self.out_w, self.out_s, self.in_w, self.in_s, self.all_w, self.all_s = boxes
            self.each = count // (n_dp * (4 if wide else 1))

        def pack(self, x):
            top = jnp.maximum(jnp.max(jnp.abs(x), axis=0, keepdims=True), 1e-30)
            q = jnp.round(x * (32767.0 / top)).astype(jnp.int32)
            h = self.each // 2
            return jnp.bitwise_or(jnp.bitwise_and(q[:h], 65535), jnp.left_shift(q[h:], 16)), top * (1.0 / 32767.0)

        def unpack(self, w, scale):
            low = jnp.right_shift(jnp.left_shift(w, 16), 16)
            high = jnp.right_shift(w, 16)
            return jnp.concatenate([low, high], 0).astype(F32) * scale

        def scatter(self, k):
            to = lax.rem(z + k, n_dp)
            return Both([
                remote(o.at[to], i.at[k - 1], rs_s.at[self.index, k - 1, q], rs_r.at[self.index, k - 1, q], {"dp": to})
                for q, (o, i) in enumerate(((self.out_w, self.in_w), (self.out_s, self.in_s)))
            ])

        def gather(self, k):
            return Both([
                remote(
                    a.at[self.lead, z], a.at[self.lead, z], ag_s.at[self.index, k - 1, q], ag_r.at[self.index, k - 1, q],
                    {"dp": lax.rem(z + k, n_dp)},
                )
                for q, a in enumerate((self.all_w, self.all_s))
            ])

        def across(self, k):
            there = lax.rem(z + n_dp - k, n_dp)
            return Both([
                remote(
                    a.at[self.lead, there], a.at[self.lead, there], xf_s.at[self.index, k, q], xf_r.at[self.index, k, q], dev(1 - g, e)
                )
                for q, a in enumerate((self.all_w, self.all_s))
            ])

        def start(self):
            for shard in range(n_dp):
                w, scale = self.pack(self.part[self.rows_of(shard), :])
                self.out_w[shard] = w
                self.out_s[shard] = scale
            for k in range(1, n_dp):
                self.scatter(k).start()

        def reduce(self, along=True):
            total = self.part[self.rows_of(z), :]
            for k in range(1, n_dp):
                self.scatter(k).wait_recv()
                total = total + self.unpack(self.in_w[k - 1], self.in_s[k - 1])
            w, scale = self.pack(total)
            self.all_w[self.lead, z] = w
            self.all_s[self.lead, z] = scale
            if along:
                for k in range(1, n_dp):
                    self.gather(k).start()
            self.across(0).start()

        def decode(self):
            for lead in range(self.all_w.shape[0]):
                for shard in range(n_dp):
                    x = self.unpack(self.all_w[lead, shard], self.all_s[lead, shard])
                    if self.wide:
                        first = (lead * n_dp + shard) * self.each
                        self.out[first : first + self.each, :] = x
                    else:
                        first = self.base + shard * self.each
                        self.out[lead, first : first + self.each, :] = x

    class Both:
        def __init__(self, copies):
            self.copies = copies

        def start(self):
            for c in self.copies:
                c.start()

        def wait_recv(self):
            for c in self.copies:
                c.wait_recv()

        def wait_send(self):
            for c in self.copies:
                c.wait_send()

    if coded:
        box_h1, box_h0, box_ac = boxes[0:6], boxes[6:12], boxes[12:18]
    if coded:
        ex_h1 = Coded(0, part_c, sum_c, HID, HID, g, False, box_h1)
        ex_h0 = Coded(1, part_c, sum_c, 0, HID, g, False, box_h0)
        ex_ac = Coded(3, part_a, sum_a, 0, 2 * HID, e, True, box_ac)
        ex_as = Exchange(4, part_a, sum_a, in_ac, 2 * HID, ACTOR_SMALL, False)
        actor = (ex_ac, ex_as)
    else:
        ex_h1 = Exchange(0, part_c, sum_c.at[g], in_h1, HID, HID, False)
        ex_h0 = Exchange(1, part_c, sum_c.at[g], in_h0, 0, HID, False)
        ex_ac = Exchange(3, part_a, sum_a, in_ac, 0, part_a.shape[0], True)
        actor = (ex_ac,)
    ex_sm = Exchange(2, part_c, sum_c.at[g], in_sm, 2 * HID, part_c.shape[0] - 2 * HID, False)

    def spread_actor(k):
        if coded:
            mine = ex_ac.all_w.at[e]
        else:
            quarter = part_a.shape[0] // 4
            mine = sum_a.at[pl.ds(pl.multiple_of(e * quarter, 8), quarter)]
        return remote(mine, mine, ef_s.at[k - 1], ef_r.at[k - 1], dev(g, lax.rem(e + k, 4)))

    def spread_scale(k):
        mine = ex_ac.all_s.at[e]
        return remote(mine, mine, ef_s.at[2 + k], ef_r.at[2 + k], dev(g, lax.rem(e + k, 4)))

    def spread_start():
        for k in range(1, 4):
            spread_actor(k).start()
            if coded:
                spread_scale(k).start()

    lane = lax.broadcasted_iota(jnp.int32, (1, HID), 1)
    rid32 = lax.broadcasted_iota(jnp.int32, (32, 1), 0)

    def local(src, dst, k):
        return pltpu.make_async_copy(src, dst, sem_out.at[k])

    def own_outputs():
        return (
            local(small_out, out_small, 0), local(high_out, out_high, 1), local(rest_out, out_rest, 2), local(low_out, out_low, 5),
        )

    def far_outputs():
        return local(small_in, out_small, 0), local(high_in, out_high, 1), local(rest_in, out_rest, 2), local(low_in, out_low, 5)

    @pl.when(online)
    def _():
        slope_sum.last()
        total = slope_sum.whole() * (1.0 / critics)
        d_sample = -valid * total
        d_logp = ALPHA * valid
        sample = pi_act[...]
        th = heads[0:8, :]
        spread_e = heads[8:16, :]
        dz = (d_sample * (1.0 - sample * sample) + d_logp * 2.0 * sample) * ok8
        dls = (dz * spread_e - d_logp) * (3.5 * (1.0 - th * th)) * ok8
        heads[24:40, :] = jnp.zeros((16, rows), F32)
        heads[24:30, :] = dz[0:ACT]
        heads[30:36, :] = dls[0:ACT]
        actor_sum = jnp.sum(valid * (ALPHA * heads[16:17, :] - total[6:7]), axis=1, keepdims=True)
        done_rows = jnp.sum(valid, axis=1, keepdims=True)
        count = counts[0].astype(F32) if fold else 0.0
        for acc in (acc_c1, acc_c0, acc_cx, acc_o):
            acc[...] = jnp.zeros_like(acc)
        one16 = (lax.broadcasted_iota(jnp.int32, (16, block), 0) == 0).astype(BF16)
        if fold:
            ah1x[HID : HID + 16, :] = h1x[HID : HID + 16, :]
            ah2x[HID : HID + 16, :] = h1x[HID : HID + 16, :]

        def body_c(i, _):
            sl = pl.ds(pl.multiple_of(i * block, block), block)
            if fold:
                tall1, tall2, top = ah1x[:, sl], ah2x[:, sl], ah3[:, sl]
                slopes = [as1[:, sl], as2[:, sl], as3[:, sl]]
            else:
                kept = actor_layers(x_b[:, sl])
                tall1, tall2 = (jnp.concatenate([kept[k][0], one16], 0) for k in range(2))
                top = kept[2][0]
                slopes = [(1.0 + t) + h * (1.0 - t) for _, h, t in kept]
            do = heads[24:40, sl].astype(BF16)
            acc_o[0:16, :] += dot_t(do, top)
            d3 = (dot(aot[...], jnp.concatenate([do, do], 0)) * (0.5 * slopes[2])).astype(BF16)
            acc_c1[...] += dot_t(tall2, d3)
            d2 = (halves(dot(ab1[...], d3)) * slopes[1]).astype(BF16)
            acc_c0[...] += dot_t(tall1, d2)
            d1 = (halves(dot(ab0[...], d2)) * slopes[0]).astype(BF16)
            acc_cx[...] += dot_t(x_b[0:32, sl], d1)
            acc_o[16:32, 0:128] += dot_t(one16, jnp.concatenate([do, jnp.zeros((112, block), BF16)], 0))
            return 0

        lax.fori_loop(0, blocks, body_c, 0)
        part_a[0:HID, :] = acc_c0[0:HID, :]
        part_a[HID : 2 * HID, :] = acc_c1[0:HID, :]
        stats = jnp.where(lane == 0, actor_sum, jnp.where(lane == 1, count, jnp.where(lane == 2, done_rows, 0.0)))
        small = acc_cx[...]
        small = small + jnp.where(rid32 == 18, acc_c0[HID : HID + 1, :], 0.0)
        small = small + jnp.where(rid32 == 19, acc_c1[HID : HID + 1, :], 0.0)
        small = small + jnp.where(rid32 == 20, acc_o[16:17, :], 0.0)
        small = small + jnp.where(rid32 == 21, stats, 0.0)
        part_a[2 * HID : 2 * HID + 32, :] = small
        part_a[2 * HID + 32 : 2 * HID + 48, :] = acc_o[0:16, :]
        rest = part_a.shape[0] - 2 * HID - 48
        part_a[2 * HID + 48 :, :] = jnp.zeros((rest, HID), F32)
        for ex in actor:
            ex.start()

    @pl.when(targetd)
    def _():
        least_in[0] = least[:, 0:rows]
        for k in range(1, 4):
            least_target(k).wait_recv()

    @pl.when(online)
    def _():
        for k in range(4):
            least_online(k).wait_recv()

    rid16 = lax.broadcasted_iota(jnp.int32, (16, 1), 0)

    def directions(sl, spread):
        code = eps_s[7:8, sl]
        valid = jnp.where(code > 1.5, 1.0, 0.0)
        low = jnp.minimum(
            jnp.minimum(least_in[0, :, sl], least_in[1, :, sl]), jnp.minimum(least_in[2, :, sl], least_in[3, :, sl])
        )
        target = eps_s[6:7, sl] + GAMMA * (1.0 + 2.0 * valid - code) * low
        unit = unit_f[0:8, sl]
        inv = unit_f[8:9, sl]
        d_unit = (2.0 * ETA / (critics - 1)) * valid * (spread - unit)
        along = jnp.sum(d_unit * unit, axis=0, keepdims=True)
        dg = (d_unit - unit * along) * inv
        gap = value[:, sl] - target
        dv = 2.0 * valid * gap
        row_sums[0:1, sl] = valid * gap * gap
        row_sums[1:2, sl] = valid * jnp.sum(unit * (spread - unit), axis=0, keepdims=True)
        row_sums[2:3, sl] = dv
        dvh[:, sl] = 0.5 * dv
        dgb = dg.astype(BF16)
        dg_b[:, sl] = jnp.concatenate([dgb, dgb], 0)
        dv_b[:, sl] = jnp.where(rid16 == 0, dv, jnp.where(rid16 == 1, 1.0, 0.0)).astype(BF16)

    if not fold:
        unit_sum.last()
        directions(slice(0, rows), unit_sum.whole())

    for acc in (acc_h1, acc_h1t, acc_h0, acc_h0t, acc_x, acc_t, acc_last):
        acc[...] = jnp.zeros_like(acc)

    def body_b1(i, _):
        sl = pl.ds(pl.multiple_of(i * block, block), block)
        if fold:
            @pl.when(i == 0)
            def _():
                unit_sum.back_of(0)

            @pl.when(i == 1)
            def _():
                unit_sum.last_of(1)
                unit_sum.back_of(1)

            directions(sl, u_total[i])
        tp = dot(t1w[...], dg_b[:, sl])
        k1[:, sl] = (k1[:, sl].astype(F32) * tp).astype(BF16)
        th1 = (s1[:, sl].astype(F32) * tp).astype(BF16)
        tp = halves(dot(f0[...], th1))
        k2[:, sl] = (k2[:, sl].astype(F32) * tp).astype(BF16)
        th2 = (s2[:, sl].astype(F32) * tp).astype(BF16)
        tp = halves(dot(f1[...], th2))
        th3 = (s3[:, sl].astype(F32) * tp).astype(BF16)
        d3 = d3s[:, sl]
        ap3 = (dvh[:, sl] * d3.astype(F32) + k3[:, sl].astype(F32) * tp).astype(BF16)
        k3[:, sl] = ap3
        rows_dv = dv_b[:, sl]
        last = dot_t(rows_dv, h3s[:, sl])
        lone = dot_t(rows_dv, th3)
        acc_last[...] += last[0:8] + jnp.where(rid == 0, lone[1:2], 0.0)
        h3s[:, sl] = th1
        acc_h1[...] += dot_t(h2x[:, sl], ap3)
        acc_h1t[...] += dot_t(th2, d3)
        return 0

    def body_b2(i, _):
        sl = pl.ds(pl.multiple_of(i * block, block), block)
        ah = halves(dot(b1[...], k3[:, sl]))
        ap2 = (s2[:, sl].astype(F32) * ah + k2[:, sl].astype(F32)).astype(BF16)
        k2[:, sl] = ap2
        acc_h0[...] += dot_t(h1x[:, sl], ap2)
        acc_h0t[...] += dot_t(h3s[:, sl], d2s[:, sl])
        return 0

    def body_b3(i, _):
        sl = pl.ds(pl.multiple_of(i * block, block), block)
        ah = halves(dot(b0[...], k2[:, sl]))
        ap1 = (s1[:, sl].astype(F32) * ah + k1[:, sl].astype(F32)).astype(BF16)
        acc_x[...] += dot_t(x_b[0:32, sl], ap1)
        acc_t[...] += dot_t(dg_b[:, sl], d1s[:, sl])
        return 0

    lax.fori_loop(0, blocks, body_b1, 0)
    part_c[HID : 2 * HID, :] = acc_h1[0:HID, :] + 0.5 * acc_h1t[...]
    ex_h1.start()

    @pl.when(online)
    def _():
        for ex in actor:
            ex.reduce(False)

    lax.fori_loop(0, blocks, body_b2, 0)
    part_c[0:HID, :] = acc_h0[0:HID, :] + 0.5 * acc_h0t[...]
    ex_h0.start()
    ex_h1.reduce()

    @pl.when(targetd)
    def _():
        for ex in actor:
            ex.detour()

    lax.fori_loop(0, blocks, body_b3, 0)
    errors, diverse, dv_sum = (jnp.sum(row_sums[k : k + 1, :], axis=1, keepdims=True) for k in range(3))
    stats = jnp.where(lane == 0, errors, jnp.where(lane == 1, diverse, 0.0))
    small = acc_x[...]
    small = small + jnp.where(rid32 == 18, acc_h0[HID : HID + 1, :], 0.0)
    small = small + jnp.where(rid32 == 19, acc_h1[HID : HID + 1, :], 0.0)
    small = small + jnp.where(rid32 == 20, stats, 0.0)
    small = small + jnp.where(rid32 == 22, jnp.where(lane == 0, dv_sum, 0.0), 0.0)
    small = small + jnp.where(rid32 == 23, acc_last[0:1, :], 0.0)
    part_c[2 * HID : 2 * HID + 24, :] = small[0:24]
    part_c[2 * HID + 24 : 2 * HID + 32, :] = small[24:32] + 0.5 * acc_t[0:8, :]
    rest = part_c.shape[0] - 2 * HID - 32
    if rest:
        part_c[2 * HID + 32 :, :] = jnp.zeros((rest, HID), F32)
    ex_sm.start()
    ex_h1.forward()
    ex_h0.reduce()
    ex_sm.reduce()

    @pl.when(targetd)
    def _():
        for ex in actor:
            ex.forward()
        spread_start()

    ex_h0.forward()
    ex_sm.forward()

    @pl.when(online)
    def _():
        for ex in actor:
            ex.back()
        spread_start()


    @pl.when(online)
    def _():
        for copy in own_outputs():
            copy.start()

    @pl.when(targetd)
    def _():
        param_copy(3).wait_recv()
        for copy in far_outputs():
            copy.start()

    for k in range(1, 4):
        spread_actor(k).wait_recv()
        if coded:
            spread_scale(k).wait_recv()
    if coded:
        ex_ac.decode()
    copy_a = local(sum_a, out_a, 3)
    copy_a.start()
    for ex in (ex_h1, ex_h0, ex_sm):
        ex.arrived()
    if coded:
        ex_h1.decode()
        ex_h0.decode()
    copy_c = local(sum_c, out_c, 4)
    copy_c.start()

    @pl.when(online)
    def _():
        for what in range(4):
            param_copy(what).wait_send()

        def pi_sent(i, _):
            pi_copy(i).wait_send()
            return 0

        lax.fori_loop(0, blocks, pi_sent, 0)

    @pl.when(targetd)
    def _():
        for k in range(1, 4):
            least_target(k).wait_send()
        for k in range(4):
            least_online(k).wait_send()

    if fold:
        @pl.when(upper)
        def _():
            for what in range(2):
                fold_copy(what, 0).wait_send()

        @pl.when(lower)
        def _():
            for what in range(2):
                fold_copy(what, 1).wait_send()

        @pl.when(jnp.logical_and(upper, targetd))
        def _():
            least_copy().wait_send()

    unit_sum.sent()
    slope_sum.sent()
    for ex in actor:
        ex.sent_detour()
    for k in range(1, 4):
        spread_actor(k).wait_send()
        if coded:
            spread_scale(k).wait_send()
    for ex in (ex_h1, ex_h0, ex_sm):
        ex.sent()
    copy_a.wait()
    copy_c.wait()

    @pl.when(online)
    def _():
        for copy in own_outputs():
            copy.wait()

    @pl.when(targetd)
    def _():
        for copy in far_outputs():
            copy.wait()


def sizes(n_dp):
    return 2 * HID + up(CRITIC_SMALL, 8 * n_dp), up(2 * HID + ACTOR_SMALL, 32 * n_dp)


def fused(n_dp, rows, block, fold, data, own, aparams):
    v = pltpu.VMEM
    big = lambda n=HID: v((n, rows), BF16)
    dma = pltpu.SemaphoreType.DMA
    size_c, size_a = sizes(n_dp)
    coded = 2 * HID % (64 * n_dp) == 0
    h8 = lambda *n: v((*n, 8, rows // 2), F32)
    sums = [h8(2), h8(), h8(), h8(3), h8(2)]
    extra = (data[0].shape[1] - rows) // 2 if fold else LANES
    moved = [v((2, 32, extra), BF16), v((2, 8, extra), F32)]
    size = data[0].shape[1]
    kept = (lambda n, t: v((n, rows), t)) if fold else (lambda n, t: v((16, LANES), t))
    scratch = [
        v((32, size), F32), v((32, size), F32), v((8, size), F32), *moved, *moved,
        v((96, rows), BF16), v((8, rows), F32),
        v((128, HID), F32), v((HID, 128), F32), v((2, HID, 128), F32), v((HID, 128), F32),
        v((64, HID), F32), v((64, HID), F32), *[v((2 * HID, HID), BF16) for _ in range(6)],
        v((HID, 96), BF16), v((512, HID), BF16), v((512, HID), BF16), v((512, HID), BF16), v((512, HID), BF16),
        v((16, HID), BF16), v((HID, 16), BF16), v((16, HID), BF16),
        v((2, HID, 96), BF16), v((2, 512, HID), BF16), v((2, 512, HID), BF16), v((2, 16, HID), BF16),
        v((HID, 96), BF16), v((512, HID), BF16), v((512, HID), BF16), v((512, HID), BF16), v((512, HID), BF16),
        v((32, HID), BF16), v((HID, 32), BF16),
        big(272), big(272), big(), big(), big(), big(), big(), big(), big(), big(), big(), big(),
        v((40, rows), F32), kept(272, BF16), kept(272, BF16), kept(HID, BF16), kept(HID, F32), kept(HID, F32), kept(HID, F32),
        v((1, rows), F32), v((24, rows), F32), *sums,
        v((16, rows), BF16), v((16, rows), BF16), v((1, rows), F32), v((8, rows), F32),
        *sums, v((1, rows), F32),
        v((1, size), F32), v((1, 2 * extra), F32), v((4, 1, rows), F32),
        v((272, HID), F32), v((HID, HID), F32), v((272, HID), F32), v((HID, HID), F32),
        v((32, HID), F32), v((16, HID), F32), v((8, HID), F32), v((32, HID), F32),
        v((272, HID), F32), v((272, HID), F32), v((32, HID), F32),
        v((size_c, HID), F32), v((size_a, HID), F32), v((2, size_c, HID), F32), v((size_a, HID), F32),
        *[v((1, 8, HID) if coded else (n_dp - 1, HID // n_dp, HID), F32) for _ in range(2)],
        v((n_dp - 1, (size_c - 2 * HID) // n_dp, HID), F32),
        v((n_dp - 1, (ACTOR_SMALL if coded else size_a // 4) // n_dp, HID), F32),
        dma((2, 2)), dma((2, 2)), dma, dma, dma((4,)), dma((4,)), dma((rows // block,)), dma((rows // block,)), dma((8,)), dma((4,)), dma((2, 5)), dma((2, 5)),
        dma((5, n_dp - 1, 2)), dma((5, n_dp - 1, 2)), dma((5, n_dp - 1, 2)), dma((5, n_dp - 1, 2)), dma((5, n_dp, 2)), dma((5, n_dp, 2)),
        dma((6,)), dma((6,)), dma((6,)),
    ]
    if coded:
        for each, lead in ((HID // n_dp, 2), (HID // n_dp, 2), (2 * HID // (4 * n_dp), 4)):
            word, scale = (each // 2, HID), (1, HID)
            for outer in ((n_dp,), (n_dp - 1,), (lead, n_dp)):
                scratch += [v((*outer, *word), jnp.int32), v((*outer, *scale), F32)]
    spec = pl.BlockSpec(memory_space=pltpu.VMEM)
    anyspace = pl.BlockSpec(memory_space=pl.ANY)
    shape = lambda *s: jax.ShapeDtypeStruct(s, F32)
    return pl.pallas_call(
        functools.partial(kernel, n_dp, rows, block, fold),
        out_shape=(
            shape(2, size_c, HID), shape(size_a, HID), shape(64, HID), *[jax.ShapeDtypeStruct((2 * HID, HID), BF16)] * 3,
        ),
        in_specs=[spec] * 5 + [pl.BlockSpec(memory_space=pltpu.SMEM)] + [spec] * 7,
        out_specs=(anyspace,) * 6,
        scratch_shapes=scratch,
        compiler_params=pltpu.CompilerParams(collective_id=0 if fold else 1, has_side_effects=True, vmem_limit_bytes=63 * 2**20),
        name="edac_gradients" if fold else "edac_rest",
    )(*data, *own, *aparams)


def adamw(param, grad, first, second):
    first_new = BETA_ONE * first + (1.0 - BETA_ONE) * grad
    second_new = BETA_TWO * second + (1.0 - BETA_TWO) * grad * grad
    ratio = first_new / (1.0 - BETA_ONE**STEP) / (jnp.sqrt(second_new / (1.0 - BETA_TWO**STEP)) + EPS)
    return (param - LEARN * (ratio + DECAY * param), first_new, second_new)


def update_kernel(*refs):
    n_in, n_out = 24, 20
    src, dst = refs[:n_in], refs[n_in : n_in + n_out]
    rest = refs[n_in + n_out :]
    buf, res = rest[:n_in], rest[n_in : n_in + n_out]
    ge, gb, gae, gab, sem_in, sem_out = rest[n_in + n_out :]
    gc, ga, own_e, own_h, own_b, on_s, on_high, on_rest, low_h, em, ev, hm, hv, bm, bv, ae, ah, ab, aem, aev, ahm, ahv, abm, abv = buf
    o_e, o_h, o_b, o_em, o_ev, o_hm, o_hv, o_bm, o_bv, o_ae, o_ah, o_ab, o_aem, o_aev, o_ahm, o_ahv, o_abm, o_abv, o_ms, o_as = res
    online = lax.axis_index("grp") == 1
    index = {id(b): k for k, b in enumerate(buf)}
    out_index = {id(r): k for k, r in enumerate(res)}

    def read(b, slot=0, at=lambda r: r):
        k = index[id(b)]
        return pltpu.make_async_copy(at(src[k]), at(b), sem_in.at[k, slot])

    def write(r, slot=0, at=lambda x: x):
        k = out_index[id(r)]
        return pltpu.make_async_copy(at(r), at(dst[k]), sem_out.at[k, slot])

    def matrix(m, k):
        rows = slice(k * HID, (k + 1) * HID)
        par = [read(low_h, k, lambda r: r.at[rows])] if m == 0 else [
            read(on_high, k, lambda r: r.at[rows]), read(on_rest, k, lambda r: r.at[rows])
        ]
        mine = [read(b, 2 * m + k, lambda r: r.at[m, k]) for b in (own_h, hm, hv)]
        return [read(gc, 2 * m + k, lambda r: r.at[1 - m, rows])] + par + mine

    def actor_matrix(k):
        rows = slice(k * HID, (k + 1) * HID)
        return [read(ga, k, lambda r: r.at[rows])] + [read(b, k, lambda r: r.at[k]) for b in (ah, ahm, ahv)]

    stats = read(ga, 2, lambda r: r.at[2 * HID : 2 * HID + ACTOR_SMALL])
    small_reads = [read(gc, 4, lambda r: r.at[:, 2 * HID :]), stats] + [
        read(b) for b in (own_e, own_b, on_s, em, ev, bm, bv, ae, ab, aem, aev, abm, abv)
    ]
    order = [(0, 0), (0, 1), (1, 0), (1, 1)]
    stats.start()
    for copy in matrix(*order[0]):
        copy.start()
    for copy in small_reads:
        if copy is not stats:
            copy.start()
    for at in order[1:]:
        for copy in matrix(*at):
            copy.start()
    for k in range(2):
        for copy in actor_matrix(k):
            copy.start()

    gas = ga.at[2 * HID : 2 * HID + ACTOR_SMALL]
    stats.wait()
    scale = 1.0 / gas[21:22, 1:2]
    writes = []

    def put(copy):
        copy.start()
        writes.append(copy)

    def critic(own, param, grad, first, second):
        master, m_new, v_new = adamw(jnp.where(online, own, param), grad, first, second)
        polyak = TAU * master.astype(BF16).astype(F32) + (1.0 - TAU) * own
        return jnp.where(online, master, polyak), m_new, v_new

    def do_matrix(m, k):
        for copy in matrix(m, k):
            copy.wait()
        rows = slice(k * HID, (k + 1) * HID)
        param = low_h[rows, :].astype(F32) if m == 0 else on_high[rows, :].astype(F32) + on_rest[rows, :].astype(F32)
        o_h[m, k], o_hm[m, k], o_hv[m, k] = critic(own_h[m, k], param, gc[1 - m, rows, :] * scale, hm[m, k], hv[m, k])
        for r in (o_h, o_hm, o_hv):
            put(write(r, 2 * m + k, lambda x: x.at[m, k]))

    do_matrix(0, 0)
    for copy in small_reads:
        if copy is not stats:
            copy.wait()
    for m in range(2):
        small = gc.at[1 - m, 2 * HID : 2 * HID + 32]
        ge[0:OBS, :] = small[0:OBS, :]
        ge[OBS : OBS + ACT, :] = small[24 : 24 + ACT, :]
        ge[23:24, :] = small[23:24, :]
        gb[0:3, :] = small[17:20, :]
        gb[3:4, :] = small[22:23, :]
        first = 32 * (1 - m)
        o_e[m], o_em[m], o_ev[m] = critic(own_e[m], on_s[first : first + 24], ge[...] * scale, em[m], ev[m])
        o_b[m], o_bm[m], o_bv[m] = critic(own_b[m], on_s[first + 24 : first + 28], gb[...] * scale, bm[m], bv[m])
        o_ms[m : m + 1, :] = small[20:21, 0:2]
    gae[0:OBS, :] = gas[0:OBS, :]
    gae[OBS : OBS + 2 * ACT, :] = gas[32 : 32 + 2 * ACT, :]
    gab[0:3, :] = gas[17:20, :]
    gab[3:4, :] = gas[20:21, :]
    o_ae[...], o_aem[...], o_aev[...] = adamw(ae[...], gae[...] * scale, aem[...], aev[...])
    o_ab[...], o_abm[...], o_abv[...] = adamw(ab[...], gab[...] * scale, abm[...], abv[...])
    o_as[...] = gas[21:22, 0:2]
    for r in (o_e, o_b, o_em, o_ev, o_bm, o_bv, o_ae, o_ab, o_aem, o_aev, o_abm, o_abv, o_ms, o_as):
        put(write(r))
    for at in order[1:]:
        do_matrix(*at)
    for k in range(2):
        for copy in actor_matrix(k):
            copy.wait()
        grad = ga[k * HID : (k + 1) * HID, :] * scale
        o_ah[k], o_ahm[k], o_ahv[k] = adamw(ah[k], grad, ahm[k], ahv[k])
        for r in (o_ah, o_ahm, o_ahv):
            put(write(r, k, lambda x: x.at[k]))
    for copy in writes:
        copy.wait()


def update(grads, own, online, moments, aparams, amoments):
    shape = lambda *s: jax.ShapeDtypeStruct(s, F32)
    e_, h_, b_ = shape(2, 24, HID), shape(2, 2, HID, HID), shape(2, 4, HID)
    ae_, ah_, ab_ = shape(29, HID), shape(2, HID, HID), shape(4, HID)
    outs = (e_, h_, b_, e_, e_, h_, h_, b_, b_, ae_, ah_, ab_, ae_, ae_, ah_, ah_, ab_, ab_, shape(2, 2), shape(1, 2))
    args = (*grads, *own, *online, *moments, *aparams, *amoments)
    anyspace = pl.BlockSpec(memory_space=pl.ANY)
    room = [pltpu.VMEM(a.shape, a.dtype) for a in args]
    return pl.pallas_call(
        update_kernel,
        out_shape=outs,
        in_specs=[anyspace] * len(args),
        out_specs=(anyspace,) * len(outs),
        scratch_shapes=room
        + [pltpu.VMEM(o.shape, o.dtype) for o in outs]
        + [pltpu.VMEM((24, HID), F32), pltpu.VMEM((4, HID), F32), pltpu.VMEM((29, HID), F32), pltpu.VMEM((4, HID), F32)]
        + [pltpu.SemaphoreType.DMA((len(args), 5)), pltpu.SemaphoreType.DMA((len(outs), 4))],
        compiler_params=pltpu.CompilerParams(vmem_limit_bytes=40 * 2**20),
        name="adamw",
    )(*args)


def body(
    n_dp,
    states, actions, rewards, done, noise, counts,
    crit_edge, crit_hidden, crit_bias, edge_m, edge_v, hidden_m, hidden_v, bias_m, bias_v,
    act_edge, act_hidden, act_bias, act_edge_m, act_edge_v, act_hidden_m, act_hidden_v, act_bias_m, act_bias_v,
):
    size = states.shape[0]
    own = (crit_edge[0], crit_hidden[0], crit_bias[0])
    aparams = (act_edge, act_hidden, act_bias)
    data = (states.T, actions.T, noise.T, rewards[None], done[None], counts)
    moments = (edge_m, edge_v, hidden_m, hidden_v, bias_m, bias_v)
    amoments = (act_edge_m, act_edge_v, act_hidden_m, act_hidden_v, act_bias_m, act_bias_v)
    rows = FOLD_ROWS if size > FOLD_ROWS else size
    grad_c, grad_a, *online = fused(n_dp, rows, rows // 2, True, (*data, rewards[None]), own, aparams)

    def finish(grad_c, grad_a):
        return update((grad_c, grad_a), own, online, moments, aparams, amoments)

    def with_rest():
        z = lax.axis_index("dp")
        partner = lax.ppermute(counts, "dp", [(k, n_dp - 1 - k) for k in range(n_dp)])
        at = jnp.arange(size, dtype=jnp.int32)
        taken = (rows // LANES - 1 - (at - rows) // LANES) * LANES >= (jnp.minimum(partner, rows) + LANES - 1) // LANES * LANES
        taken = jnp.where(z >= n_dp - n_dp // 2, taken, False)
        left = jnp.logical_and(jnp.logical_and(at >= rows, at < counts), jnp.logical_not(taken))
        more_c, more_a, *_ = fused(n_dp, size, size // 16, False, (*data, left.astype(F32)[None]), own, aparams)
        return finish(grad_c + more_c, grad_a + more_a)

    sums = grad_a[2 * HID + 21]
    out = lax.cond(sums[1] != sums[2], with_rest, lambda: finish(grad_c, grad_a))
    return (*(o[None] for o in out[:3]), *out[3:19], out[19][0])


def solution(mesh):
    member = P("grp", "ens", None, None)
    hidden = P("grp", "ens", None, None, None)
    mom = P("ens", None, None)
    mom_h = P("ens", None, None, None)
    return jax.shard_map(
        functools.partial(body, mesh.shape["dp"]),
        mesh=mesh,
        in_specs=(
            P("dp", None), P("dp", None), P("dp"), P("dp"), P("dp", None), P("dp"),
            member, hidden, member, mom, mom, mom_h, mom_h, mom, mom,
        ) + (P(),) * 9,
        out_specs=(member, hidden, member, mom, mom, mom_h, mom_h, mom, mom) + (P(),) * 9 + (P("ens", None), P()),
        check_vma=False,
    )
```

```python
import functools

import jax
import jax.numpy as jnp
from jax import lax
from jax.experimental import pallas as pl
from jax.experimental.pallas import tpu as pltpu
from jax.sharding import PartitionSpec as P

OBS = 17
ACT = 6
HID = 256
STEP = 5
FOLD_ROWS = 2816
LANES = 128

GAMMA = 0.99
ALPHA = 0.2
ETA = 1.0
LEARN = 0.03
BETA_ONE = 0.5
BETA_TWO = 0.5
DECAY = 0.01
EPS = 1e-08
TAU = 0.05
HALF_LOG_TWO_PI = 0.9189385332046727
LOG_TWO = 0.6931471805599453

F32 = jnp.float32
BF16 = jnp.bfloat16

CRITIC_SMALL, ACTOR_SMALL = 32, 64


def dot(a, b):
    return lax.dot_general(a, b, (((1,), (0,)), ((), ())), preferred_element_type=F32)


def dot_t(a, b):
    return lax.dot_general(a, b, (((1,), (1,)), ((), ())), preferred_element_type=F32)


def split(w):
    high = w.astype(BF16).astype(F32)
    return high, w - high


def halves(p):
    n = p.shape[0] // 2
    return p[:n] + p[n:]


def prep_input(stage, w1, edge, bias, n_in):
    stage[...] = jnp.zeros_like(stage)
    stage[0:OBS, :] = edge[0:OBS, :]
    stage[OBS : OBS + 1, :] = bias[0:1, :]
    if n_in > OBS:
        stage[24 : 24 + ACT, :] = edge[OBS : OBS + ACT, :]
    high, low = split(0.5 * stage[0:32, :])
    w1[...] = jnp.concatenate([high, low, high], 0).T.astype(BF16)


def prep_hidden(fwd, bwd, hidden):
    w = 0.5 * hidden
    if fwd is not None:
        high, low = split(w.T)
        fwd[...] = jnp.concatenate([high, low], 0).astype(BF16)
    if bwd is not None:
        high, low = split(w)
        bwd[...] = jnp.concatenate([high, low], 0).astype(BF16)


def silu_half(u):
    t = jnp.tanh(u)
    return u + u * t, t


def up(n, by):
    return -(-n // by) * by


def kernel(
    n_dp,
    rows,
    block,
    fold,
    states, actions, noise, rewards, done, counts, mask, c_edge, c_hidden, c_bias, a_edge, a_hidden, a_bias,
    out_c, out_a, out_small, out_high, out_rest, out_low,
    xs, ns, eps_s, far_x, far_e, here_x, here_e, x_b, pi_act, stage, vec, tvec, avec,
    small_out, small_in, high_out, high_in, rest_out, rest_in, low_out, low_in,
    w1, f0, f1, b0, b1, ga, t1w, eq, pw, pv, pq, pg, pf, pb,
    tw1, tf0, tf1, teq,
    aw1, af0, af1, ab0, ab1, ao, aot,
    h1x, h2x, h3s, s1, s2, s3, k1, k2, k3, d1s, d2s, d3s,
    heads, ah1x, ah2x, ah3, as1, as2, as3,
    value, unit_f, u_mine, u_peer, u_pair, u_far, u_total, dg_b, dv_b, dvh, row_sums,
    q_mine, q_peer, q_pair, q_far, q_total, least, far_least, least_in,
    acc_h1, acc_h1t, acc_h0, acc_h0t, acc_x, acc_t, acc_last, acc_o, acc_c1, acc_c0, acc_cx,
    part_c, part_a, sum_c, sum_a, in_h1, in_h0, in_sm, in_ac,
    fold_s, fold_r, sem_far_s, sem_far_r, sem_param_s, sem_param_r, sem_least_s, sem_least_r, es_s, es_r,
    rs_s, rs_r, ag_s, ag_r, xf_s, xf_r, ef_s, ef_r, sem_out, *boxes,
):
    g = lax.axis_index("grp")
    e = lax.axis_index("ens")
    z = lax.axis_index("dp")
    me = g * 4 + e
    blocks = rows // block
    extra = states.shape[1] - rows
    lower = z < n_dp // 2
    upper = z >= n_dp - n_dp // 2
    half = rows // 2
    online = g == 1
    targetd = g == 0
    critics = 8
    coded = bool(boxes)

    def dev(gg, ee):
        return {"grp": gg, "ens": ee}

    def remote(src, dst, send, recv, where):
        return pltpu.make_async_remote_copy(
            src_ref=src, dst_ref=dst, send_sem=send, recv_sem=recv, device_id=where, device_id_type=pl.DeviceIdType.MESH
        )

    barrier = pltpu.get_barrier_semaphore()
    for k in range(1, 8):
        p = lax.rem(me + k, 8)
        pl.semaphore_signal(barrier, inc=1, device_id=dev(p // 4, lax.rem(p, 4)), device_id_type=pl.DeviceIdType.MESH)
    for k in range(1, n_dp):
        pl.semaphore_signal(barrier, inc=1, device_id={"dp": lax.rem(z + k, n_dp)}, device_id_type=pl.DeviceIdType.MESH)

    def all_here():
        pl.semaphore_wait(barrier, 7 + n_dp - 1)

    def param_copy(what):
        src, dst = (
            (small_out.at[0:32], small_in.at[0:32]),
            (high_out, high_in),
            (rest_out, rest_in),
            (low_out, low_in),
            (small_out.at[32:64], small_in.at[32:64]),
        )[what]
        return remote(src, dst, sem_param_s.at[what], sem_param_r.at[what], dev(0, e))

    @pl.when(online)
    def _():
        small_out[...] = jnp.zeros_like(small_out)
        for k in range(2):
            small_out[32 * k : 32 * k + 24, :] = c_edge[1 - k]
            small_out[32 * k + 24 : 32 * k + 28, :] = c_bias[1 - k]
            high, low = split(c_hidden[1, k])
            high_out[k * HID : (k + 1) * HID, :] = high.astype(BF16)
            rest_out[k * HID : (k + 1) * HID, :] = low.astype(BF16)
            low_out[k * HID : (k + 1) * HID, :] = c_hidden[0, k].astype(BF16)
        all_here()
        for what in range(3):
            param_copy(what).start()

    lane_id = lax.broadcasted_iota(jnp.int32, (1, states.shape[1]), 1)
    if fold:
        code = jnp.where(lane_id < counts[0], 2.0, 0.0) + done[...].astype(F32)
    else:
        code = 2.0 * mask[...] + done[...].astype(F32)

    ones_row = jnp.ones((1, states.shape[1]), F32)
    xs[...] = jnp.zeros_like(xs)
    xs[0:OBS, :] = states[0:OBS, :]
    xs[OBS : OBS + 1, :] = ones_row
    xs[24 : 24 + ACT, :] = actions[...]
    eps_s[6:7, :] = rewards[...]
    eps_s[7:8, :] = code

    @pl.when(online)
    def _():
        eps_s[0:ACT, :] = noise[0:ACT, :]

    @pl.when(targetd)
    def _():
        eps_s[0:ACT, :] = noise[ACT : 2 * ACT, :]
        ns[...] = jnp.zeros_like(ns)
        ns[0:OBS, :] = states[OBS : 2 * OBS, :]
        ns[OBS : OBS + 1, :] = ones_row

    core = lax.rem(e, 2)
    other_core = e + 1 - 2 * core
    far_chip = lax.rem(e + 2, 4)

    def fold_copy(what, hop):
        here, there = ((here_e, far_e), (here_x, far_x))[what]
        if hop == 0:
            return remote(here.at[core], there.at[core], fold_s.at[what, 0], fold_r.at[what, 0], {"dp": n_dp - 1 - z})
        return remote(there.at[core], there.at[core], fold_s.at[what, 1], fold_r.at[what, 1], dev(g, other_core))

    def least_copy():
        return remote(least.at[:, rows:], far_least, sem_far_s, sem_far_r, {"dp": n_dp - 1 - z})

    def merge(into, blocks_of):
        first = rows - extra
        there = jnp.concatenate([blocks_of(b) for b in range(extra // LANES - 1, -1, -1)], 1).astype(F32)
        lanes = lax.broadcasted_iota(jnp.int32, (1, extra), 1) + first
        bound = (jnp.minimum(counts[0], rows) + LANES - 1) // LANES * LANES
        into[:, first:rows] = jnp.where(lanes < bound, into[:, first:rows], there)

    def in_halves(pieces):
        per = extra // LANES // 2
        return lambda b: pieces[b // per, :, (b % per) * LANES : (b % per + 1) * LANES]

    def fold_out():
        if fold:
            @pl.when(upper)
            def _():
                for h in range(2):
                    part = slice(rows + h * extra // 2, rows + (h + 1) * extra // 2)
                    here_e[h] = eps_s[:, part]
                    here_x[h] = xs[:, part].astype(BF16)
                for what in range(2):
                    fold_copy(what, 0).start()

    def fold_in():
        if fold:
            @pl.when(lower)
            def _():
                for what in range(2):
                    fold_copy(what, 0).wait_recv()
                    fold_copy(what, 1).start()
                for what in range(2):
                    fold_copy(what, 1).wait_recv()
                merge(eps_s, in_halves(far_e))
                merge(xs, in_halves(far_x))

    def put_x():
        high, low = split(xs[:, 0:rows])
        xin = high.astype(BF16)
        x_b[0:32, :] = xin
        x_b[32:64, :] = xin
        x_b[64:96, :] = low.astype(BF16)

    def prep_small(edge, bias, w1_, vec_, eq_, ga_, t1_):
        prep_input(stage, w1_, edge, bias, OBS + ACT)
        stage[...] = jnp.zeros_like(stage)
        stage[0:1, :] = 0.5 * bias[1:2, :]
        stage[1:2, :] = 0.5 * bias[2:3, :]
        stage[2:3, :] = edge[23:24, :]
        vec_[...] = stage[...].T
        vec_[0:1, 8:9] = bias[3:4, 0:1]
        stage[...] = jnp.zeros_like(stage)
        high, low = split(edge[23:24, :])
        stage[0:1, :] = high
        stage[1:2, :] = low
        eq_[...] = stage[0:16, :].astype(BF16)
        if ga_ is not None:
            stage[...] = jnp.zeros_like(stage)
            stage[0:ACT, :] = 0.5 * edge[OBS : OBS + ACT, :]
            high, low = split(stage[0:8, :])
            both = jnp.concatenate([high, low], 0)
            ga_[...] = both.astype(BF16)
            stage[0:16, :] = both
            if t1_ is not None:
                t1_[...] = stage[...].T[:, 0:16].astype(BF16)

    def prep_actor():
        prep_input(stage, aw1, a_edge, a_bias, OBS)
        prep_hidden(af0, ab0, a_hidden[0])
        prep_hidden(af1, ab1, a_hidden[1])
        stage[...] = jnp.zeros_like(stage)
        stage[0:1, :] = 0.5 * a_bias[1:2, :]
        stage[1:2, :] = 0.5 * a_bias[2:3, :]
        stage[2:3, :] = a_bias[3:4, :]
        avec[...] = stage[...].T
        stage[...] = jnp.zeros_like(stage)
        stage[0:ACT, :] = a_edge[OBS : OBS + ACT, :]
        stage[8 : 8 + ACT, :] = a_edge[OBS + ACT : OBS + 2 * ACT, :]
        high, low = split(stage[0:16, :])
        ao[...] = jnp.concatenate([high, low], 0).astype(BF16)
        stage[...] = jnp.zeros_like(stage)
        stage[0 : 2 * ACT, :] = a_edge[OBS : OBS + 2 * ACT, :]
        high, low = split(stage[0:16, :])
        stage[0:32, :] = jnp.concatenate([high, low], 0)
        aot[...] = stage[...].T[:, 0:32].astype(BF16)

    prep_actor()

    def actor_layers(src):
        kept = []
        hb = None
        for w, b in ((aw1, None), (af0, 0), (af1, 1)):
            u = dot(w[...], src) if b is None else halves(dot(w[...], hb)) + avec[:, b : b + 1]
            h, t = silu_half(u)
            hb = h.astype(BF16)
            kept.append((hb, h, t))
        return kept

    ok8 = (lax.broadcasted_iota(jnp.int32, (8, 1), 0) < ACT).astype(F32)

    def actor_heads(hb, sl):
        out = halves(dot(ao[...], hb))
        eps = eps_s[:, sl]
        center = out[0:8] + avec[0:8, 2:3] * ok8
        th = jnp.tanh(out[8:16] + avec[6:14, 2:3] * ok8)
        log_std = 3.5 * th - 1.5
        spread_e = jnp.exp(log_std) * eps
        latent = center + spread_e
        soft = jnp.maximum(-2.0 * latent, 0.0) + jnp.log(1.0 + jnp.exp(-2.0 * jnp.abs(latent)))
        terms = -0.5 * eps * eps - log_std - HALF_LOG_TWO_PI - 2.0 * (LOG_TWO - latent - soft)
        logp = jnp.sum(terms * ok8, axis=0, keepdims=True)
        sample = jnp.tanh(latent) * ok8
        return sample, logp, th, spread_e

    put_x()

    @pl.when(online)
    def _():
        fold_out()
        prep_small(c_edge.at[0], c_bias.at[0], w1, vec, eq, ga, t1w)
        prep_hidden(f0, b0, c_hidden[0, 0])
        prep_hidden(f1, b1, c_hidden[0, 1])
        for k, (fwd, bwd) in enumerate(((f0, b0), (f1, b1))):
            pf[0, k] = fwd[0:HID, :]
            pb[0, k] = bwd[0:HID, :]
            w = 0.5 * c_hidden[1, k]
            pf[1, k] = w.T.astype(BF16)
            pb[1, k] = w.astype(BF16)
        pw[0], pv[0], pq[0], pg[0] = w1[...], vec[...], eq[...], ga[...]
        prep_small(c_edge.at[1], c_bias.at[1], pw.at[1], pv.at[1], pq.at[1], pg.at[1], None)

    def least_online(k):
        return remote(least.at[:, 0:rows], least_in.at[k], sem_least_s.at[4 + k], sem_least_r.at[k], dev(1, lax.rem(e + k, 4)))

    def least_target(k):
        return remote(least.at[:, 0:rows], least_in.at[k], sem_least_s.at[k], sem_least_r.at[k], dev(0, lax.rem(e + k, 4)))

    def half_hidden(part, values):
        to = slice(part * HID, (part + 1) * HID)
        for k, (fwd, bwd) in enumerate(((f0, b0), (f1, b1))):
            w = 0.5 * values[k * HID : (k + 1) * HID, :].astype(F32)
            fwd[to, :] = w.T.astype(BF16)
            bwd[to, :] = w.astype(BF16)

    @pl.when(targetd)
    def _():
        for m in range(2):
            prep_small(c_edge.at[m], c_bias.at[m], tw1.at[m], tvec.at[m], teq.at[m], None, None)
            prep_hidden(tf0.at[m], None, c_hidden[m, 0])
            prep_hidden(tf1.at[m], None, c_hidden[m, 1])

        def body(i, _):
            @pl.when(i == 1)
            def _():
                all_here()
                fold_out()

            first = jnp.minimum(i * block, states.shape[1] - block)
            sl = pl.ds(pl.multiple_of(first, LANES), block)
            high, rest = split(ns[:, sl])
            nx, rest = high.astype(BF16), rest.astype(BF16)
            kept = actor_layers(jnp.concatenate([nx, nx, rest], 0))
            sample, logp, th, spread_e = actor_heads(kept[2][0], sl)
            high, rest = split(jnp.concatenate([ns[0:24, sl], sample], 0))
            nx = high.astype(BF16)
            nx = jnp.concatenate([nx, nx, rest.astype(BF16)], 0)
            low = None
            for m in range(2):
                h, t = silu_half(dot(tw1[m], nx))
                h, t = silu_half(halves(dot(tf0[m], h.astype(BF16))) + tvec[m, :, 0:1])
                h, t = silu_half(halves(dot(tf1[m], h.astype(BF16))) + tvec[m, :, 1:2])
                r = dot(teq[m], h.astype(BF16))
                q = r[0:1] + r[1:2] + tvec[m, 0:1, 8:9]
                low = q if low is None else jnp.minimum(low, q)
            least[:, sl] = low - ALPHA * logp
            return 0

        lax.fori_loop(0, blocks + (jnp.where(upper, 1, 0) if fold else 0), body, 0)
        if fold:
            @pl.when(upper)
            def _():
                least_copy().start()

        fold_in()
        if fold:
            put_x()
        for what in range(3):
            param_copy(what).wait_recv()
        prep_small(small_in.at[0:24], small_in.at[24:32], w1, vec, eq, ga, t1w)
        half_hidden(0, high_in)
        half_hidden(1, rest_in)

    def least_out():
        @pl.when(targetd)
        def _():
            if fold:
                @pl.when(lower)
                def _():
                    least_copy().wait_recv()
                    merge(least, lambda b: far_least[:, b * LANES : (b + 1) * LANES])

            for k in range(1, 4):
                least_target(k).start()
            for k in range(4):
                least_online(k).start()

    class EnsembleSum:
        def __init__(self, index, mine, peer, pair, far, total, only_online):
            self.index, self.mine, self.peer, self.pair, self.far, self.total = index, mine, peer, pair, far, total
            self.chips = (1,) if only_online else (0, 1, 2)

        def to_core(self):
            return remote(self.mine.at[1 - core], self.peer, es_s.at[self.index, 0], es_r.at[self.index, 0], dev(g, other_core))

        def to_chip(self, k):
            across = (1 - g, g, 1 - g)[k]
            where = dev(across, (e, far_chip, far_chip)[k])
            return remote(self.pair, self.far.at[k], es_s.at[self.index, 1 + k], es_r.at[self.index, 1 + k], where)

        def back(self):
            return remote(self.total.at[core], self.total.at[core], es_s.at[self.index, 4], es_r.at[self.index, 4], dev(g, other_core))

        def begin(self, first, second):
            self.mine[0] = first
            self.mine[1] = second
            self.to_core().start()

        def middle(self):
            self.to_core().wait_recv()
            self.pair[...] = self.mine[core] + self.peer[...]
            for k in self.chips:
                self.to_chip(k).start()

        def first_to_core(self, h, values):
            self.mine[h] = values

            @pl.when(core != h)
            def _():
                self.to_core().start()

            @pl.when(core == h)
            def _():
                self.middle()

        def last_of(self, h):
            @pl.when(core == h)
            def _():
                self.last()

        def back_of(self, h):
            @pl.when(core != h)
            def _():
                self.back().wait_recv()

        def last(self):
            total = self.pair[...]
            for k in self.chips:
                self.to_chip(k).wait_recv()
                total = total + self.far[k]
            self.total[core] = total
            self.back().start()

        def whole(self):
            self.back().wait_recv()
            return jnp.concatenate([self.total[0], self.total[1]], 1)

        def sent(self):
            self.to_core().wait_send()
            for k in self.chips:
                self.to_chip(k).wait_send()
            self.back().wait_send()

    unit_sum = EnsembleSum(0, u_mine, u_peer, u_pair, u_far, u_total, False)
    slope_sum = EnsembleSum(1, q_mine, q_peer, q_pair, q_far, q_total, True)

    rid = lax.broadcasted_iota(jnp.int32, (8, 1), 0)

    @pl.when(online)
    def _():
        def body_p(i, _):
            sl = pl.ds(pl.multiple_of(i * block, block), block)

            @pl.when(i == 1)
            def _():
                fold_in()
                if fold:
                    put_x()

            kept = actor_layers(x_b[:, sl])
            if fold:
                for store, curve, (hb, h, t) in zip((ah1x, ah2x, ah3), (as1, as2, as3), kept):
                    store[0:HID, sl] = hb
                    curve[:, sl] = (1.0 + t) + h * (1.0 - t)
            sample, logp, th, spread_e = actor_heads(kept[2][0], sl)
            pi_act[:, sl] = sample
            heads[0:8, sl] = th
            heads[8:16, sl] = spread_e
            heads[16:17, sl] = logp
            pin = jnp.concatenate([xs[0:24, sl], sample], 0).astype(BF16)
            unit_f[16:24, sl] = jnp.zeros((8, block), F32)

            def member(m, _):
                def act(u):
                    h, t = silu_half(u)
                    hb, tb = h.astype(BF16), t.astype(BF16)
                    one = jnp.ones((), BF16)
                    return hb, (one + tb) + hb * (one - tb)

                h, a1 = act(dot(pw[m][:, 0:64], jnp.concatenate([pin, pin], 0)))
                h, a2 = act(dot(pf[m, 0], h) + pv[m][:, 0:1])
                h, a3 = act(dot(pf[m, 1], h) + pv[m][:, 1:2])
                r = dot(pq[m], h)
                q = r[0:1] + r[1:2] + pv[m][0:1, 8:9]
                d = pv[m][:, 2:3].astype(BF16) * a3
                d = dot(pb[m, 1], d).astype(BF16) * a2
                d = dot(pb[m, 0], d).astype(BF16) * a1
                unit_f[16:24, sl] += halves(dot(pg[m], d)) + jnp.where(rid == 6, q, 0.0)
                return 0

            lax.fori_loop(0, 2, member, 0)
            return 0

        lax.fori_loop(0, blocks, body_p, 0)
        slope_sum.begin(unit_f[16:24, 0:half], unit_f[16:24, half:rows])

    ones = (lax.broadcasted_iota(jnp.int32, (16, rows), 0) == 0).astype(BF16)
    h1x[HID : HID + 16, :] = ones
    h2x[HID : HID + 16, :] = ones

    def curves(u):
        h, t = silu_half(u)
        c = 1.0 + t
        d = 1.0 - t
        return h, c + h * d, (c * d) * (1.0 - u * t)

    valid = jnp.where(eps_s[7:8, 0:rows] > 1.5, 1.0, 0.0)

    def body_a(i, _):
        @pl.when(i == 1)
        def _():
            @pl.when(online)
            def _():
                slope_sum.middle()

            if fold:
                unit_sum.first_to_core(0, unit_f[0:8, 0:half])
            least_out()

            @pl.when(online)
            def _():
                param_copy(3).start()
                param_copy(4).start()


        sl = pl.ds(pl.multiple_of(i * block, block), block)
        h, a1, q1 = curves(dot(w1[...], x_b[:, sl]))
        hb = h.astype(BF16)
        h1x[0:HID, sl] = hb
        s1[:, sl] = a1.astype(BF16)
        h, a2, q2 = curves(halves(dot(f0[...], hb)) + vec[:, 0:1])
        hb = h.astype(BF16)
        h2x[0:HID, sl] = hb
        s2[:, sl] = a2.astype(BF16)
        h, a3, q3 = curves(halves(dot(f1[...], hb)) + vec[:, 1:2])
        hb = h.astype(BF16)
        h3s[:, sl] = hb
        s3[:, sl] = a3.astype(BF16)
        r = dot(eq[...], hb)
        value[:, sl] = r[0:1] + r[1:2] + vec[0:1, 8:9]
        last = vec[:, 2:3]
        db = (last * a3).astype(BF16)
        d3s[:, sl] = db
        k3[:, sl] = (last * q3).astype(BF16)
        m = halves(dot(b1[...], db))
        db = (m * a2).astype(BF16)
        d2s[:, sl] = db
        k2[:, sl] = (m * q2).astype(BF16)
        m = halves(dot(b0[...], db))
        db = (m * a1).astype(BF16)
        d1s[:, sl] = db
        k1[:, sl] = (m * q1).astype(BF16)
        slope = halves(dot(ga[...], db))
        inv = lax.rsqrt(jnp.sum(slope * slope, axis=0, keepdims=True) + 0.01)
        unit_f[0:8, sl] = slope * inv
        unit_f[8:9, sl] = inv
        return 0

    lax.fori_loop(0, blocks, body_a, 0)
    if fold:
        unit_sum.first_to_core(1, unit_f[0:8, half:rows])
        unit_sum.last_of(0)
    else:
        unit_sum.begin(unit_f[0:8, 0:half], unit_f[0:8, half:rows])
        unit_sum.middle()

    class Exchange:
        def __init__(self, index, part, into, inbox, base, count, wide):
            self.index, self.part, self.into, self.inbox, self.base, self.count, self.wide = index, part, into, inbox, base, count, wide
            self.each = count // (n_dp * (4 if wide else 1))

        def rows_of(self, shard):
            first = self.base + (e * n_dp + shard if self.wide else shard) * self.each
            return pl.ds(pl.multiple_of(first, 8), self.each)

        def scatter(self, k):
            to = lax.rem(z + k, n_dp)
            return remote(
                self.part.at[self.rows_of(to)], self.inbox.at[k - 1], rs_s.at[self.index, k - 1, 0], rs_r.at[self.index, k - 1, 0], {"dp": to}
            )

        def gather(self, k):
            mine = self.into.at[self.rows_of(z)]
            return remote(mine, mine, ag_s.at[self.index, k - 1, 0], ag_r.at[self.index, k - 1, 0], {"dp": lax.rem(z + k, n_dp)})

        def across(self, k):
            there = self.into.at[self.rows_of(lax.rem(z + n_dp - k, n_dp))]
            return remote(there, there, xf_s.at[self.index, k, 0], xf_r.at[self.index, k, 0], dev(1 - g, e))

        def start(self):
            for k in range(1, n_dp):
                self.scatter(k).start()

        def reduce(self, along=True):
            total = self.part[self.rows_of(z), :]
            for k in range(1, n_dp):
                self.scatter(k).wait_recv()
                total = total + self.inbox[k - 1]
            self.into[self.rows_of(z), :] = total
            if along:
                for k in range(1, n_dp):
                    self.gather(k).start()
            self.across(0).start()

        def forward(self):
            for k in range(1, n_dp):
                self.gather(k).wait_recv()
                self.across(k).start()

        def sent(self):
            for k in range(1, n_dp):
                self.scatter(k).wait_send()
                self.gather(k).wait_send()
            for k in range(n_dp):
                self.across(k).wait_send()

        def arrived(self):
            for k in range(n_dp):
                self.across(k).wait_recv()

        def detour(self):
            self.across(0).wait_recv()
            for k in range(1, n_dp):
                self.gather(k).start()

        def back(self):
            for k in range(1, n_dp):
                self.across(k).wait_recv()

        def sent_detour(self):
            @pl.when(online)
            def _():
                for k in range(1, n_dp):
                    self.scatter(k).wait_send()
                self.across(0).wait_send()

            @pl.when(targetd)
            def _():
                for k in range(1, n_dp):
                    self.gather(k).wait_send()
                    self.across(k).wait_send()

    class Coded(Exchange):
        def __init__(self, index, part, out, base, count, lead, wide, boxes):
            self.index, self.part, self.out, self.base, self.count, self.lead, self.wide = index, part, out, base, count, lead, wide
            self.out_w, self.out_s, self.in_w, self.in_s, self.all_w, self.all_s = boxes
            self.each = count // (n_dp * (4 if wide else 1))

        def pack(self, x):
            top = jnp.maximum(jnp.max(jnp.abs(x), axis=0, keepdims=True), 1e-30)
            q = jnp.round(x * (32767.0 / top)).astype(jnp.int32)
            h = self.each // 2
            return jnp.bitwise_or(jnp.bitwise_and(q[:h], 65535), jnp.left_shift(q[h:], 16)), top * (1.0 / 32767.0)

        def unpack(self, w, scale):
            low = jnp.right_shift(jnp.left_shift(w, 16), 16)
            high = jnp.right_shift(w, 16)
            return jnp.concatenate([low, high], 0).astype(F32) * scale

        def scatter(self, k):
            to = lax.rem(z + k, n_dp)
            return Both([
                remote(o.at[to], i.at[k - 1], rs_s.at[self.index, k - 1, q], rs_r.at[self.index, k - 1, q], {"dp": to})
                for q, (o, i) in enumerate(((self.out_w, self.in_w), (self.out_s, self.in_s)))
            ])

        def gather(self, k):
            return Both([
                remote(
                    a.at[self.lead, z], a.at[self.lead, z], ag_s.at[self.index, k - 1, q], ag_r.at[self.index, k - 1, q],
                    {"dp": lax.rem(z + k, n_dp)},
                )
                for q, a in enumerate((self.all_w, self.all_s))
            ])

        def across(self, k):
            there = lax.rem(z + n_dp - k, n_dp)
            return Both([
                remote(
                    a.at[self.lead, there], a.at[self.lead, there], xf_s.at[self.index, k, q], xf_r.at[self.index, k, q], dev(1 - g, e)
                )
                for q, a in enumerate((self.all_w, self.all_s))
            ])

        def start(self):
            for shard in range(n_dp):
                w, scale = self.pack(self.part[self.rows_of(shard), :])
                self.out_w[shard] = w
                self.out_s[shard] = scale
            for k in range(1, n_dp):
                self.scatter(k).start()

        def reduce(self, along=True):
            total = self.part[self.rows_of(z), :]
            for k in range(1, n_dp):
                self.scatter(k).wait_recv()
                total = total + self.unpack(self.in_w[k - 1], self.in_s[k - 1])
            w, scale = self.pack(total)
            self.all_w[self.lead, z] = w
            self.all_s[self.lead, z] = scale
            if along:
                for k in range(1, n_dp):
                    self.gather(k).start()
            self.across(0).start()

        def decode(self):
            for lead in range(self.all_w.shape[0]):
                for shard in range(n_dp):
                    x = self.unpack(self.all_w[lead, shard], self.all_s[lead, shard])
                    if self.wide:
                        first = (lead * n_dp + shard) * self.each
                        self.out[first : first + self.each, :] = x
                    else:
                        first = self.base + shard * self.each
                        self.out[lead, first : first + self.each, :] = x

    class Both:
        def __init__(self, copies):
            self.copies = copies

        def start(self):
            for c in self.copies:
                c.start()

        def wait_recv(self):
            for c in self.copies:
                c.wait_recv()

        def wait_send(self):
            for c in self.copies:
                c.wait_send()

    if coded:
        box_h1, box_h0, box_ac = boxes[0:6], boxes[6:12], boxes[12:18]
    if coded:
        ex_h1 = Coded(0, part_c, sum_c, HID, HID, g, False, box_h1)
        ex_h0 = Coded(1, part_c, sum_c, 0, HID, g, False, box_h0)
        ex_ac = Coded(3, part_a, sum_a, 0, 2 * HID, e, True, box_ac)
        ex_as = Exchange(4, part_a, sum_a, in_ac, 2 * HID, ACTOR_SMALL, False)
        actor = (ex_ac, ex_as)
    else:
        ex_h1 = Exchange(0, part_c, sum_c.at[g], in_h1, HID, HID, False)
        ex_h0 = Exchange(1, part_c, sum_c.at[g], in_h0, 0, HID, False)
        ex_ac = Exchange(3, part_a, sum_a, in_ac, 0, part_a.shape[0], True)
        actor = (ex_ac,)
    ex_sm = Exchange(2, part_c, sum_c.at[g], in_sm, 2 * HID, part_c.shape[0] - 2 * HID, False)

    def spread_actor(k):
        if coded:
            mine = ex_ac.all_w.at[e]
        else:
            quarter = part_a.shape[0] // 4
            mine = sum_a.at[pl.ds(pl.multiple_of(e * quarter, 8), quarter)]
        return remote(mine, mine, ef_s.at[k - 1], ef_r.at[k - 1], dev(g, lax.rem(e + k, 4)))

    def spread_scale(k):
        mine = ex_ac.all_s.at[e]
        return remote(mine, mine, ef_s.at[2 + k], ef_r.at[2 + k], dev(g, lax.rem(e + k, 4)))

    def spread_start():
        for k in range(1, 4):
            spread_actor(k).start()
            if coded:
                spread_scale(k).start()

    lane = lax.broadcasted_iota(jnp.int32, (1, HID), 1)
    rid32 = lax.broadcasted_iota(jnp.int32, (32, 1), 0)

    def local(src, dst, k):
        return pltpu.make_async_copy(src, dst, sem_out.at[k])

    def own_outputs():
        return (
            local(small_out, out_small, 0), local(high_out, out_high, 1), local(rest_out, out_rest, 2), local(low_out, out_low, 5),
        )

    def far_outputs():
        return local(small_in, out_small, 0), local(high_in, out_high, 1), local(rest_in, out_rest, 2), local(low_in, out_low, 5)

    @pl.when(online)
    def _():
        slope_sum.last()
        total = slope_sum.whole() * (1.0 / critics)
        d_sample = -valid * total
        d_logp = ALPHA * valid
        sample = pi_act[...]
        th = heads[0:8, :]
        spread_e = heads[8:16, :]
        dz = (d_sample * (1.0 - sample * sample) + d_logp * 2.0 * sample) * ok8
        dls = (dz * spread_e - d_logp) * (3.5 * (1.0 - th * th)) * ok8
        heads[24:40, :] = jnp.zeros((16, rows), F32)
        heads[24:30, :] = dz[0:ACT]
        heads[30:36, :] = dls[0:ACT]
        actor_sum = jnp.sum(valid * (ALPHA * heads[16:17, :] - total[6:7]), axis=1, keepdims=True)
        done_rows = jnp.sum(valid, axis=1, keepdims=True)
        count = counts[0].astype(F32) if fold else 0.0
        for acc in (acc_c1, acc_c0, acc_cx, acc_o):
            acc[...] = jnp.zeros_like(acc)
        one16 = (lax.broadcasted_iota(jnp.int32, (16, block), 0) == 0).astype(BF16)
        if fold:
            ah1x[HID : HID + 16, :] = h1x[HID : HID + 16, :]
            ah2x[HID : HID + 16, :] = h1x[HID : HID + 16, :]

        def body_c(i, _):
            sl = pl.ds(pl.multiple_of(i * block, block), block)
            if fold:
                tall1, tall2, top = ah1x[:, sl], ah2x[:, sl], ah3[:, sl]
                slopes = [as1[:, sl], as2[:, sl], as3[:, sl]]
            else:
                kept = actor_layers(x_b[:, sl])
                tall1, tall2 = (jnp.concatenate([kept[k][0], one16], 0) for k in range(2))
                top = kept[2][0]
                slopes = [(1.0 + t) + h * (1.0 - t) for _, h, t in kept]
            do = heads[24:40, sl].astype(BF16)
            acc_o[0:16, :] += dot_t(do, top)
            d3 = (dot(aot[...], jnp.concatenate([do, do], 0)) * (0.5 * slopes[2])).astype(BF16)
            acc_c1[...] += dot_t(tall2, d3)
            d2 = (halves(dot(ab1[...], d3)) * slopes[1]).astype(BF16)
            acc_c0[...] += dot_t(tall1, d2)
            d1 = (halves(dot(ab0[...], d2)) * slopes[0]).astype(BF16)
            acc_cx[...] += dot_t(x_b[0:32, sl], d1)
            acc_o[16:32, 0:128] += dot_t(one16, jnp.concatenate([do, jnp.zeros((112, block), BF16)], 0))
            return 0

        lax.fori_loop(0, blocks, body_c, 0)
        part_a[0:HID, :] = acc_c0[0:HID, :]
        part_a[HID : 2 * HID, :] = acc_c1[0:HID, :]
        stats = jnp.where(lane == 0, actor_sum, jnp.where(lane == 1, count, jnp.where(lane == 2, done_rows, 0.0)))
        small = acc_cx[...]
        small = small + jnp.where(rid32 == 18, acc_c0[HID : HID + 1, :], 0.0)
        small = small + jnp.where(rid32 == 19, acc_c1[HID : HID + 1, :], 0.0)
        small = small + jnp.where(rid32 == 20, acc_o[16:17, :], 0.0)
        small = small + jnp.where(rid32 == 21, stats, 0.0)
        part_a[2 * HID : 2 * HID + 32, :] = small
        part_a[2 * HID + 32 : 2 * HID + 48, :] = acc_o[0:16, :]
        rest = part_a.shape[0] - 2 * HID - 48
        part_a[2 * HID + 48 :, :] = jnp.zeros((rest, HID), F32)
        for ex in actor:
            ex.start()

    @pl.when(targetd)
    def _():
        least_in[0] = least[:, 0:rows]
        for k in range(1, 4):
            least_target(k).wait_recv()

    @pl.when(online)
    def _():
        for k in range(4):
            least_online(k).wait_recv()

    rid16 = lax.broadcasted_iota(jnp.int32, (16, 1), 0)

    def directions(sl, spread):
        code = eps_s[7:8, sl]
        valid = jnp.where(code > 1.5, 1.0, 0.0)
        low = jnp.minimum(
            jnp.minimum(least_in[0, :, sl], least_in[1, :, sl]), jnp.minimum(least_in[2, :, sl], least_in[3, :, sl])
        )
        target = eps_s[6:7, sl] + GAMMA * (1.0 + 2.0 * valid - code) * low
        unit = unit_f[0:8, sl]
        inv = unit_f[8:9, sl]
        d_unit = (2.0 * ETA / (critics - 1)) * valid * (spread - unit)
        along = jnp.sum(d_unit * unit, axis=0, keepdims=True)
        dg = (d_unit - unit * along) * inv
        gap = value[:, sl] - target
        dv = 2.0 * valid * gap
        row_sums[0:1, sl] = valid * gap * gap
        row_sums[1:2, sl] = valid * jnp.sum(unit * (spread - unit), axis=0, keepdims=True)
        row_sums[2:3, sl] = dv
        dvh[:, sl] = 0.5 * dv
        dgb = dg.astype(BF16)
        dg_b[:, sl] = jnp.concatenate([dgb, dgb], 0)
        dv_b[:, sl] = jnp.where(rid16 == 0, dv, jnp.where(rid16 == 1, 1.0, 0.0)).astype(BF16)

    if not fold:
        unit_sum.last()
        directions(slice(0, rows), unit_sum.whole())

    for acc in (acc_h1, acc_h1t, acc_h0, acc_h0t, acc_x, acc_t, acc_last):
        acc[...] = jnp.zeros_like(acc)

    def body_b1(i, _):
        sl = pl.ds(pl.multiple_of(i * block, block), block)
        if fold:
            @pl.when(i == 0)
            def _():
                unit_sum.back_of(0)

            @pl.when(i == 1)
            def _():
                unit_sum.last_of(1)
                unit_sum.back_of(1)

            directions(sl, u_total[i])
        tp = dot(t1w[...], dg_b[:, sl])
        k1[:, sl] = (k1[:, sl].astype(F32) * tp).astype(BF16)
        th1 = (s1[:, sl].astype(F32) * tp).astype(BF16)
        tp = halves(dot(f0[...], th1))
        k2[:, sl] = (k2[:, sl].astype(F32) * tp).astype(BF16)
        th2 = (s2[:, sl].astype(F32) * tp).astype(BF16)
        tp = halves(dot(f1[...], th2))
        th3 = (s3[:, sl].astype(F32) * tp).astype(BF16)
        d3 = d3s[:, sl]
        ap3 = (dvh[:, sl] * d3.astype(F32) + k3[:, sl].astype(F32) * tp).astype(BF16)
        k3[:, sl] = ap3
        rows_dv = dv_b[:, sl]
        last = dot_t(rows_dv, h3s[:, sl])
        lone = dot_t(rows_dv, th3)
        acc_last[...] += last[0:8] + jnp.where(rid == 0, lone[1:2], 0.0)
        h3s[:, sl] = th1
        acc_h1[...] += dot_t(h2x[:, sl], ap3)
        acc_h1t[...] += dot_t(th2, d3)
        return 0

    def body_b2(i, _):
        sl = pl.ds(pl.multiple_of(i * block, block), block)
        ah = halves(dot(b1[...], k3[:, sl]))
        ap2 = (s2[:, sl].astype(F32) * ah + k2[:, sl].astype(F32)).astype(BF16)
        k2[:, sl] = ap2
        acc_h0[...] += dot_t(h1x[:, sl], ap2)
        acc_h0t[...] += dot_t(h3s[:, sl], d2s[:, sl])
        return 0

    def body_b3(i, _):
        sl = pl.ds(pl.multiple_of(i * block, block), block)
        ah = halves(dot(b0[...], k2[:, sl]))
        ap1 = (s1[:, sl].astype(F32) * ah + k1[:, sl].astype(F32)).astype(BF16)
        acc_x[...] += dot_t(x_b[0:32, sl], ap1)
        acc_t[...] += dot_t(dg_b[:, sl], d1s[:, sl])
        return 0

    lax.fori_loop(0, blocks, body_b1, 0)
    part_c[HID : 2 * HID, :] = acc_h1[0:HID, :] + 0.5 * acc_h1t[...]
    ex_h1.start()

    @pl.when(online)
    def _():
        for ex in actor:
            ex.reduce(False)

    lax.fori_loop(0, blocks, body_b2, 0)
    part_c[0:HID, :] = acc_h0[0:HID, :] + 0.5 * acc_h0t[...]
    ex_h0.start()
    ex_h1.reduce()

    @pl.when(targetd)
    def _():
        for ex in actor:
            ex.detour()

    lax.fori_loop(0, blocks, body_b3, 0)
    errors, diverse, dv_sum = (jnp.sum(row_sums[k : k + 1, :], axis=1, keepdims=True) for k in range(3))
    stats = jnp.where(lane == 0, errors, jnp.where(lane == 1, diverse, 0.0))
    small = acc_x[...]
    small = small + jnp.where(rid32 == 18, acc_h0[HID : HID + 1, :], 0.0)
    small = small + jnp.where(rid32 == 19, acc_h1[HID : HID + 1, :], 0.0)
    small = small + jnp.where(rid32 == 20, stats, 0.0)
    small = small + jnp.where(rid32 == 22, jnp.where(lane == 0, dv_sum, 0.0), 0.0)
    small = small + jnp.where(rid32 == 23, acc_last[0:1, :], 0.0)
    part_c[2 * HID : 2 * HID + 24, :] = small[0:24]
    part_c[2 * HID + 24 : 2 * HID + 32, :] = small[24:32] + 0.5 * acc_t[0:8, :]
    rest = part_c.shape[0] - 2 * HID - 32
    if rest:
        part_c[2 * HID + 32 :, :] = jnp.zeros((rest, HID), F32)
    ex_sm.start()
    ex_h1.forward()
    ex_h0.reduce()
    ex_sm.reduce()

    @pl.when(targetd)
    def _():
        for ex in actor:
            ex.forward()
        spread_start()

    ex_h0.forward()
    ex_sm.forward()

    @pl.when(online)
    def _():
        for ex in actor:
            ex.back()
        spread_start()


    @pl.when(online)
    def _():
        for copy in own_outputs():
            copy.start()

    @pl.when(targetd)
    def _():
        param_copy(3).wait_recv()
        param_copy(4).wait_recv()
        for copy in far_outputs():
            copy.start()

    for k in range(1, 4):
        spread_actor(k).wait_recv()
        if coded:
            spread_scale(k).wait_recv()
    if coded:
        ex_ac.decode()
    copy_a = local(sum_a, out_a, 3)
    copy_a.start()
    for ex in (ex_h1, ex_h0, ex_sm):
        ex.arrived()
    if coded:
        ex_h1.decode()
        ex_h0.decode()
    copy_c = local(sum_c, out_c, 4)
    copy_c.start()

    @pl.when(online)
    def _():
        for what in range(5):
            param_copy(what).wait_send()

    @pl.when(targetd)
    def _():
        for k in range(1, 4):
            least_target(k).wait_send()
        for k in range(4):
            least_online(k).wait_send()

    if fold:
        @pl.when(upper)
        def _():
            for what in range(2):
                fold_copy(what, 0).wait_send()

        @pl.when(lower)
        def _():
            for what in range(2):
                fold_copy(what, 1).wait_send()

        @pl.when(jnp.logical_and(upper, targetd))
        def _():
            least_copy().wait_send()

    unit_sum.sent()

    @pl.when(online)
    def _():
        slope_sum.sent()

    for ex in actor:
        ex.sent_detour()
    for k in range(1, 4):
        spread_actor(k).wait_send()
        if coded:
            spread_scale(k).wait_send()
    for ex in (ex_h1, ex_h0, ex_sm):
        ex.sent()
    copy_a.wait()
    copy_c.wait()

    @pl.when(online)
    def _():
        for copy in own_outputs():
            copy.wait()

    @pl.when(targetd)
    def _():
        for copy in far_outputs():
            copy.wait()


def sizes(n_dp):
    return 2 * HID + up(CRITIC_SMALL, 8 * n_dp), up(2 * HID + ACTOR_SMALL, 32 * n_dp)


def fused(n_dp, rows, block, fold, data, own, aparams):
    v = pltpu.VMEM
    big = lambda n=HID: v((n, rows), BF16)
    dma = pltpu.SemaphoreType.DMA
    size_c, size_a = sizes(n_dp)
    coded = 2 * HID % (64 * n_dp) == 0
    h8 = lambda *n: v((*n, 8, rows // 2), F32)
    sums = [h8(2), h8(), h8(), h8(3), h8(2)]
    extra = (data[0].shape[1] - rows) // 2 if fold else LANES
    moved = [v((2, 32, extra), BF16), v((2, 8, extra), F32)]
    size = data[0].shape[1]
    kept = (lambda n, t: v((n, rows), t)) if fold else (lambda n, t: v((16, LANES), t))
    scratch = [
        v((32, size), F32), v((32, size), F32), v((8, size), F32), *moved, *moved,
        v((96, rows), BF16), v((8, rows), F32),
        v((128, HID), F32), v((HID, 128), F32), v((2, HID, 128), F32), v((HID, 128), F32),
        v((64, HID), F32), v((64, HID), F32), *[v((2 * HID, HID), BF16) for _ in range(6)],
        v((HID, 96), BF16), v((512, HID), BF16), v((512, HID), BF16), v((512, HID), BF16), v((512, HID), BF16),
        v((16, HID), BF16), v((HID, 16), BF16), v((16, HID), BF16),
        v((2, HID, 96), BF16), v((2, HID, 128), F32), v((2, 16, HID), BF16), v((2, 16, HID), BF16),
        v((2, 2, HID, HID), BF16), v((2, 2, HID, HID), BF16),
        v((2, HID, 96), BF16), v((2, 512, HID), BF16), v((2, 512, HID), BF16), v((2, 16, HID), BF16),
        v((HID, 96), BF16), v((512, HID), BF16), v((512, HID), BF16), v((512, HID), BF16), v((512, HID), BF16),
        v((32, HID), BF16), v((HID, 32), BF16),
        big(272), big(272), big(), big(), big(), big(), big(), big(), big(), big(), big(), big(),
        v((40, rows), F32), kept(272, BF16), kept(272, BF16), kept(HID, BF16), kept(HID, F32), kept(HID, F32), kept(HID, F32),
        v((1, rows), F32), v((24, rows), F32), *sums,
        v((16, rows), BF16), v((16, rows), BF16), v((1, rows), F32), v((8, rows), F32),
        *sums,
        v((1, size), F32), v((1, 2 * extra), F32), v((4, 1, rows), F32),
        v((272, HID), F32), v((HID, HID), F32), v((272, HID), F32), v((HID, HID), F32),
        v((32, HID), F32), v((16, HID), F32), v((8, HID), F32), v((32, HID), F32),
        v((272, HID), F32), v((272, HID), F32), v((32, HID), F32),
        v((size_c, HID), F32), v((size_a, HID), F32), v((2, size_c, HID), F32), v((size_a, HID), F32),
        *[v((1, 8, HID) if coded else (n_dp - 1, HID // n_dp, HID), F32) for _ in range(2)],
        v((n_dp - 1, (size_c - 2 * HID) // n_dp, HID), F32),
        v((n_dp - 1, (ACTOR_SMALL if coded else size_a // 4) // n_dp, HID), F32),
        dma((2, 2)), dma((2, 2)), dma, dma, dma((5,)), dma((5,)), dma((8,)), dma((4,)), dma((2, 5)), dma((2, 5)),
        dma((5, n_dp - 1, 2)), dma((5, n_dp - 1, 2)), dma((5, n_dp - 1, 2)), dma((5, n_dp - 1, 2)), dma((5, n_dp, 2)), dma((5, n_dp, 2)),
        dma((6,)), dma((6,)), dma((6,)),
    ]
    if coded:
        for each, lead in ((HID // n_dp, 2), (HID // n_dp, 2), (2 * HID // (4 * n_dp), 4)):
            word, scale = (each // 2, HID), (1, HID)
            for outer in ((n_dp,), (n_dp - 1,), (lead, n_dp)):
                scratch += [v((*outer, *word), jnp.int32), v((*outer, *scale), F32)]
    spec = pl.BlockSpec(memory_space=pltpu.VMEM)
    anyspace = pl.BlockSpec(memory_space=pl.ANY)
    shape = lambda *s: jax.ShapeDtypeStruct(s, F32)
    return pl.pallas_call(
        functools.partial(kernel, n_dp, rows, block, fold),
        out_shape=(
            shape(2, size_c, HID), shape(size_a, HID), shape(64, HID), *[jax.ShapeDtypeStruct((2 * HID, HID), BF16)] * 3,
        ),
        in_specs=[spec] * 5 + [pl.BlockSpec(memory_space=pltpu.SMEM)] + [spec] * 7,
        out_specs=(anyspace,) * 6,
        scratch_shapes=scratch,
        compiler_params=pltpu.CompilerParams(collective_id=0 if fold else 1, has_side_effects=True, vmem_limit_bytes=63 * 2**20),
        name="edac_gradients" if fold else "edac_rest",
    )(*data, *own, *aparams)


def adamw(param, grad, first, second):
    first_new = BETA_ONE * first + (1.0 - BETA_ONE) * grad
    second_new = BETA_TWO * second + (1.0 - BETA_TWO) * grad * grad
    ratio = first_new / (1.0 - BETA_ONE**STEP) / (jnp.sqrt(second_new / (1.0 - BETA_TWO**STEP)) + EPS)
    return (param - LEARN * (ratio + DECAY * param), first_new, second_new)


def update_kernel(*refs):
    n_in, n_out = 24, 20
    src, dst = refs[:n_in], refs[n_in : n_in + n_out]
    rest = refs[n_in + n_out :]
    buf, res = rest[:n_in], rest[n_in : n_in + n_out]
    ge, gb, gae, gab, sem_in, sem_out = rest[n_in + n_out :]
    gc, ga, own_e, own_h, own_b, on_s, on_high, on_rest, low_h, em, ev, hm, hv, bm, bv, ae, ah, ab, aem, aev, ahm, ahv, abm, abv = buf
    o_e, o_h, o_b, o_em, o_ev, o_hm, o_hv, o_bm, o_bv, o_ae, o_ah, o_ab, o_aem, o_aev, o_ahm, o_ahv, o_abm, o_abv, o_ms, o_as = res
    online = lax.axis_index("grp") == 1
    index = {id(b): k for k, b in enumerate(buf)}
    out_index = {id(r): k for k, r in enumerate(res)}

    def read(b, slot=0, at=lambda r: r):
        k = index[id(b)]
        return pltpu.make_async_copy(at(src[k]), at(b), sem_in.at[k, slot])

    def write(r, slot=0, at=lambda x: x):
        k = out_index[id(r)]
        return pltpu.make_async_copy(at(r), at(dst[k]), sem_out.at[k, slot])

    def matrix(m, k):
        rows = slice(k * HID, (k + 1) * HID)
        par = [read(low_h, k, lambda r: r.at[rows])] if m == 0 else [
            read(on_high, k, lambda r: r.at[rows]), read(on_rest, k, lambda r: r.at[rows])
        ]
        mine = [read(b, 2 * m + k, lambda r: r.at[m, k]) for b in (own_h, hm, hv)]
        return [read(gc, 2 * m + k, lambda r: r.at[1 - m, rows])] + par + mine

    def actor_matrix(k):
        rows = slice(k * HID, (k + 1) * HID)
        return [read(ga, k, lambda r: r.at[rows])] + [read(b, k, lambda r: r.at[k]) for b in (ah, ahm, ahv)]

    stats = read(ga, 2, lambda r: r.at[2 * HID : 2 * HID + ACTOR_SMALL])
    small_reads = [read(gc, 4, lambda r: r.at[:, 2 * HID :]), stats] + [
        read(b) for b in (own_e, own_b, on_s, em, ev, bm, bv, ae, ab, aem, aev, abm, abv)
    ]
    order = [(0, 0), (0, 1), (1, 0), (1, 1)]
    stats.start()
    for copy in matrix(*order[0]):
        copy.start()
    for copy in small_reads:
        if copy is not stats:
            copy.start()
    for at in order[1:]:
        for copy in matrix(*at):
            copy.start()
    for k in range(2):
        for copy in actor_matrix(k):
            copy.start()

    gas = ga.at[2 * HID : 2 * HID + ACTOR_SMALL]
    stats.wait()
    scale = 1.0 / gas[21:22, 1:2]
    writes = []

    def put(copy):
        copy.start()
        writes.append(copy)

    def critic(own, param, grad, first, second):
        master, m_new, v_new = adamw(jnp.where(online, own, param), grad, first, second)
        polyak = TAU * master.astype(BF16).astype(F32) + (1.0 - TAU) * own
        return jnp.where(online, master, polyak), m_new, v_new

    def do_matrix(m, k):
        for copy in matrix(m, k):
            copy.wait()
        rows = slice(k * HID, (k + 1) * HID)
        param = low_h[rows, :].astype(F32) if m == 0 else on_high[rows, :].astype(F32) + on_rest[rows, :].astype(F32)
        o_h[m, k], o_hm[m, k], o_hv[m, k] = critic(own_h[m, k], param, gc[1 - m, rows, :] * scale, hm[m, k], hv[m, k])
        for r in (o_h, o_hm, o_hv):
            put(write(r, 2 * m + k, lambda x: x.at[m, k]))

    do_matrix(0, 0)
    for copy in small_reads:
        if copy is not stats:
            copy.wait()
    for m in range(2):
        small = gc.at[1 - m, 2 * HID : 2 * HID + 32]
        ge[0:OBS, :] = small[0:OBS, :]
        ge[OBS : OBS + ACT, :] = small[24 : 24 + ACT, :]
        ge[23:24, :] = small[23:24, :]
        gb[0:3, :] = small[17:20, :]
        gb[3:4, :] = small[22:23, :]
        first = 32 * (1 - m)
        o_e[m], o_em[m], o_ev[m] = critic(own_e[m], on_s[first : first + 24], ge[...] * scale, em[m], ev[m])
        o_b[m], o_bm[m], o_bv[m] = critic(own_b[m], on_s[first + 24 : first + 28], gb[...] * scale, bm[m], bv[m])
        o_ms[m : m + 1, :] = small[20:21, 0:2]
    gae[0:OBS, :] = gas[0:OBS, :]
    gae[OBS : OBS + 2 * ACT, :] = gas[32 : 32 + 2 * ACT, :]
    gab[0:3, :] = gas[17:20, :]
    gab[3:4, :] = gas[20:21, :]
    o_ae[...], o_aem[...], o_aev[...] = adamw(ae[...], gae[...] * scale, aem[...], aev[...])
    o_ab[...], o_abm[...], o_abv[...] = adamw(ab[...], gab[...] * scale, abm[...], abv[...])
    o_as[...] = gas[21:22, 0:2]
    for r in (o_e, o_b, o_em, o_ev, o_bm, o_bv, o_ae, o_ab, o_aem, o_aev, o_abm, o_abv, o_ms, o_as):
        put(write(r))
    for at in order[1:]:
        do_matrix(*at)
    for k in range(2):
        for copy in actor_matrix(k):
            copy.wait()
        grad = ga[k * HID : (k + 1) * HID, :] * scale
        o_ah[k], o_ahm[k], o_ahv[k] = adamw(ah[k], grad, ahm[k], ahv[k])
        for r in (o_ah, o_ahm, o_ahv):
            put(write(r, k, lambda x: x.at[k]))
    for copy in writes:
        copy.wait()


def update(grads, own, online, moments, aparams, amoments):
    shape = lambda *s: jax.ShapeDtypeStruct(s, F32)
    e_, h_, b_ = shape(2, 24, HID), shape(2, 2, HID, HID), shape(2, 4, HID)
    ae_, ah_, ab_ = shape(29, HID), shape(2, HID, HID), shape(4, HID)
    outs = (e_, h_, b_, e_, e_, h_, h_, b_, b_, ae_, ah_, ab_, ae_, ae_, ah_, ah_, ab_, ab_, shape(2, 2), shape(1, 2))
    args = (*grads, *own, *online, *moments, *aparams, *amoments)
    anyspace = pl.BlockSpec(memory_space=pl.ANY)
    room = [pltpu.VMEM(a.shape, a.dtype) for a in args]
    return pl.pallas_call(
        update_kernel,
        out_shape=outs,
        in_specs=[anyspace] * len(args),
        out_specs=(anyspace,) * len(outs),
        scratch_shapes=room
        + [pltpu.VMEM(o.shape, o.dtype) for o in outs]
        + [pltpu.VMEM((24, HID), F32), pltpu.VMEM((4, HID), F32), pltpu.VMEM((29, HID), F32), pltpu.VMEM((4, HID), F32)]
        + [pltpu.SemaphoreType.DMA((len(args), 5)), pltpu.SemaphoreType.DMA((len(outs), 4))],
        compiler_params=pltpu.CompilerParams(vmem_limit_bytes=40 * 2**20),
        name="adamw",
    )(*args)


def body(
    n_dp,
    states, actions, rewards, done, noise, counts,
    crit_edge, crit_hidden, crit_bias, edge_m, edge_v, hidden_m, hidden_v, bias_m, bias_v,
    act_edge, act_hidden, act_bias, act_edge_m, act_edge_v, act_hidden_m, act_hidden_v, act_bias_m, act_bias_v,
):
    size = states.shape[0]
    own = (crit_edge[0], crit_hidden[0], crit_bias[0])
    aparams = (act_edge, act_hidden, act_bias)
    data = (states.T, actions.T, noise.T, rewards[None], done[None], counts)
    moments = (edge_m, edge_v, hidden_m, hidden_v, bias_m, bias_v)
    amoments = (act_edge_m, act_edge_v, act_hidden_m, act_hidden_v, act_bias_m, act_bias_v)
    rows = FOLD_ROWS if size > FOLD_ROWS else size
    grad_c, grad_a, *online = fused(n_dp, rows, rows // 2, True, (*data, rewards[None]), own, aparams)

    def finish(grad_c, grad_a):
        return update((grad_c, grad_a), own, online, moments, aparams, amoments)

    def with_rest():
        z = lax.axis_index("dp")
        partner = lax.ppermute(counts, "dp", [(k, n_dp - 1 - k) for k in range(n_dp)])
        at = jnp.arange(size, dtype=jnp.int32)
        taken = (rows // LANES - 1 - (at - rows) // LANES) * LANES >= (jnp.minimum(partner, rows) + LANES - 1) // LANES * LANES
        taken = jnp.where(z >= n_dp - n_dp // 2, taken, False)
        left = jnp.logical_and(jnp.logical_and(at >= rows, at < counts), jnp.logical_not(taken))
        more_c, more_a, *_ = fused(n_dp, size, size // 16, False, (*data, left.astype(F32)[None]), own, aparams)
        return finish(grad_c + more_c, grad_a + more_a)

    sums = grad_a[2 * HID + 21]
    out = lax.cond(sums[1] != sums[2], with_rest, lambda: finish(grad_c, grad_a))
    return (*(o[None] for o in out[:3]), *out[3:19], out[19][0])


def solution(mesh):
    member = P("grp", "ens", None, None)
    hidden = P("grp", "ens", None, None, None)
    mom = P("ens", None, None)
    mom_h = P("ens", None, None, None)
    return jax.shard_map(
        functools.partial(body, mesh.shape["dp"]),
        mesh=mesh,
        in_specs=(
            P("dp", None), P("dp", None), P("dp"), P("dp"), P("dp", None), P("dp"),
            member, hidden, member, mom, mom, mom_h, mom_h, mom, mom,
        ) + (P(),) * 9,
        out_specs=(member, hidden, member, mom, mom, mom_h, mom_h, mom, mom) + (P(),) * 9 + (P("ens", None), P()),
        check_vma=False,
    )
```

```python
import functools

import jax
import jax.numpy as jnp
from jax import lax
from jax.experimental import pallas as pl
from jax.experimental.pallas import tpu as pltpu
from jax.sharding import PartitionSpec as P

OBS = 17
ACT = 6
HID = 256
STEP = 5
FOLD_ROWS = 2816
LANES = 128

GAMMA = 0.99
ALPHA = 0.2
ETA = 1.0
LEARN = 0.03
BETA_ONE = 0.5
BETA_TWO = 0.5
DECAY = 0.01
EPS = 1e-08
TAU = 0.05
HALF_LOG_TWO_PI = 0.9189385332046727
LOG_TWO = 0.6931471805599453

F32 = jnp.float32
BF16 = jnp.bfloat16

CRITIC_SMALL, ACTOR_SMALL = 32, 32


def dot(a, b):
    return lax.dot_general(a, b, (((1,), (0,)), ((), ())), preferred_element_type=F32)


def dot_t(a, b):
    return lax.dot_general(a, b, (((1,), (1,)), ((), ())), preferred_element_type=F32)


def split(w):
    high = w.astype(BF16).astype(F32)
    return high, w - high


def halves(p):
    n = p.shape[0] // 2
    return p[:n] + p[n:]


def prep_input(stage, w1, edge, bias, n_in):
    stage[...] = jnp.zeros_like(stage)
    stage[0:OBS, :] = edge[0:OBS, :]
    stage[OBS : OBS + 1, :] = bias[0:1, :]
    if n_in > OBS:
        stage[24 : 24 + ACT, :] = edge[OBS : OBS + ACT, :]
    high, low = split(0.5 * stage[0:32, :])
    w1[...] = jnp.concatenate([high, low, high], 0).T.astype(BF16)


def prep_hidden(fwd, bwd, hidden):
    w = 0.5 * hidden
    if fwd is not None:
        high, low = split(w.T)
        fwd[...] = jnp.concatenate([high, low], 0).astype(BF16)
    if bwd is not None:
        high, low = split(w)
        bwd[...] = jnp.concatenate([high, low], 0).astype(BF16)


def silu_half(u):
    t = jnp.tanh(u)
    return u + u * t, t


def up(n, by):
    return -(-n // by) * by


def kernel(
    n_dp,
    rows,
    block,
    fold,
    states, actions, noise, rewards, done, counts, mask, c_edge, c_hidden, c_bias, a_edge, a_hidden, a_bias,
    out_c, out_a, out_small, out_high, out_rest, out_low,
    xs, ns, eps_s, far_x, far_e, here_x, here_e, x_b, pi_act, stage, vec, tvec, avec,
    small_out, small_in, high_out, high_in, rest_out, rest_in, low_out, low_in,
    w1, f0, f1, b0, b1, ga, t1w, eq, pw, pv, pq, pg, pf, pb,
    tw1, tf0, tf1, teq,
    aw1, af0, af1, ab0, ab1, ao, aot,
    h1x, h2x, h3s, s1, s2, s3, k1, k2, k3, d1s, d2s, d3s,
    heads, ah1x, ah2x, ah3, as1, as2, as3,
    value, unit_f, u_mine, u_peer, u_pair, u_far, u_total, dg_b, dv_b, dvh, row_sums,
    q_mine, q_peer, q_pair, q_far, q_total, least, far_least, least_in,
    acc_h1, acc_h1t, acc_h0, acc_h0t, acc_x, acc_t, acc_last, acc_o, acc_c1, acc_c0, acc_cx, actor_rows,
    part_c, part_a, sum_c, sum_a, in_h1, in_h0, in_sm, in_ac,
    fold_s, fold_r, sem_far_s, sem_far_r, sem_param_s, sem_param_r, sem_least_s, sem_least_r, es_s, es_r,
    rs_s, rs_r, ag_s, ag_r, xf_s, xf_r, ef_s, ef_r, sem_out, *boxes,
):
    g = lax.axis_index("grp")
    e = lax.axis_index("ens")
    z = lax.axis_index("dp")
    me = g * 4 + e
    blocks = rows // block
    extra = states.shape[1] - rows
    lower = z < n_dp // 2
    upper = z >= n_dp - n_dp // 2
    half = rows // 2
    online = g == 1
    targetd = g == 0
    critics = 8
    coded = bool(boxes)

    def dev(gg, ee):
        return {"grp": gg, "ens": ee}

    def remote(src, dst, send, recv, where):
        return pltpu.make_async_remote_copy(
            src_ref=src, dst_ref=dst, send_sem=send, recv_sem=recv, device_id=where, device_id_type=pl.DeviceIdType.MESH
        )

    barrier = pltpu.get_barrier_semaphore()
    for k in range(1, 8):
        p = lax.rem(me + k, 8)
        pl.semaphore_signal(barrier, inc=1, device_id=dev(p // 4, lax.rem(p, 4)), device_id_type=pl.DeviceIdType.MESH)
    for k in range(1, n_dp):
        pl.semaphore_signal(barrier, inc=1, device_id={"dp": lax.rem(z + k, n_dp)}, device_id_type=pl.DeviceIdType.MESH)

    def all_here():
        pl.semaphore_wait(barrier, 7 + n_dp - 1)

    def param_copy(what):
        src, dst = (
            (small_out.at[0:32], small_in.at[0:32]),
            (high_out, high_in),
            (rest_out, rest_in),
            (low_out, low_in),
            (small_out.at[32:64], small_in.at[32:64]),
        )[what]
        return remote(src, dst, sem_param_s.at[what], sem_param_r.at[what], dev(0, e))

    @pl.when(online)
    def _():
        small_out[...] = jnp.zeros_like(small_out)
        for k in range(2):
            small_out[32 * k : 32 * k + 24, :] = c_edge[1 - k]
            small_out[32 * k + 24 : 32 * k + 28, :] = c_bias[1 - k]
            high, low = split(c_hidden[1, k])
            high_out[k * HID : (k + 1) * HID, :] = high.astype(BF16)
            rest_out[k * HID : (k + 1) * HID, :] = low.astype(BF16)
            low_out[k * HID : (k + 1) * HID, :] = c_hidden[0, k].astype(BF16)
        all_here()
        for what in range(3):
            param_copy(what).start()

    lane_id = lax.broadcasted_iota(jnp.int32, (1, states.shape[1]), 1)
    if fold:
        code = jnp.where(lane_id < counts[0], 2.0, 0.0) + done[...].astype(F32)
    else:
        code = 2.0 * mask[...] + done[...].astype(F32)

    ones_row = jnp.ones((1, states.shape[1]), F32)
    xs[...] = jnp.zeros_like(xs)
    xs[0:OBS, :] = states[0:OBS, :]
    xs[OBS : OBS + 1, :] = ones_row
    xs[24 : 24 + ACT, :] = actions[...]
    eps_s[6:7, :] = rewards[...]
    eps_s[7:8, :] = code

    @pl.when(online)
    def _():
        eps_s[0:ACT, :] = noise[0:ACT, :]

    @pl.when(targetd)
    def _():
        eps_s[0:ACT, :] = noise[ACT : 2 * ACT, :]
        ns[...] = jnp.zeros_like(ns)
        ns[0:OBS, :] = states[OBS : 2 * OBS, :]
        ns[OBS : OBS + 1, :] = ones_row

    core = lax.rem(e, 2)
    other_core = e + 1 - 2 * core
    far_chip = lax.rem(e + 2, 4)

    def fold_copy(what, hop):
        here, there = ((here_e, far_e), (here_x, far_x))[what]
        if hop == 0:
            return remote(here.at[core], there.at[core], fold_s.at[what, 0], fold_r.at[what, 0], {"dp": n_dp - 1 - z})
        return remote(there.at[core], there.at[core], fold_s.at[what, 1], fold_r.at[what, 1], dev(g, other_core))

    def least_copy():
        return remote(least.at[:, rows:], far_least, sem_far_s, sem_far_r, {"dp": n_dp - 1 - z})

    def merge(into, blocks_of):
        first = rows - extra
        there = jnp.concatenate([blocks_of(b) for b in range(extra // LANES - 1, -1, -1)], 1).astype(F32)
        lanes = lax.broadcasted_iota(jnp.int32, (1, extra), 1) + first
        bound = (jnp.minimum(counts[0], rows) + LANES - 1) // LANES * LANES
        into[:, first:rows] = jnp.where(lanes < bound, into[:, first:rows], there)

    def in_halves(pieces):
        per = extra // LANES // 2
        return lambda b: pieces[b // per, :, (b % per) * LANES : (b % per + 1) * LANES]

    def fold_out():
        if fold:
            @pl.when(upper)
            def _():
                for h in range(2):
                    part = slice(rows + h * extra // 2, rows + (h + 1) * extra // 2)
                    here_e[h] = eps_s[:, part]
                    here_x[h] = xs[:, part].astype(BF16)
                for what in range(2):
                    fold_copy(what, 0).start()

    def fold_in():
        if fold:
            @pl.when(lower)
            def _():
                for what in range(2):
                    fold_copy(what, 0).wait_recv()
                    fold_copy(what, 1).start()
                for what in range(2):
                    fold_copy(what, 1).wait_recv()
                merge(eps_s, in_halves(far_e))
                merge(xs, in_halves(far_x))

    def put_x():
        high, low = split(xs[:, 0:rows])
        xin = high.astype(BF16)
        x_b[0:32, :] = xin
        x_b[32:64, :] = xin
        x_b[64:96, :] = low.astype(BF16)

    def prep_small(edge, bias, w1_, vec_, eq_, ga_, t1_):
        prep_input(stage, w1_, edge, bias, OBS + ACT)
        stage[...] = jnp.zeros_like(stage)
        stage[0:1, :] = 0.5 * bias[1:2, :]
        stage[1:2, :] = 0.5 * bias[2:3, :]
        stage[2:3, :] = edge[23:24, :]
        vec_[...] = stage[...].T
        vec_[0:1, 8:9] = bias[3:4, 0:1]
        stage[...] = jnp.zeros_like(stage)
        high, low = split(edge[23:24, :])
        stage[0:1, :] = high
        stage[1:2, :] = low
        eq_[...] = stage[0:16, :].astype(BF16)
        if ga_ is not None:
            stage[...] = jnp.zeros_like(stage)
            stage[0:ACT, :] = 0.5 * edge[OBS : OBS + ACT, :]
            high, low = split(stage[0:8, :])
            both = jnp.concatenate([high, low], 0)
            ga_[...] = both.astype(BF16)
            stage[0:16, :] = both
            if t1_ is not None:
                t1_[...] = stage[...].T[:, 0:16].astype(BF16)

    def prep_actor():
        prep_input(stage, aw1, a_edge, a_bias, OBS)
        prep_hidden(af0, ab0, a_hidden[0])
        prep_hidden(af1, ab1, a_hidden[1])
        stage[...] = jnp.zeros_like(stage)
        stage[0:1, :] = 0.5 * a_bias[1:2, :]
        stage[1:2, :] = 0.5 * a_bias[2:3, :]
        stage[2:3, :] = a_bias[3:4, :]
        avec[...] = stage[...].T
        stage[...] = jnp.zeros_like(stage)
        stage[0:ACT, :] = a_edge[OBS : OBS + ACT, :]
        stage[8 : 8 + ACT, :] = a_edge[OBS + ACT : OBS + 2 * ACT, :]
        high, low = split(stage[0:16, :])
        ao[...] = jnp.concatenate([high, low], 0).astype(BF16)
        stage[...] = jnp.zeros_like(stage)
        stage[0 : 2 * ACT, :] = a_edge[OBS : OBS + 2 * ACT, :]
        high, low = split(stage[0:16, :])
        stage[0:32, :] = jnp.concatenate([high, low], 0)
        aot[...] = stage[...].T[:, 0:32].astype(BF16)

    prep_actor()

    def actor_layers(src):
        kept = []
        hb = None
        for w, b in ((aw1, None), (af0, 0), (af1, 1)):
            u = dot(w[...], src) if b is None else halves(dot(w[...], hb)) + avec[:, b : b + 1]
            h, t = silu_half(u)
            hb = h.astype(BF16)
            kept.append((hb, h, t))
        return kept

    ok8 = (lax.broadcasted_iota(jnp.int32, (8, 1), 0) < ACT).astype(F32)

    def actor_heads(hb, sl):
        out = halves(dot(ao[...], hb))
        eps = eps_s[:, sl]
        center = out[0:8] + avec[0:8, 2:3] * ok8
        th = jnp.tanh(out[8:16] + avec[6:14, 2:3] * ok8)
        log_std = 3.5 * th - 1.5
        spread_e = jnp.exp(log_std) * eps
        latent = center + spread_e
        soft = jnp.maximum(-2.0 * latent, 0.0) + jnp.log(1.0 + jnp.exp(-2.0 * jnp.abs(latent)))
        terms = -0.5 * eps * eps - log_std - HALF_LOG_TWO_PI - 2.0 * (LOG_TWO - latent - soft)
        logp = jnp.sum(terms * ok8, axis=0, keepdims=True)
        sample = jnp.tanh(latent) * ok8
        return sample, logp, th, spread_e

    actor_rows[...] = jnp.zeros_like(actor_rows)

    put_x()

    @pl.when(online)
    def _():
        fold_out()
        prep_small(c_edge.at[0], c_bias.at[0], w1, vec, eq, ga, t1w)
        prep_hidden(f0, b0, c_hidden[0, 0])
        prep_hidden(f1, b1, c_hidden[0, 1])
        for k, (fwd, bwd) in enumerate(((f0, b0), (f1, b1))):
            pf[0, k] = fwd[0:HID, :]
            pb[0, k] = bwd[0:HID, :]
            w = 0.5 * c_hidden[1, k]
            pf[1, k] = w.T.astype(BF16)
            pb[1, k] = w.astype(BF16)
        pw[0], pv[0], pq[0], pg[0] = w1[...], vec[...], eq[...], ga[...]
        prep_small(c_edge.at[1], c_bias.at[1], pw.at[1], pv.at[1], pq.at[1], pg.at[1], None)

    def least_online(k):
        return remote(least.at[:, 0:rows], least_in.at[k], sem_least_s.at[4 + k], sem_least_r.at[k], dev(1, lax.rem(e + k, 4)))

    def least_target(k):
        return remote(least.at[:, 0:rows], least_in.at[k], sem_least_s.at[k], sem_least_r.at[k], dev(0, lax.rem(e + k, 4)))

    def half_hidden(part, values):
        to = slice(part * HID, (part + 1) * HID)
        for k, (fwd, bwd) in enumerate(((f0, b0), (f1, b1))):
            w = 0.5 * values[k * HID : (k + 1) * HID, :].astype(F32)
            fwd[to, :] = w.T.astype(BF16)
            bwd[to, :] = w.astype(BF16)

    @pl.when(targetd)
    def _():
        for m in range(2):
            prep_small(c_edge.at[m], c_bias.at[m], tw1.at[m], tvec.at[m], teq.at[m], None, None)
            prep_hidden(tf0.at[m], None, c_hidden[m, 0])
            prep_hidden(tf1.at[m], None, c_hidden[m, 1])

        def body(i, _):
            @pl.when(i == 1)
            def _():
                all_here()
                fold_out()

            first = jnp.minimum(i * block, states.shape[1] - block)
            sl = pl.ds(pl.multiple_of(first, LANES), block)
            high, rest = split(ns[:, sl])
            nx, rest = high.astype(BF16), rest.astype(BF16)
            kept = actor_layers(jnp.concatenate([nx, nx, rest], 0))
            sample, logp, th, spread_e = actor_heads(kept[2][0], sl)
            high, rest = split(jnp.concatenate([ns[0:24, sl], sample], 0))
            nx = high.astype(BF16)
            nx = jnp.concatenate([nx, nx, rest.astype(BF16)], 0)
            low = None
            for m in range(2):
                h, t = silu_half(dot(tw1[m], nx))
                h, t = silu_half(halves(dot(tf0[m], h.astype(BF16))) + tvec[m, :, 0:1])
                h, t = silu_half(halves(dot(tf1[m], h.astype(BF16))) + tvec[m, :, 1:2])
                r = dot(teq[m], h.astype(BF16))
                q = r[0:1] + r[1:2] + tvec[m, 0:1, 8:9]
                low = q if low is None else jnp.minimum(low, q)
            least[:, sl] = low - ALPHA * logp
            return 0

        lax.fori_loop(0, blocks + (jnp.where(upper, 1, 0) if fold else 0), body, 0)
        if fold:
            @pl.when(upper)
            def _():
                least_copy().start()

        fold_in()
        if fold:
            put_x()
        param_copy(0).wait_recv()
        prep_small(small_in.at[0:24], small_in.at[24:32], w1, vec, eq, ga, t1w)
        param_copy(1).wait_recv()
        half_hidden(0, high_in)
        param_copy(2).wait_recv()
        half_hidden(1, rest_in)

    def least_out():
        @pl.when(targetd)
        def _():
            if fold:
                @pl.when(lower)
                def _():
                    least_copy().wait_recv()
                    merge(least, lambda b: far_least[:, b * LANES : (b + 1) * LANES])

            for k in range(1, 4):
                least_target(k).start()
            for k in range(4):
                least_online(k).start()

    class EnsembleSum:
        def __init__(self, index, mine, peer, pair, far, total, only_online):
            self.index, self.mine, self.peer, self.pair, self.far, self.total = index, mine, peer, pair, far, total
            self.chips = (1,) if only_online else (0, 1, 2)

        def to_core(self):
            return remote(self.mine.at[1 - core], self.peer, es_s.at[self.index, 0], es_r.at[self.index, 0], dev(g, other_core))

        def to_chip(self, k):
            across = (1 - g, g, 1 - g)[k]
            where = dev(across, (e, far_chip, far_chip)[k])
            return remote(self.pair, self.far.at[k], es_s.at[self.index, 1 + k], es_r.at[self.index, 1 + k], where)

        def back(self):
            return remote(self.total.at[core], self.total.at[core], es_s.at[self.index, 4], es_r.at[self.index, 4], dev(g, other_core))

        def begin(self, first, second):
            self.mine[0] = first
            self.mine[1] = second
            self.to_core().start()

        def middle(self):
            self.to_core().wait_recv()
            self.pair[...] = self.mine[core] + self.peer[...]
            for k in self.chips:
                self.to_chip(k).start()

        def first_to_core(self, h, values):
            self.mine[h] = values

            @pl.when(core != h)
            def _():
                self.to_core().start()

            @pl.when(core == h)
            def _():
                self.middle()

        def last_of(self, h):
            @pl.when(core == h)
            def _():
                self.last()

        def back_of(self, h):
            @pl.when(core != h)
            def _():
                self.back().wait_recv()

        def last(self):
            total = self.pair[...]
            for k in self.chips:
                self.to_chip(k).wait_recv()
                total = total + self.far[k]
            self.total[core] = total
            self.back().start()

        def whole(self):
            self.back().wait_recv()
            return jnp.concatenate([self.total[0], self.total[1]], 1)

        def sent(self):
            self.to_core().wait_send()
            for k in self.chips:
                self.to_chip(k).wait_send()
            self.back().wait_send()

    unit_sum = EnsembleSum(0, u_mine, u_peer, u_pair, u_far, u_total, False)
    slope_sum = EnsembleSum(1, q_mine, q_peer, q_pair, q_far, q_total, True)

    rid = lax.broadcasted_iota(jnp.int32, (8, 1), 0)

    @pl.when(online)
    def _():
        def body_p(i, _):
            sl = pl.ds(pl.multiple_of(i * block, block), block)

            @pl.when(i == 1)
            def _():
                fold_in()
                if fold:
                    put_x()

            kept = actor_layers(x_b[:, sl])
            if fold:
                for store, curve, (hb, h, t) in zip((ah1x, ah2x, ah3), (as1, as2, as3), kept):
                    store[0:HID, sl] = hb
                    curve[:, sl] = (1.0 + t) + h * (1.0 - t)
            sample, logp, th, spread_e = actor_heads(kept[2][0], sl)
            pi_act[:, sl] = sample
            heads[0:8, sl] = th
            heads[8:16, sl] = spread_e
            heads[16:17, sl] = logp
            pin = jnp.concatenate([xs[0:24, sl], sample], 0).astype(BF16)
            unit_f[16:24, sl] = jnp.zeros((8, block), F32)

            def member(m, _):
                def act(u):
                    h, t = silu_half(u)
                    hb, tb = h.astype(BF16), t.astype(BF16)
                    one = jnp.ones((), BF16)
                    return hb, (one + tb) + hb * (one - tb)

                h, a1 = act(dot(pw[m][:, 0:64], jnp.concatenate([pin, pin], 0)))
                h, a2 = act(dot(pf[m, 0], h) + pv[m][:, 0:1])
                h, a3 = act(dot(pf[m, 1], h) + pv[m][:, 1:2])
                r = dot(pq[m], h)
                q = r[0:1] + r[1:2] + pv[m][0:1, 8:9]
                d = pv[m][:, 2:3].astype(BF16) * a3
                d = dot(pb[m, 1], d).astype(BF16) * a2
                d = dot(pb[m, 0], d).astype(BF16) * a1
                unit_f[16:24, sl] += halves(dot(pg[m], d)) + jnp.where(rid == 6, q, 0.0)
                return 0

            lax.fori_loop(0, 2, member, 0)
            return 0

        lax.fori_loop(0, blocks, body_p, 0)
        slope_sum.begin(unit_f[16:24, 0:half], unit_f[16:24, half:rows])

    ones = (lax.broadcasted_iota(jnp.int32, (16, rows), 0) == 0).astype(BF16)
    h1x[HID : HID + 16, :] = ones
    h2x[HID : HID + 16, :] = ones

    def curves(u):
        h, t = silu_half(u)
        c = 1.0 + t
        d = 1.0 - t
        return h, c + h * d, (c * d) * (1.0 - u * t)

    valid = jnp.where(eps_s[7:8, 0:rows] > 1.5, 1.0, 0.0)

    def body_a(i, _):
        @pl.when(i == 1)
        def _():
            @pl.when(online)
            def _():
                slope_sum.middle()

            if fold:
                unit_sum.first_to_core(0, unit_f[0:8, 0:half])
            least_out()

        sl = pl.ds(pl.multiple_of(i * block, block), block)
        h, a1, q1 = curves(dot(w1[...], x_b[:, sl]))
        hb = h.astype(BF16)
        h1x[0:HID, sl] = hb
        s1[:, sl] = a1.astype(BF16)
        h, a2, q2 = curves(halves(dot(f0[...], hb)) + vec[:, 0:1])
        hb = h.astype(BF16)
        h2x[0:HID, sl] = hb
        s2[:, sl] = a2.astype(BF16)
        h, a3, q3 = curves(halves(dot(f1[...], hb)) + vec[:, 1:2])
        hb = h.astype(BF16)
        h3s[:, sl] = hb
        s3[:, sl] = a3.astype(BF16)
        r = dot(eq[...], hb)
        value[:, sl] = r[0:1] + r[1:2] + vec[0:1, 8:9]
        last = vec[:, 2:3]
        db = (last * a3).astype(BF16)
        d3s[:, sl] = db
        k3[:, sl] = (last * q3).astype(BF16)
        m = halves(dot(b1[...], db))
        db = (m * a2).astype(BF16)
        d2s[:, sl] = db
        k2[:, sl] = (m * q2).astype(BF16)
        m = halves(dot(b0[...], db))
        db = (m * a1).astype(BF16)
        d1s[:, sl] = db
        k1[:, sl] = (m * q1).astype(BF16)
        slope = halves(dot(ga[...], db))
        inv = lax.rsqrt(jnp.sum(slope * slope, axis=0, keepdims=True) + 0.01)
        unit_f[0:8, sl] = slope * inv
        unit_f[8:9, sl] = inv
        return 0

    lax.fori_loop(0, blocks, body_a, 0)
    if fold:
        unit_sum.first_to_core(1, unit_f[0:8, half:rows])
        unit_sum.last_of(0)
    else:
        unit_sum.begin(unit_f[0:8, 0:half], unit_f[0:8, half:rows])
        unit_sum.middle()

    @pl.when(online)
    def _():
        for what in (3, 4):
            param_copy(what).start()


    class Exchange:
        def __init__(self, index, part, into, inbox, base, count, wide):
            self.index, self.part, self.into, self.inbox, self.base, self.count, self.wide = index, part, into, inbox, base, count, wide
            self.each = count // (n_dp * (4 if wide else 1))

        def rows_of(self, shard):
            first = self.base + (e * n_dp + shard if self.wide else shard) * self.each
            return pl.ds(pl.multiple_of(first, 8), self.each)

        def scatter(self, k):
            to = lax.rem(z + k, n_dp)
            return remote(
                self.part.at[self.rows_of(to)], self.inbox.at[k - 1], rs_s.at[self.index, k - 1, 0], rs_r.at[self.index, k - 1, 0], {"dp": to}
            )

        def gather(self, k):
            mine = self.into.at[self.rows_of(z)]
            return remote(mine, mine, ag_s.at[self.index, k - 1, 0], ag_r.at[self.index, k - 1, 0], {"dp": lax.rem(z + k, n_dp)})

        def across(self, k):
            there = self.into.at[self.rows_of(lax.rem(z + n_dp - k, n_dp))]
            return remote(there, there, xf_s.at[self.index, k, 0], xf_r.at[self.index, k, 0], dev(1 - g, e))

        def start(self):
            for k in range(1, n_dp):
                self.scatter(k).start()

        def reduce(self, along=True):
            total = self.part[self.rows_of(z), :]
            for k in range(1, n_dp):
                self.scatter(k).wait_recv()
                total = total + self.inbox[k - 1]
            self.into[self.rows_of(z), :] = total
            if along:
                for k in range(1, n_dp):
                    self.gather(k).start()
            self.across(0).start()

        def forward(self):
            for k in range(1, n_dp):
                self.gather(k).wait_recv()
                self.across(k).start()

        def sent(self):
            for k in range(1, n_dp):
                self.scatter(k).wait_send()
                self.gather(k).wait_send()
            for k in range(n_dp):
                self.across(k).wait_send()

        def arrived(self):
            for k in range(n_dp):
                self.across(k).wait_recv()

        def detour(self):
            self.across(0).wait_recv()
            for k in range(1, n_dp):
                self.gather(k).start()

        def back(self):
            for k in range(1, n_dp):
                self.across(k).wait_recv()

        def sent_detour(self):
            @pl.when(online)
            def _():
                for k in range(1, n_dp):
                    self.scatter(k).wait_send()
                self.across(0).wait_send()

            @pl.when(targetd)
            def _():
                for k in range(1, n_dp):
                    self.gather(k).wait_send()
                    self.across(k).wait_send()

    class Coded(Exchange):
        def __init__(self, index, part, out, base, count, lead, wide, boxes):
            self.index, self.part, self.out, self.base, self.count, self.lead, self.wide = index, part, out, base, count, lead, wide
            self.out_w, self.out_s, self.in_w, self.in_s, self.all_w, self.all_s = boxes
            self.each = count // (n_dp * (4 if wide else 1))

        def pack(self, x):
            top = jnp.maximum(jnp.max(jnp.abs(x), axis=0, keepdims=True), 1e-30)
            q = jnp.round(x * (32767.0 / top)).astype(jnp.int32)
            h = self.each // 2
            return jnp.bitwise_or(jnp.bitwise_and(q[:h], 65535), jnp.left_shift(q[h:], 16)), top * (1.0 / 32767.0)

        def unpack(self, w, scale):
            low = jnp.right_shift(jnp.left_shift(w, 16), 16)
            high = jnp.right_shift(w, 16)
            return jnp.concatenate([low, high], 0).astype(F32) * scale

        def scatter(self, k):
            to = lax.rem(z + k, n_dp)
            return Both([
                remote(o.at[to], i.at[k - 1], rs_s.at[self.index, k - 1, q], rs_r.at[self.index, k - 1, q], {"dp": to})
                for q, (o, i) in enumerate(((self.out_w, self.in_w), (self.out_s, self.in_s)))
            ])

        def gather(self, k):
            return Both([
                remote(
                    a.at[self.lead, z], a.at[self.lead, z], ag_s.at[self.index, k - 1, q], ag_r.at[self.index, k - 1, q],
                    {"dp": lax.rem(z + k, n_dp)},
                )
                for q, a in enumerate((self.all_w, self.all_s))
            ])

        def across(self, k):
            there = lax.rem(z + n_dp - k, n_dp)
            return Both([
                remote(
                    a.at[self.lead, there], a.at[self.lead, there], xf_s.at[self.index, k, q], xf_r.at[self.index, k, q], dev(1 - g, e)
                )
                for q, a in enumerate((self.all_w, self.all_s))
            ])

        def start(self):
            for shard in range(n_dp):
                w, scale = self.pack(self.part[self.rows_of(shard), :])
                self.out_w[shard] = w
                self.out_s[shard] = scale
            for k in range(1, n_dp):
                self.scatter(k).start()

        def reduce(self, along=True):
            total = self.part[self.rows_of(z), :]
            for k in range(1, n_dp):
                self.scatter(k).wait_recv()
                total = total + self.unpack(self.in_w[k - 1], self.in_s[k - 1])
            w, scale = self.pack(total)
            self.all_w[self.lead, z] = w
            self.all_s[self.lead, z] = scale
            if along:
                for k in range(1, n_dp):
                    self.gather(k).start()
            self.across(0).start()

        def decode(self):
            for lead in range(self.all_w.shape[0]):
                for shard in range(n_dp):
                    x = self.unpack(self.all_w[lead, shard], self.all_s[lead, shard])
                    if self.wide:
                        first = (lead * n_dp + shard) * self.each
                        self.out[first : first + self.each, :] = x
                    else:
                        first = self.base + shard * self.each
                        self.out[lead, first : first + self.each, :] = x

    class Both:
        def __init__(self, copies):
            self.copies = copies

        def start(self):
            for c in self.copies:
                c.start()

        def wait_recv(self):
            for c in self.copies:
                c.wait_recv()

        def wait_send(self):
            for c in self.copies:
                c.wait_send()

    if coded:
        box_h1, box_h0, box_ac = boxes[0:6], boxes[6:12], boxes[12:18]
    if coded:
        ex_h1 = Coded(0, part_c, sum_c, HID, HID, g, False, box_h1)
        ex_h0 = Coded(1, part_c, sum_c, 0, HID, g, False, box_h0)
        ex_ac = Coded(3, part_a, sum_a, 0, 2 * HID, e, True, box_ac)
        ex_as = Exchange(4, part_a, sum_a, in_ac, 2 * HID, ACTOR_SMALL, False)
        actor = (ex_ac, ex_as)
    else:
        ex_h1 = Exchange(0, part_c, sum_c.at[g], in_h1, HID, HID, False)
        ex_h0 = Exchange(1, part_c, sum_c.at[g], in_h0, 0, HID, False)
        ex_ac = Exchange(3, part_a, sum_a, in_ac, 0, part_a.shape[0], True)
        actor = (ex_ac,)
    ex_sm = Exchange(2, part_c, sum_c.at[g], in_sm, 2 * HID, part_c.shape[0] - 2 * HID, False)

    def spread_actor(k):
        if coded:
            mine = ex_ac.all_w.at[e]
        else:
            quarter = part_a.shape[0] // 4
            mine = sum_a.at[pl.ds(pl.multiple_of(e * quarter, 8), quarter)]
        return remote(mine, mine, ef_s.at[k - 1], ef_r.at[k - 1], dev(g, lax.rem(e + k, 4)))

    def spread_scale(k):
        mine = ex_ac.all_s.at[e]
        return remote(mine, mine, ef_s.at[2 + k], ef_r.at[2 + k], dev(g, lax.rem(e + k, 4)))

    def spread_start():
        for k in range(1, 4):
            spread_actor(k).start()
            if coded:
                spread_scale(k).start()

    lane = lax.broadcasted_iota(jnp.int32, (1, HID), 1)
    rid32 = lax.broadcasted_iota(jnp.int32, (32, 1), 0)

    def local(src, dst, k):
        return pltpu.make_async_copy(src, dst, sem_out.at[k])

    def own_outputs():
        return (
            local(small_out, out_small, 0), local(high_out, out_high, 1), local(rest_out, out_rest, 2), local(low_out, out_low, 5),
        )

    def far_outputs():
        return local(small_in, out_small, 0), local(high_in, out_high, 1), local(rest_in, out_rest, 2), local(low_in, out_low, 5)

    @pl.when(online)
    def _():
        slope_sum.last()
        total = slope_sum.whole() * (1.0 / critics)
        d_sample = -valid * total
        d_logp = ALPHA * valid
        sample = pi_act[...]
        th = heads[0:8, :]
        spread_e = heads[8:16, :]
        dz = (d_sample * (1.0 - sample * sample) + d_logp * 2.0 * sample) * ok8
        dls = (dz * spread_e - d_logp) * (3.5 * (1.0 - th * th)) * ok8
        heads[24:40, :] = jnp.zeros((16, rows), F32)
        heads[24:30, :] = dz[0:ACT]
        heads[30:36, :] = dls[0:ACT]
        actor_sum = jnp.sum(valid * (ALPHA * heads[16:17, :] - total[6:7]), axis=1, keepdims=True)
        done_rows = jnp.sum(valid, axis=1, keepdims=True)
        count = counts[0].astype(F32) if fold else 0.0
        for acc in (acc_c1, acc_c0, acc_cx, acc_o):
            acc[...] = jnp.zeros_like(acc)
        one16 = (lax.broadcasted_iota(jnp.int32, (16, block), 0) == 0).astype(BF16)
        if fold:
            ah1x[HID : HID + 16, :] = h1x[HID : HID + 16, :]
            ah2x[HID : HID + 16, :] = h1x[HID : HID + 16, :]

        def body_c(i, _):
            sl = pl.ds(pl.multiple_of(i * block, block), block)
            if fold:
                tall1, tall2, top = ah1x[:, sl], ah2x[:, sl], ah3[:, sl]
                slopes = [as1[:, sl], as2[:, sl], as3[:, sl]]
            else:
                kept = actor_layers(x_b[:, sl])
                tall1, tall2 = (jnp.concatenate([kept[k][0], one16], 0) for k in range(2))
                top = kept[2][0]
                slopes = [(1.0 + t) + h * (1.0 - t) for _, h, t in kept]
            do = heads[24:40, sl].astype(BF16)
            acc_o[0:16, :] += dot_t(do, top)
            d3 = (dot(aot[...], jnp.concatenate([do, do], 0)) * (0.5 * slopes[2])).astype(BF16)
            acc_c1[...] += dot_t(tall2, d3)
            d2 = (halves(dot(ab1[...], d3)) * slopes[1]).astype(BF16)
            acc_c0[...] += dot_t(tall1, d2)
            d1 = (halves(dot(ab0[...], d2)) * slopes[0]).astype(BF16)
            acc_cx[...] += dot_t(x_b[0:32, sl], d1)
            acc_o[16:32, 0:128] += dot_t(one16, jnp.concatenate([do, jnp.zeros((112, block), BF16)], 0))
            return 0

        lax.fori_loop(0, blocks, body_c, 0)
        part_a[0:HID, :] = acc_c0[0:HID, :]
        part_a[HID : 2 * HID, :] = acc_c1[0:HID, :]
        actor_rows[0:1, :] = jnp.where(lane == 0, actor_sum, jnp.where(lane == 1, count, jnp.where(lane == 2, done_rows, 0.0)))
        actor_rows[1:2, :] = acc_o[16:17, :]
        first = 2 * HID
        part_a[first : first + 18, :] = acc_cx[0:18, :]
        part_a[first + 18 : first + 19, :] = acc_c0[HID : HID + 1, :]
        part_a[first + 19 : first + 20, :] = acc_c1[HID : HID + 1, :]
        part_a[first + 20 : first + 32, :] = acc_o[0 : 2 * ACT, :]
        part_a[first + 32 :, :] = jnp.zeros((part_a.shape[0] - first - 32, HID), F32)
        for ex in actor:
            ex.start()

    @pl.when(targetd)
    def _():
        least_in[0] = least[:, 0:rows]
        for k in range(1, 4):
            least_target(k).wait_recv()

    @pl.when(online)
    def _():
        for k in range(4):
            least_online(k).wait_recv()

    rid16 = lax.broadcasted_iota(jnp.int32, (16, 1), 0)

    def directions(sl, spread):
        code = eps_s[7:8, sl]
        valid = jnp.where(code > 1.5, 1.0, 0.0)
        low = jnp.minimum(
            jnp.minimum(least_in[0, :, sl], least_in[1, :, sl]), jnp.minimum(least_in[2, :, sl], least_in[3, :, sl])
        )
        target = eps_s[6:7, sl] + GAMMA * (1.0 + 2.0 * valid - code) * low
        unit = unit_f[0:8, sl]
        inv = unit_f[8:9, sl]
        d_unit = (2.0 * ETA / (critics - 1)) * valid * (spread - unit)
        along = jnp.sum(d_unit * unit, axis=0, keepdims=True)
        dg = (d_unit - unit * along) * inv
        gap = value[:, sl] - target
        dv = 2.0 * valid * gap
        row_sums[0:1, sl] = valid * gap * gap
        row_sums[1:2, sl] = valid * jnp.sum(unit * (spread - unit), axis=0, keepdims=True)
        row_sums[2:3, sl] = dv
        dvh[:, sl] = 0.5 * dv
        dgb = dg.astype(BF16)
        dg_b[:, sl] = jnp.concatenate([dgb, dgb], 0)
        dv_b[:, sl] = jnp.where(rid16 == 0, dv, jnp.where(rid16 == 1, 1.0, 0.0)).astype(BF16)

    if not fold:
        unit_sum.last()
        directions(slice(0, rows), unit_sum.whole())

    for acc in (acc_h1, acc_h1t, acc_h0, acc_h0t, acc_x, acc_t, acc_last):
        acc[...] = jnp.zeros_like(acc)

    def body_b1(i, _):
        sl = pl.ds(pl.multiple_of(i * block, block), block)
        if fold:
            @pl.when(i == 0)
            def _():
                unit_sum.back_of(0)

            @pl.when(i == 1)
            def _():
                unit_sum.last_of(1)
                unit_sum.back_of(1)

            directions(sl, u_total[i])
        tp = dot(t1w[...], dg_b[:, sl])
        k1[:, sl] = (k1[:, sl].astype(F32) * tp).astype(BF16)
        th1 = (s1[:, sl].astype(F32) * tp).astype(BF16)
        tp = halves(dot(f0[...], th1))
        k2[:, sl] = (k2[:, sl].astype(F32) * tp).astype(BF16)
        th2 = (s2[:, sl].astype(F32) * tp).astype(BF16)
        tp = halves(dot(f1[...], th2))
        th3 = (s3[:, sl].astype(F32) * tp).astype(BF16)
        d3 = d3s[:, sl]
        ap3 = (dvh[:, sl] * d3.astype(F32) + k3[:, sl].astype(F32) * tp).astype(BF16)
        k3[:, sl] = ap3
        rows_dv = dv_b[:, sl]
        last = dot_t(rows_dv, h3s[:, sl])
        lone = dot_t(rows_dv, th3)
        acc_last[...] += last[0:8] + jnp.where(rid == 0, lone[1:2], 0.0)
        h3s[:, sl] = th1
        acc_h1[...] += dot_t(h2x[:, sl], ap3)
        acc_h1t[...] += dot_t(th2, d3)
        return 0

    def body_b2(i, _):
        sl = pl.ds(pl.multiple_of(i * block, block), block)
        ah = halves(dot(b1[...], k3[:, sl]))
        ap2 = (s2[:, sl].astype(F32) * ah + k2[:, sl].astype(F32)).astype(BF16)
        k2[:, sl] = ap2
        acc_h0[...] += dot_t(h1x[:, sl], ap2)
        acc_h0t[...] += dot_t(h3s[:, sl], d2s[:, sl])
        return 0

    def body_b3(i, _):
        sl = pl.ds(pl.multiple_of(i * block, block), block)
        ah = halves(dot(b0[...], k2[:, sl]))
        ap1 = (s1[:, sl].astype(F32) * ah + k1[:, sl].astype(F32)).astype(BF16)
        acc_x[...] += dot_t(x_b[0:32, sl], ap1)
        acc_t[...] += dot_t(dg_b[:, sl], d1s[:, sl])
        return 0

    lax.fori_loop(0, blocks, body_b1, 0)
    part_c[HID : 2 * HID, :] = acc_h1[0:HID, :] + 0.5 * acc_h1t[...]
    ex_h1.start()

    @pl.when(online)
    def _():
        for ex in actor:
            ex.reduce(False)

    lax.fori_loop(0, blocks, body_b2, 0)
    part_c[0:HID, :] = acc_h0[0:HID, :] + 0.5 * acc_h0t[...]
    ex_h0.start()
    lax.fori_loop(0, blocks, body_b3, 0)
    errors, diverse, dv_sum = (jnp.sum(row_sums[k : k + 1, :], axis=1, keepdims=True) for k in range(3))
    stats = jnp.where(lane == 0, errors, jnp.where(lane == 1, diverse, 0.0))
    small = acc_x[...]
    small = small + jnp.where(rid32 == 18, acc_h0[HID : HID + 1, :], 0.0)
    small = small + jnp.where(rid32 == 19, acc_h1[HID : HID + 1, :], 0.0)
    small = small + jnp.where(rid32 == 20, stats, 0.0)
    small = small + jnp.where(rid32 == 21, actor_rows[0:1, :], 0.0) + jnp.where(rid32 == 30, actor_rows[1:2, :], 0.0)
    small = small + jnp.where(rid32 == 22, jnp.where(lane == 0, dv_sum, 0.0), 0.0)
    small = small + jnp.where(rid32 == 23, acc_last[0:1, :], 0.0)
    part_c[2 * HID : 2 * HID + 24, :] = small[0:24]
    part_c[2 * HID + 24 : 2 * HID + 32, :] = small[24:32] + 0.5 * acc_t[0:8, :]
    rest = part_c.shape[0] - 2 * HID - 32
    if rest:
        part_c[2 * HID + 32 :, :] = jnp.zeros((rest, HID), F32)
    ex_sm.start()

    @pl.when(targetd)
    def _():
        for ex in actor:
            ex.detour()

    ex_h1.reduce()
    ex_h0.reduce()
    ex_sm.reduce()
    ex_h1.forward()

    @pl.when(targetd)
    def _():
        for ex in actor:
            ex.forward()
        spread_start()

    ex_h0.forward()
    ex_sm.forward()

    @pl.when(online)
    def _():
        for ex in actor:
            ex.back()
        spread_start()


    @pl.when(online)
    def _():
        for copy in own_outputs():
            copy.start()

    @pl.when(targetd)
    def _():
        param_copy(3).wait_recv()
        param_copy(4).wait_recv()
        for copy in far_outputs():
            copy.start()

    def out_rows(first, last, k):
        return local(sum_c.at[:, first:last], out_c.at[:, first:last], k)

    copies = [out_rows(HID, 2 * HID, 4), local(sum_a, out_a, 3), out_rows(2 * HID, sum_c.shape[1], 6), out_rows(0, HID, 7)]
    ex_h1.arrived()
    if coded:
        ex_h1.decode()
    copies[0].start()
    for k in range(1, 4):
        spread_actor(k).wait_recv()
        if coded:
            spread_scale(k).wait_recv()
    if coded:
        ex_ac.decode()
    copies[1].start()
    ex_sm.arrived()
    copies[2].start()
    ex_h0.arrived()
    if coded:
        ex_h0.decode()
    copies[3].start()

    @pl.when(online)
    def _():
        for what in range(5):
            param_copy(what).wait_send()

    @pl.when(targetd)
    def _():
        for k in range(1, 4):
            least_target(k).wait_send()
        for k in range(4):
            least_online(k).wait_send()

    if fold:
        @pl.when(upper)
        def _():
            for what in range(2):
                fold_copy(what, 0).wait_send()

        @pl.when(lower)
        def _():
            for what in range(2):
                fold_copy(what, 1).wait_send()

        @pl.when(jnp.logical_and(upper, targetd))
        def _():
            least_copy().wait_send()

    unit_sum.sent()

    @pl.when(online)
    def _():
        slope_sum.sent()

    for ex in actor:
        ex.sent_detour()
    for k in range(1, 4):
        spread_actor(k).wait_send()
        if coded:
            spread_scale(k).wait_send()
    for ex in (ex_h1, ex_h0, ex_sm):
        ex.sent()
    for copy in copies:
        copy.wait()

    @pl.when(online)
    def _():
        for copy in own_outputs():
            copy.wait()

    @pl.when(targetd)
    def _():
        for copy in far_outputs():
            copy.wait()


def sizes(n_dp):
    return 2 * HID + up(CRITIC_SMALL, 8 * n_dp), up(2 * HID + ACTOR_SMALL, 32 * n_dp)


def fused(n_dp, rows, block, fold, data, own, aparams):
    v = pltpu.VMEM
    big = lambda n=HID: v((n, rows), BF16)
    dma = pltpu.SemaphoreType.DMA
    size_c, size_a = sizes(n_dp)
    coded = 2 * HID % (64 * n_dp) == 0
    h8 = lambda *n: v((*n, 8, rows // 2), F32)
    sums = [h8(2), h8(), h8(), h8(3), h8(2)]
    extra = (data[0].shape[1] - rows) // 2 if fold else LANES
    moved = [v((2, 32, extra), BF16), v((2, 8, extra), F32)]
    size = data[0].shape[1]
    kept = (lambda n, t: v((n, rows), t)) if fold else (lambda n, t: v((16, LANES), t))
    scratch = [
        v((32, size), F32), v((32, size), F32), v((8, size), F32), *moved, *moved,
        v((96, rows), BF16), v((8, rows), F32),
        v((128, HID), F32), v((HID, 128), F32), v((2, HID, 128), F32), v((HID, 128), F32),
        v((64, HID), F32), v((64, HID), F32), *[v((2 * HID, HID), BF16) for _ in range(6)],
        v((HID, 96), BF16), v((512, HID), BF16), v((512, HID), BF16), v((512, HID), BF16), v((512, HID), BF16),
        v((16, HID), BF16), v((HID, 16), BF16), v((16, HID), BF16),
        v((2, HID, 96), BF16), v((2, HID, 128), F32), v((2, 16, HID), BF16), v((2, 16, HID), BF16),
        v((2, 2, HID, HID), BF16), v((2, 2, HID, HID), BF16),
        v((2, HID, 96), BF16), v((2, 512, HID), BF16), v((2, 512, HID), BF16), v((2, 16, HID), BF16),
        v((HID, 96), BF16), v((512, HID), BF16), v((512, HID), BF16), v((512, HID), BF16), v((512, HID), BF16),
        v((32, HID), BF16), v((HID, 32), BF16),
        big(272), big(272), big(), big(), big(), big(), big(), big(), big(), big(), big(), big(),
        v((40, rows), F32), kept(272, BF16), kept(272, BF16), kept(HID, BF16), kept(HID, F32), kept(HID, F32), kept(HID, F32),
        v((1, rows), F32), v((24, rows), F32), *sums,
        v((16, rows), BF16), v((16, rows), BF16), v((1, rows), F32), v((8, rows), F32),
        *sums,
        v((1, size), F32), v((1, 2 * extra), F32), v((4, 1, rows), F32),
        v((272, HID), F32), v((HID, HID), F32), v((272, HID), F32), v((HID, HID), F32),
        v((32, HID), F32), v((16, HID), F32), v((8, HID), F32), v((32, HID), F32),
        v((272, HID), F32), v((272, HID), F32), v((32, HID), F32), v((8, HID), F32),
        v((size_c, HID), F32), v((size_a, HID), F32), v((2, size_c, HID), F32), v((size_a, HID), F32),
        *[v((1, 8, HID) if coded else (n_dp - 1, HID // n_dp, HID), F32) for _ in range(2)],
        v((n_dp - 1, (size_c - 2 * HID) // n_dp, HID), F32),
        v((n_dp - 1, (ACTOR_SMALL if coded else size_a // 4) // n_dp, HID), F32),
        dma((2, 2)), dma((2, 2)), dma, dma, dma((5,)), dma((5,)), dma((8,)), dma((4,)), dma((2, 5)), dma((2, 5)),
        dma((5, n_dp - 1, 2)), dma((5, n_dp - 1, 2)), dma((5, n_dp - 1, 2)), dma((5, n_dp - 1, 2)), dma((5, n_dp, 2)), dma((5, n_dp, 2)),
        dma((6,)), dma((6,)), dma((8,)),
    ]
    if coded:
        for each, lead in ((HID // n_dp, 2), (HID // n_dp, 2), (2 * HID // (4 * n_dp), 4)):
            word, scale = (each // 2, HID), (1, HID)
            for outer in ((n_dp,), (n_dp - 1,), (lead, n_dp)):
                scratch += [v((*outer, *word), jnp.int32), v((*outer, *scale), F32)]
    spec = pl.BlockSpec(memory_space=pltpu.VMEM)
    anyspace = pl.BlockSpec(memory_space=pl.ANY)
    shape = lambda *s: jax.ShapeDtypeStruct(s, F32)
    return pl.pallas_call(
        functools.partial(kernel, n_dp, rows, block, fold),
        out_shape=(
            shape(2, size_c, HID), shape(size_a, HID), shape(64, HID), *[jax.ShapeDtypeStruct((2 * HID, HID), BF16)] * 3,
        ),
        in_specs=[spec] * 5 + [pl.BlockSpec(memory_space=pltpu.SMEM)] + [spec] * 7,
        out_specs=(anyspace,) * 6,
        scratch_shapes=scratch,
        compiler_params=pltpu.CompilerParams(collective_id=0 if fold else 1, has_side_effects=True, vmem_limit_bytes=63 * 2**20),
        name="edac_gradients" if fold else "edac_rest",
    )(*data, *own, *aparams)


def adamw(param, grad, first, second):
    first_new = BETA_ONE * first + (1.0 - BETA_ONE) * grad
    second_new = BETA_TWO * second + (1.0 - BETA_TWO) * grad * grad
    scaled = second_new * (1.0 / (1.0 - BETA_TWO**STEP))
    root = scaled * lax.rsqrt(jnp.maximum(scaled, 1e-30)) + EPS
    inverse = pl.reciprocal(root, approx=True)
    inverse = inverse * (2.0 - root * inverse)
    ratio = first_new * (1.0 / (1.0 - BETA_ONE**STEP)) * inverse
    return (param - LEARN * (ratio + DECAY * param), first_new, second_new)


def update_kernel(*refs):
    n_in, n_out = 24, 20
    src, dst = refs[:n_in], refs[n_in : n_in + n_out]
    rest = refs[n_in + n_out :]
    buf, res = rest[:n_in], rest[n_in : n_in + n_out]
    ge, gb, gae, gab, sem_in, sem_out = rest[n_in + n_out :]
    gc, ga, own_e, own_h, own_b, on_s, on_high, on_rest, low_h, em, ev, hm, hv, bm, bv, ae, ah, ab, aem, aev, ahm, ahv, abm, abv = buf
    o_e, o_h, o_b, o_em, o_ev, o_hm, o_hv, o_bm, o_bv, o_ae, o_ah, o_ab, o_aem, o_aev, o_ahm, o_ahv, o_abm, o_abv, o_ms, o_as = res
    online = lax.axis_index("grp") == 1
    index = {id(b): k for k, b in enumerate(buf)}
    out_index = {id(r): k for k, r in enumerate(res)}

    def read(b, slot=0, at=lambda r: r):
        k = index[id(b)]
        return pltpu.make_async_copy(at(src[k]), at(b), sem_in.at[k, slot])

    def write(r, slot=0, at=lambda x: x):
        k = out_index[id(r)]
        return pltpu.make_async_copy(at(r), at(dst[k]), sem_out.at[k, slot])

    def matrix(m, k):
        rows = slice(k * HID, (k + 1) * HID)
        par = [read(low_h, k, lambda r: r.at[rows])] if m == 0 else [
            read(on_high, k, lambda r: r.at[rows]), read(on_rest, k, lambda r: r.at[rows])
        ]
        mine = [read(b, 2 * m + k, lambda r: r.at[m, k]) for b in (own_h, hm, hv)]
        return [read(gc, 2 * m + k, lambda r: r.at[1 - m, rows])] + par + mine

    def actor_matrix(k):
        rows = slice(k * HID, (k + 1) * HID)
        return [read(ga, k, lambda r: r.at[rows])] + [read(b, k, lambda r: r.at[k]) for b in (ah, ahm, ahv)]

    stats = read(gc, 4, lambda r: r.at[:, 2 * HID :])
    small_reads = [read(ga, 2, lambda r: r.at[2 * HID : 2 * HID + ACTOR_SMALL]), stats] + [
        read(b) for b in (own_e, own_b, on_s, em, ev, bm, bv, ae, ab, aem, aev, abm, abv)
    ]
    order = [(0, 0), (0, 1), (1, 0), (1, 1)]
    stats.start()
    for copy in matrix(*order[0]):
        copy.start()
    for copy in small_reads:
        if copy is not stats:
            copy.start()
    for at in order[1:]:
        for copy in matrix(*at):
            copy.start()
    for k in range(2):
        for copy in actor_matrix(k):
            copy.start()

    gas = ga.at[2 * HID : 2 * HID + ACTOR_SMALL]
    stats.wait()
    rows_a = gc.at[1, 2 * HID : 2 * HID + 32]
    scale = 1.0 / rows_a[21:22, 1:2]
    writes = []

    def put(copy):
        copy.start()
        writes.append(copy)

    def critic(own, param, grad, first, second):
        master, m_new, v_new = adamw(jnp.where(online, own, param), grad, first, second)
        polyak = TAU * master.astype(BF16).astype(F32) + (1.0 - TAU) * own
        return jnp.where(online, master, polyak), m_new, v_new

    def do_matrix(m, k):
        for copy in matrix(m, k):
            copy.wait()
        rows = slice(k * HID, (k + 1) * HID)
        param = low_h[rows, :].astype(F32) if m == 0 else on_high[rows, :].astype(F32) + on_rest[rows, :].astype(F32)
        o_h[m, k], o_hm[m, k], o_hv[m, k] = critic(own_h[m, k], param, gc[1 - m, rows, :] * scale, hm[m, k], hv[m, k])
        for r in (o_h, o_hm, o_hv):
            put(write(r, 2 * m + k, lambda x: x.at[m, k]))

    do_matrix(0, 0)
    for copy in small_reads:
        if copy is not stats:
            copy.wait()
    for m in range(2):
        small = gc.at[1 - m, 2 * HID : 2 * HID + 32]
        ge[0:OBS, :] = small[0:OBS, :]
        ge[OBS : OBS + ACT, :] = small[24 : 24 + ACT, :]
        ge[23:24, :] = small[23:24, :]
        gb[0:3, :] = small[17:20, :]
        gb[3:4, :] = small[22:23, :]
        first = 32 * (1 - m)
        o_e[m], o_em[m], o_ev[m] = critic(own_e[m], on_s[first : first + 24], ge[...] * scale, em[m], ev[m])
        o_b[m], o_bm[m], o_bv[m] = critic(own_b[m], on_s[first + 24 : first + 28], gb[...] * scale, bm[m], bv[m])
        o_ms[m : m + 1, :] = small[20:21, 0:2]
    gae[0:OBS, :] = gas[0:OBS, :]
    gae[OBS : OBS + 2 * ACT, :] = gas[20 : 20 + 2 * ACT, :]
    gab[0:3, :] = gas[17:20, :]
    gab[3:4, :] = rows_a[30:31, :]
    o_ae[...], o_aem[...], o_aev[...] = adamw(ae[...], gae[...] * scale, aem[...], aev[...])
    o_ab[...], o_abm[...], o_abv[...] = adamw(ab[...], gab[...] * scale, abm[...], abv[...])
    o_as[...] = rows_a[21:22, 0:2]
    for r in (o_e, o_b, o_em, o_ev, o_bm, o_bv, o_ae, o_ab, o_aem, o_aev, o_abm, o_abv, o_ms, o_as):
        put(write(r))
    for at in order[1:]:
        do_matrix(*at)
    for k in range(2):
        for copy in actor_matrix(k):
            copy.wait()
        grad = ga[k * HID : (k + 1) * HID, :] * scale
        o_ah[k], o_ahm[k], o_ahv[k] = adamw(ah[k], grad, ahm[k], ahv[k])
        for r in (o_ah, o_ahm, o_ahv):
            put(write(r, k, lambda x: x.at[k]))
    for copy in writes:
        copy.wait()


def update(grads, own, online, moments, aparams, amoments):
    shape = lambda *s: jax.ShapeDtypeStruct(s, F32)
    e_, h_, b_ = shape(2, 24, HID), shape(2, 2, HID, HID), shape(2, 4, HID)
    ae_, ah_, ab_ = shape(29, HID), shape(2, HID, HID), shape(4, HID)
    outs = (e_, h_, b_, e_, e_, h_, h_, b_, b_, ae_, ah_, ab_, ae_, ae_, ah_, ah_, ab_, ab_, shape(2, 2), shape(1, 2))
    args = (*grads, *own, *online, *moments, *aparams, *amoments)
    anyspace = pl.BlockSpec(memory_space=pl.ANY)
    room = [pltpu.VMEM(a.shape, a.dtype) for a in args]
    return pl.pallas_call(
        update_kernel,
        out_shape=outs,
        in_specs=[anyspace] * len(args),
        out_specs=(anyspace,) * len(outs),
        scratch_shapes=room
        + [pltpu.VMEM(o.shape, o.dtype) for o in outs]
        + [pltpu.VMEM((24, HID), F32), pltpu.VMEM((4, HID), F32), pltpu.VMEM((29, HID), F32), pltpu.VMEM((4, HID), F32)]
        + [pltpu.SemaphoreType.DMA((len(args), 5)), pltpu.SemaphoreType.DMA((len(outs), 4))],
        compiler_params=pltpu.CompilerParams(vmem_limit_bytes=40 * 2**20),
        name="adamw",
    )(*args)


def body(
    n_dp,
    states, actions, rewards, done, noise, counts,
    crit_edge, crit_hidden, crit_bias, edge_m, edge_v, hidden_m, hidden_v, bias_m, bias_v,
    act_edge, act_hidden, act_bias, act_edge_m, act_edge_v, act_hidden_m, act_hidden_v, act_bias_m, act_bias_v,
):
    size = states.shape[0]
    own = (crit_edge[0], crit_hidden[0], crit_bias[0])
    aparams = (act_edge, act_hidden, act_bias)
    data = (states.T, actions.T, noise.T, rewards[None], done[None], counts)
    moments = (edge_m, edge_v, hidden_m, hidden_v, bias_m, bias_v)
    amoments = (act_edge_m, act_edge_v, act_hidden_m, act_hidden_v, act_bias_m, act_bias_v)
    rows = FOLD_ROWS if size > FOLD_ROWS else size
    grad_c, grad_a, *online = fused(n_dp, rows, rows // 2, True, (*data, rewards[None]), own, aparams)

    def finish(grad_c, grad_a):
        return update((grad_c, grad_a), own, online, moments, aparams, amoments)

    def with_rest():
        z = lax.axis_index("dp")
        partner = lax.ppermute(counts, "dp", [(k, n_dp - 1 - k) for k in range(n_dp)])
        at = jnp.arange(size, dtype=jnp.int32)
        taken = (rows // LANES - 1 - (at - rows) // LANES) * LANES >= (jnp.minimum(partner, rows) + LANES - 1) // LANES * LANES
        taken = jnp.where(z >= n_dp - n_dp // 2, taken, False)
        left = jnp.logical_and(jnp.logical_and(at >= rows, at < counts), jnp.logical_not(taken))
        more_c, more_a, *_ = fused(n_dp, size, size // 16, False, (*data, left.astype(F32)[None]), own, aparams)
        return finish(grad_c + more_c, grad_a + more_a)

    sums = grad_c[1, 2 * HID + 21]
    out = lax.cond(sums[1] != sums[2], with_rest, lambda: finish(grad_c, grad_a))
    return (*(o[None] for o in out[:3]), *out[3:19], out[19][0])


def solution(mesh):
    member = P("grp", "ens", None, None)
    hidden = P("grp", "ens", None, None, None)
    mom = P("ens", None, None)
    mom_h = P("ens", None, None, None)
    return jax.shard_map(
        functools.partial(body, mesh.shape["dp"]),
        mesh=mesh,
        in_specs=(
            P("dp", None), P("dp", None), P("dp"), P("dp"), P("dp", None), P("dp"),
            member, hidden, member, mom, mom, mom_h, mom_h, mom, mom,
        ) + (P(),) * 9,
        out_specs=(member, hidden, member, mom, mom, mom_h, mom_h, mom, mom) + (P(),) * 9 + (P("ens", None), P()),
        check_vma=False,
    )
```

```python
import functools

import jax
import jax.numpy as jnp
from jax import lax
from jax.experimental import pallas as pl
from jax.experimental.pallas import tpu as pltpu
from jax.sharding import PartitionSpec as P

OBS = 17
ACT = 6
HID = 256
STEP = 5
FOLD_ROWS = 2816
LANES = 128

GAMMA = 0.99
ALPHA = 0.2
ETA = 1.0
LEARN = 0.03
BETA_ONE = 0.5
BETA_TWO = 0.5
DECAY = 0.01
EPS = 1e-08
TAU = 0.05
HALF_LOG_TWO_PI = 0.9189385332046727
LOG_TWO = 0.6931471805599453

F32 = jnp.float32
BF16 = jnp.bfloat16

CRITIC_SMALL, ACTOR_SMALL = 32, 32


def dot(a, b):
    return lax.dot_general(a, b, (((1,), (0,)), ((), ())), preferred_element_type=F32)


def dot_t(a, b):
    return lax.dot_general(a, b, (((1,), (1,)), ((), ())), preferred_element_type=F32)


def split(w):
    high = w.astype(BF16).astype(F32)
    return high, w - high


def halves(p):
    n = p.shape[0] // 2
    return p[:n] + p[n:]


def prep_input(stage, w1, edge, bias, n_in):
    stage[...] = jnp.zeros_like(stage)
    stage[0:OBS, :] = edge[0:OBS, :]
    stage[OBS : OBS + 1, :] = bias[0:1, :]
    if n_in > OBS:
        stage[24 : 24 + ACT, :] = edge[OBS : OBS + ACT, :]
    high, low = split(0.5 * stage[0:32, :])
    w1[...] = jnp.concatenate([high, low, high], 0).T.astype(BF16)


def prep_hidden(fwd, bwd, hidden):
    w = 0.5 * hidden
    if fwd is not None:
        high, low = split(w.T)
        fwd[...] = jnp.concatenate([high, low], 0).astype(BF16)
    if bwd is not None:
        high, low = split(w)
        bwd[...] = jnp.concatenate([high, low], 0).astype(BF16)


def silu_half(u):
    t = jnp.tanh(u)
    return u + u * t, t


def up(n, by):
    return -(-n // by) * by


def kernel(
    n_dp,
    rows,
    block,
    fold,
    states, actions, noise, rewards, done, counts, mask, c_edge, c_hidden, c_bias, a_edge, a_hidden, a_bias,
    out_c, out_a, out_small, out_high, out_rest, out_low,
    xs, ns, eps_s, far_x, far_e, here_x, here_e, x_b, pi_act, stage, vec, tvec, avec,
    small_out, small_in, high_out, high_in, rest_out, rest_in, low_out, low_in,
    w1, f0, f1, b0, b1, ga, t1w, eq, pw, pv, pq, pg, pf, pb,
    tw1, tf0, tf1, teq,
    aw1, af0, af1, ab0, ab1, ao, aot,
    h1x, h2x, h3s, s1, s2, s3, k1, k2, k3, d1s, d2s, d3s,
    heads, ah1x, ah2x, ah3, as1, as2, as3,
    value, unit_f, u_mine, u_peer, u_pair, u_far, u_total, dg_b, dv_b, dvh, row_sums,
    q_mine, q_peer, q_pair, q_far, q_total, least, far_least, least_in,
    acc_h1, acc_h1t, acc_h0, acc_h0t, acc_x, acc_t, acc_last, acc_o, acc_c1, acc_c0, acc_cx, actor_rows,
    part_c, part_a, sum_c, sum_a, in_h1, in_h0, in_sm, in_ac,
    fold_s, fold_r, sem_far_s, sem_far_r, sem_param_s, sem_param_r, sem_least_s, sem_least_r, es_s, es_r,
    rs_s, rs_r, ag_s, ag_r, xf_s, xf_r, ef_s, ef_r, sem_out, *boxes,
):
    g = lax.axis_index("grp")
    e = lax.axis_index("ens")
    z = lax.axis_index("dp")
    me = g * 4 + e
    blocks = rows // block
    extra = states.shape[1] - rows
    lower = z < n_dp // 2
    upper = z >= n_dp - n_dp // 2
    half = rows // 2
    online = g == 1
    targetd = g == 0
    critics = 8
    coded = bool(boxes)

    def dev(gg, ee):
        return {"grp": gg, "ens": ee}

    def remote(src, dst, send, recv, where):
        return pltpu.make_async_remote_copy(
            src_ref=src, dst_ref=dst, send_sem=send, recv_sem=recv, device_id=where, device_id_type=pl.DeviceIdType.MESH
        )

    barrier = pltpu.get_barrier_semaphore()
    for k in range(1, 8):
        p = lax.rem(me + k, 8)
        pl.semaphore_signal(barrier, inc=1, device_id=dev(p // 4, lax.rem(p, 4)), device_id_type=pl.DeviceIdType.MESH)
    for k in range(1, n_dp):
        pl.semaphore_signal(barrier, inc=1, device_id={"dp": lax.rem(z + k, n_dp)}, device_id_type=pl.DeviceIdType.MESH)

    def all_here():
        pl.semaphore_wait(barrier, 7 + n_dp - 1)

    def param_copy(what):
        src, dst = (
            (small_out.at[0:32], small_in.at[0:32]),
            (high_out, high_in),
            (rest_out, rest_in),
            (low_out, low_in),
            (small_out.at[32:64], small_in.at[32:64]),
        )[what]
        return remote(src, dst, sem_param_s.at[what], sem_param_r.at[what], dev(0, e))

    @pl.when(online)
    def _():
        small_out[...] = jnp.zeros_like(small_out)
        for k in range(2):
            small_out[32 * k : 32 * k + 24, :] = c_edge[1 - k]
            small_out[32 * k + 24 : 32 * k + 28, :] = c_bias[1 - k]
            high, low = split(c_hidden[1, k])
            high_out[k * HID : (k + 1) * HID, :] = high.astype(BF16)
            rest_out[k * HID : (k + 1) * HID, :] = low.astype(BF16)
            low_out[k * HID : (k + 1) * HID, :] = c_hidden[0, k].astype(BF16)
        all_here()
        for what in range(3):
            param_copy(what).start()

    lane_id = lax.broadcasted_iota(jnp.int32, (1, states.shape[1]), 1)
    if fold:
        code = jnp.where(lane_id < counts[0], 2.0, 0.0) + done[...].astype(F32)
    else:
        code = 2.0 * mask[...] + done[...].astype(F32)

    ones_row = jnp.ones((1, states.shape[1]), F32)
    xs[...] = jnp.zeros_like(xs)
    xs[0:OBS, :] = states[0:OBS, :]
    xs[OBS : OBS + 1, :] = ones_row
    xs[24 : 24 + ACT, :] = actions[...]
    eps_s[6:7, :] = rewards[...]
    eps_s[7:8, :] = code

    @pl.when(online)
    def _():
        eps_s[0:ACT, :] = noise[0:ACT, :]

    @pl.when(targetd)
    def _():
        eps_s[0:ACT, :] = noise[ACT : 2 * ACT, :]
        ns[...] = jnp.zeros_like(ns)
        ns[0:OBS, :] = states[OBS : 2 * OBS, :]
        ns[OBS : OBS + 1, :] = ones_row

    core = lax.rem(e, 2)
    other_core = e + 1 - 2 * core
    far_chip = lax.rem(e + 2, 4)

    def fold_copy(what, hop):
        here, there = ((here_e, far_e), (here_x, far_x))[what]
        if hop == 0:
            return remote(here.at[core], there.at[core], fold_s.at[what, 0], fold_r.at[what, 0], {"dp": n_dp - 1 - z})
        return remote(there.at[core], there.at[core], fold_s.at[what, 1], fold_r.at[what, 1], dev(g, other_core))

    def least_copy():
        return remote(least.at[:, rows:], far_least, sem_far_s, sem_far_r, {"dp": n_dp - 1 - z})

    def merge(into, blocks_of):
        first = rows - extra
        there = jnp.concatenate([blocks_of(b) for b in range(extra // LANES - 1, -1, -1)], 1).astype(F32)
        lanes = lax.broadcasted_iota(jnp.int32, (1, extra), 1) + first
        bound = (jnp.minimum(counts[0], rows) + LANES - 1) // LANES * LANES
        into[:, first:rows] = jnp.where(lanes < bound, into[:, first:rows], there)

    def in_halves(pieces):
        per = extra // LANES // 2
        return lambda b: pieces[b // per, :, (b % per) * LANES : (b % per + 1) * LANES]

    def fold_out():
        if fold:
            @pl.when(upper)
            def _():
                for h in range(2):
                    part = slice(rows + h * extra // 2, rows + (h + 1) * extra // 2)
                    here_e[h] = eps_s[:, part]
                    here_x[h] = xs[:, part].astype(BF16)
                for what in range(2):
                    fold_copy(what, 0).start()

    def fold_in():
        if fold:
            @pl.when(lower)
            def _():
                for what in range(2):
                    fold_copy(what, 0).wait_recv()
                    fold_copy(what, 1).start()
                for what in range(2):
                    fold_copy(what, 1).wait_recv()
                merge(eps_s, in_halves(far_e))
                merge(xs, in_halves(far_x))

    def put_x():
        high, low = split(xs[:, 0:rows])
        xin = high.astype(BF16)
        x_b[0:32, :] = xin
        x_b[32:64, :] = xin
        x_b[64:96, :] = low.astype(BF16)

    def prep_small(edge, bias, w1_, vec_, eq_, ga_, t1_):
        prep_input(stage, w1_, edge, bias, OBS + ACT)
        stage[...] = jnp.zeros_like(stage)
        stage[0:1, :] = 0.5 * bias[1:2, :]
        stage[1:2, :] = 0.5 * bias[2:3, :]
        stage[2:3, :] = edge[23:24, :]
        vec_[...] = stage[...].T
        vec_[0:1, 8:9] = bias[3:4, 0:1]
        stage[...] = jnp.zeros_like(stage)
        high, low = split(edge[23:24, :])
        stage[0:1, :] = high
        stage[1:2, :] = low
        eq_[...] = stage[0:16, :].astype(BF16)
        if ga_ is not None:
            stage[...] = jnp.zeros_like(stage)
            stage[0:ACT, :] = 0.5 * edge[OBS : OBS + ACT, :]
            high, low = split(stage[0:8, :])
            both = jnp.concatenate([high, low], 0)
            ga_[...] = both.astype(BF16)
            stage[0:16, :] = both
            if t1_ is not None:
                t1_[...] = stage[...].T[:, 0:16].astype(BF16)

    def prep_actor():
        prep_input(stage, aw1, a_edge, a_bias, OBS)
        prep_hidden(af0, ab0, a_hidden[0])
        prep_hidden(af1, ab1, a_hidden[1])
        stage[...] = jnp.zeros_like(stage)
        stage[0:1, :] = 0.5 * a_bias[1:2, :]
        stage[1:2, :] = 0.5 * a_bias[2:3, :]
        stage[2:3, :] = a_bias[3:4, :]
        avec[...] = stage[...].T
        stage[...] = jnp.zeros_like(stage)
        stage[0:ACT, :] = a_edge[OBS : OBS + ACT, :]
        stage[8 : 8 + ACT, :] = a_edge[OBS + ACT : OBS + 2 * ACT, :]
        high, low = split(stage[0:16, :])
        ao[...] = jnp.concatenate([high, low], 0).astype(BF16)
        stage[...] = jnp.zeros_like(stage)
        stage[0 : 2 * ACT, :] = a_edge[OBS : OBS + 2 * ACT, :]
        high, low = split(stage[0:16, :])
        stage[0:32, :] = jnp.concatenate([high, low], 0)
        aot[...] = stage[...].T[:, 0:32].astype(BF16)

    prep_actor()

    def actor_layers(src):
        kept = []
        hb = None
        for w, b in ((aw1, None), (af0, 0), (af1, 1)):
            u = dot(w[...], src) if b is None else halves(dot(w[...], hb)) + avec[:, b : b + 1]
            h, t = silu_half(u)
            hb = h.astype(BF16)
            kept.append((hb, h, t))
        return kept

    ok8 = (lax.broadcasted_iota(jnp.int32, (8, 1), 0) < ACT).astype(F32)

    def actor_heads(hb, sl):
        out = halves(dot(ao[...], hb))
        eps = eps_s[:, sl]
        center = out[0:8] + avec[0:8, 2:3] * ok8
        th = jnp.tanh(out[8:16] + avec[6:14, 2:3] * ok8)
        log_std = 3.5 * th - 1.5
        spread_e = jnp.exp(log_std) * eps
        latent = center + spread_e
        soft = jnp.maximum(-2.0 * latent, 0.0) + jnp.log(1.0 + jnp.exp(-2.0 * jnp.abs(latent)))
        terms = -0.5 * eps * eps - log_std - HALF_LOG_TWO_PI - 2.0 * (LOG_TWO - latent - soft)
        logp = jnp.sum(terms * ok8, axis=0, keepdims=True)
        sample = jnp.tanh(latent) * ok8
        return sample, logp, th, spread_e

    actor_rows[...] = jnp.zeros_like(actor_rows)

    put_x()

    @pl.when(online)
    def _():
        fold_out()
        prep_small(c_edge.at[0], c_bias.at[0], w1, vec, eq, ga, t1w)
        prep_hidden(f0, b0, c_hidden[0, 0])
        prep_hidden(f1, b1, c_hidden[0, 1])
        for k, (fwd, bwd) in enumerate(((f0, b0), (f1, b1))):
            pf[0, k] = fwd[0:HID, :]
            pb[0, k] = bwd[0:HID, :]
            w = 0.5 * c_hidden[1, k]
            pf[1, k] = w.T.astype(BF16)
            pb[1, k] = w.astype(BF16)
        pw[0], pv[0], pq[0], pg[0] = w1[...], vec[...], eq[...], ga[...]
        prep_small(c_edge.at[1], c_bias.at[1], pw.at[1], pv.at[1], pq.at[1], pg.at[1], None)

    def least_online(k):
        return remote(least.at[:, 0:rows], least_in.at[k], sem_least_s.at[4 + k], sem_least_r.at[k], dev(1, lax.rem(e + k, 4)))

    def least_target(k):
        return remote(least.at[:, 0:rows], least_in.at[k], sem_least_s.at[k], sem_least_r.at[k], dev(0, lax.rem(e + k, 4)))

    def half_hidden(part, values):
        to = slice(part * HID, (part + 1) * HID)
        for k, (fwd, bwd) in enumerate(((f0, b0), (f1, b1))):
            w = 0.5 * values[k * HID : (k + 1) * HID, :].astype(F32)
            fwd[to, :] = w.T.astype(BF16)
            bwd[to, :] = w.astype(BF16)

    @pl.when(targetd)
    def _():
        for m in range(2):
            prep_small(c_edge.at[m], c_bias.at[m], tw1.at[m], tvec.at[m], teq.at[m], None, None)
            prep_hidden(tf0.at[m], None, c_hidden[m, 0])
            prep_hidden(tf1.at[m], None, c_hidden[m, 1])

        def body(i, _):
            @pl.when(i == 1)
            def _():
                all_here()
                fold_out()

            first = jnp.minimum(i * block, states.shape[1] - block)
            sl = pl.ds(pl.multiple_of(first, LANES), block)
            high, rest = split(ns[:, sl])
            nx, rest = high.astype(BF16), rest.astype(BF16)
            kept = actor_layers(jnp.concatenate([nx, nx, rest], 0))
            sample, logp, th, spread_e = actor_heads(kept[2][0], sl)
            high, rest = split(jnp.concatenate([ns[0:24, sl], sample], 0))
            nx = high.astype(BF16)
            nx = jnp.concatenate([nx, nx, rest.astype(BF16)], 0)
            low = None
            for m in range(2):
                h, t = silu_half(dot(tw1[m], nx))
                h, t = silu_half(halves(dot(tf0[m], h.astype(BF16))) + tvec[m, :, 0:1])
                h, t = silu_half(halves(dot(tf1[m], h.astype(BF16))) + tvec[m, :, 1:2])
                r = dot(teq[m], h.astype(BF16))
                q = r[0:1] + r[1:2] + tvec[m, 0:1, 8:9]
                low = q if low is None else jnp.minimum(low, q)
            least[:, sl] = low - ALPHA * logp
            return 0

        lax.fori_loop(0, blocks + (jnp.where(upper, 1, 0) if fold else 0), body, 0)
        if fold:
            @pl.when(upper)
            def _():
                least_copy().start()

        fold_in()
        if fold:
            put_x()
        param_copy(0).wait_recv()
        prep_small(small_in.at[0:24], small_in.at[24:32], w1, vec, eq, ga, t1w)
        param_copy(1).wait_recv()
        half_hidden(0, high_in)
        param_copy(2).wait_recv()
        half_hidden(1, rest_in)

    def least_out():
        @pl.when(targetd)
        def _():
            if fold:
                @pl.when(lower)
                def _():
                    least_copy().wait_recv()
                    merge(least, lambda b: far_least[:, b * LANES : (b + 1) * LANES])

            for k in range(1, 4):
                least_target(k).start()
            for k in range(4):
                least_online(k).start()

    class EnsembleSum:
        def __init__(self, index, mine, peer, pair, far, total, only_online):
            self.index, self.mine, self.peer, self.pair, self.far, self.total = index, mine, peer, pair, far, total
            self.chips = (1,) if only_online else (0, 1, 2)

        def to_core(self):
            return remote(self.mine.at[1 - core], self.peer, es_s.at[self.index, 0], es_r.at[self.index, 0], dev(g, other_core))

        def to_chip(self, k):
            across = (1 - g, g, 1 - g)[k]
            where = dev(across, (e, far_chip, far_chip)[k])
            return remote(self.pair, self.far.at[k], es_s.at[self.index, 1 + k], es_r.at[self.index, 1 + k], where)

        def back(self):
            return remote(self.total.at[core], self.total.at[core], es_s.at[self.index, 4], es_r.at[self.index, 4], dev(g, other_core))

        def begin(self, first, second):
            self.mine[0] = first
            self.mine[1] = second
            self.to_core().start()

        def middle(self):
            self.to_core().wait_recv()
            self.pair[...] = self.mine[core] + self.peer[...]
            for k in self.chips:
                self.to_chip(k).start()

        def first_to_core(self, h, values):
            self.mine[h] = values

            @pl.when(core != h)
            def _():
                self.to_core().start()

            @pl.when(core == h)
            def _():
                self.middle()

        def last_of(self, h):
            @pl.when(core == h)
            def _():
                self.last()

        def back_of(self, h):
            @pl.when(core != h)
            def _():
                self.back().wait_recv()

        def last(self):
            total = self.pair[...]
            for k in self.chips:
                self.to_chip(k).wait_recv()
                total = total + self.far[k]
            self.total[core] = total
            self.back().start()

        def whole(self):
            self.back().wait_recv()
            return jnp.concatenate([self.total[0], self.total[1]], 1)

        def sent(self):
            self.to_core().wait_send()
            for k in self.chips:
                self.to_chip(k).wait_send()
            self.back().wait_send()

    unit_sum = EnsembleSum(0, u_mine, u_peer, u_pair, u_far, u_total, False)
    slope_sum = EnsembleSum(1, q_mine, q_peer, q_pair, q_far, q_total, True)

    rid = lax.broadcasted_iota(jnp.int32, (8, 1), 0)

    @pl.when(online)
    def _():
        def body_p(i, _):
            sl = pl.ds(pl.multiple_of(i * block, block), block)

            @pl.when(i == 1)
            def _():
                fold_in()
                if fold:
                    put_x()

            kept = actor_layers(x_b[:, sl])
            if fold:
                for store, curve, (hb, h, t) in zip((ah1x, ah2x, ah3), (as1, as2, as3), kept):
                    store[0:HID, sl] = hb
                    curve[:, sl] = (1.0 + t) + h * (1.0 - t)
            sample, logp, th, spread_e = actor_heads(kept[2][0], sl)
            pi_act[:, sl] = sample
            heads[0:8, sl] = th
            heads[8:16, sl] = spread_e
            heads[16:17, sl] = logp
            pin = jnp.concatenate([xs[0:24, sl], sample], 0).astype(BF16)
            unit_f[16:24, sl] = jnp.zeros((8, block), F32)

            def member(m, _):
                def act(u):
                    h, t = silu_half(u)
                    hb, tb = h.astype(BF16), t.astype(BF16)
                    one = jnp.ones((), BF16)
                    return hb, (one + tb) + hb * (one - tb)

                h, a1 = act(dot(pw[m][:, 0:64], jnp.concatenate([pin, pin], 0)))
                h, a2 = act(dot(pf[m, 0], h) + pv[m][:, 0:1])
                h, a3 = act(dot(pf[m, 1], h) + pv[m][:, 1:2])
                r = dot(pq[m], h)
                q = r[0:1] + r[1:2] + pv[m][0:1, 8:9]
                d = pv[m][:, 2:3].astype(BF16) * a3
                d = dot(pb[m, 1], d).astype(BF16) * a2
                d = dot(pb[m, 0], d).astype(BF16) * a1
                unit_f[16:24, sl] += halves(dot(pg[m], d)) + jnp.where(rid == 6, q, 0.0)
                return 0

            lax.fori_loop(0, 2, member, 0)
            return 0

        lax.fori_loop(0, blocks, body_p, 0)
        slope_sum.begin(unit_f[16:24, 0:half], unit_f[16:24, half:rows])

    ones = (lax.broadcasted_iota(jnp.int32, (16, rows), 0) == 0).astype(BF16)
    h1x[HID : HID + 16, :] = ones
    h2x[HID : HID + 16, :] = ones

    def curves(u):
        h, t = silu_half(u)
        c = 1.0 + t
        d = 1.0 - t
        return h, c + h * d, (c * d) * (1.0 - u * t)

    valid = jnp.where(eps_s[7:8, 0:rows] > 1.5, 1.0, 0.0)

    def body_a(i, _):
        @pl.when(i == 1)
        def _():
            @pl.when(online)
            def _():
                slope_sum.middle()

            if fold:
                unit_sum.first_to_core(0, unit_f[0:8, 0:half])
            least_out()

        sl = pl.ds(pl.multiple_of(i * block, block), block)
        h, a1, q1 = curves(dot(w1[...], x_b[:, sl]))
        hb = h.astype(BF16)
        h1x[0:HID, sl] = hb
        s1[:, sl] = a1.astype(BF16)
        h, a2, q2 = curves(halves(dot(f0[...], hb)) + vec[:, 0:1])
        hb = h.astype(BF16)
        h2x[0:HID, sl] = hb
        s2[:, sl] = a2.astype(BF16)
        h, a3, q3 = curves(halves(dot(f1[...], hb)) + vec[:, 1:2])
        hb = h.astype(BF16)
        h3s[:, sl] = hb
        s3[:, sl] = a3.astype(BF16)
        r = dot(eq[...], hb)
        value[:, sl] = r[0:1] + r[1:2] + vec[0:1, 8:9]
        last = vec[:, 2:3]
        db = (last * a3).astype(BF16)
        d3s[:, sl] = db
        k3[:, sl] = (last * q3).astype(BF16)
        m = halves(dot(b1[...], db))
        db = (m * a2).astype(BF16)
        d2s[:, sl] = db
        k2[:, sl] = (m * q2).astype(BF16)
        m = halves(dot(b0[...], db))
        db = (m * a1).astype(BF16)
        d1s[:, sl] = db
        k1[:, sl] = (m * q1).astype(BF16)
        slope = halves(dot(ga[...], db))
        inv = lax.rsqrt(jnp.sum(slope * slope, axis=0, keepdims=True) + 0.01)
        unit_f[0:8, sl] = slope * inv
        unit_f[8:9, sl] = inv
        return 0

    lax.fori_loop(0, blocks, body_a, 0)
    if fold:
        unit_sum.first_to_core(1, unit_f[0:8, half:rows])
        unit_sum.last_of(0)
    else:
        unit_sum.begin(unit_f[0:8, 0:half], unit_f[0:8, half:rows])
        unit_sum.middle()

    @pl.when(online)
    def _():
        for what in (3, 4):
            param_copy(what).start()


    class Exchange:
        def __init__(self, index, part, into, inbox, base, count, wide):
            self.index, self.part, self.into, self.inbox, self.base, self.count, self.wide = index, part, into, inbox, base, count, wide
            self.each = count // (n_dp * (4 if wide else 1))

        def rows_of(self, shard):
            first = self.base + (e * n_dp + shard if self.wide else shard) * self.each
            return pl.ds(pl.multiple_of(first, 8), self.each)

        def scatter(self, k):
            to = lax.rem(z + k, n_dp)
            return remote(
                self.part.at[self.rows_of(to)], self.inbox.at[k - 1], rs_s.at[self.index, k - 1, 0], rs_r.at[self.index, k - 1, 0], {"dp": to}
            )

        def gather(self, k):
            mine = self.into.at[self.rows_of(z)]
            return remote(mine, mine, ag_s.at[self.index, k - 1, 0], ag_r.at[self.index, k - 1, 0], {"dp": lax.rem(z + k, n_dp)})

        def across(self, k):
            there = self.into.at[self.rows_of(lax.rem(z + n_dp - k, n_dp))]
            return remote(there, there, xf_s.at[self.index, k, 0], xf_r.at[self.index, k, 0], dev(1 - g, e))

        def start(self):
            for k in range(1, n_dp):
                self.scatter(k).start()

        def reduce(self, along=True):
            total = self.part[self.rows_of(z), :]
            for k in range(1, n_dp):
                self.scatter(k).wait_recv()
                total = total + self.inbox[k - 1]
            self.into[self.rows_of(z), :] = total
            if along:
                for k in range(1, n_dp):
                    self.gather(k).start()
            self.across(0).start()

        def forward(self):
            for k in range(1, n_dp):
                self.gather(k).wait_recv()
                self.across(k).start()

        def sent(self):
            for k in range(1, n_dp):
                self.scatter(k).wait_send()
                self.gather(k).wait_send()
            for k in range(n_dp):
                self.across(k).wait_send()

        def arrived(self):
            for k in range(n_dp):
                self.across(k).wait_recv()

        def detour(self):
            self.across(0).wait_recv()
            for k in range(1, n_dp):
                self.gather(k).start()

        def back(self):
            for k in range(1, n_dp):
                self.across(k).wait_recv()

        def sent_detour(self):
            @pl.when(online)
            def _():
                for k in range(1, n_dp):
                    self.scatter(k).wait_send()
                self.across(0).wait_send()

            @pl.when(targetd)
            def _():
                for k in range(1, n_dp):
                    self.gather(k).wait_send()
                    self.across(k).wait_send()

    class Coded(Exchange):
        def __init__(self, index, part, out, base, count, lead, wide, boxes):
            self.index, self.part, self.out, self.base, self.count, self.lead, self.wide = index, part, out, base, count, lead, wide
            self.out_w, self.out_s, self.in_w, self.in_s, self.all_w, self.all_s = boxes
            self.each = count // (n_dp * (4 if wide else 1))

        def pack(self, x):
            top = jnp.maximum(jnp.max(jnp.abs(x), axis=0, keepdims=True), 1e-30)
            q = jnp.round(x * (32767.0 / top)).astype(jnp.int32)
            h = self.each // 2
            return jnp.bitwise_or(jnp.bitwise_and(q[:h], 65535), jnp.left_shift(q[h:], 16)), top * (1.0 / 32767.0)

        def unpack(self, w, scale):
            low = jnp.right_shift(jnp.left_shift(w, 16), 16)
            high = jnp.right_shift(w, 16)
            return jnp.concatenate([low, high], 0).astype(F32) * scale

        def scatter(self, k):
            to = lax.rem(z + k, n_dp)
            return Both([
                remote(o.at[to], i.at[k - 1], rs_s.at[self.index, k - 1, q], rs_r.at[self.index, k - 1, q], {"dp": to})
                for q, (o, i) in enumerate(((self.out_w, self.in_w), (self.out_s, self.in_s)))
            ])

        def gather(self, k):
            return Both([
                remote(
                    a.at[self.lead, z], a.at[self.lead, z], ag_s.at[self.index, k - 1, q], ag_r.at[self.index, k - 1, q],
                    {"dp": lax.rem(z + k, n_dp)},
                )
                for q, a in enumerate((self.all_w, self.all_s))
            ])

        def across(self, k):
            there = lax.rem(z + n_dp - k, n_dp)
            return Both([
                remote(
                    a.at[self.lead, there], a.at[self.lead, there], xf_s.at[self.index, k, q], xf_r.at[self.index, k, q], dev(1 - g, e)
                )
                for q, a in enumerate((self.all_w, self.all_s))
            ])

        def start(self):
            for shard in range(n_dp):
                w, scale = self.pack(self.part[self.rows_of(shard), :])
                self.out_w[shard] = w
                self.out_s[shard] = scale
            for k in range(1, n_dp):
                self.scatter(k).start()

        def reduce(self, along=True):
            total = self.part[self.rows_of(z), :]
            for k in range(1, n_dp):
                self.scatter(k).wait_recv()
                total = total + self.unpack(self.in_w[k - 1], self.in_s[k - 1])
            w, scale = self.pack(total)
            self.all_w[self.lead, z] = w
            self.all_s[self.lead, z] = scale
            if along:
                for k in range(1, n_dp):
                    self.gather(k).start()
            self.across(0).start()

        def decode(self):
            for lead in range(self.all_w.shape[0]):
                for shard in range(n_dp):
                    x = self.unpack(self.all_w[lead, shard], self.all_s[lead, shard])
                    if self.wide:
                        first = (lead * n_dp + shard) * self.each
                        self.out[first : first + self.each, :] = x
                    else:
                        first = self.base + shard * self.each
                        self.out[lead, first : first + self.each, :] = x

    class Both:
        def __init__(self, copies):
            self.copies = copies

        def start(self):
            for c in self.copies:
                c.start()

        def wait_recv(self):
            for c in self.copies:
                c.wait_recv()

        def wait_send(self):
            for c in self.copies:
                c.wait_send()

    if coded:
        box_h1, box_h0, box_ac = boxes[0:6], boxes[6:12], boxes[12:18]
    if coded:
        ex_h1 = Coded(0, part_c, sum_c, HID, HID, g, False, box_h1)
        ex_h0 = Coded(1, part_c, sum_c, 0, HID, g, False, box_h0)
        ex_ac = Coded(3, part_a, sum_a, 0, 2 * HID, e, True, box_ac)
        ex_as = Exchange(4, part_a, sum_a, in_ac, 2 * HID, ACTOR_SMALL, False)
        actor = (ex_ac, ex_as)
    else:
        ex_h1 = Exchange(0, part_c, sum_c.at[g], in_h1, HID, HID, False)
        ex_h0 = Exchange(1, part_c, sum_c.at[g], in_h0, 0, HID, False)
        ex_ac = Exchange(3, part_a, sum_a, in_ac, 0, part_a.shape[0], True)
        actor = (ex_ac,)
    ex_sm = Exchange(2, part_c, sum_c.at[g], in_sm, 2 * HID, part_c.shape[0] - 2 * HID, False)

    def spread_actor(k):
        if coded:
            mine = ex_ac.all_w.at[e]
        else:
            quarter = part_a.shape[0] // 4
            mine = sum_a.at[pl.ds(pl.multiple_of(e * quarter, 8), quarter)]
        return remote(mine, mine, ef_s.at[k - 1], ef_r.at[k - 1], dev(g, lax.rem(e + k, 4)))

    def spread_scale(k):
        mine = ex_ac.all_s.at[e]
        return remote(mine, mine, ef_s.at[2 + k], ef_r.at[2 + k], dev(g, lax.rem(e + k, 4)))

    def spread_start():
        for k in range(1, 4):
            spread_actor(k).start()
            if coded:
                spread_scale(k).start()

    lane = lax.broadcasted_iota(jnp.int32, (1, HID), 1)
    rid32 = lax.broadcasted_iota(jnp.int32, (32, 1), 0)

    def local(src, dst, k):
        return pltpu.make_async_copy(src, dst, sem_out.at[k])

    def own_outputs():
        return (
            local(small_out, out_small, 0), local(high_out, out_high, 1), local(rest_out, out_rest, 2), local(low_out, out_low, 5),
        )

    def far_outputs():
        return local(small_in, out_small, 0), local(high_in, out_high, 1), local(rest_in, out_rest, 2), local(low_in, out_low, 5)

    @pl.when(online)
    def _():
        slope_sum.last()
        total = slope_sum.whole() * (1.0 / critics)
        d_sample = -valid * total
        d_logp = ALPHA * valid
        sample = pi_act[...]
        th = heads[0:8, :]
        spread_e = heads[8:16, :]
        dz = (d_sample * (1.0 - sample * sample) + d_logp * 2.0 * sample) * ok8
        dls = (dz * spread_e - d_logp) * (3.5 * (1.0 - th * th)) * ok8
        heads[24:40, :] = jnp.zeros((16, rows), F32)
        heads[24:30, :] = dz[0:ACT]
        heads[30:36, :] = dls[0:ACT]
        actor_sum = jnp.sum(valid * (ALPHA * heads[16:17, :] - total[6:7]), axis=1, keepdims=True)
        done_rows = jnp.sum(valid, axis=1, keepdims=True)
        count = counts[0].astype(F32) if fold else 0.0
        for acc in (acc_c1, acc_c0, acc_cx, acc_o):
            acc[...] = jnp.zeros_like(acc)
        one16 = (lax.broadcasted_iota(jnp.int32, (16, block), 0) == 0).astype(BF16)
        if fold:
            ah1x[HID : HID + 16, :] = h1x[HID : HID + 16, :]
            ah2x[HID : HID + 16, :] = h1x[HID : HID + 16, :]

        def body_c(i, _):
            sl = pl.ds(pl.multiple_of(i * block, block), block)
            if fold:
                tall1, tall2, top = ah1x[:, sl], ah2x[:, sl], ah3[:, sl]
                slopes = [as1[:, sl], as2[:, sl], as3[:, sl]]
            else:
                kept = actor_layers(x_b[:, sl])
                tall1, tall2 = (jnp.concatenate([kept[k][0], one16], 0) for k in range(2))
                top = kept[2][0]
                slopes = [(1.0 + t) + h * (1.0 - t) for _, h, t in kept]
            do = heads[24:40, sl].astype(BF16)
            acc_o[0:16, :] += dot_t(do, top)
            d3 = (dot(aot[...], jnp.concatenate([do, do], 0)) * (0.5 * slopes[2])).astype(BF16)
            acc_c1[...] += dot_t(tall2, d3)
            d2 = (halves(dot(ab1[...], d3)) * slopes[1]).astype(BF16)
            acc_c0[...] += dot_t(tall1, d2)
            d1 = (halves(dot(ab0[...], d2)) * slopes[0]).astype(BF16)
            acc_cx[...] += dot_t(x_b[0:32, sl], d1)
            acc_o[16:32, 0:128] += dot_t(one16, jnp.concatenate([do, jnp.zeros((112, block), BF16)], 0))
            return 0

        lax.fori_loop(0, blocks, body_c, 0)
        part_a[0:HID, :] = acc_c0[0:HID, :]
        part_a[HID : 2 * HID, :] = acc_c1[0:HID, :]
        actor_rows[0:1, :] = jnp.where(lane == 0, actor_sum, jnp.where(lane == 1, count, jnp.where(lane == 2, done_rows, 0.0)))
        actor_rows[1:2, :] = acc_o[16:17, :]
        first = 2 * HID
        part_a[first : first + 18, :] = acc_cx[0:18, :]
        part_a[first + 18 : first + 19, :] = acc_c0[HID : HID + 1, :]
        part_a[first + 19 : first + 20, :] = acc_c1[HID : HID + 1, :]
        part_a[first + 20 : first + 32, :] = acc_o[0 : 2 * ACT, :]
        part_a[first + 32 :, :] = jnp.zeros((part_a.shape[0] - first - 32, HID), F32)
        for ex in actor:
            ex.start()

    @pl.when(targetd)
    def _():
        least_in[0] = least[:, 0:rows]
        for k in range(1, 4):
            least_target(k).wait_recv()

    @pl.when(online)
    def _():
        for k in range(4):
            least_online(k).wait_recv()

    rid16 = lax.broadcasted_iota(jnp.int32, (16, 1), 0)

    def directions(sl, spread):
        code = eps_s[7:8, sl]
        valid = jnp.where(code > 1.5, 1.0, 0.0)
        low = jnp.minimum(
            jnp.minimum(least_in[0, :, sl], least_in[1, :, sl]), jnp.minimum(least_in[2, :, sl], least_in[3, :, sl])
        )
        target = eps_s[6:7, sl] + GAMMA * (1.0 + 2.0 * valid - code) * low
        unit = unit_f[0:8, sl]
        inv = unit_f[8:9, sl]
        d_unit = (2.0 * ETA / (critics - 1)) * valid * (spread - unit)
        along = jnp.sum(d_unit * unit, axis=0, keepdims=True)
        dg = (d_unit - unit * along) * inv
        gap = value[:, sl] - target
        dv = 2.0 * valid * gap
        row_sums[0:1, sl] = valid * gap * gap
        row_sums[1:2, sl] = valid * jnp.sum(unit * (spread - unit), axis=0, keepdims=True)
        row_sums[2:3, sl] = dv
        dvh[:, sl] = 0.5 * dv
        dgb = dg.astype(BF16)
        dg_b[:, sl] = jnp.concatenate([dgb, dgb], 0)
        dv_b[:, sl] = jnp.where(rid16 == 0, dv, jnp.where(rid16 == 1, 1.0, 0.0)).astype(BF16)

    if not fold:
        unit_sum.last()
        directions(slice(0, rows), unit_sum.whole())

    for acc in (acc_h1, acc_h1t, acc_h0, acc_h0t, acc_x, acc_t, acc_last):
        acc[...] = jnp.zeros_like(acc)

    def body_b1(i, _):
        sl = pl.ds(pl.multiple_of(i * block, block), block)
        if fold:
            @pl.when(i == 0)
            def _():
                unit_sum.back_of(0)

            @pl.when(i == 1)
            def _():
                unit_sum.last_of(1)
                unit_sum.back_of(1)

            directions(sl, u_total[i])
        tp = dot(t1w[...], dg_b[:, sl])
        k1[:, sl] = (k1[:, sl].astype(F32) * tp).astype(BF16)
        th1 = (s1[:, sl].astype(F32) * tp).astype(BF16)
        tp = halves(dot(f0[...], th1))
        k2[:, sl] = (k2[:, sl].astype(F32) * tp).astype(BF16)
        th2 = (s2[:, sl].astype(F32) * tp).astype(BF16)
        tp = halves(dot(f1[...], th2))
        th3 = (s3[:, sl].astype(F32) * tp).astype(BF16)
        d3 = d3s[:, sl]
        ap3 = (dvh[:, sl] * d3.astype(F32) + k3[:, sl].astype(F32) * tp).astype(BF16)
        k3[:, sl] = ap3
        rows_dv = dv_b[:, sl]
        last = dot_t(rows_dv, h3s[:, sl])
        lone = dot_t(rows_dv, th3)
        acc_last[...] += last[0:8] + jnp.where(rid == 0, lone[1:2], 0.0)
        h3s[:, sl] = th1
        acc_h1[...] += dot_t(h2x[:, sl], ap3)
        acc_h1t[...] += dot_t(th2, d3)
        return 0

    def body_b2(i, _):
        sl = pl.ds(pl.multiple_of(i * block, block), block)
        ah = halves(dot(b1[...], k3[:, sl]))
        ap2 = (s2[:, sl].astype(F32) * ah + k2[:, sl].astype(F32)).astype(BF16)
        k2[:, sl] = ap2
        acc_h0[...] += dot_t(h1x[:, sl], ap2)
        acc_h0t[...] += dot_t(h3s[:, sl], d2s[:, sl])
        return 0

    def body_b3(i, _):
        sl = pl.ds(pl.multiple_of(i * block, block), block)
        ah = halves(dot(b0[...], k2[:, sl]))
        ap1 = (s1[:, sl].astype(F32) * ah + k1[:, sl].astype(F32)).astype(BF16)
        acc_x[...] += dot_t(x_b[0:32, sl], ap1)
        acc_t[...] += dot_t(dg_b[:, sl], d1s[:, sl])
        return 0

    lax.fori_loop(0, blocks, body_b1, 0)
    part_c[HID : 2 * HID, :] = acc_h1[0:HID, :] + 0.5 * acc_h1t[...]
    ex_h1.start()

    @pl.when(online)
    def _():
        for ex in actor:
            ex.reduce(False)

    lax.fori_loop(0, blocks, body_b2, 0)
    part_c[0:HID, :] = acc_h0[0:HID, :] + 0.5 * acc_h0t[...]
    ex_h0.start()
    lax.fori_loop(0, blocks, body_b3, 0)
    errors, diverse, dv_sum = (jnp.sum(row_sums[k : k + 1, :], axis=1, keepdims=True) for k in range(3))
    stats = jnp.where(lane == 0, errors, jnp.where(lane == 1, diverse, 0.0))
    small = acc_x[...]
    small = small + jnp.where(rid32 == 18, acc_h0[HID : HID + 1, :], 0.0)
    small = small + jnp.where(rid32 == 19, acc_h1[HID : HID + 1, :], 0.0)
    small = small + jnp.where(rid32 == 20, stats, 0.0)
    small = small + jnp.where(rid32 == 21, actor_rows[0:1, :], 0.0) + jnp.where(rid32 == 30, actor_rows[1:2, :], 0.0)
    small = small + jnp.where(rid32 == 22, jnp.where(lane == 0, dv_sum, 0.0), 0.0)
    small = small + jnp.where(rid32 == 23, acc_last[0:1, :], 0.0)
    part_c[2 * HID : 2 * HID + 24, :] = small[0:24]
    part_c[2 * HID + 24 : 2 * HID + 32, :] = small[24:32] + 0.5 * acc_t[0:8, :]
    rest = part_c.shape[0] - 2 * HID - 32
    if rest:
        part_c[2 * HID + 32 :, :] = jnp.zeros((rest, HID), F32)
    ex_sm.start()

    @pl.when(targetd)
    def _():
        for ex in actor:
            ex.detour()

    ex_h1.reduce()
    ex_h0.reduce()
    ex_sm.reduce()
    ex_h1.forward()

    @pl.when(targetd)
    def _():
        for ex in actor:
            ex.forward()
        spread_start()

    ex_h0.forward()
    ex_sm.forward()

    @pl.when(online)
    def _():
        for ex in actor:
            ex.back()
        spread_start()


    @pl.when(online)
    def _():
        for copy in own_outputs():
            copy.start()

    @pl.when(targetd)
    def _():
        param_copy(3).wait_recv()
        param_copy(4).wait_recv()
        for copy in far_outputs():
            copy.start()

    def out_rows(first, last, k):
        return local(sum_c.at[:, first:last], out_c.at[:, first:last], k)

    copies = [out_rows(HID, 2 * HID, 4), local(sum_a, out_a, 3), out_rows(2 * HID, sum_c.shape[1], 6), out_rows(0, HID, 7)]
    ex_h1.arrived()
    if coded:
        ex_h1.decode()
    copies[0].start()
    for k in range(1, 4):
        spread_actor(k).wait_recv()
        if coded:
            spread_scale(k).wait_recv()
    if coded:
        ex_ac.decode()
    copies[1].start()
    ex_sm.arrived()
    copies[2].start()
    ex_h0.arrived()
    if coded:
        ex_h0.decode()
    copies[3].start()

    @pl.when(online)
    def _():
        for what in range(5):
            param_copy(what).wait_send()

    @pl.when(targetd)
    def _():
        for k in range(1, 4):
            least_target(k).wait_send()
        for k in range(4):
            least_online(k).wait_send()

    if fold:
        @pl.when(upper)
        def _():
            for what in range(2):
                fold_copy(what, 0).wait_send()

        @pl.when(lower)
        def _():
            for what in range(2):
                fold_copy(what, 1).wait_send()

        @pl.when(jnp.logical_and(upper, targetd))
        def _():
            least_copy().wait_send()

    unit_sum.sent()

    @pl.when(online)
    def _():
        slope_sum.sent()

    for ex in actor:
        ex.sent_detour()
    for k in range(1, 4):
        spread_actor(k).wait_send()
        if coded:
            spread_scale(k).wait_send()
    for ex in (ex_h1, ex_h0, ex_sm):
        ex.sent()
    for copy in copies:
        copy.wait()

    @pl.when(online)
    def _():
        for copy in own_outputs():
            copy.wait()

    @pl.when(targetd)
    def _():
        for copy in far_outputs():
            copy.wait()


def sizes(n_dp):
    return 2 * HID + up(CRITIC_SMALL, 8 * n_dp), up(2 * HID + ACTOR_SMALL, 32 * n_dp)


def fused(n_dp, rows, block, fold, data, own, aparams):
    v = pltpu.VMEM
    big = lambda n=HID: v((n, rows), BF16)
    dma = pltpu.SemaphoreType.DMA
    size_c, size_a = sizes(n_dp)
    coded = 2 * HID % (64 * n_dp) == 0
    h8 = lambda *n: v((*n, 8, rows // 2), F32)
    sums = [h8(2), h8(), h8(), h8(3), h8(2)]
    extra = (data[0].shape[1] - rows) // 2 if fold else LANES
    moved = [v((2, 32, extra), BF16), v((2, 8, extra), F32)]
    size = data[0].shape[1]
    kept = (lambda n, t: v((n, rows), t)) if fold else (lambda n, t: v((16, LANES), t))
    scratch = [
        v((32, size), F32), v((32, size), F32), v((8, size), F32), *moved, *moved,
        v((96, rows), BF16), v((8, rows), F32),
        v((128, HID), F32), v((HID, 128), F32), v((2, HID, 128), F32), v((HID, 128), F32),
        v((64, HID), F32), v((64, HID), F32), *[v((2 * HID, HID), BF16) for _ in range(6)],
        v((HID, 96), BF16), v((512, HID), BF16), v((512, HID), BF16), v((512, HID), BF16), v((512, HID), BF16),
        v((16, HID), BF16), v((HID, 16), BF16), v((16, HID), BF16),
        v((2, HID, 96), BF16), v((2, HID, 128), F32), v((2, 16, HID), BF16), v((2, 16, HID), BF16),
        v((2, 2, HID, HID), BF16), v((2, 2, HID, HID), BF16),
        v((2, HID, 96), BF16), v((2, 512, HID), BF16), v((2, 512, HID), BF16), v((2, 16, HID), BF16),
        v((HID, 96), BF16), v((512, HID), BF16), v((512, HID), BF16), v((512, HID), BF16), v((512, HID), BF16),
        v((32, HID), BF16), v((HID, 32), BF16),
        big(272), big(272), big(), big(), big(), big(), big(), big(), big(), big(), big(), big(),
        v((40, rows), F32), kept(272, BF16), kept(272, BF16), kept(HID, BF16), kept(HID, F32), kept(HID, F32), kept(HID, F32),
        v((1, rows), F32), v((24, rows), F32), *sums,
        v((16, rows), BF16), v((16, rows), BF16), v((1, rows), F32), v((8, rows), F32),
        *sums,
        v((1, size), F32), v((1, 2 * extra), F32), v((4, 1, rows), F32),
        v((272, HID), F32), v((HID, HID), F32), v((272, HID), F32), v((HID, HID), F32),
        v((32, HID), F32), v((16, HID), F32), v((8, HID), F32), v((32, HID), F32),
        v((272, HID), F32), v((272, HID), F32), v((32, HID), F32), v((8, HID), F32),
        v((size_c, HID), F32), v((size_a, HID), F32), v((2, size_c, HID), F32), v((size_a, HID), F32),
        *[v((1, 8, HID) if coded else (n_dp - 1, HID // n_dp, HID), F32) for _ in range(2)],
        v((n_dp - 1, (size_c - 2 * HID) // n_dp, HID), F32),
        v((n_dp - 1, (ACTOR_SMALL if coded else size_a // 4) // n_dp, HID), F32),
        dma((2, 2)), dma((2, 2)), dma, dma, dma((5,)), dma((5,)), dma((8,)), dma((4,)), dma((2, 5)), dma((2, 5)),
        dma((5, n_dp - 1, 2)), dma((5, n_dp - 1, 2)), dma((5, n_dp - 1, 2)), dma((5, n_dp - 1, 2)), dma((5, n_dp, 2)), dma((5, n_dp, 2)),
        dma((6,)), dma((6,)), dma((8,)),
    ]
    if coded:
        for each, lead in ((HID // n_dp, 2), (HID // n_dp, 2), (2 * HID // (4 * n_dp), 4)):
            word, scale = (each // 2, HID), (1, HID)
            for outer in ((n_dp,), (n_dp - 1,), (lead, n_dp)):
                scratch += [v((*outer, *word), jnp.int32), v((*outer, *scale), F32)]
    spec = pl.BlockSpec(memory_space=pltpu.VMEM)
    anyspace = pl.BlockSpec(memory_space=pl.ANY)
    shape = lambda *s: jax.ShapeDtypeStruct(s, F32)
    return pl.pallas_call(
        functools.partial(kernel, n_dp, rows, block, fold),
        out_shape=(
            shape(2, size_c, HID), shape(size_a, HID), shape(64, HID), *[jax.ShapeDtypeStruct((2 * HID, HID), BF16)] * 3,
        ),
        in_specs=[spec] * 5 + [pl.BlockSpec(memory_space=pltpu.SMEM)] + [spec] * 7,
        out_specs=(anyspace,) * 6,
        scratch_shapes=scratch,
        compiler_params=pltpu.CompilerParams(collective_id=0 if fold else 1, has_side_effects=True, vmem_limit_bytes=63 * 2**20),
        name="edac_gradients" if fold else "edac_rest",
    )(*data, *own, *aparams)


def adamw(param, grad, first, second):
    first_new = BETA_ONE * first + (1.0 - BETA_ONE) * grad
    second_new = BETA_TWO * second + (1.0 - BETA_TWO) * grad * grad
    scaled = second_new * (1.0 / (1.0 - BETA_TWO**STEP))
    root = scaled * lax.rsqrt(jnp.maximum(scaled, 1e-30)) + EPS
    inverse = pl.reciprocal(root, approx=True)
    inverse = inverse * (2.0 - root * inverse)
    ratio = first_new * (1.0 / (1.0 - BETA_ONE**STEP)) * inverse
    return (param - LEARN * (ratio + DECAY * param), first_new, second_new)


def update_kernel(*refs):
    n_in, n_out = 24, 20
    src, dst = refs[:n_in], refs[n_in : n_in + n_out]
    rest = refs[n_in + n_out :]
    buf, res = rest[:n_in], rest[n_in : n_in + n_out]
    ge, gb, gae, gab, sem_in, sem_out = rest[n_in + n_out :]
    gc, ga, own_e, own_h, own_b, on_s, on_high, on_rest, low_h, em, ev, hm, hv, bm, bv, ae, ah, ab, aem, aev, ahm, ahv, abm, abv = buf
    o_e, o_h, o_b, o_em, o_ev, o_hm, o_hv, o_bm, o_bv, o_ae, o_ah, o_ab, o_aem, o_aev, o_ahm, o_ahv, o_abm, o_abv, o_ms, o_as = res
    online = lax.axis_index("grp") == 1
    index = {id(b): k for k, b in enumerate(buf)}
    out_index = {id(r): k for k, r in enumerate(res)}

    def read(b, slot=0, at=lambda r: r):
        k = index[id(b)]
        return pltpu.make_async_copy(at(src[k]), at(b), sem_in.at[k, slot])

    def write(r, slot=0, at=lambda x: x):
        k = out_index[id(r)]
        return pltpu.make_async_copy(at(r), at(dst[k]), sem_out.at[k, slot])

    def matrix(m, k):
        rows = slice(k * HID, (k + 1) * HID)
        par = [read(low_h, k, lambda r: r.at[rows])] if m == 0 else [
            read(on_high, k, lambda r: r.at[rows]), read(on_rest, k, lambda r: r.at[rows])
        ]
        mine = [read(b, 2 * m + k, lambda r: r.at[m, k]) for b in (own_h, hm, hv)]
        return [read(gc, 2 * m + k, lambda r: r.at[1 - m, rows])] + par + mine

    def actor_matrix(k):
        rows = slice(k * HID, (k + 1) * HID)
        return [read(ga, k, lambda r: r.at[rows])] + [read(b, k, lambda r: r.at[k]) for b in (ah, ahm, ahv)]

    stats = read(gc, 4, lambda r: r.at[:, 2 * HID :])
    small_reads = [read(ga, 2, lambda r: r.at[2 * HID : 2 * HID + ACTOR_SMALL]), stats] + [
        read(b) for b in (own_e, own_b, on_s, em, ev, bm, bv, ae, ab, aem, aev, abm, abv)
    ]
    order = [(0, 0), (0, 1), (1, 0), (1, 1)]
    stats.start()
    for copy in matrix(*order[0]):
        copy.start()
    for copy in small_reads:
        if copy is not stats:
            copy.start()
    for at in order[1:]:
        for copy in matrix(*at):
            copy.start()
    for k in range(2):
        for copy in actor_matrix(k):
            copy.start()

    gas = ga.at[2 * HID : 2 * HID + ACTOR_SMALL]
    stats.wait()
    rows_a = gc.at[1, 2 * HID : 2 * HID + 32]
    scale = 1.0 / rows_a[21:22, 1:2]
    writes = []

    def put(copy):
        copy.start()
        writes.append(copy)

    def critic(own, param, grad, first, second):
        master, m_new, v_new = adamw(jnp.where(online, own, param), grad, first, second)
        polyak = TAU * master.astype(BF16).astype(F32) + (1.0 - TAU) * own
        return jnp.where(online, master, polyak), m_new, v_new

    def do_matrix(m, k):
        for copy in matrix(m, k):
            copy.wait()
        rows = slice(k * HID, (k + 1) * HID)
        param = low_h[rows, :].astype(F32) if m == 0 else on_high[rows, :].astype(F32) + on_rest[rows, :].astype(F32)
        o_h[m, k], o_hm[m, k], o_hv[m, k] = critic(own_h[m, k], param, gc[1 - m, rows, :] * scale, hm[m, k], hv[m, k])
        for r in (o_h, o_hm, o_hv):
            put(write(r, 2 * m + k, lambda x: x.at[m, k]))

    do_matrix(0, 0)
    for copy in small_reads:
        if copy is not stats:
            copy.wait()
    for m in range(2):
        small = gc.at[1 - m, 2 * HID : 2 * HID + 32]
        ge[0:OBS, :] = small[0:OBS, :]
        ge[OBS : OBS + ACT, :] = small[24 : 24 + ACT, :]
        ge[23:24, :] = small[23:24, :]
        gb[0:3, :] = small[17:20, :]
        gb[3:4, :] = small[22:23, :]
        first = 32 * (1 - m)
        o_e[m], o_em[m], o_ev[m] = critic(own_e[m], on_s[first : first + 24], ge[...] * scale, em[m], ev[m])
        o_b[m], o_bm[m], o_bv[m] = critic(own_b[m], on_s[first + 24 : first + 28], gb[0:4, :] * scale, bm[m], bv[m])
    second = lax.broadcasted_iota(jnp.int32, (2, 2), 0) == 1
    row = 2 * HID + 20
    o_ms[...] = jnp.where(second, gc[0, row : row + 1, 0:2], gc[1, row : row + 1, 0:2])
    gae[0:OBS, :] = gas[0:OBS, :]
    gae[OBS : OBS + 2 * ACT, :] = gas[20 : 20 + 2 * ACT, :]
    gab[0:3, :] = gas[17:20, :]
    gab[3:4, :] = rows_a[30:31, :]
    o_ae[...], o_aem[...], o_aev[...] = adamw(ae[...], gae[0:29, :] * scale, aem[...], aev[...])
    o_ab[...], o_abm[...], o_abv[...] = adamw(ab[...], gab[0:4, :] * scale, abm[...], abv[...])
    o_as[...] = rows_a[21:22, 0:2]
    for r in (o_e, o_b, o_em, o_ev, o_bm, o_bv, o_ae, o_ab, o_aem, o_aev, o_abm, o_abv, o_ms, o_as):
        put(write(r))
    for at in order[1:]:
        do_matrix(*at)
    for k in range(2):
        for copy in actor_matrix(k):
            copy.wait()
        grad = ga[k * HID : (k + 1) * HID, :] * scale
        o_ah[k], o_ahm[k], o_ahv[k] = adamw(ah[k], grad, ahm[k], ahv[k])
        for r in (o_ah, o_ahm, o_ahv):
            put(write(r, k, lambda x: x.at[k]))
    for copy in writes:
        copy.wait()


def update(grads, own, online, moments, aparams, amoments):
    shape = lambda *s: jax.ShapeDtypeStruct(s, F32)
    e_, h_, b_ = shape(2, 24, HID), shape(2, 2, HID, HID), shape(2, 4, HID)
    ae_, ah_, ab_ = shape(29, HID), shape(2, HID, HID), shape(4, HID)
    outs = (e_, h_, b_, e_, e_, h_, h_, b_, b_, ae_, ah_, ab_, ae_, ae_, ah_, ah_, ab_, ab_, shape(2, 2), shape(1, 2))
    args = (*grads, *own, *online, *moments, *aparams, *amoments)
    anyspace = pl.BlockSpec(memory_space=pl.ANY)
    room = [pltpu.VMEM(a.shape, a.dtype) for a in args]
    return pl.pallas_call(
        update_kernel,
        out_shape=outs,
        in_specs=[anyspace] * len(args),
        out_specs=(anyspace,) * len(outs),
        scratch_shapes=room
        + [pltpu.VMEM(o.shape, o.dtype) for o in outs]
        + [pltpu.VMEM((24, HID), F32), pltpu.VMEM((8, HID), F32), pltpu.VMEM((32, HID), F32), pltpu.VMEM((8, HID), F32)]
        + [pltpu.SemaphoreType.DMA((len(args), 5)), pltpu.SemaphoreType.DMA((len(outs), 4))],
        compiler_params=pltpu.CompilerParams(vmem_limit_bytes=40 * 2**20),
        name="adamw",
    )(*args)


def body(
    n_dp,
    states, actions, rewards, done, noise, counts,
    crit_edge, crit_hidden, crit_bias, edge_m, edge_v, hidden_m, hidden_v, bias_m, bias_v,
    act_edge, act_hidden, act_bias, act_edge_m, act_edge_v, act_hidden_m, act_hidden_v, act_bias_m, act_bias_v,
):
    size = states.shape[0]
    own = (crit_edge[0], crit_hidden[0], crit_bias[0])
    aparams = (act_edge, act_hidden, act_bias)
    data = (states.T, actions.T, noise.T, rewards[None], done[None], counts)
    moments = (edge_m, edge_v, hidden_m, hidden_v, bias_m, bias_v)
    amoments = (act_edge_m, act_edge_v, act_hidden_m, act_hidden_v, act_bias_m, act_bias_v)
    rows = FOLD_ROWS if size > FOLD_ROWS else size
    grad_c, grad_a, *online = fused(n_dp, rows, rows // 2, True, (*data, rewards[None]), own, aparams)

    def finish(grad_c, grad_a):
        return update((grad_c, grad_a), own, online, moments, aparams, amoments)

    def with_rest():
        z = lax.axis_index("dp")
        partner = lax.ppermute(counts, "dp", [(k, n_dp - 1 - k) for k in range(n_dp)])
        at = jnp.arange(size, dtype=jnp.int32)
        taken = (rows // LANES - 1 - (at - rows) // LANES) * LANES >= (jnp.minimum(partner, rows) + LANES - 1) // LANES * LANES
        taken = jnp.where(z >= n_dp - n_dp // 2, taken, False)
        left = jnp.logical_and(jnp.logical_and(at >= rows, at < counts), jnp.logical_not(taken))
        more_c, more_a, *_ = fused(n_dp, size, size // 16, False, (*data, left.astype(F32)[None]), own, aparams)
        return finish(grad_c + more_c, grad_a + more_a)

    sums = grad_c[1, 2 * HID + 21]
    out = lax.cond(sums[1] != sums[2], with_rest, lambda: finish(grad_c, grad_a))
    return (*(o[None] for o in out[:3]), *out[3:19], out[19][0])


def solution(mesh):
    member = P("grp", "ens", None, None)
    hidden = P("grp", "ens", None, None, None)
    mom = P("ens", None, None)
    mom_h = P("ens", None, None, None)
    return jax.shard_map(
        functools.partial(body, mesh.shape["dp"]),
        mesh=mesh,
        in_specs=(
            P("dp", None), P("dp", None), P("dp"), P("dp"), P("dp", None), P("dp"),
            member, hidden, member, mom, mom, mom_h, mom_h, mom, mom,
        ) + (P(),) * 9,
        out_specs=(member, hidden, member, mom, mom, mom_h, mom_h, mom, mom) + (P(),) * 9 + (P("ens", None), P()),
        check_vma=False,
    )
```

```python
import functools

import jax
import jax.numpy as jnp
from jax import lax
from jax.experimental import pallas as pl
from jax.experimental.pallas import tpu as pltpu
from jax.sharding import PartitionSpec as P

OBS = 17
ACT = 6
HID = 256
STEP = 5
FOLD_ROWS = 2816
LANES = 128

GAMMA = 0.99
ALPHA = 0.2
ETA = 1.0
LEARN = 0.03
BETA_ONE = 0.5
BETA_TWO = 0.5
DECAY = 0.01
EPS = 1e-08
TAU = 0.05
HALF_LOG_TWO_PI = 0.9189385332046727
LOG_TWO = 0.6931471805599453

F32 = jnp.float32
BF16 = jnp.bfloat16

CRITIC_SMALL, ACTOR_SMALL = 32, 32


def dot(a, b):
    return lax.dot_general(a, b, (((1,), (0,)), ((), ())), preferred_element_type=F32)


def dot_t(a, b):
    return lax.dot_general(a, b, (((1,), (1,)), ((), ())), preferred_element_type=F32)


def split(w):
    high = w.astype(BF16).astype(F32)
    return high, w - high


def halves(p):
    n = p.shape[0] // 2
    return p[:n] + p[n:]


def prep_input(stage, w1, edge, bias, n_in):
    stage[...] = jnp.zeros_like(stage)
    stage[0:OBS, :] = edge[0:OBS, :]
    stage[OBS : OBS + 1, :] = bias[0:1, :]
    if n_in > OBS:
        stage[24 : 24 + ACT, :] = edge[OBS : OBS + ACT, :]
    high, low = split(0.5 * stage[0:32, :])
    w1[...] = jnp.concatenate([high, low, high], 0).T.astype(BF16)


def prep_hidden(fwd, bwd, hidden):
    w = 0.5 * hidden
    if fwd is not None:
        high, low = split(w.T)
        fwd[...] = jnp.concatenate([high, low], 0).astype(BF16)
    if bwd is not None:
        high, low = split(w)
        bwd[...] = jnp.concatenate([high, low], 0).astype(BF16)


def silu_half(u):
    t = jnp.tanh(u)
    return u + u * t, t


def up(n, by):
    return -(-n // by) * by


def kernel(
    n_dp,
    rows,
    block,
    fold,
    states, actions, noise, rewards, done, counts, mask, c_edge, c_hidden, c_bias, a_edge, a_hidden, a_bias,
    out_c, out_a, out_small, out_high, out_rest, out_low,
    xs, ns, eps_s, far_x, far_e, here_x, here_e, x_b, pi_act, stage, vec, tvec, avec,
    small_out, small_in, high_out, high_in, rest_out, rest_in, low_out, low_in,
    w1, f0, f1, b0, b1, ga, t1w, eq, pw, pv, pq, pg, pf, pb,
    tw1, tf0, tf1, teq,
    aw1, af0, af1, ab0, ab1, ao, aot,
    h1x, h2x, h3s, s1, s2, s3, k1, k2, k3, d1s, d2s, d3s,
    heads, ah1x, ah2x, ah3, as1, as2, as3,
    value, unit_f, u_mine, u_peer, u_pair, u_far, u_total, dg_b, dv_b, dvh, row_sums,
    q_mine, q_peer, q_pair, q_far, q_total, least, far_least, least_in,
    acc_h1, acc_h1t, acc_h0, acc_h0t, acc_x, acc_t, acc_last, acc_o, acc_c1, acc_c0, acc_cx, actor_rows,
    part_c, part_a, sum_c, sum_a, in_h1, in_h0, in_sm, in_ac,
    fold_s, fold_r, sem_far_s, sem_far_r, sem_param_s, sem_param_r, sem_least_s, sem_least_r, es_s, es_r,
    rs_s, rs_r, ag_s, ag_r, xf_s, xf_r, ef_s, ef_r, sem_out, *boxes,
):
    g = lax.axis_index("grp")
    e = lax.axis_index("ens")
    z = lax.axis_index("dp")
    me = g * 4 + e
    blocks = rows // block
    extra = states.shape[1] - rows
    lower = z < n_dp // 2
    upper = z >= n_dp - n_dp // 2
    half = rows // 2
    online = g == 1
    targetd = g == 0
    critics = 8
    coded = bool(boxes)

    def dev(gg, ee):
        return {"grp": gg, "ens": ee}

    def remote(src, dst, send, recv, where):
        return pltpu.make_async_remote_copy(
            src_ref=src, dst_ref=dst, send_sem=send, recv_sem=recv, device_id=where, device_id_type=pl.DeviceIdType.MESH
        )

    barrier = pltpu.get_barrier_semaphore()
    for k in range(1, 8):
        p = lax.rem(me + k, 8)
        pl.semaphore_signal(barrier, inc=1, device_id=dev(p // 4, lax.rem(p, 4)), device_id_type=pl.DeviceIdType.MESH)
    for k in range(1, n_dp):
        pl.semaphore_signal(barrier, inc=1, device_id={"dp": lax.rem(z + k, n_dp)}, device_id_type=pl.DeviceIdType.MESH)

    def all_here():
        pl.semaphore_wait(barrier, 7 + n_dp - 1)

    def param_copy(what):
        src, dst = (
            (small_out.at[0:32], small_in.at[0:32]),
            (high_out, high_in),
            (rest_out, rest_in),
            (low_out, low_in),
            (small_out.at[32:64], small_in.at[32:64]),
        )[what]
        return remote(src, dst, sem_param_s.at[what], sem_param_r.at[what], dev(0, e))

    @pl.when(online)
    def _():
        small_out[...] = jnp.zeros_like(small_out)
        for k in range(2):
            small_out[32 * k : 32 * k + 24, :] = c_edge[1 - k]
            small_out[32 * k + 24 : 32 * k + 28, :] = c_bias[1 - k]
            high, low = split(c_hidden[1, k])
            high_out[k * HID : (k + 1) * HID, :] = high.astype(BF16)
            rest_out[k * HID : (k + 1) * HID, :] = low.astype(BF16)
            low_out[k * HID : (k + 1) * HID, :] = c_hidden[0, k].astype(BF16)
        all_here()
        for what in range(3):
            param_copy(what).start()

    lane_id = lax.broadcasted_iota(jnp.int32, (1, states.shape[1]), 1)
    if fold:
        code = jnp.where(lane_id < counts[0], 2.0, 0.0) + done[...].astype(F32)
    else:
        code = 2.0 * mask[...] + done[...].astype(F32)

    ones_row = jnp.ones((1, states.shape[1]), F32)
    xs[...] = jnp.zeros_like(xs)
    xs[0:OBS, :] = states[0:OBS, :]
    xs[OBS : OBS + 1, :] = ones_row
    xs[24 : 24 + ACT, :] = actions[...]
    eps_s[6:7, :] = rewards[...]
    eps_s[7:8, :] = code

    @pl.when(online)
    def _():
        eps_s[0:ACT, :] = noise[0:ACT, :]

    @pl.when(targetd)
    def _():
        eps_s[0:ACT, :] = noise[ACT : 2 * ACT, :]
        ns[...] = jnp.zeros_like(ns)
        ns[0:OBS, :] = states[OBS : 2 * OBS, :]
        ns[OBS : OBS + 1, :] = ones_row

    core = lax.rem(e, 2)
    other_core = e + 1 - 2 * core
    far_chip = lax.rem(e + 2, 4)

    def fold_copy(what, hop):
        here, there = ((here_e, far_e), (here_x, far_x))[what]
        if hop == 0:
            return remote(here.at[core], there.at[core], fold_s.at[what, 0], fold_r.at[what, 0], {"dp": n_dp - 1 - z})
        return remote(there.at[core], there.at[core], fold_s.at[what, 1], fold_r.at[what, 1], dev(g, other_core))

    def least_copy():
        return remote(least.at[:, rows:], far_least, sem_far_s, sem_far_r, {"dp": n_dp - 1 - z})

    def merge(into, blocks_of):
        first = rows - extra
        there = jnp.concatenate([blocks_of(b) for b in range(extra // LANES - 1, -1, -1)], 1).astype(F32)
        lanes = lax.broadcasted_iota(jnp.int32, (1, extra), 1) + first
        bound = (jnp.minimum(counts[0], rows) + LANES - 1) // LANES * LANES
        into[:, first:rows] = jnp.where(lanes < bound, into[:, first:rows], there)

    def in_halves(pieces):
        per = extra // LANES // 2
        return lambda b: pieces[b // per, :, (b % per) * LANES : (b % per + 1) * LANES]

    def fold_out():
        if fold:
            @pl.when(upper)
            def _():
                for h in range(2):
                    part = slice(rows + h * extra // 2, rows + (h + 1) * extra // 2)
                    here_e[h] = eps_s[:, part]
                    here_x[h] = xs[:, part].astype(BF16)
                for what in range(2):
                    fold_copy(what, 0).start()

    def fold_in():
        if fold:
            @pl.when(lower)
            def _():
                for what in range(2):
                    fold_copy(what, 0).wait_recv()
                    fold_copy(what, 1).start()
                for what in range(2):
                    fold_copy(what, 1).wait_recv()
                merge(eps_s, in_halves(far_e))
                merge(xs, in_halves(far_x))

    def put_x():
        high, low = split(xs[:, 0:rows])
        xin = high.astype(BF16)
        x_b[0:32, :] = xin
        x_b[32:64, :] = xin
        x_b[64:96, :] = low.astype(BF16)

    def prep_small(edge, bias, w1_, vec_, eq_, ga_, t1_):
        prep_input(stage, w1_, edge, bias, OBS + ACT)
        stage[...] = jnp.zeros_like(stage)
        stage[0:1, :] = 0.5 * bias[1:2, :]
        stage[1:2, :] = 0.5 * bias[2:3, :]
        stage[2:3, :] = edge[23:24, :]
        vec_[...] = stage[...].T
        vec_[0:1, 8:9] = bias[3:4, 0:1]
        stage[...] = jnp.zeros_like(stage)
        high, low = split(edge[23:24, :])
        stage[0:1, :] = high
        stage[1:2, :] = low
        eq_[...] = stage[0:16, :].astype(BF16)
        if ga_ is not None:
            stage[...] = jnp.zeros_like(stage)
            stage[0:ACT, :] = 0.5 * edge[OBS : OBS + ACT, :]
            high, low = split(stage[0:8, :])
            both = jnp.concatenate([high, low], 0)
            ga_[...] = both.astype(BF16)
            stage[0:16, :] = both
            if t1_ is not None:
                t1_[...] = stage[...].T[:, 0:16].astype(BF16)

    def prep_actor():
        prep_input(stage, aw1, a_edge, a_bias, OBS)
        prep_hidden(af0, ab0, a_hidden[0])
        prep_hidden(af1, ab1, a_hidden[1])
        stage[...] = jnp.zeros_like(stage)
        stage[0:1, :] = 0.5 * a_bias[1:2, :]
        stage[1:2, :] = 0.5 * a_bias[2:3, :]
        stage[2:3, :] = a_bias[3:4, :]
        avec[...] = stage[...].T
        stage[...] = jnp.zeros_like(stage)
        stage[0:ACT, :] = a_edge[OBS : OBS + ACT, :]
        stage[8 : 8 + ACT, :] = a_edge[OBS + ACT : OBS + 2 * ACT, :]
        high, low = split(stage[0:16, :])
        ao[...] = jnp.concatenate([high, low], 0).astype(BF16)
        stage[...] = jnp.zeros_like(stage)
        stage[0 : 2 * ACT, :] = a_edge[OBS : OBS + 2 * ACT, :]
        high, low = split(stage[0:16, :])
        stage[0:32, :] = jnp.concatenate([high, low], 0)
        aot[...] = stage[...].T[:, 0:32].astype(BF16)

    prep_actor()

    def actor_layers(src):
        kept = []
        hb = None
        for w, b in ((aw1, None), (af0, 0), (af1, 1)):
            u = dot(w[...], src) if b is None else halves(dot(w[...], hb)) + avec[:, b : b + 1]
            h, t = silu_half(u)
            hb = h.astype(BF16)
            kept.append((hb, h, t))
        return kept

    ok8 = (lax.broadcasted_iota(jnp.int32, (8, 1), 0) < ACT).astype(F32)

    def actor_heads(hb, sl):
        out = halves(dot(ao[...], hb))
        eps = eps_s[:, sl]
        center = out[0:8] + avec[0:8, 2:3] * ok8
        th = jnp.tanh(out[8:16] + avec[6:14, 2:3] * ok8)
        log_std = 3.5 * th - 1.5
        spread_e = jnp.exp(log_std) * eps
        latent = center + spread_e
        soft = jnp.maximum(-2.0 * latent, 0.0) + jnp.log(1.0 + jnp.exp(-2.0 * jnp.abs(latent)))
        terms = -0.5 * eps * eps - log_std - HALF_LOG_TWO_PI - 2.0 * (LOG_TWO - latent - soft)
        logp = jnp.sum(terms * ok8, axis=0, keepdims=True)
        sample = jnp.tanh(latent) * ok8
        return sample, logp, th, spread_e

    actor_rows[...] = jnp.zeros_like(actor_rows)

    put_x()

    @pl.when(online)
    def _():
        fold_out()
        prep_small(c_edge.at[0], c_bias.at[0], w1, vec, eq, ga, t1w)
        prep_hidden(f0, b0, c_hidden[0, 0])
        prep_hidden(f1, b1, c_hidden[0, 1])
        for k, (fwd, bwd) in enumerate(((f0, b0), (f1, b1))):
            pf[0, k] = fwd[0:HID, :]
            pb[0, k] = bwd[0:HID, :]
            w = 0.5 * c_hidden[1, k]
            pf[1, k] = w.T.astype(BF16)
            pb[1, k] = w.astype(BF16)
        pw[0], pv[0], pq[0], pg[0] = w1[...], vec[...], eq[...], ga[...]
        prep_small(c_edge.at[1], c_bias.at[1], pw.at[1], pv.at[1], pq.at[1], pg.at[1], None)

    def least_online(k):
        return remote(least.at[:, 0:rows], least_in.at[k], sem_least_s.at[4 + k], sem_least_r.at[k], dev(1, lax.rem(e + k, 4)))

    def least_target(k):
        return remote(least.at[:, 0:rows], least_in.at[k], sem_least_s.at[k], sem_least_r.at[k], dev(0, lax.rem(e + k, 4)))

    def half_hidden(part, values):
        to = slice(part * HID, (part + 1) * HID)
        for k, (fwd, bwd) in enumerate(((f0, b0), (f1, b1))):
            w = 0.5 * values[k * HID : (k + 1) * HID, :].astype(F32)
            fwd[to, :] = w.T.astype(BF16)
            bwd[to, :] = w.astype(BF16)

    @pl.when(targetd)
    def _():
        for m in range(2):
            prep_small(c_edge.at[m], c_bias.at[m], tw1.at[m], tvec.at[m], teq.at[m], None, None)
            prep_hidden(tf0.at[m], None, c_hidden[m, 0])
            prep_hidden(tf1.at[m], None, c_hidden[m, 1])

        def body(i, _):
            @pl.when(i == 1)
            def _():
                all_here()
                fold_out()

            first = jnp.minimum(i * block, states.shape[1] - block)
            sl = pl.ds(pl.multiple_of(first, LANES), block)
            high, rest = split(ns[:, sl])
            nx, rest = high.astype(BF16), rest.astype(BF16)
            kept = actor_layers(jnp.concatenate([nx, nx, rest], 0))
            sample, logp, th, spread_e = actor_heads(kept[2][0], sl)
            high, rest = split(jnp.concatenate([ns[0:24, sl], sample], 0))
            nx = high.astype(BF16)
            nx = jnp.concatenate([nx, nx, rest.astype(BF16)], 0)
            low = None
            for m in range(2):
                h, t = silu_half(dot(tw1[m], nx))
                h, t = silu_half(halves(dot(tf0[m], h.astype(BF16))) + tvec[m, :, 0:1])
                h, t = silu_half(halves(dot(tf1[m], h.astype(BF16))) + tvec[m, :, 1:2])
                r = dot(teq[m], h.astype(BF16))
                q = r[0:1] + r[1:2] + tvec[m, 0:1, 8:9]
                low = q if low is None else jnp.minimum(low, q)
            least[:, sl] = low - ALPHA * logp
            return 0

        lax.fori_loop(0, blocks + (jnp.where(upper, 1, 0) if fold else 0), body, 0)
        if fold:
            @pl.when(upper)
            def _():
                least_copy().start()

        fold_in()
        if fold:
            put_x()
        param_copy(0).wait_recv()
        prep_small(small_in.at[0:24], small_in.at[24:32], w1, vec, eq, ga, t1w)
        param_copy(1).wait_recv()
        half_hidden(0, high_in)
        param_copy(2).wait_recv()
        half_hidden(1, rest_in)

    def least_out():
        @pl.when(targetd)
        def _():
            if fold:
                @pl.when(lower)
                def _():
                    least_copy().wait_recv()
                    merge(least, lambda b: far_least[:, b * LANES : (b + 1) * LANES])

            for k in range(1, 4):
                least_target(k).start()
            for k in range(4):
                least_online(k).start()

    class EnsembleSum:
        def __init__(self, index, mine, peer, pair, far, total, only_online):
            self.index, self.mine, self.peer, self.pair, self.far, self.total = index, mine, peer, pair, far, total
            self.chips = (1,) if only_online else (0, 1, 2)

        def to_core(self):
            return remote(self.mine.at[1 - core], self.peer, es_s.at[self.index, 0], es_r.at[self.index, 0], dev(g, other_core))

        def to_chip(self, k):
            across = (1 - g, g, 1 - g)[k]
            where = dev(across, (e, far_chip, far_chip)[k])
            return remote(self.pair, self.far.at[k], es_s.at[self.index, 1 + k], es_r.at[self.index, 1 + k], where)

        def back(self):
            return remote(self.total.at[core], self.total.at[core], es_s.at[self.index, 4], es_r.at[self.index, 4], dev(g, other_core))

        def begin(self, first, second):
            self.mine[0] = first
            self.mine[1] = second
            self.to_core().start()

        def middle(self):
            self.to_core().wait_recv()
            self.pair[...] = self.mine[core] + self.peer[...]
            for k in self.chips:
                self.to_chip(k).start()

        def first_to_core(self, h, values):
            self.mine[h] = values

            @pl.when(core != h)
            def _():
                self.to_core().start()

            @pl.when(core == h)
            def _():
                self.middle()

        def last_of(self, h):
            @pl.when(core == h)
            def _():
                self.last()

        def back_of(self, h):
            @pl.when(core != h)
            def _():
                self.back().wait_recv()

        def last(self):
            total = self.pair[...]
            for k in self.chips:
                self.to_chip(k).wait_recv()
                total = total + self.far[k]
            self.total[core] = total
            self.back().start()

        def whole(self):
            self.back().wait_recv()
            return jnp.concatenate([self.total[0], self.total[1]], 1)

        def sent(self):
            self.to_core().wait_send()
            for k in self.chips:
                self.to_chip(k).wait_send()
            self.back().wait_send()

    unit_sum = EnsembleSum(0, u_mine, u_peer, u_pair, u_far, u_total, False)
    slope_sum = EnsembleSum(1, q_mine, q_peer, q_pair, q_far, q_total, True)

    rid = lax.broadcasted_iota(jnp.int32, (8, 1), 0)

    @pl.when(online)
    def _():
        def body_p(i, _):
            sl = pl.ds(pl.multiple_of(i * block, block), block)

            @pl.when(i == 1)
            def _():
                fold_in()
                if fold:
                    put_x()

            kept = actor_layers(x_b[:, sl])
            if fold:
                for store, curve, (hb, h, t) in zip((ah1x, ah2x, ah3), (as1, as2, as3), kept):
                    store[0:HID, sl] = hb
                    curve[:, sl] = (1.0 + t) + h * (1.0 - t)
            sample, logp, th, spread_e = actor_heads(kept[2][0], sl)
            pi_act[:, sl] = sample
            heads[0:8, sl] = th
            heads[8:16, sl] = spread_e
            heads[16:17, sl] = logp
            pin = jnp.concatenate([xs[0:24, sl], sample], 0).astype(BF16)
            unit_f[16:24, sl] = jnp.zeros((8, block), F32)

            def member(m, _):
                def act(u):
                    h, t = silu_half(u)
                    hb, tb = h.astype(BF16), t.astype(BF16)
                    one = jnp.ones((), BF16)
                    return hb, (one + tb) + hb * (one - tb)

                h, a1 = act(dot(pw[m][:, 0:64], jnp.concatenate([pin, pin], 0)))
                h, a2 = act(dot(pf[m, 0], h) + pv[m][:, 0:1])
                h, a3 = act(dot(pf[m, 1], h) + pv[m][:, 1:2])
                r = dot(pq[m], h)
                q = r[0:1] + r[1:2] + pv[m][0:1, 8:9]
                d = pv[m][:, 2:3].astype(BF16) * a3
                d = dot(pb[m, 1], d).astype(BF16) * a2
                d = dot(pb[m, 0], d).astype(BF16) * a1
                unit_f[16:24, sl] += halves(dot(pg[m], d)) + jnp.where(rid == 6, q, 0.0)
                return 0

            lax.fori_loop(0, 2, member, 0)
            return 0

        lax.fori_loop(0, blocks, body_p, 0)
        slope_sum.begin(unit_f[16:24, 0:half], unit_f[16:24, half:rows])

    ones = (lax.broadcasted_iota(jnp.int32, (16, rows), 0) == 0).astype(BF16)
    h1x[HID : HID + 16, :] = ones
    h2x[HID : HID + 16, :] = ones

    def curves(u):
        h, t = silu_half(u)
        c = 1.0 + t
        d = 1.0 - t
        return h, c + h * d, (c * d) * (1.0 - u * t)

    valid = jnp.where(eps_s[7:8, 0:rows] > 1.5, 1.0, 0.0)

    def body_a(i, _):
        @pl.when(i == 1)
        def _():
            @pl.when(online)
            def _():
                slope_sum.middle()

            if fold:
                unit_sum.first_to_core(0, unit_f[0:8, 0:half])
            least_out()

        sl = pl.ds(pl.multiple_of(i * block, block), block)
        h, a1, q1 = curves(dot(w1[...], x_b[:, sl]))
        hb = h.astype(BF16)
        h1x[0:HID, sl] = hb
        s1[:, sl] = a1.astype(BF16)
        h, a2, q2 = curves(halves(dot(f0[...], hb)) + vec[:, 0:1])
        hb = h.astype(BF16)
        h2x[0:HID, sl] = hb
        s2[:, sl] = a2.astype(BF16)
        h, a3, q3 = curves(halves(dot(f1[...], hb)) + vec[:, 1:2])
        hb = h.astype(BF16)
        h3s[:, sl] = hb
        s3[:, sl] = a3.astype(BF16)
        r = dot(eq[...], hb)
        value[:, sl] = r[0:1] + r[1:2] + vec[0:1, 8:9]
        last = vec[:, 2:3]
        db = (last * a3).astype(BF16)
        d3s[:, sl] = db
        k3[:, sl] = (last * q3).astype(BF16)
        m = halves(dot(b1[...], db))
        db = (m * a2).astype(BF16)
        d2s[:, sl] = db
        k2[:, sl] = (m * q2).astype(BF16)
        m = halves(dot(b0[...], db))
        db = (m * a1).astype(BF16)
        d1s[:, sl] = db
        k1[:, sl] = (m * q1).astype(BF16)
        slope = halves(dot(ga[...], db))
        inv = lax.rsqrt(jnp.sum(slope * slope, axis=0, keepdims=True) + 0.01)
        unit_f[0:8, sl] = slope * inv
        unit_f[8:9, sl] = inv
        return 0

    lax.fori_loop(0, blocks, body_a, 0)
    if fold:
        unit_sum.first_to_core(1, unit_f[0:8, half:rows])
        unit_sum.last_of(0)
    else:
        unit_sum.begin(unit_f[0:8, 0:half], unit_f[0:8, half:rows])
        unit_sum.middle()

    @pl.when(online)
    def _():
        for what in (3, 4):
            param_copy(what).start()


    class Exchange:
        def __init__(self, index, part, into, inbox, base, count, wide):
            self.index, self.part, self.into, self.inbox, self.base, self.count, self.wide = index, part, into, inbox, base, count, wide
            self.each = count // (n_dp * (4 if wide else 1))

        def rows_of(self, shard):
            first = self.base + (e * n_dp + shard if self.wide else shard) * self.each
            return pl.ds(pl.multiple_of(first, 8), self.each)

        def scatter(self, k):
            to = lax.rem(z + k, n_dp)
            return remote(
                self.part.at[self.rows_of(to)], self.inbox.at[k - 1], rs_s.at[self.index, k - 1, 0], rs_r.at[self.index, k - 1, 0], {"dp": to}
            )

        def gather(self, k):
            mine = self.into.at[self.rows_of(z)]
            return remote(mine, mine, ag_s.at[self.index, k - 1, 0], ag_r.at[self.index, k - 1, 0], {"dp": lax.rem(z + k, n_dp)})

        def across(self, k):
            there = self.into.at[self.rows_of(lax.rem(z + n_dp - k, n_dp))]
            return remote(there, there, xf_s.at[self.index, k, 0], xf_r.at[self.index, k, 0], dev(1 - g, e))

        def start(self):
            for k in range(1, n_dp):
                self.scatter(k).start()

        def reduce(self, along=True):
            total = self.part[self.rows_of(z), :]
            for k in range(1, n_dp):
                self.scatter(k).wait_recv()
                total = total + self.inbox[k - 1]
            self.into[self.rows_of(z), :] = total
            if along:
                for k in range(1, n_dp):
                    self.gather(k).start()
            self.across(0).start()

        def forward(self):
            for k in range(1, n_dp):
                self.gather(k).wait_recv()
                self.across(k).start()

        def sent(self):
            for k in range(1, n_dp):
                self.scatter(k).wait_send()
                self.gather(k).wait_send()
            for k in range(n_dp):
                self.across(k).wait_send()

        def arrived(self):
            for k in range(n_dp):
                self.across(k).wait_recv()

        def detour(self):
            self.across(0).wait_recv()
            for k in range(1, n_dp):
                self.gather(k).start()

        def back(self):
            for k in range(1, n_dp):
                self.across(k).wait_recv()

        def sent_detour(self):
            @pl.when(online)
            def _():
                for k in range(1, n_dp):
                    self.scatter(k).wait_send()
                self.across(0).wait_send()

            @pl.when(targetd)
            def _():
                for k in range(1, n_dp):
                    self.gather(k).wait_send()
                    self.across(k).wait_send()

    class Coded(Exchange):
        def __init__(self, index, part, out, base, count, lead, wide, boxes):
            self.index, self.part, self.out, self.base, self.count, self.lead, self.wide = index, part, out, base, count, lead, wide
            self.out_w, self.out_s, self.in_w, self.in_s, self.all_w, self.all_s = boxes
            self.each = count // (n_dp * (4 if wide else 1))

        def pack(self, x):
            top = jnp.maximum(jnp.max(jnp.abs(x), axis=0, keepdims=True), 1e-30)
            q = jnp.round(x * (32767.0 / top)).astype(jnp.int32)
            h = self.each // 2
            return jnp.bitwise_or(jnp.bitwise_and(q[:h], 65535), jnp.left_shift(q[h:], 16)), top * (1.0 / 32767.0)

        def unpack(self, w, scale):
            low = jnp.right_shift(jnp.left_shift(w, 16), 16)
            high = jnp.right_shift(w, 16)
            return jnp.concatenate([low, high], 0).astype(F32) * scale

        def scatter(self, k):
            to = lax.rem(z + k, n_dp)
            return Both([
                remote(o.at[to], i.at[k - 1], rs_s.at[self.index, k - 1, q], rs_r.at[self.index, k - 1, q], {"dp": to})
                for q, (o, i) in enumerate(((self.out_w, self.in_w), (self.out_s, self.in_s)))
            ])

        def gather(self, k):
            return Both([
                remote(
                    a.at[self.lead, z], a.at[self.lead, z], ag_s.at[self.index, k - 1, q], ag_r.at[self.index, k - 1, q],
                    {"dp": lax.rem(z + k, n_dp)},
                )
                for q, a in enumerate((self.all_w, self.all_s))
            ])

        def across(self, k):
            there = lax.rem(z + n_dp - k, n_dp)
            return Both([
                remote(
                    a.at[self.lead, there], a.at[self.lead, there], xf_s.at[self.index, k, q], xf_r.at[self.index, k, q], dev(1 - g, e)
                )
                for q, a in enumerate((self.all_w, self.all_s))
            ])

        def start(self):
            for shard in range(n_dp):
                w, scale = self.pack(self.part[self.rows_of(shard), :])
                self.out_w[shard] = w
                self.out_s[shard] = scale
            for k in range(1, n_dp):
                self.scatter(k).start()

        def reduce(self, along=True):
            total = self.part[self.rows_of(z), :]
            for k in range(1, n_dp):
                self.scatter(k).wait_recv()
                total = total + self.unpack(self.in_w[k - 1], self.in_s[k - 1])
            w, scale = self.pack(total)
            self.all_w[self.lead, z] = w
            self.all_s[self.lead, z] = scale
            if along:
                for k in range(1, n_dp):
                    self.gather(k).start()
            self.across(0).start()

        def decode(self):
            for lead in range(self.all_w.shape[0]):
                for shard in range(n_dp):
                    x = self.unpack(self.all_w[lead, shard], self.all_s[lead, shard])
                    if self.wide:
                        first = (lead * n_dp + shard) * self.each
                        self.out[first : first + self.each, :] = x
                    else:
                        first = self.base + shard * self.each
                        self.out[lead, first : first + self.each, :] = x

    class Both:
        def __init__(self, copies):
            self.copies = copies

        def start(self):
            for c in self.copies:
                c.start()

        def wait_recv(self):
            for c in self.copies:
                c.wait_recv()

        def wait_send(self):
            for c in self.copies:
                c.wait_send()

    if coded:
        box_h1, box_h0, box_ac = boxes[0:6], boxes[6:12], boxes[12:18]
    if coded:
        ex_h1 = Coded(0, part_c, sum_c, HID, HID, g, False, box_h1)
        ex_h0 = Coded(1, part_c, sum_c, 0, HID, g, False, box_h0)
        ex_ac = Coded(3, part_a, sum_a, 0, 2 * HID, e, True, box_ac)
        ex_as = Exchange(4, part_a, sum_a, in_ac, 2 * HID, ACTOR_SMALL, False)
        actor = (ex_ac, ex_as)
    else:
        ex_h1 = Exchange(0, part_c, sum_c.at[g], in_h1, HID, HID, False)
        ex_h0 = Exchange(1, part_c, sum_c.at[g], in_h0, 0, HID, False)
        ex_ac = Exchange(3, part_a, sum_a, in_ac, 0, part_a.shape[0], True)
        actor = (ex_ac,)
    ex_sm = Exchange(2, part_c, sum_c.at[g], in_sm, 2 * HID, part_c.shape[0] - 2 * HID, False)

    def spread_actor(k):
        if coded:
            mine = ex_ac.all_w.at[e]
        else:
            quarter = part_a.shape[0] // 4
            mine = sum_a.at[pl.ds(pl.multiple_of(e * quarter, 8), quarter)]
        return remote(mine, mine, ef_s.at[k - 1], ef_r.at[k - 1], dev(g, lax.rem(e + k, 4)))

    def spread_scale(k):
        mine = ex_ac.all_s.at[e]
        return remote(mine, mine, ef_s.at[2 + k], ef_r.at[2 + k], dev(g, lax.rem(e + k, 4)))

    def spread_start():
        for k in range(1, 4):
            spread_actor(k).start()
            if coded:
                spread_scale(k).start()

    lane = lax.broadcasted_iota(jnp.int32, (1, HID), 1)
    rid32 = lax.broadcasted_iota(jnp.int32, (32, 1), 0)

    def local(src, dst, k):
        return pltpu.make_async_copy(src, dst, sem_out.at[k])

    def own_outputs():
        return (
            local(small_out, out_small, 0), local(high_out, out_high, 1), local(rest_out, out_rest, 2), local(low_out, out_low, 5),
        )

    def far_outputs():
        return local(small_in, out_small, 0), local(high_in, out_high, 1), local(rest_in, out_rest, 2), local(low_in, out_low, 5)

    @pl.when(online)
    def _():
        slope_sum.last()
        total = slope_sum.whole() * (1.0 / critics)
        d_sample = -valid * total
        d_logp = ALPHA * valid
        sample = pi_act[...]
        th = heads[0:8, :]
        spread_e = heads[8:16, :]
        dz = (d_sample * (1.0 - sample * sample) + d_logp * 2.0 * sample) * ok8
        dls = (dz * spread_e - d_logp) * (3.5 * (1.0 - th * th)) * ok8
        heads[24:40, :] = jnp.zeros((16, rows), F32)
        heads[24:30, :] = dz[0:ACT]
        heads[30:36, :] = dls[0:ACT]
        actor_sum = jnp.sum(valid * (ALPHA * heads[16:17, :] - total[6:7]), axis=1, keepdims=True)
        done_rows = jnp.sum(valid, axis=1, keepdims=True)
        count = counts[0].astype(F32) if fold else 0.0
        for acc in (acc_c1, acc_c0, acc_cx, acc_o):
            acc[...] = jnp.zeros_like(acc)
        one16 = (lax.broadcasted_iota(jnp.int32, (16, block), 0) == 0).astype(BF16)
        if fold:
            ah1x[HID : HID + 16, :] = h1x[HID : HID + 16, :]
            ah2x[HID : HID + 16, :] = h1x[HID : HID + 16, :]

        def body_c(i, _):
            sl = pl.ds(pl.multiple_of(i * block, block), block)
            if fold:
                tall1, tall2, top = ah1x[:, sl], ah2x[:, sl], ah3[:, sl]
                slopes = [as1[:, sl], as2[:, sl], as3[:, sl]]
            else:
                kept = actor_layers(x_b[:, sl])
                tall1, tall2 = (jnp.concatenate([kept[k][0], one16], 0) for k in range(2))
                top = kept[2][0]
                slopes = [(1.0 + t) + h * (1.0 - t) for _, h, t in kept]
            do = heads[24:40, sl].astype(BF16)
            acc_o[0:16, :] += dot_t(do, top)
            d3 = (dot(aot[...], jnp.concatenate([do, do], 0)) * (0.5 * slopes[2])).astype(BF16)
            acc_c1[...] += dot_t(tall2, d3)
            d2 = (halves(dot(ab1[...], d3)) * slopes[1]).astype(BF16)
            acc_c0[...] += dot_t(tall1, d2)
            d1 = (halves(dot(ab0[...], d2)) * slopes[0]).astype(BF16)
            acc_cx[...] += dot_t(x_b[0:32, sl], d1)
            acc_o[16:32, 0:128] += dot_t(one16, jnp.concatenate([do, jnp.zeros((112, block), BF16)], 0))
            return 0

        lax.fori_loop(0, blocks, body_c, 0)
        part_a[0:HID, :] = acc_c0[0:HID, :]
        part_a[HID : 2 * HID, :] = acc_c1[0:HID, :]
        actor_rows[0:1, :] = jnp.where(lane == 0, actor_sum, jnp.where(lane == 1, count, jnp.where(lane == 2, done_rows, 0.0)))
        actor_rows[1:2, :] = acc_o[16:17, :]
        first = 2 * HID
        part_a[first : first + 18, :] = acc_cx[0:18, :]
        part_a[first + 18 : first + 19, :] = acc_c0[HID : HID + 1, :]
        part_a[first + 19 : first + 20, :] = acc_c1[HID : HID + 1, :]
        part_a[first + 20 : first + 32, :] = acc_o[0 : 2 * ACT, :]
        part_a[first + 32 :, :] = jnp.zeros((part_a.shape[0] - first - 32, HID), F32)
        for ex in actor:
            ex.start()

    @pl.when(targetd)
    def _():
        least_in[0] = least[:, 0:rows]
        for k in range(1, 4):
            least_target(k).wait_recv()

    @pl.when(online)
    def _():
        for k in range(4):
            least_online(k).wait_recv()

    rid16 = lax.broadcasted_iota(jnp.int32, (16, 1), 0)

    def directions(sl, spread):
        code = eps_s[7:8, sl]
        valid = jnp.where(code > 1.5, 1.0, 0.0)
        low = jnp.minimum(
            jnp.minimum(least_in[0, :, sl], least_in[1, :, sl]), jnp.minimum(least_in[2, :, sl], least_in[3, :, sl])
        )
        target = eps_s[6:7, sl] + GAMMA * (1.0 + 2.0 * valid - code) * low
        unit = unit_f[0:8, sl]
        inv = unit_f[8:9, sl]
        d_unit = (2.0 * ETA / (critics - 1)) * valid * (spread - unit)
        along = jnp.sum(d_unit * unit, axis=0, keepdims=True)
        dg = (d_unit - unit * along) * inv
        gap = value[:, sl] - target
        dv = 2.0 * valid * gap
        row_sums[0:1, sl] = valid * gap * gap
        row_sums[1:2, sl] = valid * jnp.sum(unit * (spread - unit), axis=0, keepdims=True)
        row_sums[2:3, sl] = dv
        dvh[:, sl] = 0.5 * dv
        dgb = dg.astype(BF16)
        dg_b[:, sl] = jnp.concatenate([dgb, dgb], 0)
        dv_b[:, sl] = jnp.where(rid16 == 0, dv, jnp.where(rid16 == 1, 1.0, 0.0)).astype(BF16)

    if not fold:
        unit_sum.last()
        directions(slice(0, rows), unit_sum.whole())

    for acc in (acc_h1, acc_h1t, acc_h0, acc_h0t, acc_x, acc_t, acc_last):
        acc[...] = jnp.zeros_like(acc)

    def body_b1(i, _):
        sl = pl.ds(pl.multiple_of(i * block, block), block)
        if fold:
            @pl.when(i == 0)
            def _():
                unit_sum.back_of(0)

            @pl.when(i == 1)
            def _():
                unit_sum.last_of(1)
                unit_sum.back_of(1)

            directions(sl, u_total[i])
        tp = dot(t1w[...], dg_b[:, sl])
        k1[:, sl] = (k1[:, sl].astype(F32) * tp).astype(BF16)
        th1 = (s1[:, sl].astype(F32) * tp).astype(BF16)
        tp = halves(dot(f0[...], th1))
        k2[:, sl] = (k2[:, sl].astype(F32) * tp).astype(BF16)
        th2 = (s2[:, sl].astype(F32) * tp).astype(BF16)
        tp = halves(dot(f1[...], th2))
        th3 = (s3[:, sl].astype(F32) * tp).astype(BF16)
        d3 = d3s[:, sl]
        ap3 = (dvh[:, sl] * d3.astype(F32) + k3[:, sl].astype(F32) * tp).astype(BF16)
        k3[:, sl] = ap3
        rows_dv = dv_b[:, sl]
        last = dot_t(rows_dv, h3s[:, sl])
        lone = dot_t(rows_dv, th3)
        acc_last[...] += last[0:8] + jnp.where(rid == 0, lone[1:2], 0.0)
        h3s[:, sl] = th1
        acc_h1[...] += dot_t(h2x[:, sl], ap3)
        acc_h1t[...] += dot_t(th2, d3)
        return 0

    def body_b2(i, _):
        sl = pl.ds(pl.multiple_of(i * block, block), block)
        ah = halves(dot(b1[...], k3[:, sl]))
        ap2 = (s2[:, sl].astype(F32) * ah + k2[:, sl].astype(F32)).astype(BF16)
        k2[:, sl] = ap2
        acc_h0[...] += dot_t(h1x[:, sl], ap2)
        acc_h0t[...] += dot_t(h3s[:, sl], d2s[:, sl])
        return 0

    def body_b3(i, _):
        sl = pl.ds(pl.multiple_of(i * block, block), block)
        ah = halves(dot(b0[...], k2[:, sl]))
        ap1 = (s1[:, sl].astype(F32) * ah + k1[:, sl].astype(F32)).astype(BF16)
        acc_x[...] += dot_t(x_b[0:32, sl], ap1)
        acc_t[...] += dot_t(dg_b[:, sl], d1s[:, sl])
        return 0

    lax.fori_loop(0, blocks, body_b1, 0)
    part_c[HID : 2 * HID, :] = acc_h1[0:HID, :] + 0.5 * acc_h1t[...]
    ex_h1.start()

    @pl.when(online)
    def _():
        for ex in actor:
            ex.reduce(False)

    lax.fori_loop(0, blocks, body_b2, 0)
    part_c[0:HID, :] = acc_h0[0:HID, :] + 0.5 * acc_h0t[...]
    ex_h0.start()
    lax.fori_loop(0, blocks, body_b3, 0)
    errors, diverse, dv_sum = (jnp.sum(row_sums[k : k + 1, :], axis=1, keepdims=True) for k in range(3))
    stats = jnp.where(lane == 0, errors, jnp.where(lane == 1, diverse, 0.0))
    small = acc_x[...]
    small = small + jnp.where(rid32 == 18, acc_h0[HID : HID + 1, :], 0.0)
    small = small + jnp.where(rid32 == 19, acc_h1[HID : HID + 1, :], 0.0)
    small = small + jnp.where(rid32 == 20, stats, 0.0)
    small = small + jnp.where(rid32 == 21, actor_rows[0:1, :], 0.0) + jnp.where(rid32 == 30, actor_rows[1:2, :], 0.0)
    small = small + jnp.where(rid32 == 22, jnp.where(lane == 0, dv_sum, 0.0), 0.0)
    small = small + jnp.where(rid32 == 23, acc_last[0:1, :], 0.0)
    part_c[2 * HID : 2 * HID + 24, :] = small[0:24]
    part_c[2 * HID + 24 : 2 * HID + 32, :] = small[24:32] + 0.5 * acc_t[0:8, :]
    rest = part_c.shape[0] - 2 * HID - 32
    if rest:
        part_c[2 * HID + 32 :, :] = jnp.zeros((rest, HID), F32)
    ex_sm.start()

    @pl.when(targetd)
    def _():
        for ex in actor:
            ex.detour()

    ex_h1.reduce()
    ex_h0.reduce()
    ex_sm.reduce()

    @pl.when(targetd)
    def _():
        for ex in actor:
            ex.forward()
        spread_start()

    @pl.when(online)
    def _():
        for ex in actor:
            ex.back()
        spread_start()

    ex_h1.forward()

    ex_h0.forward()
    ex_sm.forward()


    @pl.when(online)
    def _():
        for copy in own_outputs():
            copy.start()

    @pl.when(targetd)
    def _():
        param_copy(3).wait_recv()
        param_copy(4).wait_recv()
        for copy in far_outputs():
            copy.start()

    def out_rows(first, last, k):
        return local(sum_c.at[:, first:last], out_c.at[:, first:last], k)

    copies = [out_rows(HID, 2 * HID, 4), local(sum_a, out_a, 3), out_rows(2 * HID, sum_c.shape[1], 6), out_rows(0, HID, 7)]
    ex_h1.arrived()
    if coded:
        ex_h1.decode()
    copies[0].start()
    for k in range(1, 4):
        spread_actor(k).wait_recv()
        if coded:
            spread_scale(k).wait_recv()
    if coded:
        ex_ac.decode()
    copies[1].start()
    ex_sm.arrived()
    copies[2].start()
    ex_h0.arrived()
    if coded:
        ex_h0.decode()
    copies[3].start()

    @pl.when(online)
    def _():
        for what in range(5):
            param_copy(what).wait_send()

    @pl.when(targetd)
    def _():
        for k in range(1, 4):
            least_target(k).wait_send()
        for k in range(4):
            least_online(k).wait_send()

    if fold:
        @pl.when(upper)
        def _():
            for what in range(2):
                fold_copy(what, 0).wait_send()

        @pl.when(lower)
        def _():
            for what in range(2):
                fold_copy(what, 1).wait_send()

        @pl.when(jnp.logical_and(upper, targetd))
        def _():
            least_copy().wait_send()

    unit_sum.sent()

    @pl.when(online)
    def _():
        slope_sum.sent()

    for ex in actor:
        ex.sent_detour()
    for k in range(1, 4):
        spread_actor(k).wait_send()
        if coded:
            spread_scale(k).wait_send()
    for ex in (ex_h1, ex_h0, ex_sm):
        ex.sent()
    for copy in copies:
        copy.wait()

    @pl.when(online)
    def _():
        for copy in own_outputs():
            copy.wait()

    @pl.when(targetd)
    def _():
        for copy in far_outputs():
            copy.wait()


def sizes(n_dp):
    return 2 * HID + up(CRITIC_SMALL, 8 * n_dp), up(2 * HID + ACTOR_SMALL, 32 * n_dp)


def fused(n_dp, rows, block, fold, data, own, aparams):
    v = pltpu.VMEM
    big = lambda n=HID: v((n, rows), BF16)
    dma = pltpu.SemaphoreType.DMA
    size_c, size_a = sizes(n_dp)
    coded = 2 * HID % (64 * n_dp) == 0
    h8 = lambda *n: v((*n, 8, rows // 2), F32)
    sums = [h8(2), h8(), h8(), h8(3), h8(2)]
    extra = (data[0].shape[1] - rows) // 2 if fold else LANES
    moved = [v((2, 32, extra), BF16), v((2, 8, extra), F32)]
    size = data[0].shape[1]
    kept = (lambda n, t: v((n, rows), t)) if fold else (lambda n, t: v((16, LANES), t))
    scratch = [
        v((32, size), F32), v((32, size), F32), v((8, size), F32), *moved, *moved,
        v((96, rows), BF16), v((8, rows), F32),
        v((128, HID), F32), v((HID, 128), F32), v((2, HID, 128), F32), v((HID, 128), F32),
        v((64, HID), F32), v((64, HID), F32), *[v((2 * HID, HID), BF16) for _ in range(6)],
        v((HID, 96), BF16), v((512, HID), BF16), v((512, HID), BF16), v((512, HID), BF16), v((512, HID), BF16),
        v((16, HID), BF16), v((HID, 16), BF16), v((16, HID), BF16),
        v((2, HID, 96), BF16), v((2, HID, 128), F32), v((2, 16, HID), BF16), v((2, 16, HID), BF16),
        v((2, 2, HID, HID), BF16), v((2, 2, HID, HID), BF16),
        v((2, HID, 96), BF16), v((2, 512, HID), BF16), v((2, 512, HID), BF16), v((2, 16, HID), BF16),
        v((HID, 96), BF16), v((512, HID), BF16), v((512, HID), BF16), v((512, HID), BF16), v((512, HID), BF16),
        v((32, HID), BF16), v((HID, 32), BF16),
        big(272), big(272), big(), big(), big(), big(), big(), big(), big(), big(), big(), big(),
        v((40, rows), F32), kept(272, BF16), kept(272, BF16), kept(HID, BF16), kept(HID, F32), kept(HID, F32), kept(HID, F32),
        v((1, rows), F32), v((24, rows), F32), *sums,
        v((16, rows), BF16), v((16, rows), BF16), v((1, rows), F32), v((8, rows), F32),
        *sums,
        v((1, size), F32), v((1, 2 * extra), F32), v((4, 1, rows), F32),
        v((272, HID), F32), v((HID, HID), F32), v((272, HID), F32), v((HID, HID), F32),
        v((32, HID), F32), v((16, HID), F32), v((8, HID), F32), v((32, HID), F32),
        v((272, HID), F32), v((272, HID), F32), v((32, HID), F32), v((8, HID), F32),
        v((size_c, HID), F32), v((size_a, HID), F32), v((2, size_c, HID), F32), v((size_a, HID), F32),
        *[v((1, 8, HID) if coded else (n_dp - 1, HID // n_dp, HID), F32) for _ in range(2)],
        v((n_dp - 1, (size_c - 2 * HID) // n_dp, HID), F32),
        v((n_dp - 1, (ACTOR_SMALL if coded else size_a // 4) // n_dp, HID), F32),
        dma((2, 2)), dma((2, 2)), dma, dma, dma((5,)), dma((5,)), dma((8,)), dma((4,)), dma((2, 5)), dma((2, 5)),
        dma((5, n_dp - 1, 2)), dma((5, n_dp - 1, 2)), dma((5, n_dp - 1, 2)), dma((5, n_dp - 1, 2)), dma((5, n_dp, 2)), dma((5, n_dp, 2)),
        dma((6,)), dma((6,)), dma((8,)),
    ]
    if coded:
        for each, lead in ((HID // n_dp, 2), (HID // n_dp, 2), (2 * HID // (4 * n_dp), 4)):
            word, scale = (each // 2, HID), (1, HID)
            for outer in ((n_dp,), (n_dp - 1,), (lead, n_dp)):
                scratch += [v((*outer, *word), jnp.int32), v((*outer, *scale), F32)]
    spec = pl.BlockSpec(memory_space=pltpu.VMEM)
    anyspace = pl.BlockSpec(memory_space=pl.ANY)
    shape = lambda *s: jax.ShapeDtypeStruct(s, F32)
    return pl.pallas_call(
        functools.partial(kernel, n_dp, rows, block, fold),
        out_shape=(
            shape(2, size_c, HID), shape(size_a, HID), shape(64, HID), *[jax.ShapeDtypeStruct((2 * HID, HID), BF16)] * 3,
        ),
        in_specs=[spec] * 5 + [pl.BlockSpec(memory_space=pltpu.SMEM)] + [spec] * 7,
        out_specs=(anyspace,) * 6,
        scratch_shapes=scratch,
        compiler_params=pltpu.CompilerParams(collective_id=0 if fold else 1, has_side_effects=True, vmem_limit_bytes=63 * 2**20),
        name="edac_gradients" if fold else "edac_rest",
    )(*data, *own, *aparams)


def adamw(param, grad, first, second):
    first_new = BETA_ONE * first + (1.0 - BETA_ONE) * grad
    second_new = BETA_TWO * second + (1.0 - BETA_TWO) * grad * grad
    scaled = second_new * (1.0 / (1.0 - BETA_TWO**STEP))
    root = scaled * lax.rsqrt(jnp.maximum(scaled, 1e-30)) + EPS
    inverse = pl.reciprocal(root, approx=True)
    inverse = inverse * (2.0 - root * inverse)
    ratio = first_new * (1.0 / (1.0 - BETA_ONE**STEP)) * inverse
    return (param - LEARN * (ratio + DECAY * param), first_new, second_new)


def update_kernel(*refs):
    n_in, n_out = 24, 20
    src, dst = refs[:n_in], refs[n_in : n_in + n_out]
    rest = refs[n_in + n_out :]
    buf, res = rest[:n_in], rest[n_in : n_in + n_out]
    ge, gb, gae, gab, sem_in, sem_out = rest[n_in + n_out :]
    gc, ga, own_e, own_h, own_b, on_s, on_high, on_rest, low_h, em, ev, hm, hv, bm, bv, ae, ah, ab, aem, aev, ahm, ahv, abm, abv = buf
    o_e, o_h, o_b, o_em, o_ev, o_hm, o_hv, o_bm, o_bv, o_ae, o_ah, o_ab, o_aem, o_aev, o_ahm, o_ahv, o_abm, o_abv, o_ms, o_as = res
    online = lax.axis_index("grp") == 1
    index = {id(b): k for k, b in enumerate(buf)}
    out_index = {id(r): k for k, r in enumerate(res)}

    def read(b, slot=0, at=lambda r: r):
        k = index[id(b)]
        return pltpu.make_async_copy(at(src[k]), at(b), sem_in.at[k, slot])

    def write(r, slot=0, at=lambda x: x):
        k = out_index[id(r)]
        return pltpu.make_async_copy(at(r), at(dst[k]), sem_out.at[k, slot])

    def matrix(m, k):
        rows = slice(k * HID, (k + 1) * HID)
        par = [read(low_h, k, lambda r: r.at[rows])] if m == 0 else [
            read(on_high, k, lambda r: r.at[rows]), read(on_rest, k, lambda r: r.at[rows])
        ]
        mine = [read(b, 2 * m + k, lambda r: r.at[m, k]) for b in (own_h, hm, hv)]
        return [read(gc, 2 * m + k, lambda r: r.at[1 - m, rows])] + par + mine

    def actor_matrix(k):
        rows = slice(k * HID, (k + 1) * HID)
        return [read(ga, k, lambda r: r.at[rows])] + [read(b, k, lambda r: r.at[k]) for b in (ah, ahm, ahv)]

    stats = read(gc, 4, lambda r: r.at[:, 2 * HID :])
    small_reads = [read(ga, 2, lambda r: r.at[2 * HID : 2 * HID + ACTOR_SMALL]), stats] + [
        read(b) for b in (own_e, own_b, on_s, em, ev, bm, bv, ae, ab, aem, aev, abm, abv)
    ]
    order = [(0, 0), (0, 1), (1, 0), (1, 1)]
    stats.start()
    for copy in matrix(*order[0]):
        copy.start()
    for copy in small_reads:
        if copy is not stats:
            copy.start()
    for at in order[1:]:
        for copy in matrix(*at):
            copy.start()
    for k in range(2):
        for copy in actor_matrix(k):
            copy.start()

    gas = ga.at[2 * HID : 2 * HID + ACTOR_SMALL]
    stats.wait()
    rows_a = gc.at[1, 2 * HID : 2 * HID + 32]
    scale = 1.0 / rows_a[21:22, 1:2]
    writes = []

    def put(copy):
        copy.start()
        writes.append(copy)

    def critic(own, param, grad, first, second):
        master, m_new, v_new = adamw(jnp.where(online, own, param), grad, first, second)
        polyak = TAU * master.astype(BF16).astype(F32) + (1.0 - TAU) * own
        return jnp.where(online, master, polyak), m_new, v_new

    def do_matrix(m, k):
        for copy in matrix(m, k):
            copy.wait()
        rows = slice(k * HID, (k + 1) * HID)
        param = low_h[rows, :].astype(F32) if m == 0 else on_high[rows, :].astype(F32) + on_rest[rows, :].astype(F32)
        o_h[m, k], o_hm[m, k], o_hv[m, k] = critic(own_h[m, k], param, gc[1 - m, rows, :] * scale, hm[m, k], hv[m, k])
        for r in (o_h, o_hm, o_hv):
            put(write(r, 2 * m + k, lambda x: x.at[m, k]))

    do_matrix(0, 0)
    for copy in small_reads:
        if copy is not stats:
            copy.wait()
    for m in range(2):
        small = gc.at[1 - m, 2 * HID : 2 * HID + 32]
        ge[0:OBS, :] = small[0:OBS, :]
        ge[OBS : OBS + ACT, :] = small[24 : 24 + ACT, :]
        ge[23:24, :] = small[23:24, :]
        gb[0:3, :] = small[17:20, :]
        gb[3:4, :] = small[22:23, :]
        first = 32 * (1 - m)
        o_e[m], o_em[m], o_ev[m] = critic(own_e[m], on_s[first : first + 24], ge[...] * scale, em[m], ev[m])
        o_b[m], o_bm[m], o_bv[m] = critic(own_b[m], on_s[first + 24 : first + 28], gb[0:4, :] * scale, bm[m], bv[m])
    second = lax.broadcasted_iota(jnp.int32, (2, 2), 0) == 1
    row = 2 * HID + 20
    o_ms[...] = jnp.where(second, gc[0, row : row + 1, 0:2], gc[1, row : row + 1, 0:2])
    gae[0:OBS, :] = gas[0:OBS, :]
    gae[OBS : OBS + 2 * ACT, :] = gas[20 : 20 + 2 * ACT, :]
    gab[0:3, :] = gas[17:20, :]
    gab[3:4, :] = rows_a[30:31, :]
    o_ae[...], o_aem[...], o_aev[...] = adamw(ae[...], gae[0:29, :] * scale, aem[...], aev[...])
    o_ab[...], o_abm[...], o_abv[...] = adamw(ab[...], gab[0:4, :] * scale, abm[...], abv[...])
    o_as[...] = rows_a[21:22, 0:2]
    for r in (o_e, o_b, o_em, o_ev, o_bm, o_bv, o_ae, o_ab, o_aem, o_aev, o_abm, o_abv, o_ms, o_as):
        put(write(r))
    for at in order[1:]:
        do_matrix(*at)
    for k in range(2):
        for copy in actor_matrix(k):
            copy.wait()
        grad = ga[k * HID : (k + 1) * HID, :] * scale
        o_ah[k], o_ahm[k], o_ahv[k] = adamw(ah[k], grad, ahm[k], ahv[k])
        for r in (o_ah, o_ahm, o_ahv):
            put(write(r, k, lambda x: x.at[k]))
    for copy in writes:
        copy.wait()


def update(grads, own, online, moments, aparams, amoments):
    shape = lambda *s: jax.ShapeDtypeStruct(s, F32)
    e_, h_, b_ = shape(2, 24, HID), shape(2, 2, HID, HID), shape(2, 4, HID)
    ae_, ah_, ab_ = shape(29, HID), shape(2, HID, HID), shape(4, HID)
    outs = (e_, h_, b_, e_, e_, h_, h_, b_, b_, ae_, ah_, ab_, ae_, ae_, ah_, ah_, ab_, ab_, shape(2, 2), shape(1, 2))
    args = (*grads, *own, *online, *moments, *aparams, *amoments)
    anyspace = pl.BlockSpec(memory_space=pl.ANY)
    room = [pltpu.VMEM(a.shape, a.dtype) for a in args]
    return pl.pallas_call(
        update_kernel,
        out_shape=outs,
        in_specs=[anyspace] * len(args),
        out_specs=(anyspace,) * len(outs),
        scratch_shapes=room
        + [pltpu.VMEM(o.shape, o.dtype) for o in outs]
        + [pltpu.VMEM((24, HID), F32), pltpu.VMEM((8, HID), F32), pltpu.VMEM((32, HID), F32), pltpu.VMEM((8, HID), F32)]
        + [pltpu.SemaphoreType.DMA((len(args), 5)), pltpu.SemaphoreType.DMA((len(outs), 4))],
        compiler_params=pltpu.CompilerParams(vmem_limit_bytes=40 * 2**20),
        name="adamw",
    )(*args)


def body(
    n_dp,
    states, actions, rewards, done, noise, counts,
    crit_edge, crit_hidden, crit_bias, edge_m, edge_v, hidden_m, hidden_v, bias_m, bias_v,
    act_edge, act_hidden, act_bias, act_edge_m, act_edge_v, act_hidden_m, act_hidden_v, act_bias_m, act_bias_v,
):
    size = states.shape[0]
    own = (crit_edge[0], crit_hidden[0], crit_bias[0])
    aparams = (act_edge, act_hidden, act_bias)
    data = (states.T, actions.T, noise.T, rewards[None], done[None], counts)
    moments = (edge_m, edge_v, hidden_m, hidden_v, bias_m, bias_v)
    amoments = (act_edge_m, act_edge_v, act_hidden_m, act_hidden_v, act_bias_m, act_bias_v)
    rows = FOLD_ROWS if size > FOLD_ROWS else size
    grad_c, grad_a, *online = fused(n_dp, rows, rows // 2, True, (*data, rewards[None]), own, aparams)

    def finish(grad_c, grad_a):
        return update((grad_c, grad_a), own, online, moments, aparams, amoments)

    def with_rest():
        z = lax.axis_index("dp")
        partner = lax.ppermute(counts, "dp", [(k, n_dp - 1 - k) for k in range(n_dp)])
        at = jnp.arange(size, dtype=jnp.int32)
        taken = (rows // LANES - 1 - (at - rows) // LANES) * LANES >= (jnp.minimum(partner, rows) + LANES - 1) // LANES * LANES
        taken = jnp.where(z >= n_dp - n_dp // 2, taken, False)
        left = jnp.logical_and(jnp.logical_and(at >= rows, at < counts), jnp.logical_not(taken))
        more_c, more_a, *_ = fused(n_dp, size, size // 16, False, (*data, left.astype(F32)[None]), own, aparams)
        return finish(grad_c + more_c, grad_a + more_a)

    sums = grad_c[1, 2 * HID + 21]
    out = lax.cond(sums[1] != sums[2], with_rest, lambda: finish(grad_c, grad_a))
    return (*(o[None] for o in out[:3]), *out[3:19], out[19][0])


def solution(mesh):
    member = P("grp", "ens", None, None)
    hidden = P("grp", "ens", None, None, None)
    mom = P("ens", None, None)
    mom_h = P("ens", None, None, None)
    return jax.shard_map(
        functools.partial(body, mesh.shape["dp"]),
        mesh=mesh,
        in_specs=(
            P("dp", None), P("dp", None), P("dp"), P("dp"), P("dp", None), P("dp"),
            member, hidden, member, mom, mom, mom_h, mom_h, mom, mom,
        ) + (P(),) * 9,
        out_specs=(member, hidden, member, mom, mom, mom_h, mom_h, mom, mom) + (P(),) * 9 + (P("ens", None), P()),
        check_vma=False,
    )
```
